32 devices in a mesh: dp: 4 (over z), row: 4 (over y, core), col: 2 (over x).
Axes of the slice: x: 2, y: 2, z: 4, core: 2. Of those that a mesh axis runs over, the one named last changes fastest.
Arguments:
- tokens: bfloat16 [768, 4096], P('dp', ('row', 'col')), may hold values from -6 to 6
- in_weight: bfloat16 [4096, 3, 4096], P('dp', None, ('row', 'col')), may hold values from -0.09375 to 0.09375
- short_filter: float32 [3, 3, 4096], P(None, None, ('row', 'col')), may hold values from -3 to 3
- long_filter: bfloat16 [256, 128], P(('row', 'col')), may hold values from -0.59765625 to 0.59765625
- grad_out: bfloat16 [768, 4096], P('dp', ('row', 'col')), may hold values from -6 to 6
Outputs:
- mixed: bfloat16 [768, 4096], P('dp', ('row', 'col'))
- grad_in: bfloat16 [768, 4096], P('dp', ('row', 'col'))
- grad_weight: float32 [4096, 3, 4096], P('dp', None, ('row', 'col'))
- grad_long: float32 [256, 128], P(('row', 'col'))
- grad_short: float32 [3, 3, 4096], P(None, None, ('row', 'col'))
The draws below stay inside these ranges and needn't reach their ends.
All inputs are finite; a program needn't handle non-finite values.
Results may differ from the reference program's by a relative error of at most 0.019.
Values may be sent and summed in bfloat16 or wider, within the bound.
No kernel may reach another device: no remote copies, remote signals or barrier semaphores. Data moves between devices by JAX's collectives and lax.ppermute only.
A program may use at most 128 MiB of HBM per device.

```python
import jax
import jax.numpy as jnp
from jax import lax

DIN = 4096
CH = 4096
GROUP = 16
LTAPS = 128
SHORT = 3
TOK_DEV = 192
TOKENS = 768
GROUPS = 256
N_DP = 4


def strengthened(entries, rng, source, target, shards_of, factor):
    def block_of(axis_at):
        return (jnp.arange(entries.shape[axis_at]) // (entries.shape[axis_at] // shards_of)).reshape((-1,) + (1,) * (entries.ndim - 1 - axis_at))

    first = jax.random.permutation(rng, shards_of)[block_of(target)]
    other_side = (block_of(target) + shards_of // 2) % shards_of
    return jnp.where((block_of(source) == first) | (block_of(source) == other_side), factor * entries, entries)


def steps_of(own_key, dims, split, smallest, high):
    def one(axis_at, blocks):
        draws = jax.random.uniform(jax.random.fold_in(jax.random.fold_in(own_key, 6), axis_at), (blocks,), jnp.float32, smallest / len(split), high / len(split))
        return jnp.repeat(jnp.exp(draws), dims[axis_at] // blocks).reshape((-1,) + (1,) * (len(dims) - axis_at - 1))

    level = one(*split[0])
    for cut in split[1:]:
        level = level * one(*cut)
    return level


def noise(stream_key, extent, spread, limit, cuts=(), kind=jnp.bfloat16):
    drawn = spread * jax.random.normal(stream_key, extent, jnp.float32)
    if cuts:
        drawn = drawn * steps_of(stream_key, extent, cuts, -0.22, 0.18)
    return jnp.clip(drawn, -limit, limit).astype(kind)


def gaussian_with(own_key, dims, spread, most, cuts, heavy, kind=jnp.bfloat16):
    values = spread * jax.random.normal(own_key, dims, jnp.float32)
    if cuts:
        values = values * steps_of(own_key, dims, cuts, -0.22, 0.18)
    return jnp.clip(strengthened(values, jax.random.fold_in(own_key, 3), *heavy), -most, most).astype(kind)


def setup_inputs(seed: int = 0) -> dict:
    streams_of = jax.random.split(jax.random.key(seed), 6)
    tokens = gaussian_with(streams_of[0], (TOKENS, DIN), 1.0, 6.0, ((0, 4), (1, 8)), (0, 1, 8, 2.0))
    in_weight = noise(streams_of[1], (DIN, 3, CH), DIN ** -0.5, 0.09375, ((0, 4), (2, 8)))
    short_filter = noise(streams_of[2], (SHORT, 3, CH), 0.5, 3.0, ((2, 8),), jnp.float32)
    long_filter = noise(streams_of[3], (GROUPS, LTAPS), 0.1, 0.59765625, ((0, 8),))
    grad_out = noise(streams_of[4], (TOKENS, CH), 1.0, 6.0, ((0, 4), (1, 8)))
    return {"tokens": tokens, "in_weight": in_weight, "short_filter": short_filter, "long_filter": long_filter, "grad_out": grad_out}


def reference(tokens, in_weight, short_filter, long_filter, grad_out):
    scale = float(TOKENS) ** -0.5
    flat_w = in_weight.reshape(DIN, 3 * CH)
    mixed_in = jnp.dot(tokens, flat_w, preferred_element_type=jnp.float32).astype(jnp.bfloat16).reshape(TOKENS, 3, CH)
    lead = SHORT - 1
    padded = jnp.pad(mixed_in.astype(jnp.float32), ((lead, 0), (0, 0), (0, 0)))
    feats = jnp.zeros((TOKENS, 3, CH), jnp.float32)
    for j in range(SHORT):
        feats = feats + short_filter[j][None] * padded[lead - j: lead - j + TOKENS]
    product = (feats[:, 1] * feats[:, 2]).astype(jnp.bfloat16)
    taps = jnp.repeat(long_filter.astype(jnp.float32), GROUP, axis=0)
    margin = LTAPS - 1
    prod_pad = jnp.pad(product.astype(jnp.float32), ((margin, 0), (0, 0)))

    def tap_column(j):
        return lax.dynamic_slice_in_dim(taps, j.astype(jnp.int32), 1, 1).reshape(1, CH)

    def conv_step(j, total):
        start = (margin - j).astype(jnp.int32)
        piece = lax.dynamic_slice_in_dim(prod_pad, start, TOKENS, 0)
        return total + tap_column(j) * piece

    conv = lax.fori_loop(0, LTAPS, conv_step, jnp.zeros((TOKENS, CH), jnp.float32))
    mixed = (feats[:, 0] * conv).astype(jnp.bfloat16)

    upstream = grad_out.astype(jnp.float32)
    grad_query = upstream * conv
    grad_conv = (upstream * feats[:, 0]).astype(jnp.bfloat16)
    grad_conv32 = grad_conv.astype(jnp.float32)
    grad_pad = jnp.pad(grad_conv32, ((0, margin), (0, 0)))

    def back_step(j, total):
        piece = lax.dynamic_slice_in_dim(grad_pad, j.astype(jnp.int32), TOKENS, 0)
        return total + tap_column(j) * piece

    grad_product = lax.fori_loop(0, LTAPS, back_step, jnp.zeros((TOKENS, CH), jnp.float32))

    def filter_tap(j):
        start = (margin - j).astype(jnp.int32)
        piece = lax.dynamic_slice_in_dim(prod_pad, start, TOKENS, 0)
        return jnp.sum(grad_conv32 * piece, axis=0).reshape(GROUPS, GROUP).sum(axis=1)

    grad_long = lax.map(filter_tap, jnp.arange(LTAPS, dtype=jnp.int32)).T * scale

    grad_feats = jnp.stack([grad_query, grad_product * feats[:, 2], grad_product * feats[:, 1]], axis=1)
    feats_pad = jnp.pad(grad_feats, ((0, lead), (0, 0), (0, 0)))
    grad_acc = jnp.zeros((TOKENS, 3, CH), jnp.float32)
    for j in range(SHORT):
        grad_acc = grad_acc + short_filter[j][None] * feats_pad[j: j + TOKENS]
    grad_mixed = grad_acc.astype(jnp.bfloat16)
    grad_short = jnp.stack([jnp.sum(grad_feats * padded[lead - j: lead - j + TOKENS], axis=0) for j in range(SHORT)]) * scale

    flat_grad = grad_mixed.reshape(TOKENS, 3 * CH)
    grad_in = jnp.dot(flat_grad, flat_w.T, preferred_element_type=jnp.float32).astype(jnp.bfloat16)

    token_blocks = tokens.reshape(N_DP, TOK_DEV, DIN)
    grad_blocks = flat_grad.reshape(N_DP, TOK_DEV, 3 * CH)

    def add_block(total, pair):
        term = jnp.dot(pair[0].T, pair[1], preferred_element_type=jnp.float32) * scale
        rounded = lax.optimization_barrier(term.astype(jnp.bfloat16))
        return total + rounded.astype(jnp.float32), None

    grad_flat, unused = lax.scan(add_block, jnp.zeros((DIN, 3 * CH), jnp.float32), (token_blocks, grad_blocks))
    grad_weight = grad_flat.reshape(DIN, 3, CH)
    return mixed, grad_in, grad_weight, grad_long, grad_short
```

```python
import functools

import jax
import jax.numpy as jnp
from jax import lax
from jax.experimental import pallas as pl
from jax.experimental.pallas import tpu as pltpu
from jax.sharding import PartitionSpec as P

VMEM_BYTES = 48 * 2**20
F32 = jnp.float32
BF16 = jnp.bfloat16


def kernel_call(body, outs, grid=None, in_specs=None, out_specs=None, flops=0, nbytes=0):
    kwargs = {}
    if grid is not None:
        kwargs = dict(grid=grid, in_specs=in_specs, out_specs=out_specs)
    return pl.pallas_call(
        body,
        out_shape=outs,
        compiler_params=pltpu.CompilerParams(vmem_limit_bytes=VMEM_BYTES),
        cost_estimate=pl.CostEstimate(flops=flops, bytes_accessed=nbytes, transcendentals=0),
        **kwargs,
    )


def shaped(shape, dtype):
    return jax.ShapeDtypeStruct(shape, dtype)


def bands_body(base_ref, out_ref):
    groups, wide = base_ref.shape
    rows = out_ref.shape[1]
    row = lax.broadcasted_iota(jnp.int32, (8, wide), 0)
    for g in range(groups):
        band = jnp.broadcast_to(base_ref[g : g + 1, :], (8, wide))
        for bit in (1, 2, 4):
            band = jnp.where((row & bit) != 0, pltpu.roll(band, bit, 1), band)
        count = 8
        while count < rows:
            band = jnp.concatenate([band, pltpu.roll(band, count, 1)], axis=0)
            count *= 2
        out_ref[g] = band.astype(out_ref.dtype)


def project_body(x_ref, w_ref, out_ref):
    parts, pieces, rows, depth = x_ref.shape
    owners, _, tokens, width = out_ref.shape
    total = jnp.zeros((tokens, w_ref.shape[2]), F32)
    for e in range(pieces):
        total += jnp.dot(
            x_ref[:, e].reshape(tokens, depth),
            w_ref[0, e * depth : (e + 1) * depth],
            preferred_element_type=F32,
        )
    for z in range(owners):
        out_ref[z, 0] = total[:, z * width : (z + 1) * width].astype(BF16)


def input_grad_body(gm_ref, w_ref, out_ref):
    parts, _, rows, depth = out_ref.shape
    owners = gm_ref.shape[0]
    tokens = parts * rows
    total = jnp.zeros((tokens, depth), F32)
    for i in range(w_ref.shape[0]):
        gm = jnp.concatenate([gm_ref[z, i * tokens : (i + 1) * tokens] for z in range(owners)], axis=1)
        total += lax.dot_general(gm, w_ref[i], (((1,), (1,)), ((), ())), preferred_element_type=F32)
    out_ref[:, 0] = total.reshape(parts, rows, depth).astype(BF16)


def weight_grad_body(scale, x_ref, gm_ref, out_ref):
    parts, _, rows, depth = x_ref.shape
    owners, tokens, width = gm_ref.shape
    gm = jnp.concatenate([gm_ref[z] for z in range(owners)], axis=1)
    x = x_ref[:, 0].reshape(tokens, depth)
    out_ref[0] = scale * lax.dot_general(x, gm, (((0,), (0,)), ((), ())), preferred_element_type=F32)


def delayed(values, count):
    row = lax.broadcasted_iota(jnp.int32, values.shape, 0)
    return jnp.where(row >= count, pltpu.roll(values, count, 0), 0.0)


def advanced(values, count):
    rows = values.shape[0]
    row = lax.broadcasted_iota(jnp.int32, values.shape, 0)
    return jnp.where(row < rows - count, pltpu.roll(values, rows - count, 0), 0.0)


def middle_body(scale, nshort, m_ref, sf_ref, causal_ref, anti_ref, go_ref, gm_ref, mixed_ref):
    tokens, width = go_ref.shape
    groups, block, span = causal_ref.shape
    members = width // groups
    nblocks = tokens // block
    lane = lax.broadcasted_iota(jnp.int32, (block, width), 1) // members
    lanes = lax.broadcasted_iota(jnp.int32, (block, 2 * width), 1) % width // members

    def past(i, j):
        held = m_ref[i * tokens : (i + 1) * tokens].astype(F32)
        return held if j == 0 else delayed(held, j)

    def taps(j, i):
        return sf_ref[3 * j + i : 3 * j + i + 1, :]

    feats = [sum(taps(j, i) * past(i, j) for j in range(nshort)) for i in range(3)]
    product = (feats[1] * feats[2]).astype(BF16)
    zero = jnp.zeros((block, width), BF16)
    p_blocks = [zero] + [product[b * block : (b + 1) * block] for b in range(nblocks)]
    p_pairs = [jnp.concatenate(p_blocks[b : b + 2], axis=0) for b in range(nblocks)]

    def filtered(band_ref, pairs):
        bands = band_ref[...].reshape(groups * block, span)
        out = []
        for b in range(0, nblocks, 2):
            both = jnp.dot(bands, jnp.concatenate(pairs[b : b + 2], axis=1), preferred_element_type=F32)
            for h in range(2):
                part = both[:, h * width : (h + 1) * width]
                picked = part[:block]
                for g in range(1, groups):
                    picked = jnp.where(lane == g, part[g * block : (g + 1) * block], picked)
                out.append(picked)
        return jnp.concatenate(out, axis=0)

    conv = filtered(causal_ref, p_pairs)
    upstream = go_ref[...].astype(F32)
    mixed_ref[...] = (feats[0] * conv).astype(BF16)
    grad_conv = (upstream * feats[0]).astype(BF16)
    c_blocks = [grad_conv[b * block : (b + 1) * block] for b in range(nblocks)] + [zero]
    c_pairs = [jnp.concatenate(c_blocks[b : b + 2], axis=0) for b in range(nblocks)]
    grad_product = filtered(anti_ref, c_pairs)

    corr = jnp.zeros((groups * block, span), F32)
    for b in range(0, nblocks, 2):
        left = jnp.concatenate(c_blocks[b : b + 2], axis=1)
        stacked = jnp.concatenate(
            [jnp.where(lanes == g, left, jnp.zeros_like(left)) for g in range(groups)], axis=0
        )
        right = jnp.concatenate(p_pairs[b : b + 2], axis=1)
        corr += lax.dot_general(stacked, right, (((1,), (1,)), ((), ())), preferred_element_type=F32)
    row = lax.broadcasted_iota(jnp.int32, (8, span), 0)
    sums = []
    for g in range(groups):
        part = corr[g * block : (g + 1) * block]
        count = block
        while count > 8:
            count //= 2
            part = part[:count] + pltpu.roll(part[count:], span - count, 1)
        for bit in (1, 2, 4):
            part = jnp.where((row & bit) != 0, pltpu.roll(part, span - bit, 1), part)
        sums.append(jnp.sum(part, axis=0, keepdims=True))
    by_lag = jnp.concatenate(sums, axis=0)
    by_lag = scale * pltpu.roll(by_lag, span - 1, 1)[:, :block]

    grad_feats = [upstream * conv, grad_product * feats[2], grad_product * feats[1]]
    short_rows = []
    for j in range(nshort):
        for i in range(3):
            short_rows.append(scale * jnp.sum(grad_feats[i] * past(i, j), axis=0, keepdims=True))
    for i in range(3):
        total = taps(0, i) * grad_feats[i]
        for j in range(1, nshort):
            total += taps(j, i) * advanced(grad_feats[i], j)
        gm_ref[i * tokens : (i + 1) * tokens] = total.astype(BF16)
    tail = gm_ref.shape[0] - 3 * tokens - groups - 3 * nshort
    small = jnp.concatenate([by_lag] + short_rows + [jnp.zeros((tail, width), F32)], axis=0)
    gm_ref[3 * tokens :] = small.astype(BF16)


def move_activations(tokens, in_weight, short_filter, long_filter, grad_out):
    ndp, nrow, ncol = (lax.axis_size(a) for a in ("dp", "row", "col"))
    z = lax.axis_index("dp")
    rows, dcol = tokens.shape
    local = grad_out.shape[1]
    nshort = short_filter.shape[0]
    ngroups, ntaps = long_filter.shape
    seq = rows * ndp
    width, groups = local // ndp, ngroups // ndp
    drow = in_weight.shape[0]
    scale = float(seq) ** -0.5
    swap = [(a * nrow + b, b * nrow + a) for a in range(ndp) for b in range(nrow)]

    w = jnp.transpose(in_weight, (1, 0, 2))
    moved = lax.ppermute(tokens, ("dp", "row"), swap)
    x = lax.all_gather(moved, ("row", "col"), axis=0).reshape(nrow, ncol, rows, dcol)
    upstream = lax.all_to_all(grad_out, "dp", split_axis=1, concat_axis=0, tiled=True)

    sf = lax.dynamic_slice_in_dim(short_filter, z * width, width, 2).reshape(3 * nshort, width)
    lf = lax.dynamic_slice_in_dim(long_filter, z * groups, groups, 0).astype(F32)
    zeros = functools.partial(jnp.zeros, dtype=F32)
    bases = jnp.concatenate(
        [
            jnp.concatenate([zeros((groups, 1)), lf[:, ::-1], zeros((groups, ntaps - 1))], axis=1),
            jnp.concatenate([lf, zeros((groups, ntaps))], axis=1),
        ],
        axis=0,
    )
    bands = kernel_call(bands_body, shaped((2 * groups, ntaps, 2 * ntaps), BF16))(bases)

    mm_flops = 2 * seq * drow * 3 * local
    partial = kernel_call(
        project_body,
        shaped((ndp, 3, seq, width), BF16),
        grid=(3,),
        in_specs=[
            pl.BlockSpec((nrow, ncol, rows, dcol), lambda i: (0, 0, 0, 0)),
            pl.BlockSpec((1, drow, local), lambda i: (i, 0, 0)),
        ],
        out_specs=pl.BlockSpec((ndp, 1, seq, width), lambda i: (0, i, 0, 0)),
        flops=mm_flops,
        nbytes=2 * (seq * drow + 3 * drow * local + 3 * seq * local),
    )(x, w)
    mixed_in = lax.psum_scatter(partial.reshape(ndp, 3 * seq, width), "dp", scatter_dimension=0)

    extra = -(-(groups + 3 * nshort) // 16) * 16
    half = pl.BlockSpec((groups, ntaps, 2 * ntaps), lambda i: (0, 0, 0))
    other = pl.BlockSpec((groups, ntaps, 2 * ntaps), lambda i: (1, 0, 0))
    whole = lambda shape: pl.BlockSpec(shape, lambda i: (0,) * len(shape))
    gm_rows = 3 * seq + extra
    grad_mixed, mixed = kernel_call(
        functools.partial(middle_body, scale, nshort),
        (shaped((gm_rows, width), BF16), shaped((seq, width), BF16)),
        grid=(1,),
        in_specs=[whole((3 * seq, width)), whole((3 * nshort, width)), half, other, whole((seq, width))],
        out_specs=(whole((gm_rows, width)), whole((seq, width))),
        flops=3 * 2 * groups * ntaps * 2 * ntaps * width * (seq // ntaps),
        nbytes=2 * width * seq * 10,
    )(mixed_in, sf, bands, bands, upstream)
    gathered = lax.all_gather(grad_mixed, "dp", axis=0)
    mixed = lax.all_to_all(mixed, "dp", split_axis=0, concat_axis=1, tiled=True)

    partial_in = kernel_call(
        input_grad_body,
        shaped((nrow, ncol, rows, dcol), BF16),
        grid=(ncol,),
        in_specs=[
            pl.BlockSpec((ndp, gm_rows, width), lambda e: (0, 0, 0)),
            pl.BlockSpec((3, dcol, local), lambda e: (0, e, 0)),
        ],
        out_specs=pl.BlockSpec((nrow, 1, rows, dcol), lambda e: (0, e, 0, 0)),
        flops=mm_flops,
        nbytes=2 * (seq * drow + 3 * drow * local + 3 * seq * local),
    )(gathered, w)
    summed = lax.psum_scatter(
        partial_in.reshape(nrow * ncol, rows, dcol), ("row", "col"), scatter_dimension=0
    )
    grad_in = lax.ppermute(summed, ("dp", "row"), swap)

    grad_weight = kernel_call(
        functools.partial(weight_grad_body, scale),
        shaped((3, drow, local), F32),
        grid=(3, ncol),
        in_specs=[
            pl.BlockSpec((nrow, 1, rows, dcol), lambda i, e: (0, e, 0, 0)),
            pl.BlockSpec((ndp, seq, width), lambda i, e: (0, i, 0)),
        ],
        out_specs=pl.BlockSpec((1, dcol, local), lambda i, e: (i, e, 0)),
        flops=mm_flops,
        nbytes=2 * (seq * drow + 6 * drow * local + 3 * seq * local),
    )(x, gathered)
    grad_weight = jnp.transpose(grad_weight, (1, 0, 2))
    small = gathered[:, 3 * seq :].astype(F32)
    grad_long = small[:, :groups, ::-1].reshape(ngroups, ntaps)
    grad_short = (
        small[:, groups : groups + 3 * nshort].transpose(1, 0, 2).reshape(nshort, 3, local)
    )
    return (mixed, grad_in, grad_weight, grad_long, grad_short)


def from_behind(block, axis, distance):
    devices = range(lax.axis_size(axis))
    route = [(i - distance, i) for i in devices if i - distance in devices]
    return lax.ppermute(block, axis, route)


def toeplitz(leading, rows, span):
    groups = leading.shape[0]
    width = rows + span
    seed_row = jnp.concatenate(
        [leading, jnp.zeros((groups, width - leading.shape[1]), leading.dtype)], axis=1
    )
    tiled = jnp.tile(seed_row, (1, rows))
    skewed = tiled[:, : rows * (width - 1)].reshape(groups, rows, width - 1)
    return skewed[:, :, :span]


def to_groups(values, ngroups, members):
    count = values.shape[0]
    return values.reshape(count, ngroups, members).transpose(1, 2, 0)


def from_groups(values):
    groups, members, count = values.shape
    return values.transpose(2, 0, 1).reshape(count, groups * members)


def move_weights(tokens, in_weight, short_filter, long_filter, grad_out):
    rows = tokens.shape[0]
    local = grad_out.shape[1]
    nshort = short_filter.shape[0]
    ntaps = long_filter.shape[1]
    ngroups = long_filter.shape[0]
    members = local // ngroups
    margin = ntaps - 1
    span = rows + margin
    scale = float(rows * lax.axis_size("dp")) ** (-0.5)
    whole = lax.all_gather(tokens, ("row", "col"), axis=1, tiled=True)
    full_w = lax.all_gather(in_weight, "dp", axis=0, tiled=True)
    mixed_in = jnp.einsum("sd,dic->sic", whole, full_w, preferred_element_type=jnp.float32).astype(
        jnp.bfloat16
    )
    before = from_behind(mixed_in[rows - margin - nshort + 1 :], "dp", 1)
    extended = jnp.concatenate([before, mixed_in], axis=0).astype(jnp.float32)
    long_feats = jnp.zeros((span, 3, local), jnp.float32)
    for j in range(nshort):
        long_feats = (
            long_feats + short_filter[j][None] * extended[nshort - 1 - j : nshort - 1 - j + span]
        )
    product_ext = (long_feats[:, 1] * long_feats[:, 2]).astype(jnp.bfloat16)
    feats = long_feats[margin:]
    short_rows = extended[margin:]
    product_cols = to_groups(product_ext, ngroups, members)
    causal = toeplitz(long_filter[:, ::-1], rows, span)
    conv = from_groups(
        jnp.einsum("gst,gct->gcs", causal, product_cols, preferred_element_type=jnp.float32)
    )
    mixed = (feats[:, 0] * conv).astype(jnp.bfloat16)
    upstream = grad_out.astype(jnp.float32)
    grad_query = upstream * conv
    grad_conv = (upstream * feats[:, 0]).astype(jnp.bfloat16)
    after = from_behind(grad_conv[:margin], "dp", -1)
    grad_ext = jnp.concatenate([grad_conv, after], axis=0)
    anti = toeplitz(long_filter, rows, span)
    grad_product = from_groups(
        jnp.einsum(
            "gst,gct->gcs",
            anti,
            to_groups(grad_ext, ngroups, members),
            preferred_element_type=jnp.float32,
        )
    )
    reversed_cols = jnp.concatenate(
        [product_cols[:, :, ::-1], jnp.zeros((ngroups, members, rows), product_cols.dtype)], axis=2
    )
    width = span + rows
    pairs = jnp.einsum(
        "gcs,gcu->gsu",
        to_groups(grad_conv, ngroups, members),
        reversed_cols,
        preferred_element_type=jnp.float32,
    )
    diagonal = pairs.reshape(ngroups, rows * width)[:, : rows * (width - 1)].reshape(
        ngroups, rows, width - 1
    )
    filter_part = jnp.sum(diagonal[:, :, rows - 1 : rows - 1 + ntaps], axis=1)
    grad_feats = jnp.stack(
        [grad_query, grad_product * feats[:, 2], grad_product * feats[:, 1]], axis=1
    )
    later = from_behind(grad_feats[: nshort - 1], "dp", -1)
    feats_ext = jnp.concatenate([grad_feats, later], axis=0)
    grad_acc = jnp.zeros((rows, 3, local), jnp.float32)
    for j in range(nshort):
        grad_acc = grad_acc + short_filter[j][None] * feats_ext[j : j + rows]
    grad_mixed = grad_acc.astype(jnp.bfloat16)
    short_part = jnp.stack(
        [
            jnp.sum(grad_feats * short_rows[nshort - 1 - j : nshort - 1 - j + rows], axis=0)
            for j in range(nshort)
        ]
    )
    filter_total, short_total = (
        lax.psum(filter_part.astype(jnp.bfloat16), "dp").astype(jnp.float32),
        lax.psum(short_part.astype(jnp.bfloat16), "dp").astype(jnp.float32),
    )
    grad_long = filter_total * scale
    grad_short = short_total * scale
    partial_in = jnp.einsum("sic,dic->sd", grad_mixed, full_w, preferred_element_type=jnp.float32)
    summed_in = lax.psum_scatter(
        partial_in.astype(jnp.bfloat16), ("row", "col"), scatter_dimension=1, tiled=True
    )
    weight_term = (
        jnp.einsum("sd,sic->dic", whole, grad_mixed, preferred_element_type=jnp.float32) * scale
    )
    grad_weight = lax.psum_scatter(
        weight_term.astype(jnp.bfloat16), "dp", scatter_dimension=0, tiled=True
    ).astype(jnp.float32)
    return (mixed, summed_in, grad_weight, grad_long, grad_short)


def fits_whole_sequences(mesh, tokens, in_weight, short_filter, long_filter, grad_out):
    ndp, nrow, ncol = (mesh.shape[a] for a in ("dp", "row", "col"))
    seq, channels = grad_out.shape
    groups, ntaps = long_filter.shape
    local = channels // (nrow * ncol)
    width, rows = local // ndp, seq // ndp
    return (
        seq < tokens.shape[1]
        and ndp == nrow
        and ntaps == width == 128
        and seq % (2 * ntaps) == 0
        and rows % 16 == 0
        and groups % (8 * ndp * nrow * ncol) == 0
    )


def solution(mesh):
    placed = (
        P("dp", ("row", "col")),
        P("dp", None, ("row", "col")),
        P(None, None, ("row", "col")),
        P(("row", "col"), None),
        P("dp", ("row", "col")),
    )
    gives = (
        P("dp", ("row", "col")),
        P("dp", ("row", "col")),
        P("dp", None, ("row", "col")),
        P(("row", "col"), None),
        P(None, None, ("row", "col")),
    )

    def run(*arrays):
        plan = move_activations if fits_whole_sequences(mesh, *arrays) else move_weights
        return jax.shard_map(
            plan, mesh=mesh, in_specs=placed, out_specs=gives, check_vma=False
        )(*arrays)

    return run
```

```python
import functools

import jax
import jax.numpy as jnp
from jax import lax
from jax.experimental import pallas as pl
from jax.experimental.pallas import tpu as pltpu
from jax.sharding import PartitionSpec as P

VMEM_BYTES = 48 * 2**20
F32 = jnp.float32
BF16 = jnp.bfloat16


def kernel_call(body, outs, grid=None, in_specs=None, out_specs=None, flops=0, nbytes=0):
    kwargs = {}
    if grid is not None:
        kwargs = dict(grid=grid, in_specs=in_specs, out_specs=out_specs)
    return pl.pallas_call(
        body,
        out_shape=outs,
        compiler_params=pltpu.CompilerParams(vmem_limit_bytes=VMEM_BYTES),
        cost_estimate=pl.CostEstimate(flops=flops, bytes_accessed=nbytes, transcendentals=0),
        **kwargs,
    )


def shaped(shape, dtype):
    return jax.ShapeDtypeStruct(shape, dtype)


def bands_body(base_ref, out_ref):
    groups, wide = base_ref.shape
    rows = out_ref.shape[1]
    row = lax.broadcasted_iota(jnp.int32, (8, wide), 0)
    for g in range(groups):
        band = jnp.broadcast_to(base_ref[g : g + 1, :], (8, wide))
        for bit in (1, 2, 4):
            band = jnp.where((row & bit) != 0, pltpu.roll(band, bit, 1), band)
        count = 8
        while count < rows:
            band = jnp.concatenate([band, pltpu.roll(band, count, 1)], axis=0)
            count *= 2
        out_ref[g] = band.astype(out_ref.dtype)


def project_body(x_ref, w_ref, out_ref):
    parts, pieces, rows, depth = x_ref.shape
    owners, _, tokens, width = out_ref.shape
    total = jnp.zeros((tokens, w_ref.shape[2]), F32)
    for e in range(pieces):
        total += jnp.dot(
            x_ref[:, e].reshape(tokens, depth),
            w_ref[0, e * depth : (e + 1) * depth],
            preferred_element_type=F32,
        )
    for z in range(owners):
        out_ref[z, 0] = total[:, z * width : (z + 1) * width].astype(BF16)


def input_grad_body(gm_ref, w_ref, out_ref):
    parts, _, rows, depth = out_ref.shape
    owners = gm_ref.shape[0]
    tokens = parts * rows
    total = jnp.zeros((tokens, depth), F32)
    for i in range(w_ref.shape[0]):
        gm = jnp.concatenate([gm_ref[z, i * tokens : (i + 1) * tokens] for z in range(owners)], axis=1)
        total += lax.dot_general(gm, w_ref[i], (((1,), (1,)), ((), ())), preferred_element_type=F32)
    out_ref[:, 0] = total.reshape(parts, rows, depth).astype(BF16)


def weight_grad_body(scale, x_ref, gm_ref, out_ref):
    parts, _, rows, depth = x_ref.shape
    owners, tokens, width = gm_ref.shape
    gm = jnp.concatenate([gm_ref[z] for z in range(owners)], axis=1)
    x = x_ref[:, 0].reshape(tokens, depth)
    out_ref[0] = scale * lax.dot_general(x, gm, (((0,), (0,)), ((), ())), preferred_element_type=F32)


def delayed(values, count):
    row = lax.broadcasted_iota(jnp.int32, values.shape, 0)
    return jnp.where(row >= count, pltpu.roll(values, count, 0), 0.0)


def advanced(values, count):
    rows = values.shape[0]
    row = lax.broadcasted_iota(jnp.int32, values.shape, 0)
    return jnp.where(row < rows - count, pltpu.roll(values, rows - count, 0), 0.0)


def middle_body(scale, nshort, m_ref, sf_ref, causal_ref, anti_ref, go_ref, gm_ref, mixed_ref):
    tokens, width = go_ref.shape
    groups, block, span = causal_ref.shape
    members = width // groups
    nblocks = tokens // block
    lane = lax.broadcasted_iota(jnp.int32, (block, width), 1) // members
    lanes = lax.broadcasted_iota(jnp.int32, (block, 2 * width), 1) % width // members

    def past(i, j):
        held = m_ref[i * tokens : (i + 1) * tokens].astype(F32)
        return held if j == 0 else delayed(held, j)

    def taps(j, i):
        return sf_ref[3 * j + i : 3 * j + i + 1, :]

    feats = [sum(taps(j, i) * past(i, j) for j in range(nshort)) for i in range(3)]
    product = (feats[1] * feats[2]).astype(BF16)
    zero = jnp.zeros((block, width), BF16)
    p_blocks = [zero] + [product[b * block : (b + 1) * block] for b in range(nblocks)]
    p_pairs = [jnp.concatenate(p_blocks[b : b + 2], axis=0) for b in range(nblocks)]

    def filtered(band_ref, pairs):
        bands = band_ref[...].reshape(groups * block, span)
        out = []
        for b in range(0, nblocks, 2):
            both = jnp.dot(bands, jnp.concatenate(pairs[b : b + 2], axis=1), preferred_element_type=F32)
            for h in range(2):
                part = both[:, h * width : (h + 1) * width]
                picked = part[:block]
                for g in range(1, groups):
                    picked = jnp.where(lane == g, part[g * block : (g + 1) * block], picked)
                out.append(picked)
        return jnp.concatenate(out, axis=0)

    conv = filtered(causal_ref, p_pairs)
    upstream = go_ref[...].astype(F32)
    mixed_ref[...] = (feats[0] * conv).astype(BF16)
    grad_conv = (upstream * feats[0]).astype(BF16)
    c_blocks = [grad_conv[b * block : (b + 1) * block] for b in range(nblocks)] + [zero]
    c_pairs = [jnp.concatenate(c_blocks[b : b + 2], axis=0) for b in range(nblocks)]
    grad_product = filtered(anti_ref, c_pairs)

    corr = jnp.zeros((groups * block, span), F32)
    for b in range(0, nblocks, 2):
        left = jnp.concatenate(c_blocks[b : b + 2], axis=1)
        stacked = jnp.concatenate(
            [jnp.where(lanes == g, left, jnp.zeros_like(left)) for g in range(groups)], axis=0
        )
        right = jnp.concatenate(p_pairs[b : b + 2], axis=1)
        corr += lax.dot_general(stacked, right, (((1,), (1,)), ((), ())), preferred_element_type=F32)
    row = lax.broadcasted_iota(jnp.int32, (8, span), 0)
    sums = []
    for g in range(groups):
        part = corr[g * block : (g + 1) * block]
        count = block
        while count > 8:
            count //= 2
            part = part[:count] + pltpu.roll(part[count:], span - count, 1)
        for bit in (1, 2, 4):
            part = jnp.where((row & bit) != 0, pltpu.roll(part, span - bit, 1), part)
        sums.append(jnp.sum(part, axis=0, keepdims=True))
    by_lag = jnp.concatenate(sums, axis=0)
    by_lag = scale * pltpu.roll(by_lag, span - 1, 1)[:, :block]

    grad_feats = [upstream * conv, grad_product * feats[2], grad_product * feats[1]]
    short_rows = []
    for j in range(nshort):
        for i in range(3):
            short_rows.append(scale * jnp.sum(grad_feats[i] * past(i, j), axis=0, keepdims=True))
    for i in range(3):
        total = taps(0, i) * grad_feats[i]
        for j in range(1, nshort):
            total += taps(j, i) * advanced(grad_feats[i], j)
        gm_ref[i * tokens : (i + 1) * tokens] = total.astype(BF16)
    tail = gm_ref.shape[0] - 3 * tokens - groups - 3 * nshort
    small = jnp.concatenate([by_lag] + short_rows + [jnp.zeros((tail, width), F32)], axis=0)
    gm_ref[3 * tokens :] = small.astype(BF16)


def move_activations(tokens, in_weight, short_filter, long_filter, grad_out):
    ndp, nrow, ncol = (lax.axis_size(a) for a in ("dp", "row", "col"))
    z = lax.axis_index("dp")
    rows, dcol = tokens.shape
    local = grad_out.shape[1]
    nshort = short_filter.shape[0]
    ngroups, ntaps = long_filter.shape
    seq = rows * ndp
    width, groups = local // ndp, ngroups // ndp
    drow = in_weight.shape[0]
    scale = float(seq) ** -0.5
    swap = [(a * nrow + b, b * nrow + a) for a in range(ndp) for b in range(nrow)]

    w = jnp.transpose(in_weight, (1, 0, 2))
    moved = lax.ppermute(tokens, ("dp", "row"), swap)
    x = lax.all_gather(moved, ("row", "col"), axis=0).reshape(nrow, ncol, rows, dcol)
    upstream = lax.all_to_all(grad_out, "dp", split_axis=1, concat_axis=0, tiled=True)

    sf = lax.dynamic_slice_in_dim(short_filter, z * width, width, 2).reshape(3 * nshort, width)
    lf = lax.dynamic_slice_in_dim(long_filter, z * groups, groups, 0).astype(F32)
    zeros = functools.partial(jnp.zeros, dtype=F32)
    bases = jnp.concatenate(
        [
            jnp.concatenate([zeros((groups, 1)), lf[:, ::-1], zeros((groups, ntaps - 1))], axis=1),
            jnp.concatenate([lf, zeros((groups, ntaps))], axis=1),
        ],
        axis=0,
    )
    bands = kernel_call(bands_body, shaped((2 * groups, ntaps, 2 * ntaps), BF16))(bases)

    mm_flops = 2 * seq * drow * 3 * local
    partial = kernel_call(
        project_body,
        shaped((ndp, 3, seq, width), BF16),
        grid=(3,),
        in_specs=[
            pl.BlockSpec((nrow, ncol, rows, dcol), lambda i: (0, 0, 0, 0)),
            pl.BlockSpec((1, drow, local), lambda i: (i, 0, 0)),
        ],
        out_specs=pl.BlockSpec((ndp, 1, seq, width), lambda i: (0, i, 0, 0)),
        flops=mm_flops,
        nbytes=2 * (seq * drow + 3 * drow * local + 3 * seq * local),
    )(x, w)
    mixed_in = lax.psum_scatter(partial.reshape(ndp, 3 * seq, width), "dp", scatter_dimension=0)

    extra = -(-(groups + 3 * nshort) // 16) * 16
    half = pl.BlockSpec((groups, ntaps, 2 * ntaps), lambda i: (0, 0, 0))
    other = pl.BlockSpec((groups, ntaps, 2 * ntaps), lambda i: (1, 0, 0))
    whole = lambda shape: pl.BlockSpec(shape, lambda i: (0,) * len(shape))
    gm_rows = 3 * seq + extra
    grad_mixed, mixed = kernel_call(
        functools.partial(middle_body, scale, nshort),
        (shaped((gm_rows, width), BF16), shaped((seq, width), BF16)),
        grid=(1,),
        in_specs=[whole((3 * seq, width)), whole((3 * nshort, width)), half, other, whole((seq, width))],
        out_specs=(whole((gm_rows, width)), whole((seq, width))),
        flops=3 * 2 * groups * ntaps * 2 * ntaps * width * (seq // ntaps),
        nbytes=2 * width * seq * 10,
    )(mixed_in, sf, bands, bands, upstream)
    gathered = lax.all_gather(grad_mixed, "dp", axis=0)
    mixed = lax.all_to_all(mixed, "dp", split_axis=0, concat_axis=1, tiled=True)

    partial_in = kernel_call(
        input_grad_body,
        shaped((nrow, ncol, rows, dcol), BF16),
        grid=(ncol,),
        in_specs=[
            pl.BlockSpec((ndp, gm_rows, width), lambda e: (0, 0, 0)),
            pl.BlockSpec((3, dcol, local), lambda e: (0, e, 0)),
        ],
        out_specs=pl.BlockSpec((nrow, 1, rows, dcol), lambda e: (0, e, 0, 0)),
        flops=mm_flops,
        nbytes=2 * (seq * drow + 3 * drow * local + 3 * seq * local),
    )(gathered, w)
    spread = lax.all_to_all(
        partial_in.reshape(nrow * ncol, rows, dcol), ("row", "col"), split_axis=0, concat_axis=0, tiled=True
    )
    summed = jnp.sum(spread.astype(F32), axis=0).astype(BF16)
    grad_in = lax.ppermute(summed, ("dp", "row"), swap)

    grad_weight = kernel_call(
        functools.partial(weight_grad_body, scale),
        shaped((3, drow, local), F32),
        grid=(3, ncol),
        in_specs=[
            pl.BlockSpec((nrow, 1, rows, dcol), lambda i, e: (0, e, 0, 0)),
            pl.BlockSpec((ndp, seq, width), lambda i, e: (0, i, 0)),
        ],
        out_specs=pl.BlockSpec((1, dcol, local), lambda i, e: (i, e, 0)),
        flops=mm_flops,
        nbytes=2 * (seq * drow + 6 * drow * local + 3 * seq * local),
    )(x, gathered)
    grad_weight = jnp.transpose(grad_weight, (1, 0, 2))
    small = gathered[:, 3 * seq :].astype(F32)
    grad_long = small[:, :groups, ::-1].reshape(ngroups, ntaps)
    grad_short = (
        small[:, groups : groups + 3 * nshort].transpose(1, 0, 2).reshape(nshort, 3, local)
    )
    return (mixed, grad_in, grad_weight, grad_long, grad_short)


def from_behind(block, axis, distance):
    devices = range(lax.axis_size(axis))
    route = [(i - distance, i) for i in devices if i - distance in devices]
    return lax.ppermute(block, axis, route)


def toeplitz(leading, rows, span):
    groups = leading.shape[0]
    width = rows + span
    seed_row = jnp.concatenate(
        [leading, jnp.zeros((groups, width - leading.shape[1]), leading.dtype)], axis=1
    )
    tiled = jnp.tile(seed_row, (1, rows))
    skewed = tiled[:, : rows * (width - 1)].reshape(groups, rows, width - 1)
    return skewed[:, :, :span]


def to_groups(values, ngroups, members):
    count = values.shape[0]
    return values.reshape(count, ngroups, members).transpose(1, 2, 0)


def from_groups(values):
    groups, members, count = values.shape
    return values.transpose(2, 0, 1).reshape(count, groups * members)


def move_weights(tokens, in_weight, short_filter, long_filter, grad_out):
    rows = tokens.shape[0]
    local = grad_out.shape[1]
    nshort = short_filter.shape[0]
    ntaps = long_filter.shape[1]
    ngroups = long_filter.shape[0]
    members = local // ngroups
    margin = ntaps - 1
    span = rows + margin
    scale = float(rows * lax.axis_size("dp")) ** (-0.5)
    whole = lax.all_gather(tokens, ("row", "col"), axis=1, tiled=True)
    full_w = lax.all_gather(in_weight, "dp", axis=0, tiled=True)
    mixed_in = jnp.einsum("sd,dic->sic", whole, full_w, preferred_element_type=jnp.float32).astype(
        jnp.bfloat16
    )
    before = from_behind(mixed_in[rows - margin - nshort + 1 :], "dp", 1)
    extended = jnp.concatenate([before, mixed_in], axis=0).astype(jnp.float32)
    long_feats = jnp.zeros((span, 3, local), jnp.float32)
    for j in range(nshort):
        long_feats = (
            long_feats + short_filter[j][None] * extended[nshort - 1 - j : nshort - 1 - j + span]
        )
    product_ext = (long_feats[:, 1] * long_feats[:, 2]).astype(jnp.bfloat16)
    feats = long_feats[margin:]
    short_rows = extended[margin:]
    product_cols = to_groups(product_ext, ngroups, members)
    causal = toeplitz(long_filter[:, ::-1], rows, span)
    conv = from_groups(
        jnp.einsum("gst,gct->gcs", causal, product_cols, preferred_element_type=jnp.float32)
    )
    mixed = (feats[:, 0] * conv).astype(jnp.bfloat16)
    upstream = grad_out.astype(jnp.float32)
    grad_query = upstream * conv
    grad_conv = (upstream * feats[:, 0]).astype(jnp.bfloat16)
    after = from_behind(grad_conv[:margin], "dp", -1)
    grad_ext = jnp.concatenate([grad_conv, after], axis=0)
    anti = toeplitz(long_filter, rows, span)
    grad_product = from_groups(
        jnp.einsum(
            "gst,gct->gcs",
            anti,
            to_groups(grad_ext, ngroups, members),
            preferred_element_type=jnp.float32,
        )
    )
    reversed_cols = jnp.concatenate(
        [product_cols[:, :, ::-1], jnp.zeros((ngroups, members, rows), product_cols.dtype)], axis=2
    )
    width = span + rows
    pairs = jnp.einsum(
        "gcs,gcu->gsu",
        to_groups(grad_conv, ngroups, members),
        reversed_cols,
        preferred_element_type=jnp.float32,
    )
    diagonal = pairs.reshape(ngroups, rows * width)[:, : rows * (width - 1)].reshape(
        ngroups, rows, width - 1
    )
    filter_part = jnp.sum(diagonal[:, :, rows - 1 : rows - 1 + ntaps], axis=1)
    grad_feats = jnp.stack(
        [grad_query, grad_product * feats[:, 2], grad_product * feats[:, 1]], axis=1
    )
    later = from_behind(grad_feats[: nshort - 1], "dp", -1)
    feats_ext = jnp.concatenate([grad_feats, later], axis=0)
    grad_acc = jnp.zeros((rows, 3, local), jnp.float32)
    for j in range(nshort):
        grad_acc = grad_acc + short_filter[j][None] * feats_ext[j : j + rows]
    grad_mixed = grad_acc.astype(jnp.bfloat16)
    short_part = jnp.stack(
        [
            jnp.sum(grad_feats * short_rows[nshort - 1 - j : nshort - 1 - j + rows], axis=0)
            for j in range(nshort)
        ]
    )
    filter_total, short_total = (
        lax.psum(filter_part.astype(jnp.bfloat16), "dp").astype(jnp.float32),
        lax.psum(short_part.astype(jnp.bfloat16), "dp").astype(jnp.float32),
    )
    grad_long = filter_total * scale
    grad_short = short_total * scale
    partial_in = jnp.einsum("sic,dic->sd", grad_mixed, full_w, preferred_element_type=jnp.float32)
    summed_in = lax.psum_scatter(
        partial_in.astype(jnp.bfloat16), ("row", "col"), scatter_dimension=1, tiled=True
    )
    weight_term = (
        jnp.einsum("sd,sic->dic", whole, grad_mixed, preferred_element_type=jnp.float32) * scale
    )
    grad_weight = lax.psum_scatter(
        weight_term.astype(jnp.bfloat16), "dp", scatter_dimension=0, tiled=True
    ).astype(jnp.float32)
    return (mixed, summed_in, grad_weight, grad_long, grad_short)


def fits_whole_sequences(mesh, tokens, in_weight, short_filter, long_filter, grad_out):
    ndp, nrow, ncol = (mesh.shape[a] for a in ("dp", "row", "col"))
    seq, channels = grad_out.shape
    groups, ntaps = long_filter.shape
    local = channels // (nrow * ncol)
    width, rows = local // ndp, seq // ndp
    return (
        seq < tokens.shape[1]
        and ndp == nrow
        and ntaps == width == 128
        and seq % (2 * ntaps) == 0
        and rows % 16 == 0
        and groups % (8 * ndp * nrow * ncol) == 0
    )


def solution(mesh):
    placed = (
        P("dp", ("row", "col")),
        P("dp", None, ("row", "col")),
        P(None, None, ("row", "col")),
        P(("row", "col"), None),
        P("dp", ("row", "col")),
    )
    gives = (
        P("dp", ("row", "col")),
        P("dp", ("row", "col")),
        P("dp", None, ("row", "col")),
        P(("row", "col"), None),
        P(None, None, ("row", "col")),
    )

    def run(*arrays):
        plan = move_activations if fits_whole_sequences(mesh, *arrays) else move_weights
        return jax.shard_map(
            plan, mesh=mesh, in_specs=placed, out_specs=gives, check_vma=False
        )(*arrays)

    return run
```

```python
import functools

import jax
import jax.numpy as jnp
from jax import lax
from jax.experimental import pallas as pl
from jax.experimental.pallas import tpu as pltpu
from jax.sharding import PartitionSpec as P

VMEM_BYTES = 48 * 2**20
F32 = jnp.float32
BF16 = jnp.bfloat16


def kernel_call(body, outs, grid=None, in_specs=None, out_specs=None, scratch=(), flops=0, nbytes=0):
    kwargs = {}
    if grid is not None:
        kwargs = dict(grid=grid, in_specs=in_specs, out_specs=out_specs)
    return pl.pallas_call(
        body,
        out_shape=outs,
        scratch_shapes=scratch,
        compiler_params=pltpu.CompilerParams(vmem_limit_bytes=VMEM_BYTES),
        cost_estimate=pl.CostEstimate(flops=flops, bytes_accessed=nbytes, transcendentals=0),
        **kwargs,
    )


def shaped(shape, dtype):
    return jax.ShapeDtypeStruct(shape, dtype)


def bands_body(base_ref, out_ref):
    groups, wide = base_ref.shape
    rows = out_ref.shape[1]
    row = lax.broadcasted_iota(jnp.int32, (8, wide), 0)
    for g in range(groups):
        band = jnp.broadcast_to(base_ref[g : g + 1, :], (8, wide))
        for bit in (1, 2, 4):
            band = jnp.where((row & bit) != 0, pltpu.roll(band, bit, 1), band)
        count = 8
        while count < rows:
            band = jnp.concatenate([band, pltpu.roll(band, count, 1)], axis=0)
            count *= 2
        out_ref[g] = band.astype(out_ref.dtype)


def wrapped(value, size):
    return lax.rem(value + 2 * size, size)


def project_body(x_ref, w_ref, *refs):
    *out_refs, held = refs
    z, col = lax.axis_index("dp"), lax.axis_index("col")
    nblocks, ncol, rows, depth = x_ref.shape
    width = held.shape[2]
    total = jnp.zeros((nblocks * rows, w_ref.shape[2]), F32)
    for dx in range(ncol):
        start = pl.multiple_of(wrapped(col - dx, ncol) * depth, depth)
        total += jnp.dot(
            x_ref[:, dx].reshape(nblocks * rows, depth),
            w_ref[0, pl.ds(start, depth), :],
            preferred_element_type=F32,
        )
    for owner in range(len(out_refs)):
        held[owner] = total[:, owner * width : (owner + 1) * width].astype(BF16)
    for ahead, out_ref in enumerate(out_refs):
        out_ref[0] = held[wrapped(z + ahead, len(out_refs))]


def assemble(pieces, held, ndp):
    z = lax.axis_index("dp")
    own, before, after, far_before, far_after = pieces
    held[z] = own[...]
    held[wrapped(z - 1, ndp)] = before[...]
    held[wrapped(z + 1, ndp)] = after[...]

    @pl.when(z >= ndp // 2)
    def _():
        held[z - ndp // 2] = far_before[...]

    @pl.when(z < ndp // 2)
    def _():
        held[z + ndp // 2] = far_after[...]


def input_grads(held, w_ref, all_ref, ncol):
    ndp = held.shape[0]
    tokens, depth = all_ref.shape[1], w_ref.shape[1] // ncol
    col = lax.axis_index("col")
    for i in range(3):
        for owner in range(ndp):
            width = held.shape[2]
            all_ref[i, :, owner * width : (owner + 1) * width] = held[owner, i * tokens : (i + 1) * tokens]
    for dx in range(ncol):
        start = pl.multiple_of(wrapped(col - dx, ncol) * depth, depth)
        total = jnp.zeros((tokens, depth), F32)
        for i in range(3):
            total += lax.dot_general(
                all_ref[i],
                w_ref[i, pl.ds(start, depth), :],
                (((1,), (1,)), ((), ())),
                preferred_element_type=F32,
            )
        yield dx, total


def first_grad_body(own, before, after, far_before, far_after, w_ref, out_ref, all_ref, small_ref, held):
    nblocks, ncol, rows, depth = out_ref.shape
    assemble((own, before, after, far_before, far_after), held, held.shape[0])
    small_ref[...] = held[:, 3 * nblocks * rows :]
    for dx, total in input_grads(held, w_ref, all_ref, ncol):
        out_ref[:, dx] = total.reshape(nblocks, rows, depth).astype(BF16)


def second_grad_body(own, before, after, far_before, far_after, w_ref, other_ref, all_ref, *refs):
    *out_refs, held = refs
    nblocks, ncol, rows, depth = other_ref.shape
    assemble((own, before, after, far_before, far_after), held, held.shape[0])
    for dx, total in input_grads(held, w_ref, all_ref, ncol):
        for block in range(nblocks):
            both = total[block * rows : (block + 1) * rows] + other_ref[block, dx].astype(F32)
            out_refs[block * ncol + dx][...] = both.astype(BF16)


def weight_grad_body(scale, x0_ref, x1_ref, g0_ref, g1_ref, out_ref):
    nblocks, ncol, rows, depth = x0_ref.shape
    col = lax.axis_index("col")
    gm = jnp.concatenate([g0_ref[0], g1_ref[0]], axis=0)
    for dx in range(ncol):
        start = pl.multiple_of(wrapped(col - dx, ncol) * depth, depth)
        x = jnp.concatenate(
            [x_ref[:, dx].reshape(nblocks * rows, depth) for x_ref in (x0_ref, x1_ref)], axis=0
        )
        out_ref[0, pl.ds(start, depth), :] = scale * lax.dot_general(
            x, gm, (((0,), (0,)), ((), ())), preferred_element_type=F32
        )


def delayed(values, count):
    row = lax.broadcasted_iota(jnp.int32, values.shape, 0)
    return jnp.where(row >= count, pltpu.roll(values, count, 0), 0.0)


def advanced(values, count):
    rows = values.shape[0]
    row = lax.broadcasted_iota(jnp.int32, values.shape, 0)
    return jnp.where(row < rows - count, pltpu.roll(values, rows - count, 0), 0.0)


def middle_body(scale, nshort, nrow, *refs):
    sums, refs = (refs[:3], refs[3:6]), refs[6:]
    sf_ref, causal_ref, anti_ref, go_ref, near_ref, other_ref, mixed_ref, m_ref, gm_ref = refs
    tokens, width = go_ref.shape
    row = lax.axis_index("row")
    nblocks = nrow // 2
    rows = tokens // nrow

    def places():
        for chunk, start in enumerate((row, row + 1 - 2 * lax.rem(row, 2))):
            for block in range(nblocks):
                at = wrapped(start - 2 * block, nrow) * rows
                for i in range(3):
                    yield chunk, (i * nblocks + block) * rows, pl.multiple_of(i * tokens + at, 16)

    for chunk, place, at in places():
        held = [ref[place : place + rows].astype(F32) for ref in sums[chunk]]
        m_ref[pl.ds(at, rows)] = held[0] + held[1] + held[2]
    groups, block, span = causal_ref.shape
    members = width // groups
    nspans = tokens // block
    lane = lax.broadcasted_iota(jnp.int32, (block, width), 1) // members
    lanes = lax.broadcasted_iota(jnp.int32, (block, 2 * width), 1) % width // members

    def past(i, j):
        held = m_ref[i * tokens : (i + 1) * tokens]
        return held if j == 0 else delayed(held, j)

    def taps(j, i):
        return sf_ref[3 * j + i : 3 * j + i + 1, :]

    feats = [sum(taps(j, i) * past(i, j) for j in range(nshort)) for i in range(3)]
    product = (feats[1] * feats[2]).astype(BF16)
    zero = jnp.zeros((block, width), BF16)
    p_blocks = [zero] + [product[b * block : (b + 1) * block] for b in range(nspans)]
    p_pairs = [jnp.concatenate(p_blocks[b : b + 2], axis=0) for b in range(nspans)]

    def filtered(band_ref, pairs):
        bands = band_ref[...].reshape(groups * block, span)
        out = []
        for b in range(0, nspans, 2):
            both = jnp.dot(bands, jnp.concatenate(pairs[b : b + 2], axis=1), preferred_element_type=F32)
            for h in range(2):
                part = both[:, h * width : (h + 1) * width]
                picked = part[:block]
                for g in range(1, groups):
                    picked = jnp.where(lane == g, part[g * block : (g + 1) * block], picked)
                out.append(picked)
        return jnp.concatenate(out, axis=0)

    conv = filtered(causal_ref, p_pairs)
    upstream = go_ref[...].astype(F32)
    mixed_ref[...] = (feats[0] * conv).astype(BF16)
    grad_conv = (upstream * feats[0]).astype(BF16)
    c_blocks = [grad_conv[b * block : (b + 1) * block] for b in range(nspans)] + [zero]
    c_pairs = [jnp.concatenate(c_blocks[b : b + 2], axis=0) for b in range(nspans)]
    grad_product = filtered(anti_ref, c_pairs)

    corr = jnp.zeros((groups * block, span), F32)
    for b in range(0, nspans, 2):
        left = jnp.concatenate(c_blocks[b : b + 2], axis=1)
        stacked = jnp.concatenate(
            [jnp.where(lanes == g, left, jnp.zeros_like(left)) for g in range(groups)], axis=0
        )
        right = jnp.concatenate(p_pairs[b : b + 2], axis=1)
        corr += lax.dot_general(stacked, right, (((1,), (1,)), ((), ())), preferred_element_type=F32)
    turn = lax.broadcasted_iota(jnp.int32, (8, span), 0)
    sums = []
    for g in range(groups):
        part = corr[g * block : (g + 1) * block]
        count = block
        while count > 8:
            count //= 2
            part = part[:count] + pltpu.roll(part[count:], span - count, 1)
        for bit in (1, 2, 4):
            part = jnp.where((turn & bit) != 0, pltpu.roll(part, span - bit, 1), part)
        sums.append(jnp.sum(part, axis=0, keepdims=True))
    by_lag = jnp.concatenate(sums, axis=0)
    by_lag = scale * pltpu.roll(by_lag, span - 1, 1)[:, :block]

    grad_feats = [upstream * conv, grad_product * feats[2], grad_product * feats[1]]
    short_rows = []
    for j in range(nshort):
        for i in range(3):
            short_rows.append(scale * jnp.sum(grad_feats[i] * past(i, j), axis=0, keepdims=True))
    for i in range(3):
        total = taps(0, i) * grad_feats[i]
        for j in range(1, nshort):
            total += taps(j, i) * advanced(grad_feats[i], j)
        gm_ref[i * tokens : (i + 1) * tokens] = total.astype(BF16)
    for chunk, place, at in places():
        (near_ref, other_ref)[chunk][place : place + rows] = gm_ref[pl.ds(at, rows)]
    tail = other_ref.shape[0] - 3 * tokens // 2 - groups - 3 * nshort
    small = jnp.concatenate([by_lag] + short_rows + [jnp.zeros((tail, width), F32)], axis=0)
    other_ref[3 * tokens // 2 :] = small.astype(BF16)


def sum_over_line(own, right, far, left):
    ndp = lax.axis_size("dp")
    from_left = lax.ppermute(far, "dp", [(a, a + 1) for a in range(ndp // 2)])
    from_right = lax.ppermute(far, "dp", [(a, a - 1) for a in range(ndp // 2, ndp)])
    rightward = lax.ppermute(right + from_left, "dp", [(a, (a + 1) % ndp) for a in range(ndp)])
    leftward = lax.ppermute(left + from_right, "dp", [(a, (a - 1) % ndp) for a in range(ndp)])
    return own, rightward, leftward


def gather_over_line(own):
    ndp = lax.axis_size("dp")
    before = lax.ppermute(own, "dp", [(a, (a + 1) % ndp) for a in range(ndp)])
    after = lax.ppermute(own, "dp", [(a, (a - 1) % ndp) for a in range(ndp)])
    far_before = lax.ppermute(before, "dp", [(a - 1, a) for a in range(ndp // 2, ndp)])
    far_after = lax.ppermute(after, "dp", [(a + 1, a) for a in range(ndp // 2)])
    return own, before, after, far_before, far_after


def move_activations(tokens, in_weight, short_filter, long_filter, grad_out):
    ndp, nrow, ncol = (lax.axis_size(a) for a in ("dp", "row", "col"))
    z = lax.axis_index("dp")
    rows, dcol = tokens.shape
    local = grad_out.shape[1]
    nshort = short_filter.shape[0]
    ngroups, ntaps = long_filter.shape
    seq = rows * ndp
    width, groups = local // ndp, ngroups // ndp
    drow = in_weight.shape[0]
    scale = float(seq) ** -0.5
    nblocks = nrow // 2
    chunk = nblocks * rows
    swap = [(a * nrow + b, b * nrow + a) for a in range(ndp) for b in range(nrow)]
    partner = [(a, a + 1 - 2 * (a % 2)) for a in range(nrow)]
    places = [(dy, dx) for dy in range(nblocks) for dx in range(ncol)]

    def offset(dy, dx):
        return [
            (a * ncol + b, (a + 2 * dy) % nrow * ncol + (b + dx) % ncol) for a in range(nrow) for b in range(ncol)
        ]

    w = jnp.transpose(in_weight, (1, 0, 2))
    moved = lax.ppermute(tokens, ("dp", "row"), swap)
    near = [moved] + [lax.ppermute(moved, ("row", "col"), offset(*p)) for p in places[1:]]
    x0 = jnp.stack(near).reshape(nblocks, ncol, rows, dcol)
    x1 = lax.ppermute(x0, "row", partner)
    upstream = lax.all_to_all(grad_out, "dp", split_axis=1, concat_axis=0, tiled=True)

    sf = lax.dynamic_slice_in_dim(short_filter, z * width, width, 2).reshape(3 * nshort, width)
    lf = lax.dynamic_slice_in_dim(long_filter, z * groups, groups, 0).astype(F32)
    zeros = functools.partial(jnp.zeros, dtype=F32)
    bases = jnp.concatenate(
        [
            jnp.concatenate([zeros((groups, 1)), lf[:, ::-1], zeros((groups, ntaps - 1))], axis=1),
            jnp.concatenate([lf, zeros((groups, ntaps))], axis=1),
        ],
        axis=0,
    )
    bands = kernel_call(bands_body, shaped((2 * groups, ntaps, 2 * ntaps), BF16))(bases)

    mm_flops = seq * drow * 3 * local
    mm_bytes = seq * drow + 6 * drow * local + 3 * seq * local
    sums = []
    for x in (x0, x1):
        parts = kernel_call(
            project_body,
            [shaped((3, chunk, width), BF16)] * ndp,
            grid=(3,),
            in_specs=[
                pl.BlockSpec((nblocks, ncol, rows, dcol), lambda i: (0, 0, 0, 0)),
                pl.BlockSpec((1, drow, local), lambda i: (i, 0, 0)),
            ],
            out_specs=[pl.BlockSpec((1, chunk, width), lambda i: (i, 0, 0))] * ndp,
            scratch=[pltpu.VMEM((ndp, chunk, width), BF16)],
            flops=mm_flops,
            nbytes=mm_bytes,
        )(x, w)
        sums += sum_over_line(*(p.reshape(3 * chunk, width) for p in parts))

    extra = -(-(groups + 3 * nshort) // 16) * 16
    half = pl.BlockSpec((groups, ntaps, 2 * ntaps), lambda i: (0, 0, 0))
    other = pl.BlockSpec((groups, ntaps, 2 * ntaps), lambda i: (1, 0, 0))
    whole = lambda *shape: pl.BlockSpec(shape, lambda i: (0,) * len(shape))
    grad_near, grad_other, mixed = kernel_call(
        functools.partial(middle_body, scale, nshort, nrow),
        (
            shaped((3 * chunk, width), BF16),
            shaped((3 * chunk + extra, width), BF16),
            shaped((seq, width), BF16),
        ),
        grid=(1,),
        in_specs=[whole(3 * chunk, width)] * 6
        + [whole(3 * nshort, width), half, other, whole(seq, width)],
        out_specs=(whole(3 * chunk, width), whole(3 * chunk + extra, width), whole(seq, width)),
        scratch=[pltpu.VMEM((3 * seq, width), F32), pltpu.VMEM((3 * seq, width), BF16)],
        flops=3 * 2 * groups * ntaps * 2 * ntaps * width * (seq // ntaps),
        nbytes=2 * width * seq * 14,
    )(*sums, sf, bands, bands, upstream)
    mixed = lax.all_to_all(mixed, "dp", split_axis=0, concat_axis=1, tiled=True)

    block = shaped((rows, dcol), BF16)
    all_shape = shaped((3, chunk, local), BF16)
    out_first, all_other, small = kernel_call(
        first_grad_body,
        (shaped((nblocks, ncol, rows, dcol), BF16), all_shape, shaped((ndp, extra, width), BF16)),
        scratch=[pltpu.VMEM((ndp, 3 * chunk + extra, width), BF16)],
        flops=mm_flops,
        nbytes=mm_bytes,
    )(*gather_over_line(grad_other), w)
    from_partner = lax.ppermute(out_first, "row", partner)
    all_near, *blocks = kernel_call(
        second_grad_body,
        [all_shape] + [block] * len(places),
        scratch=[pltpu.VMEM((ndp, 3 * chunk, width), BF16)],
        flops=mm_flops,
        nbytes=mm_bytes,
    )(*gather_over_line(grad_near), w, from_partner)
    arrived = blocks[0].astype(F32)
    for (dy, dx), sent in zip(places[1:], blocks[1:]):
        back = [(b, a) for a, b in offset(dy, dx)]
        arrived += lax.ppermute(sent, ("row", "col"), back).astype(F32)
    grad_in = lax.ppermute(arrived.astype(BF16), ("dp", "row"), swap)

    x_spec = pl.BlockSpec((nblocks, ncol, rows, dcol), lambda i: (0, 0, 0, 0))
    g_spec = pl.BlockSpec((1, chunk, local), lambda i: (i, 0, 0))
    grad_weight = kernel_call(
        functools.partial(weight_grad_body, scale),
        shaped((3, drow, local), F32),
        grid=(3,),
        in_specs=[x_spec, x_spec, g_spec, g_spec],
        out_specs=pl.BlockSpec((1, drow, local), lambda i: (i, 0, 0)),
        flops=2 * mm_flops,
        nbytes=2 * mm_bytes,
    )(x0, x1, all_near, all_other)
    grad_weight = jnp.transpose(grad_weight, (1, 0, 2))
    small = small.astype(F32)
    grad_long = small[:, :groups, ::-1].reshape(ngroups, ntaps)
    grad_short = (
        small[:, groups : groups + 3 * nshort].transpose(1, 0, 2).reshape(nshort, 3, local)
    )
    return (mixed, grad_in, grad_weight, grad_long, grad_short)


def from_behind(block, axis, distance):
    devices = range(lax.axis_size(axis))
    route = [(i - distance, i) for i in devices if i - distance in devices]
    return lax.ppermute(block, axis, route)


def toeplitz(leading, rows, span):
    groups = leading.shape[0]
    width = rows + span
    seed_row = jnp.concatenate(
        [leading, jnp.zeros((groups, width - leading.shape[1]), leading.dtype)], axis=1
    )
    tiled = jnp.tile(seed_row, (1, rows))
    skewed = tiled[:, : rows * (width - 1)].reshape(groups, rows, width - 1)
    return skewed[:, :, :span]


def to_groups(values, ngroups, members):
    count = values.shape[0]
    return values.reshape(count, ngroups, members).transpose(1, 2, 0)


def from_groups(values):
    groups, members, count = values.shape
    return values.transpose(2, 0, 1).reshape(count, groups * members)


def move_weights(tokens, in_weight, short_filter, long_filter, grad_out):
    rows = tokens.shape[0]
    local = grad_out.shape[1]
    nshort = short_filter.shape[0]
    ntaps = long_filter.shape[1]
    ngroups = long_filter.shape[0]
    members = local // ngroups
    margin = ntaps - 1
    span = rows + margin
    scale = float(rows * lax.axis_size("dp")) ** (-0.5)
    whole = lax.all_gather(tokens, ("row", "col"), axis=1, tiled=True)
    full_w = lax.all_gather(in_weight, "dp", axis=0, tiled=True)
    mixed_in = jnp.einsum("sd,dic->sic", whole, full_w, preferred_element_type=jnp.float32).astype(
        jnp.bfloat16
    )
    before = from_behind(mixed_in[rows - margin - nshort + 1 :], "dp", 1)
    extended = jnp.concatenate([before, mixed_in], axis=0).astype(jnp.float32)
    long_feats = jnp.zeros((span, 3, local), jnp.float32)
    for j in range(nshort):
        long_feats = (
            long_feats + short_filter[j][None] * extended[nshort - 1 - j : nshort - 1 - j + span]
        )
    product_ext = (long_feats[:, 1] * long_feats[:, 2]).astype(jnp.bfloat16)
    feats = long_feats[margin:]
    short_rows = extended[margin:]
    product_cols = to_groups(product_ext, ngroups, members)
    causal = toeplitz(long_filter[:, ::-1], rows, span)
    conv = from_groups(
        jnp.einsum("gst,gct->gcs", causal, product_cols, preferred_element_type=jnp.float32)
    )
    mixed = (feats[:, 0] * conv).astype(jnp.bfloat16)
    upstream = grad_out.astype(jnp.float32)
    grad_query = upstream * conv
    grad_conv = (upstream * feats[:, 0]).astype(jnp.bfloat16)
    after = from_behind(grad_conv[:margin], "dp", -1)
    grad_ext = jnp.concatenate([grad_conv, after], axis=0)
    anti = toeplitz(long_filter, rows, span)
    grad_product = from_groups(
        jnp.einsum(
            "gst,gct->gcs",
            anti,
            to_groups(grad_ext, ngroups, members),
            preferred_element_type=jnp.float32,
        )
    )
    reversed_cols = jnp.concatenate(
        [product_cols[:, :, ::-1], jnp.zeros((ngroups, members, rows), product_cols.dtype)], axis=2
    )
    width = span + rows
    pairs = jnp.einsum(
        "gcs,gcu->gsu",
        to_groups(grad_conv, ngroups, members),
        reversed_cols,
        preferred_element_type=jnp.float32,
    )
    diagonal = pairs.reshape(ngroups, rows * width)[:, : rows * (width - 1)].reshape(
        ngroups, rows, width - 1
    )
    filter_part = jnp.sum(diagonal[:, :, rows - 1 : rows - 1 + ntaps], axis=1)
    grad_feats = jnp.stack(
        [grad_query, grad_product * feats[:, 2], grad_product * feats[:, 1]], axis=1
    )
    later = from_behind(grad_feats[: nshort - 1], "dp", -1)
    feats_ext = jnp.concatenate([grad_feats, later], axis=0)
    grad_acc = jnp.zeros((rows, 3, local), jnp.float32)
    for j in range(nshort):
        grad_acc = grad_acc + short_filter[j][None] * feats_ext[j : j + rows]
    grad_mixed = grad_acc.astype(jnp.bfloat16)
    short_part = jnp.stack(
        [
            jnp.sum(grad_feats * short_rows[nshort - 1 - j : nshort - 1 - j + rows], axis=0)
            for j in range(nshort)
        ]
    )
    filter_total, short_total = (
        lax.psum(filter_part.astype(jnp.bfloat16), "dp").astype(jnp.float32),
        lax.psum(short_part.astype(jnp.bfloat16), "dp").astype(jnp.float32),
    )
    grad_long = filter_total * scale
    grad_short = short_total * scale
    partial_in = jnp.einsum("sic,dic->sd", grad_mixed, full_w, preferred_element_type=jnp.float32)
    summed_in = lax.psum_scatter(
        partial_in.astype(jnp.bfloat16), ("row", "col"), scatter_dimension=1, tiled=True
    )
    weight_term = (
        jnp.einsum("sd,sic->dic", whole, grad_mixed, preferred_element_type=jnp.float32) * scale
    )
    grad_weight = lax.psum_scatter(
        weight_term.astype(jnp.bfloat16), "dp", scatter_dimension=0, tiled=True
    ).astype(jnp.float32)
    return (mixed, summed_in, grad_weight, grad_long, grad_short)


def fits_whole_sequences(mesh, tokens, in_weight, short_filter, long_filter, grad_out):
    ndp, nrow, ncol = (mesh.shape[a] for a in ("dp", "row", "col"))
    seq, channels = grad_out.shape
    groups, ntaps = long_filter.shape
    local = channels // (nrow * ncol)
    width, rows = local // ndp, seq // ndp
    return (
        seq < tokens.shape[1]
        and ndp == nrow == 4
        and ncol * (tokens.shape[1] // (nrow * ncol)) == in_weight.shape[0] // ndp
        and ntaps == width == 128
        and seq % (2 * ntaps) == 0
        and rows % 16 == 0
        and groups % (8 * ndp * nrow * ncol) == 0
    )


def solution(mesh):
    placed = (
        P("dp", ("row", "col")),
        P("dp", None, ("row", "col")),
        P(None, None, ("row", "col")),
        P(("row", "col"), None),
        P("dp", ("row", "col")),
    )
    gives = (
        P("dp", ("row", "col")),
        P("dp", ("row", "col")),
        P("dp", None, ("row", "col")),
        P(("row", "col"), None),
        P(None, None, ("row", "col")),
    )

    def run(*arrays):
        plan = move_activations if fits_whole_sequences(mesh, *arrays) else move_weights
        return jax.shard_map(
            plan, mesh=mesh, in_specs=placed, out_specs=gives, check_vma=False
        )(*arrays)

    return run
```

```python
import functools

import jax
import jax.numpy as jnp
from jax import lax
from jax.experimental import pallas as pl
from jax.experimental.pallas import tpu as pltpu
from jax.sharding import PartitionSpec as P

VMEM_BYTES = 20 * 2**20
F32 = jnp.float32
BF16 = jnp.bfloat16


def kernel_call(body, outs, grid=None, in_specs=None, out_specs=None, scratch=(), flops=0, nbytes=0):
    kwargs = {}
    if grid is not None:
        kwargs = dict(grid=grid, in_specs=in_specs, out_specs=out_specs)
    return pl.pallas_call(
        body,
        out_shape=outs,
        scratch_shapes=scratch,
        compiler_params=pltpu.CompilerParams(vmem_limit_bytes=VMEM_BYTES),
        cost_estimate=pl.CostEstimate(flops=flops, bytes_accessed=nbytes, transcendentals=0),
        **kwargs,
    )


def shaped(shape, dtype):
    return jax.ShapeDtypeStruct(shape, dtype)


def bands_body(base_ref, out_ref):
    groups, wide = base_ref.shape
    rows = out_ref.shape[1]
    row = lax.broadcasted_iota(jnp.int32, (8, wide), 0)
    for g in range(groups):
        band = jnp.broadcast_to(base_ref[g : g + 1, :], (8, wide))
        for bit in (1, 2, 4):
            band = jnp.where((row & bit) != 0, pltpu.roll(band, bit, 1), band)
        count = 8
        while count < rows:
            band = jnp.concatenate([band, pltpu.roll(band, count, 1)], axis=0)
            count *= 2
        out_ref[g] = band.astype(out_ref.dtype)


def wrapped(value, size):
    return lax.rem(value + 2 * size, size)


def project_body(x_ref, w_ref, *refs):
    *out_refs, held = refs
    z, col = lax.axis_index("dp"), lax.axis_index("col")
    nblocks, ncol, rows, depth = x_ref.shape
    width = out_refs[0].shape[-1]
    total = jnp.zeros((nblocks * rows, w_ref.shape[2]), F32)
    for dx in range(ncol):
        start = pl.multiple_of(wrapped(col - dx, ncol) * depth, depth)
        total += jnp.dot(
            x_ref[:, dx].reshape(nblocks * rows, depth),
            w_ref[0, pl.ds(start, depth), :],
            preferred_element_type=F32,
        )
    if len(out_refs) == 1:
        (held,) = (ref.at[:, 0] for ref in out_refs)
    for owner in range(held.shape[0]):
        held[owner] = total[:, owner * width : (owner + 1) * width].astype(BF16)
    if len(out_refs) > 1:
        for ahead, out_ref in enumerate(out_refs):
            out_ref[0] = held[wrapped(z + ahead, len(out_refs))]


def assemble(pieces, held, ndp):
    z = lax.axis_index("dp")
    own, before, after, far_before, far_after = pieces
    held[z] = own[...]
    held[wrapped(z - 1, ndp)] = before[...]
    held[wrapped(z + 1, ndp)] = after[...]

    @pl.when(z >= ndp // 2)
    def _():
        held[z - ndp // 2] = far_before[...]

    @pl.when(z < ndp // 2)
    def _():
        held[z + ndp // 2] = far_after[...]


def input_grads(held, w_ref, all_ref, ncol):
    ndp = held.shape[0]
    tokens, depth = all_ref.shape[1], w_ref.shape[1] // ncol
    col = lax.axis_index("col")
    for i in range(3):
        for owner in range(ndp):
            width = held.shape[2]
            all_ref[i, :, owner * width : (owner + 1) * width] = held[owner, i * tokens : (i + 1) * tokens]
    for dx in range(ncol):
        start = pl.multiple_of(wrapped(col - dx, ncol) * depth, depth)
        total = jnp.zeros((tokens, depth), F32)
        for i in range(3):
            total += lax.dot_general(
                all_ref[i],
                w_ref[i, pl.ds(start, depth), :],
                (((1,), (1,)), ((), ())),
                preferred_element_type=F32,
            )
        yield dx, total


def first_grad_body(own, before, after, far_before, far_after, w_ref, out_ref, all_ref, small_ref, held):
    nblocks, ncol, rows, depth = out_ref.shape
    assemble((own, before, after, far_before, far_after), held, held.shape[0])
    small_ref[...] = held[:, 3 * nblocks * rows :]
    for dx, total in input_grads(held, w_ref, all_ref, ncol):
        out_ref[:, dx] = total.reshape(nblocks, rows, depth).astype(BF16)


def second_grad_body(held, w_ref, other_ref, all_ref, *out_refs):
    nblocks, ncol, rows, depth = other_ref.shape
    for dx, total in input_grads(held, w_ref, all_ref, ncol):
        for block in range(nblocks):
            both = total[block * rows : (block + 1) * rows] + other_ref[block, dx].astype(F32)
            out_refs[block * ncol + dx][...] = both.astype(BF16)


def weight_grad_body(scale, x0_ref, x1_ref, g0_ref, g1_ref, out_ref):
    nblocks, ncol, rows, depth = x0_ref.shape
    col = lax.axis_index("col")
    gm = jnp.concatenate([g0_ref[0], g1_ref[0]], axis=0)
    for dx in range(ncol):
        start = pl.multiple_of(wrapped(col - dx, ncol) * depth, depth)
        x = jnp.concatenate(
            [x_ref[:, dx].reshape(nblocks * rows, depth) for x_ref in (x0_ref, x1_ref)], axis=0
        )
        out_ref[0, pl.ds(start, depth), :] = scale * lax.dot_general(
            x, gm, (((0,), (0,)), ((), ())), preferred_element_type=F32
        )


def delayed(values, count):
    row = lax.broadcasted_iota(jnp.int32, values.shape, 0)
    return jnp.where(row >= count, pltpu.roll(values, count, 0), 0.0)


def advanced(values, count):
    rows = values.shape[0]
    row = lax.broadcasted_iota(jnp.int32, values.shape, 0)
    return jnp.where(row < rows - count, pltpu.roll(values, rows - count, 0), 0.0)


def middle_body(scale, nshort, nrow, *refs):
    sums, refs = (refs[:3], refs[3:4]), refs[4:]
    sf_ref, causal_ref, anti_ref, go_ref, near_ref, other_ref, mixed_ref, m_ref, gm_ref = refs
    tokens, width = go_ref.shape
    row = lax.axis_index("row")
    nblocks = nrow // 2
    rows = tokens // nrow

    def places():
        for chunk, start in enumerate((row, row + 1 - 2 * lax.rem(row, 2))):
            for block in range(nblocks):
                at = wrapped(start - 2 * block, nrow) * rows
                for i in range(3):
                    yield chunk, (i * nblocks + block) * rows, pl.multiple_of(i * tokens + at, 16)

    for chunk, place, at in places():
        m_ref[pl.ds(at, rows)] = sum(ref[place : place + rows].astype(F32) for ref in sums[chunk])
    groups, block, span = causal_ref.shape
    members = width // groups
    nspans = tokens // block
    lane = lax.broadcasted_iota(jnp.int32, (block, width), 1) // members
    lanes = lax.broadcasted_iota(jnp.int32, (block, 2 * width), 1) % width // members

    def past(i, j):
        held = m_ref[i * tokens : (i + 1) * tokens]
        return held if j == 0 else delayed(held, j)

    def taps(j, i):
        return sf_ref[3 * j + i : 3 * j + i + 1, :]

    feats = [sum(taps(j, i) * past(i, j) for j in range(nshort)) for i in range(3)]
    product = (feats[1] * feats[2]).astype(BF16)
    zero = jnp.zeros((block, width), BF16)
    p_blocks = [zero] + [product[b * block : (b + 1) * block] for b in range(nspans)]
    p_pairs = [jnp.concatenate(p_blocks[b : b + 2], axis=0) for b in range(nspans)]

    def filtered(band_ref, pairs):
        bands = band_ref[...].reshape(groups * block, span)
        out = []
        for b in range(0, nspans, 2):
            both = jnp.dot(bands, jnp.concatenate(pairs[b : b + 2], axis=1), preferred_element_type=F32)
            for h in range(2):
                part = both[:, h * width : (h + 1) * width]
                picked = part[:block]
                for g in range(1, groups):
                    picked = jnp.where(lane == g, part[g * block : (g + 1) * block], picked)
                out.append(picked)
        return jnp.concatenate(out, axis=0)

    conv = filtered(causal_ref, p_pairs)
    upstream = go_ref[...].astype(F32)
    mixed_ref[...] = (feats[0] * conv).astype(BF16)
    grad_conv = (upstream * feats[0]).astype(BF16)
    c_blocks = [grad_conv[b * block : (b + 1) * block] for b in range(nspans)] + [zero]
    c_pairs = [jnp.concatenate(c_blocks[b : b + 2], axis=0) for b in range(nspans)]
    grad_product = filtered(anti_ref, c_pairs)

    corr = jnp.zeros((groups * block, span), F32)
    for b in range(0, nspans, 2):
        left = jnp.concatenate(c_blocks[b : b + 2], axis=1)
        stacked = jnp.concatenate(
            [jnp.where(lanes == g, left, jnp.zeros_like(left)) for g in range(groups)], axis=0
        )
        right = jnp.concatenate(p_pairs[b : b + 2], axis=1)
        corr += lax.dot_general(stacked, right, (((1,), (1,)), ((), ())), preferred_element_type=F32)
    turn = lax.broadcasted_iota(jnp.int32, (8, span), 0)
    sums = []
    for g in range(groups):
        part = corr[g * block : (g + 1) * block]
        count = block
        while count > 8:
            count //= 2
            part = part[:count] + pltpu.roll(part[count:], span - count, 1)
        for bit in (1, 2, 4):
            part = jnp.where((turn & bit) != 0, pltpu.roll(part, span - bit, 1), part)
        sums.append(jnp.sum(part, axis=0, keepdims=True))
    by_lag = jnp.concatenate(sums, axis=0)
    by_lag = scale * pltpu.roll(by_lag, span - 1, 1)[:, :block]

    grad_feats = [upstream * conv, grad_product * feats[2], grad_product * feats[1]]
    short_rows = []
    for j in range(nshort):
        for i in range(3):
            short_rows.append(scale * jnp.sum(grad_feats[i] * past(i, j), axis=0, keepdims=True))
    for i in range(3):
        total = taps(0, i) * grad_feats[i]
        for j in range(1, nshort):
            total += taps(j, i) * advanced(grad_feats[i], j)
        gm_ref[i * tokens : (i + 1) * tokens] = total.astype(BF16)
    for chunk, place, at in places():
        (near_ref, other_ref)[chunk][place : place + rows] = gm_ref[pl.ds(at, rows)]
    tail = other_ref.shape[0] - 3 * tokens // 2 - groups - 3 * nshort
    small = jnp.concatenate([by_lag] + short_rows + [jnp.zeros((tail, width), F32)], axis=0)
    other_ref[3 * tokens // 2 :] = small.astype(BF16)


def sum_over_line(own, right, far, left):
    ndp = lax.axis_size("dp")
    from_left = lax.ppermute(far, "dp", [(a, a + 1) for a in range(ndp // 2)])
    from_right = lax.ppermute(far, "dp", [(a, a - 1) for a in range(ndp // 2, ndp)])
    rightward = lax.ppermute(right + from_left, "dp", [(a, (a + 1) % ndp) for a in range(ndp)])
    leftward = lax.ppermute(left + from_right, "dp", [(a, (a - 1) % ndp) for a in range(ndp)])
    return own, rightward, leftward


def gather_over_line(own):
    ndp = lax.axis_size("dp")
    before = lax.ppermute(own, "dp", [(a, (a + 1) % ndp) for a in range(ndp)])
    after = lax.ppermute(own, "dp", [(a, (a - 1) % ndp) for a in range(ndp)])
    far_before = lax.ppermute(before, "dp", [(a - 1, a) for a in range(ndp // 2, ndp)])
    far_after = lax.ppermute(after, "dp", [(a + 1, a) for a in range(ndp // 2)])
    return own, before, after, far_before, far_after


def move_activations(tokens, in_weight, short_filter, long_filter, grad_out):
    ndp, nrow, ncol = (lax.axis_size(a) for a in ("dp", "row", "col"))
    z = lax.axis_index("dp")
    rows, dcol = tokens.shape
    local = grad_out.shape[1]
    nshort = short_filter.shape[0]
    ngroups, ntaps = long_filter.shape
    seq = rows * ndp
    width, groups = local // ndp, ngroups // ndp
    drow = in_weight.shape[0]
    scale = float(seq) ** -0.5
    nblocks = nrow // 2
    chunk = nblocks * rows
    swap = [(a * nrow + b, b * nrow + a) for a in range(ndp) for b in range(nrow)]
    partner = [(a, a + 1 - 2 * (a % 2)) for a in range(nrow)]
    places = [(dy, dx) for dy in range(nblocks) for dx in range(ncol)]

    def offset(dy, dx):
        return [
            (a * ncol + b, (a + 2 * dy) % nrow * ncol + (b + dx) % ncol) for a in range(nrow) for b in range(ncol)
        ]

    w = jnp.transpose(in_weight, (1, 0, 2))
    moved = lax.ppermute(tokens, ("dp", "row"), swap)
    moved, grad_out = lax.optimization_barrier((moved, grad_out))
    near = [moved] + [lax.ppermute(moved, ("row", "col"), offset(*p)) for p in places[1:]]
    upstream = lax.all_to_all(grad_out, "dp", split_axis=1, concat_axis=0, tiled=True)
    x0 = jnp.stack(near).reshape(nblocks, ncol, rows, dcol)
    x1 = lax.ppermute(x0, "row", partner)
    x0, upstream = lax.optimization_barrier((x0, upstream))

    sf = lax.dynamic_slice_in_dim(short_filter, z * width, width, 2).reshape(3 * nshort, width)
    lf = lax.dynamic_slice_in_dim(long_filter, z * groups, groups, 0).astype(F32)
    zeros = functools.partial(jnp.zeros, dtype=F32)
    bases = jnp.concatenate(
        [
            jnp.concatenate([zeros((groups, 1)), lf[:, ::-1], zeros((groups, ntaps - 1))], axis=1),
            jnp.concatenate([lf, zeros((groups, ntaps))], axis=1),
        ],
        axis=0,
    )
    bands = kernel_call(bands_body, shaped((2 * groups, ntaps, 2 * ntaps), BF16))(bases)

    mm_flops = seq * drow * 3 * local
    mm_bytes = seq * drow + 6 * drow * local + 3 * seq * local
    sums = []
    project_specs = [
        pl.BlockSpec((nblocks, ncol, rows, dcol), lambda i: (0, 0, 0, 0)),
        pl.BlockSpec((1, drow, local), lambda i: (i, 0, 0)),
    ]
    parts = kernel_call(
        project_body,
        [shaped((3, chunk, width), BF16)] * ndp,
        grid=(3,),
        in_specs=project_specs,
        out_specs=[pl.BlockSpec((1, chunk, width), lambda i: (i, 0, 0))] * ndp,
        scratch=[pltpu.VMEM((ndp, chunk, width), BF16)],
        flops=mm_flops,
        nbytes=mm_bytes,
    )(x0, w)
    sums = [*sum_over_line(*(p.reshape(3 * chunk, width) for p in parts))]
    part = kernel_call(
        project_body,
        [shaped((ndp, 3, chunk, width), BF16)],
        grid=(3,),
        in_specs=project_specs,
        out_specs=[pl.BlockSpec((ndp, 1, chunk, width), lambda i: (0, i, 0, 0))],
        scratch=[pltpu.VMEM((8, width), BF16)],
        flops=mm_flops,
        nbytes=mm_bytes,
    )(x1, w)[0]
    sums.append(lax.psum_scatter(part.reshape(ndp, 3 * chunk, width), "dp", scatter_dimension=0))

    extra = -(-(groups + 3 * nshort) // 16) * 16
    half = pl.BlockSpec((groups, ntaps, 2 * ntaps), lambda i: (0, 0, 0))
    other = pl.BlockSpec((groups, ntaps, 2 * ntaps), lambda i: (1, 0, 0))
    whole = lambda *shape: pl.BlockSpec(shape, lambda i: (0,) * len(shape))
    grad_near, grad_other, mixed = kernel_call(
        functools.partial(middle_body, scale, nshort, nrow),
        (
            shaped((3 * chunk, width), BF16),
            shaped((3 * chunk + extra, width), BF16),
            shaped((seq, width), BF16),
        ),
        grid=(1,),
        in_specs=[whole(3 * chunk, width)] * 4
        + [whole(3 * nshort, width), half, other, whole(seq, width)],
        out_specs=(whole(3 * chunk, width), whole(3 * chunk + extra, width), whole(seq, width)),
        scratch=[pltpu.VMEM((3 * seq, width), F32), pltpu.VMEM((3 * seq, width), BF16)],
        flops=3 * 2 * groups * ntaps * 2 * ntaps * width * (seq // ntaps),
        nbytes=2 * width * seq * 14,
    )(*sums, sf, bands, bands, upstream)
    mixed = lax.all_to_all(mixed, "dp", split_axis=0, concat_axis=1, tiled=True)

    gathered = lax.all_gather(grad_near, "dp", axis=0)
    block = shaped((rows, dcol), BF16)
    all_shape = shaped((3, chunk, local), BF16)
    pieces = gather_over_line(grad_other)
    gathered, *pieces = lax.optimization_barrier((gathered, *pieces))
    out_first, all_other, small = kernel_call(
        first_grad_body,
        (shaped((nblocks, ncol, rows, dcol), BF16), all_shape, shaped((ndp, extra, width), BF16)),
        scratch=[pltpu.VMEM((ndp, 3 * chunk + extra, width), BF16)],
        flops=0,
        nbytes=0,
    )(*pieces, w)
    from_partner = lax.ppermute(out_first, "row", partner)
    all_near, *blocks = kernel_call(
        second_grad_body,
        [all_shape] + [block] * len(places),
        flops=mm_flops,
        nbytes=mm_bytes,
    )(gathered, w, from_partner)
    arrived = blocks[0].astype(F32)
    for (dy, dx), sent in zip(places[1:], blocks[1:]):
        back = [(b, a) for a, b in offset(dy, dx)]
        arrived += lax.ppermute(sent, ("row", "col"), back).astype(F32)
    grad_in = lax.ppermute(arrived.astype(BF16), ("dp", "row"), swap)

    x_spec = pl.BlockSpec((nblocks, ncol, rows, dcol), lambda i: (0, 0, 0, 0))
    g_spec = pl.BlockSpec((1, chunk, local), lambda i: (i, 0, 0))
    grad_weight = kernel_call(
        functools.partial(weight_grad_body, scale),
        shaped((3, drow, local), F32),
        grid=(3,),
        in_specs=[x_spec, x_spec, g_spec, g_spec],
        out_specs=pl.BlockSpec((1, drow, local), lambda i: (i, 0, 0)),
        flops=2 * mm_flops,
        nbytes=2 * mm_bytes,
    )(x0, x1, all_near, all_other)
    grad_weight = jnp.transpose(grad_weight, (1, 0, 2))
    small = small.astype(F32)
    grad_long = small[:, :groups, ::-1].reshape(ngroups, ntaps)
    grad_short = (
        small[:, groups : groups + 3 * nshort].transpose(1, 0, 2).reshape(nshort, 3, local)
    )
    return (mixed, grad_in, grad_weight, grad_long, grad_short)


def from_behind(block, axis, distance):
    devices = range(lax.axis_size(axis))
    route = [(i - distance, i) for i in devices if i - distance in devices]
    return lax.ppermute(block, axis, route)


def toeplitz(leading, rows, span):
    groups = leading.shape[0]
    width = rows + span
    seed_row = jnp.concatenate(
        [leading, jnp.zeros((groups, width - leading.shape[1]), leading.dtype)], axis=1
    )
    tiled = jnp.tile(seed_row, (1, rows))
    skewed = tiled[:, : rows * (width - 1)].reshape(groups, rows, width - 1)
    return skewed[:, :, :span]


def to_groups(values, ngroups, members):
    count = values.shape[0]
    return values.reshape(count, ngroups, members).transpose(1, 2, 0)


def from_groups(values):
    groups, members, count = values.shape
    return values.transpose(2, 0, 1).reshape(count, groups * members)


def move_weights(tokens, in_weight, short_filter, long_filter, grad_out):
    rows = tokens.shape[0]
    local = grad_out.shape[1]
    nshort = short_filter.shape[0]
    ntaps = long_filter.shape[1]
    ngroups = long_filter.shape[0]
    members = local // ngroups
    margin = ntaps - 1
    span = rows + margin
    scale = float(rows * lax.axis_size("dp")) ** (-0.5)
    whole = lax.all_gather(tokens, ("row", "col"), axis=1, tiled=True)
    full_w = lax.all_gather(in_weight, "dp", axis=0, tiled=True)
    mixed_in = jnp.einsum("sd,dic->sic", whole, full_w, preferred_element_type=jnp.float32).astype(
        jnp.bfloat16
    )
    before = from_behind(mixed_in[rows - margin - nshort + 1 :], "dp", 1)
    extended = jnp.concatenate([before, mixed_in], axis=0).astype(jnp.float32)
    long_feats = jnp.zeros((span, 3, local), jnp.float32)
    for j in range(nshort):
        long_feats = (
            long_feats + short_filter[j][None] * extended[nshort - 1 - j : nshort - 1 - j + span]
        )
    product_ext = (long_feats[:, 1] * long_feats[:, 2]).astype(jnp.bfloat16)
    feats = long_feats[margin:]
    short_rows = extended[margin:]
    product_cols = to_groups(product_ext, ngroups, members)
    causal = toeplitz(long_filter[:, ::-1], rows, span)
    conv = from_groups(
        jnp.einsum("gst,gct->gcs", causal, product_cols, preferred_element_type=jnp.float32)
    )
    mixed = (feats[:, 0] * conv).astype(jnp.bfloat16)
    upstream = grad_out.astype(jnp.float32)
    grad_query = upstream * conv
    grad_conv = (upstream * feats[:, 0]).astype(jnp.bfloat16)
    after = from_behind(grad_conv[:margin], "dp", -1)
    grad_ext = jnp.concatenate([grad_conv, after], axis=0)
    anti = toeplitz(long_filter, rows, span)
    grad_product = from_groups(
        jnp.einsum(
            "gst,gct->gcs",
            anti,
            to_groups(grad_ext, ngroups, members),
            preferred_element_type=jnp.float32,
        )
    )
    reversed_cols = jnp.concatenate(
        [product_cols[:, :, ::-1], jnp.zeros((ngroups, members, rows), product_cols.dtype)], axis=2
    )
    width = span + rows
    pairs = jnp.einsum(
        "gcs,gcu->gsu",
        to_groups(grad_conv, ngroups, members),
        reversed_cols,
        preferred_element_type=jnp.float32,
    )
    diagonal = pairs.reshape(ngroups, rows * width)[:, : rows * (width - 1)].reshape(
        ngroups, rows, width - 1
    )
    filter_part = jnp.sum(diagonal[:, :, rows - 1 : rows - 1 + ntaps], axis=1)
    grad_feats = jnp.stack(
        [grad_query, grad_product * feats[:, 2], grad_product * feats[:, 1]], axis=1
    )
    later = from_behind(grad_feats[: nshort - 1], "dp", -1)
    feats_ext = jnp.concatenate([grad_feats, later], axis=0)
    grad_acc = jnp.zeros((rows, 3, local), jnp.float32)
    for j in range(nshort):
        grad_acc = grad_acc + short_filter[j][None] * feats_ext[j : j + rows]
    grad_mixed = grad_acc.astype(jnp.bfloat16)
    short_part = jnp.stack(
        [
            jnp.sum(grad_feats * short_rows[nshort - 1 - j : nshort - 1 - j + rows], axis=0)
            for j in range(nshort)
        ]
    )
    filter_total, short_total = (
        lax.psum(filter_part.astype(jnp.bfloat16), "dp").astype(jnp.float32),
        lax.psum(short_part.astype(jnp.bfloat16), "dp").astype(jnp.float32),
    )
    grad_long = filter_total * scale
    grad_short = short_total * scale
    partial_in = jnp.einsum("sic,dic->sd", grad_mixed, full_w, preferred_element_type=jnp.float32)
    summed_in = lax.psum_scatter(
        partial_in.astype(jnp.bfloat16), ("row", "col"), scatter_dimension=1, tiled=True
    )
    weight_term = (
        jnp.einsum("sd,sic->dic", whole, grad_mixed, preferred_element_type=jnp.float32) * scale
    )
    grad_weight = lax.psum_scatter(
        weight_term.astype(jnp.bfloat16), "dp", scatter_dimension=0, tiled=True
    ).astype(jnp.float32)
    return (mixed, summed_in, grad_weight, grad_long, grad_short)


def fits_whole_sequences(mesh, tokens, in_weight, short_filter, long_filter, grad_out):
    ndp, nrow, ncol = (mesh.shape[a] for a in ("dp", "row", "col"))
    seq, channels = grad_out.shape
    groups, ntaps = long_filter.shape
    local = channels // (nrow * ncol)
    width, rows = local // ndp, seq // ndp
    return (
        seq < tokens.shape[1]
        and ndp == nrow == 4
        and ncol * (tokens.shape[1] // (nrow * ncol)) == in_weight.shape[0] // ndp
        and ntaps == width == 128
        and seq % (2 * ntaps) == 0
        and rows % 16 == 0
        and groups % (8 * ndp * nrow * ncol) == 0
    )


def solution(mesh):
    placed = (
        P("dp", ("row", "col")),
        P("dp", None, ("row", "col")),
        P(None, None, ("row", "col")),
        P(("row", "col"), None),
        P("dp", ("row", "col")),
    )
    gives = (
        P("dp", ("row", "col")),
        P("dp", ("row", "col")),
        P("dp", None, ("row", "col")),
        P(("row", "col"), None),
        P(None, None, ("row", "col")),
    )

    def run(*arrays):
        plan = move_activations if fits_whole_sequences(mesh, *arrays) else move_weights
        return jax.shard_map(
            plan, mesh=mesh, in_specs=placed, out_specs=gives, check_vma=False
        )(*arrays)

    return run
```

```python
import functools

import jax
import jax.numpy as jnp
from jax import lax
from jax.experimental import pallas as pl
from jax.experimental.pallas import tpu as pltpu
from jax.sharding import PartitionSpec as P

VMEM_BYTES = 20 * 2**20
F32 = jnp.float32
BF16 = jnp.bfloat16


def kernel_call(body, outs, grid=None, in_specs=None, out_specs=None, scratch=(), flops=0, nbytes=0):
    kwargs = {}
    if grid is not None:
        kwargs = dict(grid=grid, in_specs=in_specs, out_specs=out_specs)
    call = pl.pallas_call(
        body,
        out_shape=outs,
        scratch_shapes=scratch,
        compiler_params=pltpu.CompilerParams(vmem_limit_bytes=VMEM_BYTES),
        cost_estimate=pl.CostEstimate(flops=flops, bytes_accessed=nbytes, transcendentals=0),
        **kwargs,
    )
    return lambda *args: call(*(pltpu.with_memory_space_constraint(arg, pltpu.VMEM) for arg in args))


def shaped(shape, dtype):
    return jax.ShapeDtypeStruct(shape, dtype)


def near_core(shape, dtype):
    return pltpu.VMEM(shape, dtype)


def bring_body(far_ref, near_ref):
    pltpu.sync_copy(far_ref, near_ref)


def bands_body(base_ref, out_ref):
    groups, wide = base_ref.shape
    rows = out_ref.shape[1]
    row = lax.broadcasted_iota(jnp.int32, (8, wide), 0)
    for g in range(groups):
        band = jnp.broadcast_to(base_ref[g : g + 1, :], (8, wide))
        for bit in (1, 2, 4):
            band = jnp.where((row & bit) != 0, pltpu.roll(band, bit, 1), band)
        count = 8
        while count < rows:
            band = jnp.concatenate([band, pltpu.roll(band, count, 1)], axis=0)
            count *= 2
        out_ref[g] = band.astype(out_ref.dtype)


def wrapped(value, size):
    return lax.rem(value + 2 * size, size)


def project_body(x_ref, w_ref, *refs):
    *out_refs, held = refs
    z, col = lax.axis_index("dp"), lax.axis_index("col")
    nblocks, ncol, rows, depth = x_ref.shape
    width = held.shape[2]
    total = jnp.zeros((nblocks * rows, w_ref.shape[2]), F32)
    for dx in range(ncol):
        start = pl.multiple_of(wrapped(col - dx, ncol) * depth, depth)
        total += jnp.dot(
            x_ref[:, dx].reshape(nblocks * rows, depth),
            w_ref[0, pl.ds(start, depth), :],
            preferred_element_type=F32,
        )
    for owner in range(len(out_refs)):
        held[owner] = total[:, owner * width : (owner + 1) * width].astype(BF16)
    for ahead, out_ref in enumerate(out_refs):
        out_ref[0] = held[wrapped(z + ahead, len(out_refs))]


def assemble(pieces, held, ndp):
    z = lax.axis_index("dp")
    own, before, after, far_before, far_after = pieces
    held[z] = own[...]
    held[wrapped(z - 1, ndp)] = before[...]
    held[wrapped(z + 1, ndp)] = after[...]

    @pl.when(z >= ndp // 2)
    def _():
        held[z - ndp // 2] = far_before[...]

    @pl.when(z < ndp // 2)
    def _():
        held[z + ndp // 2] = far_after[...]


def input_grads(held, w_ref, all_ref, ncol):
    ndp = held.shape[0]
    tokens, depth = all_ref.shape[1], w_ref.shape[1] // ncol
    col = lax.axis_index("col")
    for i in range(3):
        for owner in range(ndp):
            width = held.shape[2]
            all_ref[i, :, owner * width : (owner + 1) * width] = held[owner, i * tokens : (i + 1) * tokens]
    for dx in range(ncol):
        start = pl.multiple_of(wrapped(col - dx, ncol) * depth, depth)
        total = jnp.zeros((tokens, depth), F32)
        for i in range(3):
            total += lax.dot_general(
                all_ref[i],
                w_ref[i, pl.ds(start, depth), :],
                (((1,), (1,)), ((), ())),
                preferred_element_type=F32,
            )
        yield dx, total


def first_grad_body(own, before, after, far_before, far_after, w_ref, out_ref, all_ref, small_ref, held):
    nblocks, ncol, rows, depth = out_ref.shape
    assemble((own, before, after, far_before, far_after), held, held.shape[0])
    small_ref[...] = held[:, 3 * nblocks * rows :]
    for dx, total in input_grads(held, w_ref, all_ref, ncol):
        out_ref[:, dx] = total.reshape(nblocks, rows, depth).astype(BF16)


def second_grad_body(held, w_ref, other_ref, all_ref, *out_refs):
    nblocks, ncol, rows, depth = other_ref.shape
    for dx, total in input_grads(held, w_ref, all_ref, ncol):
        for block in range(nblocks):
            both = total[block * rows : (block + 1) * rows] + other_ref[block, dx].astype(F32)
            out_refs[block * ncol + dx][...] = both.astype(BF16)


def weight_grad_body(scale, x0_ref, x1_ref, g0_ref, g1_ref, out_ref):
    nblocks, ncol, rows, depth = x0_ref.shape
    col = lax.axis_index("col")
    gm = jnp.concatenate([g0_ref[0], g1_ref[0]], axis=0)
    for dx in range(ncol):
        start = pl.multiple_of(wrapped(col - dx, ncol) * depth, depth)
        x = jnp.concatenate(
            [x_ref[:, dx].reshape(nblocks * rows, depth) for x_ref in (x0_ref, x1_ref)], axis=0
        )
        out_ref[0, pl.ds(start, depth), :] = scale * lax.dot_general(
            x, gm, (((0,), (0,)), ((), ())), preferred_element_type=F32
        )


def delayed(values, count):
    row = lax.broadcasted_iota(jnp.int32, values.shape, 0)
    return jnp.where(row >= count, pltpu.roll(values, count, 0), 0.0)


def advanced(values, count):
    rows = values.shape[0]
    row = lax.broadcasted_iota(jnp.int32, values.shape, 0)
    return jnp.where(row < rows - count, pltpu.roll(values, rows - count, 0), 0.0)


def middle_body(scale, nshort, nrow, *refs):
    sums, refs = (refs[:3], refs[3:6]), refs[6:]
    sf_ref, causal_ref, anti_ref, go_ref, near_ref, other_ref, mixed_ref, m_ref, gm_ref = refs
    tokens, width = go_ref.shape
    row = lax.axis_index("row")
    nblocks = nrow // 2
    rows = tokens // nrow

    def places():
        for chunk, start in enumerate((row, row + 1 - 2 * lax.rem(row, 2))):
            for block in range(nblocks):
                at = wrapped(start - 2 * block, nrow) * rows
                for i in range(3):
                    yield chunk, (i * nblocks + block) * rows, pl.multiple_of(i * tokens + at, 16)

    for chunk, place, at in places():
        held = [ref[place : place + rows].astype(F32) for ref in sums[chunk]]
        m_ref[pl.ds(at, rows)] = held[0] + held[1] + held[2]
    groups, block, span = causal_ref.shape
    members = width // groups
    nspans = tokens // block
    lane = lax.broadcasted_iota(jnp.int32, (block, width), 1) // members
    lanes = lax.broadcasted_iota(jnp.int32, (block, 2 * width), 1) % width // members

    def past(i, j):
        held = m_ref[i * tokens : (i + 1) * tokens]
        return held if j == 0 else delayed(held, j)

    def taps(j, i):
        return sf_ref[3 * j + i : 3 * j + i + 1, :]

    feats = [sum(taps(j, i) * past(i, j) for j in range(nshort)) for i in range(3)]
    product = (feats[1] * feats[2]).astype(BF16)
    zero = jnp.zeros((block, width), BF16)
    p_blocks = [zero] + [product[b * block : (b + 1) * block] for b in range(nspans)]
    p_pairs = [jnp.concatenate(p_blocks[b : b + 2], axis=0) for b in range(nspans)]

    def filtered(band_ref, pairs):
        bands = band_ref[...].reshape(groups * block, span)
        out = []
        for b in range(0, nspans, 2):
            both = jnp.dot(bands, jnp.concatenate(pairs[b : b + 2], axis=1), preferred_element_type=F32)
            for h in range(2):
                part = both[:, h * width : (h + 1) * width]
                picked = part[:block]
                for g in range(1, groups):
                    picked = jnp.where(lane == g, part[g * block : (g + 1) * block], picked)
                out.append(picked)
        return jnp.concatenate(out, axis=0)

    conv = filtered(causal_ref, p_pairs)
    upstream = go_ref[...].astype(F32)
    mixed_ref[...] = (feats[0] * conv).astype(BF16)
    grad_conv = (upstream * feats[0]).astype(BF16)
    c_blocks = [grad_conv[b * block : (b + 1) * block] for b in range(nspans)] + [zero]
    c_pairs = [jnp.concatenate(c_blocks[b : b + 2], axis=0) for b in range(nspans)]
    grad_product = filtered(anti_ref, c_pairs)

    corr = jnp.zeros((groups * block, span), F32)
    for b in range(0, nspans, 2):
        left = jnp.concatenate(c_blocks[b : b + 2], axis=1)
        stacked = jnp.concatenate(
            [jnp.where(lanes == g, left, jnp.zeros_like(left)) for g in range(groups)], axis=0
        )
        right = jnp.concatenate(p_pairs[b : b + 2], axis=1)
        corr += lax.dot_general(stacked, right, (((1,), (1,)), ((), ())), preferred_element_type=F32)
    turn = lax.broadcasted_iota(jnp.int32, (8, span), 0)
    sums = []
    for g in range(groups):
        part = corr[g * block : (g + 1) * block]
        count = block
        while count > 8:
            count //= 2
            part = part[:count] + pltpu.roll(part[count:], span - count, 1)
        for bit in (1, 2, 4):
            part = jnp.where((turn & bit) != 0, pltpu.roll(part, span - bit, 1), part)
        sums.append(jnp.sum(part, axis=0, keepdims=True))
    by_lag = jnp.concatenate(sums, axis=0)
    by_lag = scale * pltpu.roll(by_lag, span - 1, 1)[:, :block]

    grad_feats = [upstream * conv, grad_product * feats[2], grad_product * feats[1]]
    short_rows = []
    for j in range(nshort):
        for i in range(3):
            short_rows.append(scale * jnp.sum(grad_feats[i] * past(i, j), axis=0, keepdims=True))
    for i in range(3):
        total = taps(0, i) * grad_feats[i]
        for j in range(1, nshort):
            total += taps(j, i) * advanced(grad_feats[i], j)
        gm_ref[i * tokens : (i + 1) * tokens] = total.astype(BF16)
    for chunk, place, at in places():
        (near_ref, other_ref)[chunk][place : place + rows] = gm_ref[pl.ds(at, rows)]
    tail = other_ref.shape[0] - 3 * tokens // 2 - groups - 3 * nshort
    small = jnp.concatenate([by_lag] + short_rows + [jnp.zeros((tail, width), F32)], axis=0)
    other_ref[3 * tokens // 2 :] = small.astype(BF16)


def sum_over_line(own, right, far, left):
    ndp = lax.axis_size("dp")
    from_left = lax.ppermute(far, "dp", [(a, a + 1) for a in range(ndp // 2)])
    from_right = lax.ppermute(far, "dp", [(a, a - 1) for a in range(ndp // 2, ndp)])
    rightward = lax.ppermute(right + from_left, "dp", [(a, (a + 1) % ndp) for a in range(ndp)])
    leftward = lax.ppermute(left + from_right, "dp", [(a, (a - 1) % ndp) for a in range(ndp)])
    return own, rightward, leftward


def gather_over_line(own):
    ndp = lax.axis_size("dp")
    before = lax.ppermute(own, "dp", [(a, (a + 1) % ndp) for a in range(ndp)])
    after = lax.ppermute(own, "dp", [(a, (a - 1) % ndp) for a in range(ndp)])
    far_before = lax.ppermute(before, "dp", [(a - 1, a) for a in range(ndp // 2, ndp)])
    far_after = lax.ppermute(after, "dp", [(a + 1, a) for a in range(ndp // 2)])
    return own, before, after, far_before, far_after


def move_activations(tokens, in_weight, short_filter, long_filter, grad_out):
    ndp, nrow, ncol = (lax.axis_size(a) for a in ("dp", "row", "col"))
    z = lax.axis_index("dp")
    rows, dcol = tokens.shape
    local = grad_out.shape[1]
    nshort = short_filter.shape[0]
    ngroups, ntaps = long_filter.shape
    seq = rows * ndp
    width, groups = local // ndp, ngroups // ndp
    drow = in_weight.shape[0]
    scale = float(seq) ** -0.5
    nblocks = nrow // 2
    chunk = nblocks * rows
    swap = [(a * nrow + b, b * nrow + a) for a in range(ndp) for b in range(nrow)]
    partner = [(a, a + 1 - 2 * (a % 2)) for a in range(nrow)]
    places = [(dy, dx) for dy in range(nblocks) for dx in range(ncol)]

    def offset(dy, dx):
        return [
            (a * ncol + b, (a + 2 * dy) % nrow * ncol + (b + dx) % ncol) for a in range(nrow) for b in range(ncol)
        ]

    w = jnp.transpose(in_weight, (1, 0, 2))
    moved = lax.ppermute(tokens, ("dp", "row"), swap)
    w = pl.pallas_call(
        bring_body,
        out_shape=near_core(w.shape, BF16),
        in_specs=[pl.BlockSpec(memory_space=pl.ANY)],
        compiler_params=pltpu.CompilerParams(vmem_limit_bytes=VMEM_BYTES),
    )(w)
    moved, grad_out, w = lax.optimization_barrier((moved, grad_out, w))
    near = [moved] + [lax.ppermute(moved, ("row", "col"), offset(*p)) for p in places[1:]]
    upstream = lax.all_to_all(grad_out, "dp", split_axis=1, concat_axis=0, tiled=True)
    upstream, *near = lax.optimization_barrier((upstream, *near))
    x0 = jnp.stack(near).reshape(nblocks, ncol, rows, dcol)
    x1 = lax.ppermute(x0, "row", partner)

    sf = lax.dynamic_slice_in_dim(short_filter, z * width, width, 2).reshape(3 * nshort, width)
    lf = lax.dynamic_slice_in_dim(long_filter, z * groups, groups, 0).astype(F32)
    zeros = functools.partial(jnp.zeros, dtype=F32)
    bases = jnp.concatenate(
        [
            jnp.concatenate([zeros((groups, 1)), lf[:, ::-1], zeros((groups, ntaps - 1))], axis=1),
            jnp.concatenate([lf, zeros((groups, ntaps))], axis=1),
        ],
        axis=0,
    )
    bands = kernel_call(bands_body, near_core((2 * groups, ntaps, 2 * ntaps), BF16))(bases)

    mm_flops = seq * drow * 3 * local
    mm_bytes = seq * drow + 6 * drow * local + 3 * seq * local
    sums = []
    for x in (x0, x1):
        parts = kernel_call(
            project_body,
            [near_core((3, chunk, width), BF16)] * ndp,
            grid=(3,),
            in_specs=[
                pl.BlockSpec((nblocks, ncol, rows, dcol), lambda i: (0, 0, 0, 0)),
                pl.BlockSpec((1, drow, local), lambda i: (i, 0, 0)),
            ],
            out_specs=[pl.BlockSpec((1, chunk, width), lambda i: (i, 0, 0))] * ndp,
            scratch=[pltpu.VMEM((ndp, chunk, width), BF16)],
            flops=mm_flops,
            nbytes=mm_bytes,
        )(x, w)
        sums += sum_over_line(*(p.reshape(3 * chunk, width) for p in parts))

    extra = -(-(groups + 3 * nshort) // 16) * 16
    half = pl.BlockSpec((groups, ntaps, 2 * ntaps), lambda i: (0, 0, 0))
    other = pl.BlockSpec((groups, ntaps, 2 * ntaps), lambda i: (1, 0, 0))
    whole = lambda *shape: pl.BlockSpec(shape, lambda i: (0,) * len(shape))
    grad_near, grad_other, mixed = kernel_call(
        functools.partial(middle_body, scale, nshort, nrow),
        (
            shaped((3 * chunk, width), BF16),
            near_core((3 * chunk + extra, width), BF16),
            shaped((seq, width), BF16),
        ),
        grid=(1,),
        in_specs=[whole(3 * chunk, width)] * 6
        + [whole(3 * nshort, width), half, other, whole(seq, width)],
        out_specs=(whole(3 * chunk, width), whole(3 * chunk + extra, width), whole(seq, width)),
        scratch=[pltpu.VMEM((3 * seq, width), F32), pltpu.VMEM((3 * seq, width), BF16)],
        flops=3 * 2 * groups * ntaps * 2 * ntaps * width * (seq // ntaps),
        nbytes=2 * width * seq * 14,
    )(*sums, sf, bands, bands, upstream)
    mixed = lax.all_to_all(mixed, "dp", split_axis=0, concat_axis=1, tiled=True)
    mixed, *pieces = lax.optimization_barrier((mixed, *gather_over_line(grad_other)))
    block = near_core((rows, dcol), BF16)
    all_shape = near_core((3, chunk, local), BF16)
    out_first, all_other, small = kernel_call(
        first_grad_body,
        (near_core((nblocks, ncol, rows, dcol), BF16), all_shape, near_core((ndp, extra, width), BF16)),
        scratch=[pltpu.VMEM((ndp, 3 * chunk + extra, width), BF16)],
        flops=mm_flops,
        nbytes=mm_bytes,
    )(*pieces, w)
    gathered = lax.all_gather(grad_near, "dp", axis=0)
    gathered, out_first = lax.optimization_barrier((gathered, out_first))
    from_partner = lax.ppermute(out_first, "row", partner)
    all_near, *blocks = kernel_call(
        second_grad_body,
        [all_shape] + [block] * len(places),
        flops=mm_flops,
        nbytes=mm_bytes,
    )(gathered, w, from_partner)
    arrived = blocks[0].astype(F32)
    for (dy, dx), sent in zip(places[1:], blocks[1:]):
        back = [(b, a) for a, b in offset(dy, dx)]
        arrived += lax.ppermute(sent, ("row", "col"), back).astype(F32)
    grad_in = lax.ppermute(arrived.astype(BF16), ("dp", "row"), swap)

    x_spec = pl.BlockSpec((nblocks, ncol, rows, dcol), lambda i: (0, 0, 0, 0))
    g_spec = pl.BlockSpec((1, chunk, local), lambda i: (i, 0, 0))
    grad_weight = kernel_call(
        functools.partial(weight_grad_body, scale),
        shaped((3, drow, local), F32),
        grid=(3,),
        in_specs=[x_spec, x_spec, g_spec, g_spec],
        out_specs=pl.BlockSpec((1, drow, local), lambda i: (i, 0, 0)),
        flops=2 * mm_flops,
        nbytes=2 * mm_bytes,
    )(x0, x1, all_near, all_other)
    grad_weight = jnp.transpose(grad_weight, (1, 0, 2))
    small = small.astype(F32)
    grad_long = small[:, :groups, ::-1].reshape(ngroups, ntaps)
    grad_short = (
        small[:, groups : groups + 3 * nshort].transpose(1, 0, 2).reshape(nshort, 3, local)
    )
    return (mixed, grad_in, grad_weight, grad_long, grad_short)


def from_behind(block, axis, distance):
    devices = range(lax.axis_size(axis))
    route = [(i - distance, i) for i in devices if i - distance in devices]
    return lax.ppermute(block, axis, route)


def toeplitz(leading, rows, span):
    groups = leading.shape[0]
    width = rows + span
    seed_row = jnp.concatenate(
        [leading, jnp.zeros((groups, width - leading.shape[1]), leading.dtype)], axis=1
    )
    tiled = jnp.tile(seed_row, (1, rows))
    skewed = tiled[:, : rows * (width - 1)].reshape(groups, rows, width - 1)
    return skewed[:, :, :span]


def to_groups(values, ngroups, members):
    count = values.shape[0]
    return values.reshape(count, ngroups, members).transpose(1, 2, 0)


def from_groups(values):
    groups, members, count = values.shape
    return values.transpose(2, 0, 1).reshape(count, groups * members)


def move_weights(tokens, in_weight, short_filter, long_filter, grad_out):
    rows = tokens.shape[0]
    local = grad_out.shape[1]
    nshort = short_filter.shape[0]
    ntaps = long_filter.shape[1]
    ngroups = long_filter.shape[0]
    members = local // ngroups
    margin = ntaps - 1
    span = rows + margin
    scale = float(rows * lax.axis_size("dp")) ** (-0.5)
    whole = lax.all_gather(tokens, ("row", "col"), axis=1, tiled=True)
    full_w = lax.all_gather(in_weight, "dp", axis=0, tiled=True)
    mixed_in = jnp.einsum("sd,dic->sic", whole, full_w, preferred_element_type=jnp.float32).astype(
        jnp.bfloat16
    )
    before = from_behind(mixed_in[rows - margin - nshort + 1 :], "dp", 1)
    extended = jnp.concatenate([before, mixed_in], axis=0).astype(jnp.float32)
    long_feats = jnp.zeros((span, 3, local), jnp.float32)
    for j in range(nshort):
        long_feats = (
            long_feats + short_filter[j][None] * extended[nshort - 1 - j : nshort - 1 - j + span]
        )
    product_ext = (long_feats[:, 1] * long_feats[:, 2]).astype(jnp.bfloat16)
    feats = long_feats[margin:]
    short_rows = extended[margin:]
    product_cols = to_groups(product_ext, ngroups, members)
    causal = toeplitz(long_filter[:, ::-1], rows, span)
    conv = from_groups(
        jnp.einsum("gst,gct->gcs", causal, product_cols, preferred_element_type=jnp.float32)
    )
    mixed = (feats[:, 0] * conv).astype(jnp.bfloat16)
    upstream = grad_out.astype(jnp.float32)
    grad_query = upstream * conv
    grad_conv = (upstream * feats[:, 0]).astype(jnp.bfloat16)
    after = from_behind(grad_conv[:margin], "dp", -1)
    grad_ext = jnp.concatenate([grad_conv, after], axis=0)
    anti = toeplitz(long_filter, rows, span)
    grad_product = from_groups(
        jnp.einsum(
            "gst,gct->gcs",
            anti,
            to_groups(grad_ext, ngroups, members),
            preferred_element_type=jnp.float32,
        )
    )
    reversed_cols = jnp.concatenate(
        [product_cols[:, :, ::-1], jnp.zeros((ngroups, members, rows), product_cols.dtype)], axis=2
    )
    width = span + rows
    pairs = jnp.einsum(
        "gcs,gcu->gsu",
        to_groups(grad_conv, ngroups, members),
        reversed_cols,
        preferred_element_type=jnp.float32,
    )
    diagonal = pairs.reshape(ngroups, rows * width)[:, : rows * (width - 1)].reshape(
        ngroups, rows, width - 1
    )
    filter_part = jnp.sum(diagonal[:, :, rows - 1 : rows - 1 + ntaps], axis=1)
    grad_feats = jnp.stack(
        [grad_query, grad_product * feats[:, 2], grad_product * feats[:, 1]], axis=1
    )
    later = from_behind(grad_feats[: nshort - 1], "dp", -1)
    feats_ext = jnp.concatenate([grad_feats, later], axis=0)
    grad_acc = jnp.zeros((rows, 3, local), jnp.float32)
    for j in range(nshort):
        grad_acc = grad_acc + short_filter[j][None] * feats_ext[j : j + rows]
    grad_mixed = grad_acc.astype(jnp.bfloat16)
    short_part = jnp.stack(
        [
            jnp.sum(grad_feats * short_rows[nshort - 1 - j : nshort - 1 - j + rows], axis=0)
            for j in range(nshort)
        ]
    )
    filter_total, short_total = (
        lax.psum(filter_part.astype(jnp.bfloat16), "dp").astype(jnp.float32),
        lax.psum(short_part.astype(jnp.bfloat16), "dp").astype(jnp.float32),
    )
    grad_long = filter_total * scale
    grad_short = short_total * scale
    partial_in = jnp.einsum("sic,dic->sd", grad_mixed, full_w, preferred_element_type=jnp.float32)
    summed_in = lax.psum_scatter(
        partial_in.astype(jnp.bfloat16), ("row", "col"), scatter_dimension=1, tiled=True
    )
    weight_term = (
        jnp.einsum("sd,sic->dic", whole, grad_mixed, preferred_element_type=jnp.float32) * scale
    )
    grad_weight = lax.psum_scatter(
        weight_term.astype(jnp.bfloat16), "dp", scatter_dimension=0, tiled=True
    ).astype(jnp.float32)
    return (mixed, summed_in, grad_weight, grad_long, grad_short)


def fits_whole_sequences(mesh, tokens, in_weight, short_filter, long_filter, grad_out):
    ndp, nrow, ncol = (mesh.shape[a] for a in ("dp", "row", "col"))
    seq, channels = grad_out.shape
    groups, ntaps = long_filter.shape
    local = channels // (nrow * ncol)
    width, rows = local // ndp, seq // ndp
    return (
        seq < tokens.shape[1]
        and ndp == nrow == 4
        and ncol * (tokens.shape[1] // (nrow * ncol)) == in_weight.shape[0] // ndp
        and ntaps == width == 128
        and seq % (2 * ntaps) == 0
        and rows % 16 == 0
        and groups % (8 * ndp * nrow * ncol) == 0
    )


def solution(mesh):
    placed = (
        P("dp", ("row", "col")),
        P("dp", None, ("row", "col")),
        P(None, None, ("row", "col")),
        P(("row", "col"), None),
        P("dp", ("row", "col")),
    )
    gives = (
        P("dp", ("row", "col")),
        P("dp", ("row", "col")),
        P("dp", None, ("row", "col")),
        P(("row", "col"), None),
        P(None, None, ("row", "col")),
    )

    def run(*arrays):
        plan = move_activations if fits_whole_sequences(mesh, *arrays) else move_weights
        return jax.shard_map(
            plan, mesh=mesh, in_specs=placed, out_specs=gives, check_vma=False
        )(*arrays)

    return run
```

```python
import functools

import jax
import jax.numpy as jnp
from jax import lax
from jax.experimental import pallas as pl
from jax.experimental.pallas import tpu as pltpu
from jax.sharding import PartitionSpec as P

VMEM_BYTES = 48 * 2**20
F32 = jnp.float32
BF16 = jnp.bfloat16


def kernel_call(body, outs, grid=None, in_specs=None, out_specs=None, scratch=(), flops=0, nbytes=0):
    kwargs = {}
    if grid is not None:
        kwargs = dict(grid=grid, in_specs=in_specs, out_specs=out_specs)
    return pl.pallas_call(
        body,
        out_shape=outs,
        scratch_shapes=scratch,
        compiler_params=pltpu.CompilerParams(vmem_limit_bytes=VMEM_BYTES),
        cost_estimate=pl.CostEstimate(flops=flops, bytes_accessed=nbytes, transcendentals=0),
        **kwargs,
    )


def shaped(shape, dtype):
    return jax.ShapeDtypeStruct(shape, dtype)


def bands_body(base_ref, out_ref):
    groups, wide = base_ref.shape
    rows = out_ref.shape[1]
    row = lax.broadcasted_iota(jnp.int32, (8, wide), 0)
    for g in range(groups):
        band = jnp.broadcast_to(base_ref[g : g + 1, :], (8, wide))
        for bit in (1, 2, 4):
            band = jnp.where((row & bit) != 0, pltpu.roll(band, bit, 1), band)
        count = 8
        while count < rows:
            band = jnp.concatenate([band, pltpu.roll(band, count, 1)], axis=0)
            count *= 2
        out_ref[g] = band.astype(out_ref.dtype)


def wrapped(value, size):
    return lax.rem(value + 2 * size, size)


def project_body(x_ref, w_ref, *refs):
    *out_refs, held = refs
    z, col = lax.axis_index("dp"), lax.axis_index("col")
    nblocks, ncol, rows, depth = x_ref.shape
    width = held.shape[2]
    total = jnp.zeros((nblocks * rows, w_ref.shape[2]), F32)
    for dx in range(ncol):
        start = pl.multiple_of(wrapped(col - dx, ncol) * depth, depth)
        total += jnp.dot(
            x_ref[:, dx].reshape(nblocks * rows, depth),
            w_ref[0, pl.ds(start, depth), :],
            preferred_element_type=F32,
        )
    for owner in range(len(out_refs)):
        held[owner] = total[:, owner * width : (owner + 1) * width].astype(BF16)
    for ahead, out_ref in enumerate(out_refs):
        out_ref[0] = held[wrapped(z + ahead, len(out_refs))]


def assemble(pieces, held, ndp):
    z = lax.axis_index("dp")
    own, before, after, far_before, far_after = pieces
    held[z] = own[...]
    held[wrapped(z - 1, ndp)] = before[...]
    held[wrapped(z + 1, ndp)] = after[...]

    @pl.when(z >= ndp // 2)
    def _():
        held[z - ndp // 2] = far_before[...]

    @pl.when(z < ndp // 2)
    def _():
        held[z + ndp // 2] = far_after[...]


def input_grad_body(*refs):
    pieces, (w_ref, partner_w_ref, near_ref, far_ref, small_ref), refs = refs[:10], refs[10:15], refs[15:]
    *out_refs, near_held, far_held = refs
    tokens = near_ref.shape[1]
    rows, depth = out_refs[0].shape
    ndp, _, width = near_held.shape
    ncol = w_ref.shape[1] // depth
    col = lax.axis_index("col")
    assemble(pieces[:5], near_held, ndp)
    assemble(pieces[5:], far_held, ndp)
    small_ref[...] = near_held[:, 3 * tokens :]
    for held, all_ref in ((near_held, near_ref), (far_held, far_ref)):
        for i in range(3):
            for owner in range(ndp):
                all_ref[i, :, owner * width : (owner + 1) * width] = held[owner, i * tokens : (i + 1) * tokens]
    for dx in range(ncol):
        start = pl.multiple_of(wrapped(col - dx, ncol) * depth, depth)
        total = jnp.zeros((tokens, depth), F32)
        for all_ref, weights in ((near_ref, w_ref), (far_ref, partner_w_ref)):
            for i in range(3):
                total += lax.dot_general(
                    all_ref[i],
                    weights[i, pl.ds(start, depth), :],
                    (((1,), (1,)), ((), ())),
                    preferred_element_type=F32,
                )
        for block in range(tokens // rows):
            out_refs[block * ncol + dx][...] = total[block * rows : (block + 1) * rows].astype(BF16)


def weight_grad_body(scale, x0_ref, x1_ref, g0_ref, g1_ref, out_ref):
    nblocks, ncol, rows, depth = x0_ref.shape
    col = lax.axis_index("col")
    gm = jnp.concatenate([g0_ref[0], g1_ref[0]], axis=0)
    for dx in range(ncol):
        start = pl.multiple_of(wrapped(col - dx, ncol) * depth, depth)
        x = jnp.concatenate(
            [x_ref[:, dx].reshape(nblocks * rows, depth) for x_ref in (x0_ref, x1_ref)], axis=0
        )
        out_ref[0, pl.ds(start, depth), :] = scale * lax.dot_general(
            x, gm, (((0,), (0,)), ((), ())), preferred_element_type=F32
        )


def delayed(values, count):
    row = lax.broadcasted_iota(jnp.int32, values.shape, 0)
    return jnp.where(row >= count, pltpu.roll(values, count, 0), 0.0)


def advanced(values, count):
    rows = values.shape[0]
    row = lax.broadcasted_iota(jnp.int32, values.shape, 0)
    return jnp.where(row < rows - count, pltpu.roll(values, rows - count, 0), 0.0)


def middle_body(scale, nshort, nrow, *refs):
    sums, refs = (refs[:3], refs[3:6]), refs[6:]
    sf_ref, causal_ref, anti_ref, go_ref, near_ref, other_ref, mixed_ref, m_ref, gm_ref = refs
    tokens, width = go_ref.shape
    row = lax.axis_index("row")
    nblocks = nrow // 2
    rows = tokens // nrow

    def places():
        for chunk, start in enumerate((row, row + 1 - 2 * lax.rem(row, 2))):
            for block in range(nblocks):
                at = wrapped(start - 2 * block, nrow) * rows
                for i in range(3):
                    yield chunk, (i * nblocks + block) * rows, pl.multiple_of(i * tokens + at, 16)

    for chunk, place, at in places():
        held = [ref[place : place + rows].astype(F32) for ref in sums[chunk]]
        m_ref[pl.ds(at, rows)] = held[0] + held[1] + held[2]
    groups, block, span = causal_ref.shape
    members = width // groups
    nspans = tokens // block
    lane = lax.broadcasted_iota(jnp.int32, (block, width), 1) // members
    lanes = lax.broadcasted_iota(jnp.int32, (block, 2 * width), 1) % width // members

    def past(i, j):
        held = m_ref[i * tokens : (i + 1) * tokens]
        return held if j == 0 else delayed(held, j)

    def taps(j, i):
        return sf_ref[3 * j + i : 3 * j + i + 1, :]

    feats = [sum(taps(j, i) * past(i, j) for j in range(nshort)) for i in range(3)]
    product = (feats[1] * feats[2]).astype(BF16)
    zero = jnp.zeros((block, width), BF16)
    p_blocks = [zero] + [product[b * block : (b + 1) * block] for b in range(nspans)]
    p_pairs = [jnp.concatenate(p_blocks[b : b + 2], axis=0) for b in range(nspans)]

    def filtered(band_ref, pairs):
        bands = band_ref[...].reshape(groups * block, span)
        out = []
        for b in range(0, nspans, 2):
            both = jnp.dot(bands, jnp.concatenate(pairs[b : b + 2], axis=1), preferred_element_type=F32)
            for h in range(2):
                part = both[:, h * width : (h + 1) * width]
                picked = part[:block]
                for g in range(1, groups):
                    picked = jnp.where(lane == g, part[g * block : (g + 1) * block], picked)
                out.append(picked)
        return jnp.concatenate(out, axis=0)

    conv = filtered(causal_ref, p_pairs)
    upstream = go_ref[...].astype(F32)
    mixed_ref[...] = (feats[0] * conv).astype(BF16)
    grad_conv = (upstream * feats[0]).astype(BF16)
    c_blocks = [grad_conv[b * block : (b + 1) * block] for b in range(nspans)] + [zero]
    c_pairs = [jnp.concatenate(c_blocks[b : b + 2], axis=0) for b in range(nspans)]
    grad_product = filtered(anti_ref, c_pairs)

    corr = jnp.zeros((groups * block, span), F32)
    for b in range(0, nspans, 2):
        left = jnp.concatenate(c_blocks[b : b + 2], axis=1)
        stacked = jnp.concatenate(
            [jnp.where(lanes == g, left, jnp.zeros_like(left)) for g in range(groups)], axis=0
        )
        right = jnp.concatenate(p_pairs[b : b + 2], axis=1)
        corr += lax.dot_general(stacked, right, (((1,), (1,)), ((), ())), preferred_element_type=F32)
    turn = lax.broadcasted_iota(jnp.int32, (8, span), 0)
    sums = []
    for g in range(groups):
        part = corr[g * block : (g + 1) * block]
        count = block
        while count > 8:
            count //= 2
            part = part[:count] + pltpu.roll(part[count:], span - count, 1)
        for bit in (1, 2, 4):
            part = jnp.where((turn & bit) != 0, pltpu.roll(part, span - bit, 1), part)
        sums.append(jnp.sum(part, axis=0, keepdims=True))
    by_lag = jnp.concatenate(sums, axis=0)
    by_lag = scale * pltpu.roll(by_lag, span - 1, 1)[:, :block]

    grad_feats = [upstream * conv, grad_product * feats[2], grad_product * feats[1]]
    short_rows = []
    for j in range(nshort):
        for i in range(3):
            short_rows.append(scale * jnp.sum(grad_feats[i] * past(i, j), axis=0, keepdims=True))
    for i in range(3):
        total = taps(0, i) * grad_feats[i]
        for j in range(1, nshort):
            total += taps(j, i) * advanced(grad_feats[i], j)
        gm_ref[i * tokens : (i + 1) * tokens] = total.astype(BF16)
    for chunk, place, at in places():
        (near_ref, other_ref)[chunk][place : place + rows] = gm_ref[pl.ds(at, rows)]
    tail = near_ref.shape[0] - 3 * tokens // 2 - groups - 3 * nshort
    small = jnp.concatenate([by_lag] + short_rows + [jnp.zeros((tail, width), F32)], axis=0)
    near_ref[3 * tokens // 2 :] = small.astype(BF16)


def sum_over_line(own, right, far, left):
    ndp = lax.axis_size("dp")
    from_left = lax.ppermute(far, "dp", [(a, a + 1) for a in range(ndp // 2)])
    from_right = lax.ppermute(far, "dp", [(a, a - 1) for a in range(ndp // 2, ndp)])
    rightward = lax.ppermute(right + from_left, "dp", [(a, (a + 1) % ndp) for a in range(ndp)])
    leftward = lax.ppermute(left + from_right, "dp", [(a, (a - 1) % ndp) for a in range(ndp)])
    return own, rightward, leftward


def gather_over_line(own, across):
    ndp, nrow = lax.axis_size("dp"), lax.axis_size("row")

    def shift(count):
        return [
            (a * nrow + r, (a + count) % ndp * nrow + (r + 1 - 2 * (r % 2) if across else r))
            for a in range(ndp)
            for r in range(nrow)
        ]

    before = lax.ppermute(own, ("dp", "row"), shift(1))
    after = lax.ppermute(own, ("dp", "row"), shift(-1))
    here = lax.ppermute(own, ("dp", "row"), shift(0)) if across else own
    far_before = lax.ppermute(before, "dp", [(a - 1, a) for a in range(ndp // 2, ndp)])
    far_after = lax.ppermute(after, "dp", [(a + 1, a) for a in range(ndp // 2)])
    return here, before, after, far_before, far_after


def move_activations(tokens, in_weight, short_filter, long_filter, grad_out):
    ndp, nrow, ncol = (lax.axis_size(a) for a in ("dp", "row", "col"))
    z = lax.axis_index("dp")
    rows, dcol = tokens.shape
    local = grad_out.shape[1]
    nshort = short_filter.shape[0]
    ngroups, ntaps = long_filter.shape
    seq = rows * ndp
    width, groups = local // ndp, ngroups // ndp
    drow = in_weight.shape[0]
    scale = float(seq) ** -0.5
    nblocks = nrow // 2
    chunk = nblocks * rows
    swap = [(a * nrow + b, b * nrow + a) for a in range(ndp) for b in range(nrow)]
    partner = [(a, a + 1 - 2 * (a % 2)) for a in range(nrow)]
    places = [(dy, dx) for dy in range(nblocks) for dx in range(ncol)]

    def offset(dy, dx):
        return [
            (a * ncol + b, (a + 2 * dy) % nrow * ncol + (b + dx) % ncol) for a in range(nrow) for b in range(ncol)
        ]

    w = jnp.transpose(in_weight, (1, 0, 2))
    moved = lax.ppermute(tokens, ("dp", "row"), swap)
    near = [moved] + [lax.ppermute(moved, ("row", "col"), offset(*p)) for p in places[1:]]
    upstream = lax.all_to_all(grad_out, "dp", split_axis=1, concat_axis=0, tiled=True)
    upstream, *near = lax.optimization_barrier((upstream, *near))
    x0 = jnp.stack(near).reshape(nblocks, ncol, rows, dcol)
    x1 = lax.ppermute(x0, "row", partner)

    sf = lax.dynamic_slice_in_dim(short_filter, z * width, width, 2).reshape(3 * nshort, width)
    lf = lax.dynamic_slice_in_dim(long_filter, z * groups, groups, 0).astype(F32)
    zeros = functools.partial(jnp.zeros, dtype=F32)
    bases = jnp.concatenate(
        [
            jnp.concatenate([zeros((groups, 1)), lf[:, ::-1], zeros((groups, ntaps - 1))], axis=1),
            jnp.concatenate([lf, zeros((groups, ntaps))], axis=1),
        ],
        axis=0,
    )
    bands = kernel_call(bands_body, shaped((2 * groups, ntaps, 2 * ntaps), BF16))(bases)

    mm_flops = seq * drow * 3 * local
    mm_bytes = seq * drow + 6 * drow * local + 3 * seq * local
    sums = []
    for x in (x0, x1):
        parts = kernel_call(
            project_body,
            [shaped((3, chunk, width), BF16)] * ndp,
            grid=(3,),
            in_specs=[
                pl.BlockSpec((nblocks, ncol, rows, dcol), lambda i: (0, 0, 0, 0)),
                pl.BlockSpec((1, drow, local), lambda i: (i, 0, 0)),
            ],
            out_specs=[pl.BlockSpec((1, chunk, width), lambda i: (i, 0, 0))] * ndp,
            scratch=[pltpu.VMEM((ndp, chunk, width), BF16)],
            flops=mm_flops,
            nbytes=mm_bytes,
        )(x, w)
        sums += sum_over_line(*(p.reshape(3 * chunk, width) for p in parts))

    extra = -(-(groups + 3 * nshort) // 16) * 16
    half = pl.BlockSpec((groups, ntaps, 2 * ntaps), lambda i: (0, 0, 0))
    other = pl.BlockSpec((groups, ntaps, 2 * ntaps), lambda i: (1, 0, 0))
    whole = lambda *shape: pl.BlockSpec(shape, lambda i: (0,) * len(shape))
    grad_near, grad_other, mixed = kernel_call(
        functools.partial(middle_body, scale, nshort, nrow),
        (
            shaped((3 * chunk + extra, width), BF16),
            shaped((3 * chunk, width), BF16),
            shaped((seq, width), BF16),
        ),
        grid=(1,),
        in_specs=[whole(3 * chunk, width)] * 6
        + [whole(3 * nshort, width), half, other, whole(seq, width)],
        out_specs=(whole(3 * chunk + extra, width), whole(3 * chunk, width), whole(seq, width)),
        scratch=[pltpu.VMEM((3 * seq, width), F32), pltpu.VMEM((3 * seq, width), BF16)],
        flops=3 * 2 * groups * ntaps * 2 * ntaps * width * (seq // ntaps),
        nbytes=2 * width * seq * 14,
    )(*sums, sf, bands, bands, upstream)
    mixed = lax.all_to_all(mixed, "dp", split_axis=0, concat_axis=1, tiled=True)
    pieces = (*gather_over_line(grad_near, False), *gather_over_line(grad_other, True))
    mixed, *pieces = lax.optimization_barrier((mixed, *pieces))
    block = shaped((rows, dcol), BF16)
    all_shape = shaped((3, chunk, local), BF16)
    all_near, all_far, small, *blocks = kernel_call(
        input_grad_body,
        [all_shape, all_shape, shaped((ndp, extra, width), BF16)] + [block] * len(places),
        scratch=[
            pltpu.VMEM((ndp, 3 * chunk + extra, width), BF16),
            pltpu.VMEM((ndp, 3 * chunk, width), BF16),
        ],
        flops=2 * mm_flops,
        nbytes=2 * mm_bytes,
    )(*pieces, w, lax.ppermute(w, "row", partner))
    arrivals = [
        lax.ppermute(sent, ("row", "col"), [(b, a) for a, b in offset(*p)])
        for p, sent in zip(places[1:], blocks[1:])
    ]
    arrived = sum((a.astype(F32) for a in arrivals), blocks[0].astype(F32)).astype(BF16)
    all_other = lax.ppermute(all_far, "row", partner)
    arrived, all_other = lax.optimization_barrier((arrived, all_other))
    grad_in = lax.ppermute(arrived, ("dp", "row"), swap)

    x_spec = pl.BlockSpec((nblocks, ncol, rows, dcol), lambda i: (0, 0, 0, 0))
    g_spec = pl.BlockSpec((1, chunk, local), lambda i: (i, 0, 0))
    grad_weight = kernel_call(
        functools.partial(weight_grad_body, scale),
        shaped((3, drow, local), F32),
        grid=(3,),
        in_specs=[x_spec, x_spec, g_spec, g_spec],
        out_specs=pl.BlockSpec((1, drow, local), lambda i: (i, 0, 0)),
        flops=2 * mm_flops,
        nbytes=2 * mm_bytes,
    )(x0, x1, all_near, all_other)
    grad_weight = jnp.transpose(grad_weight, (1, 0, 2))
    small = small.astype(F32)
    grad_long = small[:, :groups, ::-1].reshape(ngroups, ntaps)
    grad_short = (
        small[:, groups : groups + 3 * nshort].transpose(1, 0, 2).reshape(nshort, 3, local)
    )
    return (mixed, grad_in, grad_weight, grad_long, grad_short)


def from_behind(block, axis, distance):
    devices = range(lax.axis_size(axis))
    route = [(i - distance, i) for i in devices if i - distance in devices]
    return lax.ppermute(block, axis, route)


def toeplitz(leading, rows, span):
    groups = leading.shape[0]
    width = rows + span
    seed_row = jnp.concatenate(
        [leading, jnp.zeros((groups, width - leading.shape[1]), leading.dtype)], axis=1
    )
    tiled = jnp.tile(seed_row, (1, rows))
    skewed = tiled[:, : rows * (width - 1)].reshape(groups, rows, width - 1)
    return skewed[:, :, :span]


def to_groups(values, ngroups, members):
    count = values.shape[0]
    return values.reshape(count, ngroups, members).transpose(1, 2, 0)


def from_groups(values):
    groups, members, count = values.shape
    return values.transpose(2, 0, 1).reshape(count, groups * members)


def move_weights(tokens, in_weight, short_filter, long_filter, grad_out):
    rows = tokens.shape[0]
    local = grad_out.shape[1]
    nshort = short_filter.shape[0]
    ntaps = long_filter.shape[1]
    ngroups = long_filter.shape[0]
    members = local // ngroups
    margin = ntaps - 1
    span = rows + margin
    scale = float(rows * lax.axis_size("dp")) ** (-0.5)
    whole = lax.all_gather(tokens, ("row", "col"), axis=1, tiled=True)
    full_w = lax.all_gather(in_weight, "dp", axis=0, tiled=True)
    mixed_in = jnp.einsum("sd,dic->sic", whole, full_w, preferred_element_type=jnp.float32).astype(
        jnp.bfloat16
    )
    before = from_behind(mixed_in[rows - margin - nshort + 1 :], "dp", 1)
    extended = jnp.concatenate([before, mixed_in], axis=0).astype(jnp.float32)
    long_feats = jnp.zeros((span, 3, local), jnp.float32)
    for j in range(nshort):
        long_feats = (
            long_feats + short_filter[j][None] * extended[nshort - 1 - j : nshort - 1 - j + span]
        )
    product_ext = (long_feats[:, 1] * long_feats[:, 2]).astype(jnp.bfloat16)
    feats = long_feats[margin:]
    short_rows = extended[margin:]
    product_cols = to_groups(product_ext, ngroups, members)
    causal = toeplitz(long_filter[:, ::-1], rows, span)
    conv = from_groups(
        jnp.einsum("gst,gct->gcs", causal, product_cols, preferred_element_type=jnp.float32)
    )
    mixed = (feats[:, 0] * conv).astype(jnp.bfloat16)
    upstream = grad_out.astype(jnp.float32)
    grad_query = upstream * conv
    grad_conv = (upstream * feats[:, 0]).astype(jnp.bfloat16)
    after = from_behind(grad_conv[:margin], "dp", -1)
    grad_ext = jnp.concatenate([grad_conv, after], axis=0)
    anti = toeplitz(long_filter, rows, span)
    grad_product = from_groups(
        jnp.einsum(
            "gst,gct->gcs",
            anti,
            to_groups(grad_ext, ngroups, members),
            preferred_element_type=jnp.float32,
        )
    )
    reversed_cols = jnp.concatenate(
        [product_cols[:, :, ::-1], jnp.zeros((ngroups, members, rows), product_cols.dtype)], axis=2
    )
    width = span + rows
    pairs = jnp.einsum(
        "gcs,gcu->gsu",
        to_groups(grad_conv, ngroups, members),
        reversed_cols,
        preferred_element_type=jnp.float32,
    )
    diagonal = pairs.reshape(ngroups, rows * width)[:, : rows * (width - 1)].reshape(
        ngroups, rows, width - 1
    )
    filter_part = jnp.sum(diagonal[:, :, rows - 1 : rows - 1 + ntaps], axis=1)
    grad_feats = jnp.stack(
        [grad_query, grad_product * feats[:, 2], grad_product * feats[:, 1]], axis=1
    )
    later = from_behind(grad_feats[: nshort - 1], "dp", -1)
    feats_ext = jnp.concatenate([grad_feats, later], axis=0)
    grad_acc = jnp.zeros((rows, 3, local), jnp.float32)
    for j in range(nshort):
        grad_acc = grad_acc + short_filter[j][None] * feats_ext[j : j + rows]
    grad_mixed = grad_acc.astype(jnp.bfloat16)
    short_part = jnp.stack(
        [
            jnp.sum(grad_feats * short_rows[nshort - 1 - j : nshort - 1 - j + rows], axis=0)
            for j in range(nshort)
        ]
    )
    filter_total, short_total = (
        lax.psum(filter_part.astype(jnp.bfloat16), "dp").astype(jnp.float32),
        lax.psum(short_part.astype(jnp.bfloat16), "dp").astype(jnp.float32),
    )
    grad_long = filter_total * scale
    grad_short = short_total * scale
    partial_in = jnp.einsum("sic,dic->sd", grad_mixed, full_w, preferred_element_type=jnp.float32)
    summed_in = lax.psum_scatter(
        partial_in.astype(jnp.bfloat16), ("row", "col"), scatter_dimension=1, tiled=True
    )
    weight_term = (
        jnp.einsum("sd,sic->dic", whole, grad_mixed, preferred_element_type=jnp.float32) * scale
    )
    grad_weight = lax.psum_scatter(
        weight_term.astype(jnp.bfloat16), "dp", scatter_dimension=0, tiled=True
    ).astype(jnp.float32)
    return (mixed, summed_in, grad_weight, grad_long, grad_short)


def fits_whole_sequences(mesh, tokens, in_weight, short_filter, long_filter, grad_out):
    ndp, nrow, ncol = (mesh.shape[a] for a in ("dp", "row", "col"))
    seq, channels = grad_out.shape
    groups, ntaps = long_filter.shape
    local = channels // (nrow * ncol)
    width, rows = local // ndp, seq // ndp
    return (
        seq < tokens.shape[1]
        and ndp == nrow == 4
        and ncol * (tokens.shape[1] // (nrow * ncol)) == in_weight.shape[0] // ndp
        and ntaps == width == 128
        and seq % (2 * ntaps) == 0
        and rows % 16 == 0
        and groups % (8 * ndp * nrow * ncol) == 0
    )


def solution(mesh):
    placed = (
        P("dp", ("row", "col")),
        P("dp", None, ("row", "col")),
        P(None, None, ("row", "col")),
        P(("row", "col"), None),
        P("dp", ("row", "col")),
    )
    gives = (
        P("dp", ("row", "col")),
        P("dp", ("row", "col")),
        P("dp", None, ("row", "col")),
        P(("row", "col"), None),
        P(None, None, ("row", "col")),
    )

    def run(*arrays):
        plan = move_activations if fits_whole_sequences(mesh, *arrays) else move_weights
        return jax.shard_map(
            plan, mesh=mesh, in_specs=placed, out_specs=gives, check_vma=False
        )(*arrays)

    return run
```

```python
import functools

import jax
import jax.numpy as jnp
from jax import lax
from jax.experimental import pallas as pl
from jax.experimental.pallas import tpu as pltpu
from jax.sharding import PartitionSpec as P

VMEM_BYTES = 48 * 2**20
F32 = jnp.float32
BF16 = jnp.bfloat16


def kernel_call(body, outs, grid=None, in_specs=None, out_specs=None, scratch=(), flops=0, nbytes=0, vmem=VMEM_BYTES):
    kwargs = {}
    if grid is not None:
        kwargs = dict(grid=grid, in_specs=in_specs, out_specs=out_specs)
    return pl.pallas_call(
        body,
        out_shape=outs,
        scratch_shapes=scratch,
        compiler_params=pltpu.CompilerParams(vmem_limit_bytes=vmem),
        cost_estimate=pl.CostEstimate(flops=flops, bytes_accessed=nbytes, transcendentals=0),
        **kwargs,
    )


def shaped(shape, dtype):
    return jax.ShapeDtypeStruct(shape, dtype)


def bands_body(base_ref, out_ref):
    groups, wide = base_ref.shape
    rows = out_ref.shape[1]
    row = lax.broadcasted_iota(jnp.int32, (8, wide), 0)
    for g in range(groups):
        band = jnp.broadcast_to(base_ref[g : g + 1, :], (8, wide))
        for bit in (1, 2, 4):
            band = jnp.where((row & bit) != 0, pltpu.roll(band, bit, 1), band)
        count = 8
        while count < rows:
            band = jnp.concatenate([band, pltpu.roll(band, count, 1)], axis=0)
            count *= 2
        out_ref[g] = band.astype(out_ref.dtype)


def tokens_of(row, nrow):
    return row % 2 * (nrow // 2) + row // 2


def wrapped(value, size):
    return lax.rem(value + 2 * size, size)


def project_body(x_ref, w_ref, *refs):
    *out_refs, held = refs
    z, col = lax.axis_index("dp"), lax.axis_index("col")
    nblocks, ncol, rows, depth = x_ref.shape
    width = held.shape[2]
    total = jnp.zeros((nblocks * rows, w_ref.shape[2]), F32)
    for dx in range(ncol):
        start = pl.multiple_of(wrapped(col - dx, ncol) * depth, depth)
        total += jnp.dot(
            x_ref[:, dx].reshape(nblocks * rows, depth),
            w_ref[0, pl.ds(start, depth), :],
            preferred_element_type=F32,
        )
    for owner in range(len(out_refs)):
        held[owner] = total[:, owner * width : (owner + 1) * width].astype(BF16)
    for ahead, out_ref in enumerate(out_refs):
        out_ref[0] = held[wrapped(z + ahead, len(out_refs))]


def assemble(pieces, held, ndp):
    z = lax.axis_index("dp")
    own, before, after, far_before, far_after = pieces
    held[z] = own[...]
    held[wrapped(z - 1, ndp)] = before[...]
    held[wrapped(z + 1, ndp)] = after[...]

    @pl.when(z >= ndp // 2)
    def _():
        held[z - ndp // 2] = far_before[...]

    @pl.when(z < ndp // 2)
    def _():
        held[z + ndp // 2] = far_after[...]


def input_grad_body(*refs):
    pieces, (w_ref, partner_w_ref, near_ref, far_ref, long_ref, short_ref), refs = refs[:10], refs[10:16], refs[16:]
    *out_refs, near_held, far_held = refs
    tokens = near_ref.shape[1]
    rows, depth = out_refs[0].shape
    ndp, _, width = near_held.shape
    ncol = w_ref.shape[1] // depth
    col = lax.axis_index("col")
    assemble(pieces[:5], near_held, ndp)
    assemble(pieces[5:], far_held, ndp)
    groups = long_ref.shape[0] // ndp
    for owner in range(ndp):
        small = near_held[owner, 3 * tokens :].astype(F32)
        long_ref[owner * groups : (owner + 1) * groups] = small[:groups]
        short_ref[:, owner * width : (owner + 1) * width] = small[groups : groups + short_ref.shape[0]]
    for held, all_ref in ((near_held, near_ref), (far_held, far_ref)):
        for i in range(3):
            for owner in range(ndp):
                all_ref[i, :, owner * width : (owner + 1) * width] = held[owner, i * tokens : (i + 1) * tokens]
    for dx in range(ncol):
        start = pl.multiple_of(wrapped(col - dx, ncol) * depth, depth)
        total = jnp.zeros((tokens, depth), F32)
        for all_ref, weights in ((near_ref, w_ref), (far_ref, partner_w_ref)):
            for i in range(3):
                total += lax.dot_general(
                    all_ref[i],
                    weights[i, pl.ds(start, depth), :],
                    (((1,), (1,)), ((), ())),
                    preferred_element_type=F32,
                )
        for block in range(tokens // rows):
            out_refs[block * ncol + dx][...] = total[block * rows : (block + 1) * rows].astype(BF16)


def weight_grad_body(scale, x0_ref, x1_ref, g0_ref, g1_ref, out_ref):
    nblocks, ncol, rows, depth = x0_ref.shape
    col = lax.axis_index("col")
    gm = jnp.concatenate([g0_ref[0], g1_ref[0]], axis=0)
    for dx in range(ncol):
        start = pl.multiple_of(wrapped(col - dx, ncol) * depth, depth)
        x = jnp.concatenate(
            [x_ref[:, dx].reshape(nblocks * rows, depth) for x_ref in (x0_ref, x1_ref)], axis=0
        )
        out_ref[0, pl.ds(start, depth), :] = scale * lax.dot_general(
            x, gm, (((0,), (0,)), ((), ())), preferred_element_type=F32
        )


def delayed(values, count):
    row = lax.broadcasted_iota(jnp.int32, values.shape, 0)
    return jnp.where(row >= count, pltpu.roll(values, count, 0), 0.0)


def advanced(values, count):
    rows = values.shape[0]
    row = lax.broadcasted_iota(jnp.int32, values.shape, 0)
    return jnp.where(row < rows - count, pltpu.roll(values, rows - count, 0), 0.0)


def middle_body(scale, nshort, nrow, *refs):
    sums, refs = (refs[:3], refs[3:6]), refs[6:]
    sf_ref, causal_ref, anti_ref, go_ref, near_ref, other_ref, mixed_ref, m_ref, gm_ref = refs
    tokens, width = go_ref.shape
    row = lax.axis_index("row")
    nblocks = nrow // 2
    rows = tokens // nrow

    def places():
        for chunk, start in enumerate((row, row + 1 - 2 * lax.rem(row, 2))):
            for block in range(nblocks):
                at = tokens_of(wrapped(start - 2 * block, nrow), nrow) * rows
                for i in range(3):
                    yield chunk, (i * nblocks + block) * rows, pl.multiple_of(i * tokens + at, 16)

    for chunk, place, at in places():
        held = [ref[place : place + rows].astype(F32) for ref in sums[chunk]]
        m_ref[pl.ds(at, rows)] = held[0] + held[1] + held[2]
    groups, block, span = causal_ref.shape
    members = width // groups
    nspans = tokens // block
    lane = lax.broadcasted_iota(jnp.int32, (block, width), 1) // members
    lanes = lax.broadcasted_iota(jnp.int32, (block, 2 * width), 1) % width // members

    def past(i, j):
        held = m_ref[i * tokens : (i + 1) * tokens]
        return held if j == 0 else delayed(held, j)

    def taps(j, i):
        return sf_ref[3 * j + i : 3 * j + i + 1, :]

    feats = [sum(taps(j, i) * past(i, j) for j in range(nshort)) for i in range(3)]
    product = (feats[1] * feats[2]).astype(BF16)
    zero = jnp.zeros((block, width), BF16)
    p_blocks = [zero] + [product[b * block : (b + 1) * block] for b in range(nspans)]
    p_pairs = [jnp.concatenate(p_blocks[b : b + 2], axis=0) for b in range(nspans)]

    def filtered(band_ref, pairs):
        bands = band_ref[...].reshape(groups * block, span)
        out = []
        for b in range(0, nspans, 2):
            both = jnp.dot(bands, jnp.concatenate(pairs[b : b + 2], axis=1), preferred_element_type=F32)
            for h in range(2):
                part = both[:, h * width : (h + 1) * width]
                picked = part[:block]
                for g in range(1, groups):
                    picked = jnp.where(lane == g, part[g * block : (g + 1) * block], picked)
                out.append(picked)
        return jnp.concatenate(out, axis=0)

    conv = filtered(causal_ref, p_pairs)
    upstream = go_ref[...].astype(F32)
    mixed_ref[...] = (feats[0] * conv).astype(BF16)
    grad_conv = (upstream * feats[0]).astype(BF16)
    c_blocks = [grad_conv[b * block : (b + 1) * block] for b in range(nspans)] + [zero]
    c_pairs = [jnp.concatenate(c_blocks[b : b + 2], axis=0) for b in range(nspans)]
    grad_product = filtered(anti_ref, c_pairs)

    corr = jnp.zeros((groups * block, span), F32)
    for b in range(0, nspans, 2):
        left = jnp.concatenate(c_blocks[b : b + 2], axis=1)
        stacked = jnp.concatenate(
            [jnp.where(lanes == g, left, jnp.zeros_like(left)) for g in range(groups)], axis=0
        )
        right = jnp.concatenate(p_pairs[b : b + 2], axis=1)
        corr += lax.dot_general(stacked, right, (((1,), (1,)), ((), ())), preferred_element_type=F32)
    turn = lax.broadcasted_iota(jnp.int32, (8, span), 0)
    sums = []
    for g in range(groups):
        part = corr[g * block : (g + 1) * block]
        count = block
        while count > 8:
            count //= 2
            part = part[:count] + pltpu.roll(part[count:], span - count, 1)
        for bit in (1, 2, 4):
            part = jnp.where((turn & bit) != 0, pltpu.roll(part, span - bit, 1), part)
        sums.append(jnp.sum(part, axis=0, keepdims=True))
    by_lag = jnp.concatenate(sums, axis=0)
    by_lag = (scale * pltpu.roll(by_lag, span - 1, 1)[:, :block]).astype(BF16)
    ahead = lax.broadcasted_iota(jnp.int32, (block, block), 0)
    back = lax.broadcasted_iota(jnp.int32, (block, block), 1)
    turned = jnp.where(ahead + back == block - 1, 1.0, 0.0).astype(BF16)
    by_lag = jnp.dot(by_lag, turned, preferred_element_type=F32)

    grad_feats = [upstream * conv, grad_product * feats[2], grad_product * feats[1]]
    short_rows = []
    for j in range(nshort):
        for i in range(3):
            short_rows.append(scale * jnp.sum(grad_feats[i] * past(i, j), axis=0, keepdims=True))
    for i in range(3):
        total = taps(0, i) * grad_feats[i]
        for j in range(1, nshort):
            total += taps(j, i) * advanced(grad_feats[i], j)
        gm_ref[i * tokens : (i + 1) * tokens] = total.astype(BF16)
    for chunk, place, at in places():
        (near_ref, other_ref)[chunk][place : place + rows] = gm_ref[pl.ds(at, rows)]
    tail = near_ref.shape[0] - 3 * tokens // 2 - groups - 3 * nshort
    small = jnp.concatenate([by_lag] + short_rows + [jnp.zeros((tail, width), F32)], axis=0)
    near_ref[3 * tokens // 2 :] = small.astype(BF16)


def sum_over_line(own, right, far, left):
    ndp = lax.axis_size("dp")
    from_left = lax.ppermute(far, "dp", [(a, a + 1) for a in range(ndp // 2)])
    from_right = lax.ppermute(far, "dp", [(a, a - 1) for a in range(ndp // 2, ndp)])
    rightward = lax.ppermute(right + from_left, "dp", [(a, (a + 1) % ndp) for a in range(ndp)])
    leftward = lax.ppermute(left + from_right, "dp", [(a, (a - 1) % ndp) for a in range(ndp)])
    return own, rightward, leftward


def gather_over_line(own, across):
    ndp, nrow = lax.axis_size("dp"), lax.axis_size("row")

    def shift(count):
        return [
            (a * nrow + r, (a + count) % ndp * nrow + (r + 1 - 2 * (r % 2) if across else r))
            for a in range(ndp)
            for r in range(nrow)
        ]

    before = lax.ppermute(own, ("dp", "row"), shift(1))
    after = lax.ppermute(own, ("dp", "row"), shift(-1))
    here = lax.ppermute(own, ("dp", "row"), shift(0)) if across else own
    far_before = lax.ppermute(before, "dp", [(a - 1, a) for a in range(ndp // 2, ndp)])
    far_after = lax.ppermute(after, "dp", [(a + 1, a) for a in range(ndp // 2)])
    return here, before, after, far_before, far_after


def move_activations(tokens, in_weight, short_filter, long_filter, grad_out):
    ndp, nrow, ncol = (lax.axis_size(a) for a in ("dp", "row", "col"))
    z = lax.axis_index("dp")
    rows, dcol = tokens.shape
    local = grad_out.shape[1]
    nshort = short_filter.shape[0]
    ngroups, ntaps = long_filter.shape
    seq = rows * ndp
    width, groups = local // ndp, ngroups // ndp
    drow = in_weight.shape[0]
    scale = float(seq) ** -0.5
    nblocks = nrow // 2
    chunk = nblocks * rows
    swap = [(tokens_of(b, nrow) * nrow + a, a * nrow + b) for a in range(ndp) for b in range(nrow)]
    swap_back = [(b, a) for a, b in swap]
    partner = [(a, a + 1 - 2 * (a % 2)) for a in range(nrow)]
    places = [(dy, dx) for dy in range(nblocks) for dx in range(ncol)]

    def offset(dy, dx):
        return [
            (a * ncol + b, (a + 2 * dy) % nrow * ncol + (b + dx) % ncol) for a in range(nrow) for b in range(ncol)
        ]

    w = jnp.transpose(in_weight, (1, 0, 2))
    moved = lax.ppermute(tokens, ("dp", "row"), swap)
    near = [moved] + [lax.ppermute(moved, ("row", "col"), offset(*p)) for p in places[1:]]
    upstream = lax.all_to_all(grad_out, "dp", split_axis=1, concat_axis=0, tiled=True)
    upstream, *near = lax.optimization_barrier((upstream, *near))
    x0 = jnp.stack(near).reshape(nblocks, ncol, rows, dcol)
    x1 = lax.ppermute(x0, "row", partner)

    sf = lax.dynamic_slice_in_dim(short_filter, z * width, width, 2).reshape(3 * nshort, width)
    lf = lax.dynamic_slice_in_dim(long_filter, z * groups, groups, 0).astype(F32)
    zeros = functools.partial(jnp.zeros, dtype=F32)
    bases = jnp.concatenate(
        [
            jnp.concatenate([zeros((groups, 1)), lf[:, ::-1], zeros((groups, ntaps - 1))], axis=1),
            jnp.concatenate([lf, zeros((groups, ntaps))], axis=1),
        ],
        axis=0,
    )
    bands = kernel_call(bands_body, shaped((2 * groups, ntaps, 2 * ntaps), BF16))(bases)

    mm_flops = seq * drow * 3 * local
    mm_bytes = seq * drow + 6 * drow * local + 3 * seq * local
    sums = []
    for x in (x0, x1):
        parts = kernel_call(
            project_body,
            [shaped((3, chunk, width), BF16)] * ndp,
            grid=(3,),
            in_specs=[
                pl.BlockSpec((nblocks, ncol, rows, dcol), lambda i: (0, 0, 0, 0)),
                pl.BlockSpec((1, drow, local), lambda i: (i, 0, 0)),
            ],
            out_specs=[pl.BlockSpec((1, chunk, width), lambda i: (i, 0, 0))] * ndp,
            scratch=[pltpu.VMEM((ndp, chunk, width), BF16)],
            flops=mm_flops,
            nbytes=mm_bytes,
        )(x, w)
        sums += sum_over_line(*(p.reshape(3 * chunk, width) for p in parts))

    extra = -(-(groups + 3 * nshort) // 16) * 16
    half = pl.BlockSpec((groups, ntaps, 2 * ntaps), lambda i: (0, 0, 0))
    other = pl.BlockSpec((groups, ntaps, 2 * ntaps), lambda i: (1, 0, 0))
    whole = lambda *shape: pl.BlockSpec(shape, lambda i: (0,) * len(shape))
    grad_near, grad_other, mixed = kernel_call(
        functools.partial(middle_body, scale, nshort, nrow),
        (
            shaped((3 * chunk + extra, width), BF16),
            shaped((3 * chunk, width), BF16),
            shaped((seq, width), BF16),
        ),
        grid=(1,),
        in_specs=[whole(3 * chunk, width)] * 6
        + [whole(3 * nshort, width), half, other, whole(seq, width)],
        out_specs=(whole(3 * chunk + extra, width), whole(3 * chunk, width), whole(seq, width)),
        scratch=[pltpu.VMEM((3 * seq, width), F32), pltpu.VMEM((3 * seq, width), BF16)],
        flops=3 * 2 * groups * ntaps * 2 * ntaps * width * (seq // ntaps),
        nbytes=2 * width * seq * 14,
    )(*sums, sf, bands, bands, upstream)
    mixed = lax.all_to_all(mixed, "dp", split_axis=0, concat_axis=1, tiled=True)
    pieces = (*gather_over_line(grad_near, False), *gather_over_line(grad_other, True))
    mixed, *pieces = lax.optimization_barrier((mixed, *pieces))
    block = shaped((rows, dcol), BF16)
    all_shape = shaped((3, chunk, local), BF16)
    all_near, all_far, grad_long, grad_short, *blocks = kernel_call(
        input_grad_body,
        [all_shape, all_shape, shaped((ngroups, ntaps), F32), shaped((3 * nshort, local), F32)]
        + [block] * len(places),
        scratch=[
            pltpu.VMEM((ndp, 3 * chunk + extra, width), BF16),
            pltpu.VMEM((ndp, 3 * chunk, width), BF16),
        ],
        flops=2 * mm_flops,
        nbytes=2 * mm_bytes,
        vmem=62 * 2**20,
    )(*pieces, w, lax.ppermute(w, "row", partner))
    arrivals = [
        lax.ppermute(sent, ("row", "col"), [(b, a) for a, b in offset(*p)])
        for p, sent in zip(places[1:], blocks[1:])
    ]
    arrived = sum((a.astype(F32) for a in arrivals), blocks[0].astype(F32)).astype(BF16)
    all_other = lax.ppermute(all_far, "row", partner)
    arrived, all_other = lax.optimization_barrier((arrived, all_other))
    grad_in = lax.ppermute(arrived, ("dp", "row"), swap_back)

    x_spec = pl.BlockSpec((nblocks, ncol, rows, dcol), lambda i: (0, 0, 0, 0))
    g_spec = pl.BlockSpec((1, chunk, local), lambda i: (i, 0, 0))
    grad_weight = kernel_call(
        functools.partial(weight_grad_body, scale),
        shaped((3, drow, local), F32),
        grid=(3,),
        in_specs=[x_spec, x_spec, g_spec, g_spec],
        out_specs=pl.BlockSpec((1, drow, local), lambda i: (i, 0, 0)),
        flops=2 * mm_flops,
        nbytes=2 * mm_bytes,
    )(x0, x1, all_near, all_other)
    grad_weight = jnp.transpose(grad_weight, (1, 0, 2))
    grad_short = grad_short.reshape(nshort, 3, local)
    return (mixed, grad_in, grad_weight, grad_long, grad_short)


def from_behind(block, axis, distance):
    devices = range(lax.axis_size(axis))
    route = [(i - distance, i) for i in devices if i - distance in devices]
    return lax.ppermute(block, axis, route)


def toeplitz(leading, rows, span):
    groups = leading.shape[0]
    width = rows + span
    seed_row = jnp.concatenate(
        [leading, jnp.zeros((groups, width - leading.shape[1]), leading.dtype)], axis=1
    )
    tiled = jnp.tile(seed_row, (1, rows))
    skewed = tiled[:, : rows * (width - 1)].reshape(groups, rows, width - 1)
    return skewed[:, :, :span]


def to_groups(values, ngroups, members):
    count = values.shape[0]
    return values.reshape(count, ngroups, members).transpose(1, 2, 0)


def from_groups(values):
    groups, members, count = values.shape
    return values.transpose(2, 0, 1).reshape(count, groups * members)


def move_weights(tokens, in_weight, short_filter, long_filter, grad_out):
    rows = tokens.shape[0]
    local = grad_out.shape[1]
    nshort = short_filter.shape[0]
    ntaps = long_filter.shape[1]
    ngroups = long_filter.shape[0]
    members = local // ngroups
    margin = ntaps - 1
    span = rows + margin
    scale = float(rows * lax.axis_size("dp")) ** (-0.5)
    whole = lax.all_gather(tokens, ("row", "col"), axis=1, tiled=True)
    full_w = lax.all_gather(in_weight, "dp", axis=0, tiled=True)
    mixed_in = jnp.einsum("sd,dic->sic", whole, full_w, preferred_element_type=jnp.float32).astype(
        jnp.bfloat16
    )
    before = from_behind(mixed_in[rows - margin - nshort + 1 :], "dp", 1)
    extended = jnp.concatenate([before, mixed_in], axis=0).astype(jnp.float32)
    long_feats = jnp.zeros((span, 3, local), jnp.float32)
    for j in range(nshort):
        long_feats = (
            long_feats + short_filter[j][None] * extended[nshort - 1 - j : nshort - 1 - j + span]
        )
    product_ext = (long_feats[:, 1] * long_feats[:, 2]).astype(jnp.bfloat16)
    feats = long_feats[margin:]
    short_rows = extended[margin:]
    product_cols = to_groups(product_ext, ngroups, members)
    causal = toeplitz(long_filter[:, ::-1], rows, span)
    conv = from_groups(
        jnp.einsum("gst,gct->gcs", causal, product_cols, preferred_element_type=jnp.float32)
    )
    mixed = (feats[:, 0] * conv).astype(jnp.bfloat16)
    upstream = grad_out.astype(jnp.float32)
    grad_query = upstream * conv
    grad_conv = (upstream * feats[:, 0]).astype(jnp.bfloat16)
    after = from_behind(grad_conv[:margin], "dp", -1)
    grad_ext = jnp.concatenate([grad_conv, after], axis=0)
    anti = toeplitz(long_filter, rows, span)
    grad_product = from_groups(
        jnp.einsum(
            "gst,gct->gcs",
            anti,
            to_groups(grad_ext, ngroups, members),
            preferred_element_type=jnp.float32,
        )
    )
    reversed_cols = jnp.concatenate(
        [product_cols[:, :, ::-1], jnp.zeros((ngroups, members, rows), product_cols.dtype)], axis=2
    )
    width = span + rows
    pairs = jnp.einsum(
        "gcs,gcu->gsu",
        to_groups(grad_conv, ngroups, members),
        reversed_cols,
        preferred_element_type=jnp.float32,
    )
    diagonal = pairs.reshape(ngroups, rows * width)[:, : rows * (width - 1)].reshape(
        ngroups, rows, width - 1
    )
    filter_part = jnp.sum(diagonal[:, :, rows - 1 : rows - 1 + ntaps], axis=1)
    grad_feats = jnp.stack(
        [grad_query, grad_product * feats[:, 2], grad_product * feats[:, 1]], axis=1
    )
    later = from_behind(grad_feats[: nshort - 1], "dp", -1)
    feats_ext = jnp.concatenate([grad_feats, later], axis=0)
    grad_acc = jnp.zeros((rows, 3, local), jnp.float32)
    for j in range(nshort):
        grad_acc = grad_acc + short_filter[j][None] * feats_ext[j : j + rows]
    grad_mixed = grad_acc.astype(jnp.bfloat16)
    short_part = jnp.stack(
        [
            jnp.sum(grad_feats * short_rows[nshort - 1 - j : nshort - 1 - j + rows], axis=0)
            for j in range(nshort)
        ]
    )
    filter_total, short_total = (
        lax.psum(filter_part.astype(jnp.bfloat16), "dp").astype(jnp.float32),
        lax.psum(short_part.astype(jnp.bfloat16), "dp").astype(jnp.float32),
    )
    grad_long = filter_total * scale
    grad_short = short_total * scale
    partial_in = jnp.einsum("sic,dic->sd", grad_mixed, full_w, preferred_element_type=jnp.float32)
    summed_in = lax.psum_scatter(
        partial_in.astype(jnp.bfloat16), ("row", "col"), scatter_dimension=1, tiled=True
    )
    weight_term = (
        jnp.einsum("sd,sic->dic", whole, grad_mixed, preferred_element_type=jnp.float32) * scale
    )
    grad_weight = lax.psum_scatter(
        weight_term.astype(jnp.bfloat16), "dp", scatter_dimension=0, tiled=True
    ).astype(jnp.float32)
    return (mixed, summed_in, grad_weight, grad_long, grad_short)


def fits_whole_sequences(mesh, tokens, in_weight, short_filter, long_filter, grad_out):
    ndp, nrow, ncol = (mesh.shape[a] for a in ("dp", "row", "col"))
    seq, channels = grad_out.shape
    groups, ntaps = long_filter.shape
    local = channels // (nrow * ncol)
    width, rows = local // ndp, seq // ndp
    return (
        seq < tokens.shape[1]
        and ndp == nrow == 4
        and ncol * (tokens.shape[1] // (nrow * ncol)) == in_weight.shape[0] // ndp
        and ntaps == width == 128
        and seq % (2 * ntaps) == 0
        and rows % 16 == 0
        and groups % (8 * ndp * nrow * ncol) == 0
    )


def solution(mesh):
    placed = (
        P("dp", ("row", "col")),
        P("dp", None, ("row", "col")),
        P(None, None, ("row", "col")),
        P(("row", "col"), None),
        P("dp", ("row", "col")),
    )
    gives = (
        P("dp", ("row", "col")),
        P("dp", ("row", "col")),
        P("dp", None, ("row", "col")),
        P(("row", "col"), None),
        P(None, None, ("row", "col")),
    )

    def run(*arrays):
        plan = move_activations if fits_whole_sequences(mesh, *arrays) else move_weights
        return jax.shard_map(
            plan, mesh=mesh, in_specs=placed, out_specs=gives, check_vma=False
        )(*arrays)

    return run
```

```python
import functools

import jax
import jax.numpy as jnp
from jax import lax
from jax.experimental import pallas as pl
from jax.experimental.pallas import tpu as pltpu
from jax.sharding import PartitionSpec as P

VMEM_BYTES = 48 * 2**20
MOST_VMEM_BYTES = 62 * 2**20
F32 = jnp.float32
BF16 = jnp.bfloat16


def kernel_call(body, outs, grid=(), in_specs=None, out_specs=None, scratch=(), flops=0, nbytes=0, vmem=VMEM_BYTES):
    kwargs = {}
    if in_specs is not None:
        kwargs = dict(grid=grid, in_specs=in_specs, out_specs=out_specs)
    return pl.pallas_call(
        body,
        out_shape=outs,
        scratch_shapes=scratch,
        compiler_params=pltpu.CompilerParams(vmem_limit_bytes=vmem),
        cost_estimate=pl.CostEstimate(flops=flops, bytes_accessed=nbytes, transcendentals=0),
        **kwargs,
    )


def shaped(shape, dtype):
    return jax.ShapeDtypeStruct(shape, dtype)


def bands_body(base_ref, out_ref):
    groups, wide = base_ref.shape
    rows = out_ref.shape[1]
    row = lax.broadcasted_iota(jnp.int32, (8, wide), 0)
    for g in range(groups):
        band = jnp.broadcast_to(base_ref[g : g + 1, :], (8, wide))
        for bit in (1, 2, 4):
            band = jnp.where((row & bit) != 0, pltpu.roll(band, bit, 1), band)
        count = 8
        while count < rows:
            band = jnp.concatenate([band, pltpu.roll(band, count, 1)], axis=0)
            count *= 2
        out_ref[g] = band.astype(out_ref.dtype)


def tokens_of(row, nrow):
    return row % 2 * (nrow // 2) + row // 2


def wrapped(value, size):
    return lax.rem(value + 2 * size, size)


def project_body(x_ref, w_ref, *refs):
    *out_refs, held = refs
    z, col = lax.axis_index("dp"), lax.axis_index("col")
    nblocks, ncol, rows, depth = x_ref.shape
    width = held.shape[2]
    total = jnp.zeros((nblocks * rows, w_ref.shape[2]), F32)
    for dx in range(ncol):
        start = pl.multiple_of(wrapped(col - dx, ncol) * depth, depth)
        total += jnp.dot(
            x_ref[:, dx].reshape(nblocks * rows, depth),
            w_ref[0, pl.ds(start, depth), :],
            preferred_element_type=F32,
        )
    for owner in range(len(out_refs)):
        held[owner] = total[:, owner * width : (owner + 1) * width].astype(BF16)
    for ahead, out_ref in enumerate(out_refs):
        out_ref[0] = held[wrapped(z + ahead, len(out_refs))]


def first_grad_body(near, near_before, near_after, far, far_before, far_after, w_ref, partner_w_ref, out_ref, far_ref, held):
    ndp, _, width = held.shape
    ncol, tokens, depth = out_ref.shape
    z, col = lax.axis_index("dp"), lax.axis_index("col")
    far_ref[0], far_ref[1], far_ref[2] = far[...], far_before[...], far_after[...]
    for pieces, weights, first in (
        ((near, near_before, near_after), w_ref, True),
        ((far, far_before, far_after), partner_w_ref, False),
    ):
        held[wrapped(z + ndp // 2, ndp)] = jnp.zeros(held.shape[1:], BF16)
        for ahead, piece in zip((0, -1, 1), pieces):
            held[wrapped(z + ahead, ndp)] = piece[: 3 * tokens]
        for dx in range(ncol):
            start = pl.multiple_of(wrapped(col - dx, ncol) * depth, depth)
            total = jnp.zeros((tokens, depth), F32) if first else out_ref[dx]
            for i in range(3):
                rows = slice(i * tokens, (i + 1) * tokens)
                total += lax.dot_general(
                    jnp.concatenate([held[owner, rows] for owner in range(ndp)], axis=1),
                    weights[i, pl.ds(start, depth), :],
                    (((1,), (1,)), ((), ())),
                    preferred_element_type=F32,
                )
            out_ref[dx] = total


def second_grad_body(ndp, part_ref, *refs):
    arrived, weights, refs = (refs[:2], refs[2:4]), refs[4:6], refs[6:]
    (near_ref, far_ref), refs = refs[:2], refs[2:]
    *out_refs, held_w, held_part, sems = refs
    ncol, tokens, depth = held_part.shape
    rows = out_refs[0].shape[0]
    width = near_ref.shape[1]
    z, col = lax.axis_index("dp"), lax.axis_index("col")
    lanes = pl.ds(pl.multiple_of(wrapped(z + ndp // 2, ndp) * width, width), width)
    copies = [
        pltpu.make_async_copy(w_ref.at[:, :, lanes], held_w.at[k], sems.at[k]) for k, w_ref in enumerate(weights)
    ]
    copies.append(pltpu.make_async_copy(part_ref, held_part, sems.at[2]))
    for copy in copies:
        copy.start()
    for k, (pair, target) in enumerate(zip(arrived, (near_ref, far_ref))):
        for source, here in zip(pair, (z >= ndp // 2, z < ndp // 2)):

            @pl.when(here)
            def _(source=source, target=target, k=k):
                copy = pltpu.make_async_copy(source, target, sems.at[3 + k])
                copy.start()
                copy.wait()

    for copy in copies:
        copy.wait()
    left = jnp.concatenate(
        [ref[i * tokens : (i + 1) * tokens] for ref in (near_ref, far_ref) for i in range(3)], axis=1
    )
    for dx in range(ncol):
        start = pl.multiple_of(wrapped(col - dx, ncol) * depth, depth)
        right = jnp.concatenate([held_w[k, i, pl.ds(start, depth), :] for k in range(2) for i in range(3)], axis=1)
        total = held_part[dx] + lax.dot_general(
            left, right, (((1,), (1,)), ((), ())), preferred_element_type=F32
        )
        for block in range(tokens // rows):
            out_refs[block * ncol + dx][...] = total[block * rows : (block + 1) * rows].astype(BF16)


def weight_grad_body(scale, *refs):
    (x0_ref, x1_ref), near_refs, (far_ref, far_last_ref), mixed_refs, refs = (
        refs[:2],
        refs[2:6],
        refs[6:8],
        refs[8:12],
        refs[12:],
    )
    out_ref, mixed_ref, long_ref, short_ref, held, held_mixed = refs
    nblocks, ncol, rows, depth = x0_ref.shape
    _, ndp, _, width = held.shape
    tokens = nblocks * rows
    i = pl.program_id(0)
    z, col = lax.axis_index("dp"), lax.axis_index("col")

    @pl.when(i == 0)
    def _():
        groups = long_ref.shape[0] // ndp
        for k, ahead in enumerate((0, -1, 1, 2)):
            owner = wrapped(z + ahead, ndp)
            held[0, owner] = near_refs[k][...]
            held[1, owner, : 3 * tokens] = far_ref[k] if k < 3 else far_last_ref[...]
        for back in range(ndp):
            held_mixed[wrapped(z - back, ndp)] = mixed_refs[back][...]
        for owner in range(ndp):
            lanes = slice(owner * width, (owner + 1) * width)
            mixed_ref[:, lanes] = held_mixed[owner]
            small = held[0, owner, 3 * tokens :].astype(F32)
            long_ref[owner * groups : (owner + 1) * groups] = small[:groups]
            short_ref[:, lanes] = small[groups : groups + short_ref.shape[0]]

    at = pl.ds(pl.multiple_of(i * tokens, 16), tokens)
    gm = jnp.concatenate(
        [jnp.concatenate([held[k, owner, at, :] for owner in range(ndp)], axis=1) for k in range(2)], axis=0
    )
    for dx in range(ncol):
        start = pl.multiple_of(wrapped(col - dx, ncol) * depth, depth)
        x = jnp.concatenate(
            [x_ref[:, dx].reshape(tokens, depth) for x_ref in (x0_ref, x1_ref)], axis=0
        )
        out_ref[0, pl.ds(start, depth), :] = scale * lax.dot_general(
            x, gm, (((0,), (0,)), ((), ())), preferred_element_type=F32
        )


def delayed(values, count):
    row = lax.broadcasted_iota(jnp.int32, values.shape, 0)
    return jnp.where(row >= count, pltpu.roll(values, count, 0), 0.0)


def advanced(values, count):
    rows = values.shape[0]
    row = lax.broadcasted_iota(jnp.int32, values.shape, 0)
    return jnp.where(row < rows - count, pltpu.roll(values, rows - count, 0), 0.0)


def middle_body(scale, nshort, nrow, *refs):
    sums, refs = (refs[:3], refs[3:6]), refs[6:]
    sf_ref, causal_ref, anti_ref, go_ref, near_ref, other_ref, *mixed_refs, m_ref, gm_ref, mixed_ref = refs
    tokens, width = go_ref.shape
    row = lax.axis_index("row")
    nblocks = nrow // 2
    rows = tokens // nrow

    def places():
        for chunk, start in enumerate((row, row + 1 - 2 * lax.rem(row, 2))):
            for block in range(nblocks):
                at = tokens_of(wrapped(start - 2 * block, nrow), nrow) * rows
                for i in range(3):
                    yield chunk, (i * nblocks + block) * rows, pl.multiple_of(i * tokens + at, 16)

    for chunk, place, at in places():
        held = [ref[place : place + rows].astype(F32) for ref in sums[chunk]]
        m_ref[pl.ds(at, rows)] = held[0] + held[1] + held[2]
    groups, block, span = causal_ref.shape
    members = width // groups
    nspans = tokens // block
    lane = lax.broadcasted_iota(jnp.int32, (block, width), 1) // members
    lanes = lax.broadcasted_iota(jnp.int32, (block, 2 * width), 1) % width // members

    def past(i, j):
        held = m_ref[i * tokens : (i + 1) * tokens]
        return held if j == 0 else delayed(held, j)

    def taps(j, i):
        return sf_ref[3 * j + i : 3 * j + i + 1, :]

    feats = [sum(taps(j, i) * past(i, j) for j in range(nshort)) for i in range(3)]
    product = (feats[1] * feats[2]).astype(BF16)
    zero = jnp.zeros((block, width), BF16)
    p_blocks = [zero] + [product[b * block : (b + 1) * block] for b in range(nspans)]
    p_pairs = [jnp.concatenate(p_blocks[b : b + 2], axis=0) for b in range(nspans)]

    def filtered(band_ref, pairs):
        bands = band_ref[...].reshape(groups * block, span)
        out = []
        for b in range(0, nspans, 2):
            both = jnp.dot(bands, jnp.concatenate(pairs[b : b + 2], axis=1), preferred_element_type=F32)
            for h in range(2):
                part = both[:, h * width : (h + 1) * width]
                picked = part[:block]
                for g in range(1, groups):
                    picked = jnp.where(lane == g, part[g * block : (g + 1) * block], picked)
                out.append(picked)
        return jnp.concatenate(out, axis=0)

    conv = filtered(causal_ref, p_pairs)
    upstream = go_ref[...].astype(F32)
    mixed_ref[...] = (feats[0] * conv).astype(BF16)
    ndp = len(mixed_refs)
    for ahead, out_ref in enumerate(mixed_refs):
        at = pl.multiple_of(wrapped(lax.axis_index("dp") + ahead, ndp) * (tokens // ndp), 16)
        out_ref[...] = mixed_ref[pl.ds(at, tokens // ndp)]
    grad_conv = (upstream * feats[0]).astype(BF16)
    c_blocks = [grad_conv[b * block : (b + 1) * block] for b in range(nspans)] + [zero]
    c_pairs = [jnp.concatenate(c_blocks[b : b + 2], axis=0) for b in range(nspans)]
    grad_product = filtered(anti_ref, c_pairs)

    corr = jnp.zeros((groups * block, span), F32)
    for b in range(0, nspans, 2):
        left = jnp.concatenate(c_blocks[b : b + 2], axis=1)
        stacked = jnp.concatenate(
            [jnp.where(lanes == g, left, jnp.zeros_like(left)) for g in range(groups)], axis=0
        )
        right = jnp.concatenate(p_pairs[b : b + 2], axis=1)
        corr += lax.dot_general(stacked, right, (((1,), (1,)), ((), ())), preferred_element_type=F32)
    turn = lax.broadcasted_iota(jnp.int32, (8, span), 0)
    sums = []
    for g in range(groups):
        part = corr[g * block : (g + 1) * block]
        count = block
        while count > 8:
            count //= 2
            part = part[:count] + pltpu.roll(part[count:], span - count, 1)
        for bit in (1, 2, 4):
            part = jnp.where((turn & bit) != 0, pltpu.roll(part, span - bit, 1), part)
        sums.append(jnp.sum(part, axis=0, keepdims=True))
    by_lag = jnp.concatenate(sums, axis=0)
    by_lag = (scale * pltpu.roll(by_lag, span - 1, 1)[:, :block]).astype(BF16)
    ahead = lax.broadcasted_iota(jnp.int32, (block, block), 0)
    back = lax.broadcasted_iota(jnp.int32, (block, block), 1)
    turned = jnp.where(ahead + back == block - 1, 1.0, 0.0).astype(BF16)
    by_lag = jnp.dot(by_lag, turned, preferred_element_type=F32)

    grad_feats = [upstream * conv, grad_product * feats[2], grad_product * feats[1]]
    short_rows = []
    for j in range(nshort):
        for i in range(3):
            short_rows.append(scale * jnp.sum(grad_feats[i] * past(i, j), axis=0, keepdims=True))
    for i in range(3):
        total = taps(0, i) * grad_feats[i]
        for j in range(1, nshort):
            total += taps(j, i) * advanced(grad_feats[i], j)
        gm_ref[i * tokens : (i + 1) * tokens] = total.astype(BF16)
    for chunk, place, at in places():
        (near_ref, other_ref)[chunk][place : place + rows] = gm_ref[pl.ds(at, rows)]
    tail = near_ref.shape[0] - 3 * tokens // 2 - groups - 3 * nshort
    small = jnp.concatenate([by_lag] + short_rows + [jnp.zeros((tail, width), F32)], axis=0)
    near_ref[3 * tokens // 2 :] = small.astype(BF16)


def sum_over_line(own, right, far, left):
    ndp = lax.axis_size("dp")
    from_left = lax.ppermute(far, "dp", [(a, a + 1) for a in range(ndp // 2)])
    from_right = lax.ppermute(far, "dp", [(a, a - 1) for a in range(ndp // 2, ndp)])
    rightward = lax.ppermute(right + from_left, "dp", [(a, (a + 1) % ndp) for a in range(ndp)])
    leftward = lax.ppermute(left + from_right, "dp", [(a, (a - 1) % ndp) for a in range(ndp)])
    return own, rightward, leftward


def gather_over_line(own, across):
    ndp, nrow = lax.axis_size("dp"), lax.axis_size("row")

    def shift(count):
        return [
            (a * nrow + r, (a + count) % ndp * nrow + (r + 1 - 2 * (r % 2) if across else r))
            for a in range(ndp)
            for r in range(nrow)
        ]

    before = lax.ppermute(own, ("dp", "row"), shift(1))
    after = lax.ppermute(own, ("dp", "row"), shift(-1))
    here = lax.ppermute(own, ("dp", "row"), shift(0)) if across else own
    far_before = lax.ppermute(before, "dp", [(a - 1, a) for a in range(ndp // 2, ndp)])
    far_after = lax.ppermute(after, "dp", [(a + 1, a) for a in range(ndp // 2)])
    return here, before, after, far_before, far_after


def move_activations(tokens, in_weight, short_filter, long_filter, grad_out):
    ndp, nrow, ncol = (lax.axis_size(a) for a in ("dp", "row", "col"))
    z = lax.axis_index("dp")
    rows, dcol = tokens.shape
    local = grad_out.shape[1]
    nshort = short_filter.shape[0]
    ngroups, ntaps = long_filter.shape
    seq = rows * ndp
    width, groups = local // ndp, ngroups // ndp
    drow = in_weight.shape[0]
    scale = float(seq) ** -0.5
    nblocks = nrow // 2
    chunk = nblocks * rows
    swap = [(tokens_of(b, nrow) * nrow + a, a * nrow + b) for a in range(ndp) for b in range(nrow)]
    swap_back = [(b, a) for a, b in swap]
    partner = [(a, a + 1 - 2 * (a % 2)) for a in range(nrow)]
    places = [(dy, dx) for dy in range(nblocks) for dx in range(ncol)]

    def offset(dy, dx):
        return [
            (a * ncol + b, (a + 2 * dy) % nrow * ncol + (b + dx) % ncol) for a in range(nrow) for b in range(ncol)
        ]

    w = jnp.transpose(in_weight, (1, 0, 2))
    moved = lax.ppermute(tokens, ("dp", "row"), swap)
    near = [moved] + [lax.ppermute(moved, ("row", "col"), offset(*p)) for p in places[1:]]
    upstream = lax.all_to_all(grad_out, "dp", split_axis=1, concat_axis=0, tiled=True)
    upstream, *near = lax.optimization_barrier((upstream, *near))
    x0 = jnp.stack(near).reshape(nblocks, ncol, rows, dcol)
    x1 = lax.ppermute(x0, "row", partner)

    sf = lax.dynamic_slice_in_dim(short_filter, z * width, width, 2).reshape(3 * nshort, width)
    lf = lax.dynamic_slice_in_dim(long_filter, z * groups, groups, 0).astype(F32)
    zeros = functools.partial(jnp.zeros, dtype=F32)
    bases = jnp.concatenate(
        [
            jnp.concatenate([zeros((groups, 1)), lf[:, ::-1], zeros((groups, ntaps - 1))], axis=1),
            jnp.concatenate([lf, zeros((groups, ntaps))], axis=1),
        ],
        axis=0,
    )
    bands = kernel_call(bands_body, shaped((2 * groups, ntaps, 2 * ntaps), BF16))(bases)

    mm_flops = seq * drow * 3 * local
    mm_bytes = seq * drow + 6 * drow * local + 3 * seq * local
    sums = []
    for x in (x0, x1):
        parts = kernel_call(
            project_body,
            [shaped((3, chunk, width), BF16)] * ndp,
            grid=(3,),
            in_specs=[
                pl.BlockSpec((nblocks, ncol, rows, dcol), lambda i: (0, 0, 0, 0)),
                pl.BlockSpec((1, drow, local), lambda i: (i, 0, 0)),
            ],
            out_specs=[pl.BlockSpec((1, chunk, width), lambda i: (i, 0, 0))] * ndp,
            scratch=[pltpu.VMEM((ndp, chunk, width), BF16)],
            flops=mm_flops,
            nbytes=mm_bytes,
        )(x, w)
        sums += sum_over_line(*(p.reshape(3 * chunk, width) for p in parts))

    extra = -(-(groups + 3 * nshort) // 16) * 16
    half = pl.BlockSpec((groups, ntaps, 2 * ntaps), lambda i: (0, 0, 0))
    other = pl.BlockSpec((groups, ntaps, 2 * ntaps), lambda i: (1, 0, 0))
    whole = lambda *shape: pl.BlockSpec(shape, lambda i: (0,) * len(shape))
    grad_near, grad_other, *mixed = kernel_call(
        functools.partial(middle_body, scale, nshort, nrow),
        [shaped((3 * chunk + extra, width), BF16), shaped((3 * chunk, width), BF16)]
        + [shaped((rows, width), BF16)] * ndp,
        grid=(1,),
        in_specs=[whole(3 * chunk, width)] * 6
        + [whole(3 * nshort, width), half, other, whole(seq, width)],
        out_specs=[whole(3 * chunk + extra, width), whole(3 * chunk, width)] + [whole(rows, width)] * ndp,
        scratch=[
            pltpu.VMEM((3 * seq, width), F32),
            pltpu.VMEM((3 * seq, width), BF16),
            pltpu.VMEM((seq, width), BF16),
        ],
        flops=3 * 2 * groups * ntaps * 2 * ntaps * width * (seq // ntaps),
        nbytes=2 * width * seq * 14,
        vmem=MOST_VMEM_BYTES,
    )(*sums, sf, bands, bands, upstream)
    mixed = [mixed[0]] + [
        lax.ppermute(part, "dp", [(a, (a + ahead) % ndp) for a in range(ndp)])
        for ahead, part in enumerate(mixed)
        if ahead
    ]
    *near, near_far_before, near_far_after = gather_over_line(grad_near, False)
    *far, far_far_before, far_far_after = gather_over_line(grad_other, True)
    partner_w = lax.ppermute(w, "row", partner)
    part, far_three = kernel_call(
        first_grad_body,
        [shaped((ncol, chunk, dcol), F32), shaped((3, 3 * chunk, width), BF16)],
        scratch=[pltpu.VMEM((ndp, 3 * chunk, width), BF16)],
        flops=2 * mm_flops,
        nbytes=2 * mm_bytes,
    )(*near, *far, w, partner_w)
    everywhere = pl.BlockSpec(memory_space=pl.ANY)
    in_vmem = pl.BlockSpec(memory_space=pltpu.VMEM)
    near_last, far_last, *blocks = kernel_call(
        functools.partial(second_grad_body, ndp),
        [shaped(grad_near.shape, BF16), shaped(grad_other.shape, BF16)]
        + [shaped((rows, dcol), BF16)] * len(places),
        grid=(),
        in_specs=[everywhere] * 7,
        out_specs=[in_vmem] * (2 + len(places)),
        scratch=[
            pltpu.VMEM((2, 3, drow, width), BF16),
            pltpu.VMEM((ncol, chunk, dcol), F32),
            pltpu.SemaphoreType.DMA((5,)),
        ],
        flops=mm_flops // 2,
        nbytes=mm_bytes // 2,
        vmem=MOST_VMEM_BYTES,
    )(part, near_far_before, near_far_after, far_far_before, far_far_after, w, partner_w)
    far_three, far_last = lax.optimization_barrier((far_three, far_last))
    far_three, far_last = (lax.ppermute(part, "row", partner) for part in (far_three, far_last))
    arrivals = [
        lax.ppermute(sent, ("row", "col"), [(b, a) for a, b in offset(*p)])
        for p, sent in zip(places[1:], blocks[1:])
    ]
    arrived = sum((a.astype(F32) for a in arrivals), blocks[0].astype(F32)).astype(BF16)
    arrived, far_three, far_last, *mixed = lax.optimization_barrier((arrived, far_three, far_last, *mixed))
    grad_in = lax.ppermute(arrived, ("dp", "row"), swap_back)

    grad_weight, mixed, grad_long, grad_short = kernel_call(
        functools.partial(weight_grad_body, scale),
        [
            shaped((3, drow, local), F32),
            shaped((rows, local), BF16),
            shaped((ngroups, ntaps), F32),
            shaped((3 * nshort, local), F32),
        ],
        grid=(3,),
        in_specs=[whole(nblocks, ncol, rows, dcol)] * 2
        + [whole(*grad_near.shape)] * 4
        + [whole(*far_three.shape), whole(*far_last.shape)]
        + [whole(rows, width)] * ndp,
        out_specs=[
            pl.BlockSpec((1, drow, local), lambda i: (i, 0, 0)),
            whole(rows, local),
            whole(ngroups, ntaps),
            whole(3 * nshort, local),
        ],
        scratch=[
            pltpu.VMEM((2, ndp, 3 * chunk + extra, width), BF16),
            pltpu.VMEM((ndp, rows, width), BF16),
        ],
        flops=2 * mm_flops,
        nbytes=2 * mm_bytes,
        vmem=MOST_VMEM_BYTES,
    )(x0, x1, *near, near_last, far_three, far_last, *mixed)
    grad_weight = jnp.transpose(grad_weight, (1, 0, 2))
    grad_short = grad_short.reshape(nshort, 3, local)
    return (mixed, grad_in, grad_weight, grad_long, grad_short)


def from_behind(block, axis, distance):
    devices = range(lax.axis_size(axis))
    route = [(i - distance, i) for i in devices if i - distance in devices]
    return lax.ppermute(block, axis, route)


def toeplitz(leading, rows, span):
    groups = leading.shape[0]
    width = rows + span
    seed_row = jnp.concatenate(
        [leading, jnp.zeros((groups, width - leading.shape[1]), leading.dtype)], axis=1
    )
    tiled = jnp.tile(seed_row, (1, rows))
    skewed = tiled[:, : rows * (width - 1)].reshape(groups, rows, width - 1)
    return skewed[:, :, :span]


def to_groups(values, ngroups, members):
    count = values.shape[0]
    return values.reshape(count, ngroups, members).transpose(1, 2, 0)


def from_groups(values):
    groups, members, count = values.shape
    return values.transpose(2, 0, 1).reshape(count, groups * members)


def move_weights(tokens, in_weight, short_filter, long_filter, grad_out):
    rows = tokens.shape[0]
    local = grad_out.shape[1]
    nshort = short_filter.shape[0]
    ntaps = long_filter.shape[1]
    ngroups = long_filter.shape[0]
    members = local // ngroups
    margin = ntaps - 1
    span = rows + margin
    scale = float(rows * lax.axis_size("dp")) ** (-0.5)
    whole = lax.all_gather(tokens, ("row", "col"), axis=1, tiled=True)
    full_w = lax.all_gather(in_weight, "dp", axis=0, tiled=True)
    mixed_in = jnp.einsum("sd,dic->sic", whole, full_w, preferred_element_type=jnp.float32).astype(
        jnp.bfloat16
    )
    before = from_behind(mixed_in[rows - margin - nshort + 1 :], "dp", 1)
    extended = jnp.concatenate([before, mixed_in], axis=0).astype(jnp.float32)
    long_feats = jnp.zeros((span, 3, local), jnp.float32)
    for j in range(nshort):
        long_feats = (
            long_feats + short_filter[j][None] * extended[nshort - 1 - j : nshort - 1 - j + span]
        )
    product_ext = (long_feats[:, 1] * long_feats[:, 2]).astype(jnp.bfloat16)
    feats = long_feats[margin:]
    short_rows = extended[margin:]
    product_cols = to_groups(product_ext, ngroups, members)
    causal = toeplitz(long_filter[:, ::-1], rows, span)
    conv = from_groups(
        jnp.einsum("gst,gct->gcs", causal, product_cols, preferred_element_type=jnp.float32)
    )
    mixed = (feats[:, 0] * conv).astype(jnp.bfloat16)
    upstream = grad_out.astype(jnp.float32)
    grad_query = upstream * conv
    grad_conv = (upstream * feats[:, 0]).astype(jnp.bfloat16)
    after = from_behind(grad_conv[:margin], "dp", -1)
    grad_ext = jnp.concatenate([grad_conv, after], axis=0)
    anti = toeplitz(long_filter, rows, span)
    grad_product = from_groups(
        jnp.einsum(
            "gst,gct->gcs",
            anti,
            to_groups(grad_ext, ngroups, members),
            preferred_element_type=jnp.float32,
        )
    )
    reversed_cols = jnp.concatenate(
        [product_cols[:, :, ::-1], jnp.zeros((ngroups, members, rows), product_cols.dtype)], axis=2
    )
    width = span + rows
    pairs = jnp.einsum(
        "gcs,gcu->gsu",
        to_groups(grad_conv, ngroups, members),
        reversed_cols,
        preferred_element_type=jnp.float32,
    )
    diagonal = pairs.reshape(ngroups, rows * width)[:, : rows * (width - 1)].reshape(
        ngroups, rows, width - 1
    )
    filter_part = jnp.sum(diagonal[:, :, rows - 1 : rows - 1 + ntaps], axis=1)
    grad_feats = jnp.stack(
        [grad_query, grad_product * feats[:, 2], grad_product * feats[:, 1]], axis=1
    )
    later = from_behind(grad_feats[: nshort - 1], "dp", -1)
    feats_ext = jnp.concatenate([grad_feats, later], axis=0)
    grad_acc = jnp.zeros((rows, 3, local), jnp.float32)
    for j in range(nshort):
        grad_acc = grad_acc + short_filter[j][None] * feats_ext[j : j + rows]
    grad_mixed = grad_acc.astype(jnp.bfloat16)
    short_part = jnp.stack(
        [
            jnp.sum(grad_feats * short_rows[nshort - 1 - j : nshort - 1 - j + rows], axis=0)
            for j in range(nshort)
        ]
    )
    filter_total, short_total = (
        lax.psum(filter_part.astype(jnp.bfloat16), "dp").astype(jnp.float32),
        lax.psum(short_part.astype(jnp.bfloat16), "dp").astype(jnp.float32),
    )
    grad_long = filter_total * scale
    grad_short = short_total * scale
    partial_in = jnp.einsum("sic,dic->sd", grad_mixed, full_w, preferred_element_type=jnp.float32)
    summed_in = lax.psum_scatter(
        partial_in.astype(jnp.bfloat16), ("row", "col"), scatter_dimension=1, tiled=True
    )
    weight_term = (
        jnp.einsum("sd,sic->dic", whole, grad_mixed, preferred_element_type=jnp.float32) * scale
    )
    grad_weight = lax.psum_scatter(
        weight_term.astype(jnp.bfloat16), "dp", scatter_dimension=0, tiled=True
    ).astype(jnp.float32)
    return (mixed, summed_in, grad_weight, grad_long, grad_short)


def fits_whole_sequences(mesh, tokens, in_weight, short_filter, long_filter, grad_out):
    ndp, nrow, ncol = (mesh.shape[a] for a in ("dp", "row", "col"))
    seq, channels = grad_out.shape
    groups, ntaps = long_filter.shape
    local = channels // (nrow * ncol)
    width, rows = local // ndp, seq // ndp
    return (
        seq < tokens.shape[1]
        and ndp == nrow == 4
        and ncol * (tokens.shape[1] // (nrow * ncol)) == in_weight.shape[0] // ndp
        and ntaps == width == 128
        and seq % (2 * ntaps) == 0
        and rows % 16 == 0
        and groups % (8 * ndp * nrow * ncol) == 0
    )


def solution(mesh):
    placed = (
        P("dp", ("row", "col")),
        P("dp", None, ("row", "col")),
        P(None, None, ("row", "col")),
        P(("row", "col"), None),
        P("dp", ("row", "col")),
    )
    gives = (
        P("dp", ("row", "col")),
        P("dp", ("row", "col")),
        P("dp", None, ("row", "col")),
        P(("row", "col"), None),
        P(None, None, ("row", "col")),
    )

    def run(*arrays):
        plan = move_activations if fits_whole_sequences(mesh, *arrays) else move_weights
        return jax.shard_map(
            plan, mesh=mesh, in_specs=placed, out_specs=gives, check_vma=False
        )(*arrays)

    return run
```

```python
import functools

import jax
import jax.numpy as jnp
from jax import lax
from jax.experimental import pallas as pl
from jax.experimental.pallas import tpu as pltpu
from jax.sharding import PartitionSpec as P

VMEM_BYTES = 48 * 2**20
MOST_VMEM_BYTES = 62 * 2**20
F32 = jnp.float32
BF16 = jnp.bfloat16


def kernel_call(body, outs, grid=(), in_specs=None, out_specs=None, scratch=(), flops=0, nbytes=0, vmem=VMEM_BYTES):
    kwargs = {}
    if in_specs is not None:
        kwargs = dict(grid=grid, in_specs=in_specs, out_specs=out_specs)
    return pl.pallas_call(
        body,
        out_shape=outs,
        scratch_shapes=scratch,
        compiler_params=pltpu.CompilerParams(vmem_limit_bytes=vmem),
        cost_estimate=pl.CostEstimate(flops=flops, bytes_accessed=nbytes, transcendentals=0),
        **kwargs,
    )


def shaped(shape, dtype):
    return jax.ShapeDtypeStruct(shape, dtype)


def bands_body(base_ref, out_ref):
    groups, wide = base_ref.shape
    rows = out_ref.shape[1]
    row = lax.broadcasted_iota(jnp.int32, (8, wide), 0)
    for g in range(groups):
        band = jnp.broadcast_to(base_ref[g : g + 1, :], (8, wide))
        for bit in (1, 2, 4):
            band = jnp.where((row & bit) != 0, pltpu.roll(band, bit, 1), band)
        count = 8
        while count < rows:
            band = jnp.concatenate([band, pltpu.roll(band, count, 1)], axis=0)
            count *= 2
        out_ref[g] = band.astype(out_ref.dtype)


def tokens_of(row, nrow):
    return row % 2 * (nrow // 2) + row // 2


def wrapped(value, size):
    return lax.rem(value + 2 * size, size)


def split_body(all_ref, *out_refs):
    width = out_refs[0].shape[1]
    for ahead, out_ref in enumerate(out_refs):
        at = wrapped(lax.axis_index("dp") + ahead, len(out_refs)) * width
        out_ref[...] = all_ref[:, pl.ds(pl.multiple_of(at, width), width)]


def project_body(x_ref, w_ref, partner_w_ref, *refs):
    *out_refs, held = refs
    ndp, _, width = held.shape
    z, col = lax.axis_index("dp"), lax.axis_index("col")
    nblocks, ncol, rows, depth = x_ref.shape
    for weights, targets in ((w_ref, out_refs[:ndp]), (partner_w_ref, out_refs[ndp:])):
        total = jnp.zeros((nblocks * rows, w_ref.shape[2]), F32)
        for dx in range(ncol):
            start = pl.multiple_of(wrapped(col - dx, ncol) * depth, depth)
            total += jnp.dot(
                x_ref[:, dx].reshape(nblocks * rows, depth),
                weights[0, pl.ds(start, depth), :],
                preferred_element_type=F32,
            )
        for owner in range(ndp):
            held[owner] = total[:, owner * width : (owner + 1) * width].astype(BF16)
        for ahead, out_ref in enumerate(targets):
            out_ref[0] = held[wrapped(z + ahead, ndp)]


def first_grad_body(near, near_before, near_after, far, far_before, far_after, w_ref, partner_w_ref, out_ref, far_ref, held):
    ndp, _, width = held.shape
    ncol, tokens, depth = out_ref.shape
    z, col = lax.axis_index("dp"), lax.axis_index("col")
    far_ref[0], far_ref[1], far_ref[2] = far[...], far_before[...], far_after[...]
    for pieces, weights, first in (
        ((near, near_before, near_after), w_ref, True),
        ((far, far_before, far_after), partner_w_ref, False),
    ):
        held[wrapped(z + ndp // 2, ndp)] = jnp.zeros(held.shape[1:], BF16)
        for ahead, piece in zip((0, -1, 1), pieces):
            held[wrapped(z + ahead, ndp)] = piece[: 3 * tokens]
        for dx in range(ncol):
            start = pl.multiple_of(wrapped(col - dx, ncol) * depth, depth)
            total = jnp.zeros((tokens, depth), F32) if first else out_ref[dx]
            for i in range(3):
                rows = slice(i * tokens, (i + 1) * tokens)
                total += lax.dot_general(
                    jnp.concatenate([held[owner, rows] for owner in range(ndp)], axis=1),
                    weights[i, pl.ds(start, depth), :],
                    (((1,), (1,)), ((), ())),
                    preferred_element_type=F32,
                )
            out_ref[dx] = total


def second_grad_body(ndp, part_ref, far_three_ref, *refs):
    arrived, weights, refs = (refs[:2], refs[2:4]), refs[4:6], refs[6:]
    (near_ref, far_all_ref), refs = refs[:2], refs[2:]
    *out_refs, held_w, held_part, far_ref, sems = refs
    ncol, tokens, depth = held_part.shape
    rows = out_refs[0].shape[0]
    width = near_ref.shape[1]
    z, col = lax.axis_index("dp"), lax.axis_index("col")
    lanes = pl.ds(pl.multiple_of(wrapped(z + ndp // 2, ndp) * width, width), width)
    copies = [
        pltpu.make_async_copy(w_ref.at[:, :, lanes], held_w.at[k], sems.at[k]) for k, w_ref in enumerate(weights)
    ]
    copies.append(pltpu.make_async_copy(part_ref, held_part, sems.at[2]))
    for copy in copies:
        copy.start()
    handed_on = pltpu.make_async_copy(far_three_ref, far_all_ref.at[pl.ds(0, ndp - 1)], sems.at[5])
    handed_on.start()
    for k, (pair, target) in enumerate(zip(arrived, (near_ref, far_ref))):
        for source, here in zip(pair, (z >= ndp // 2, z < ndp // 2)):

            @pl.when(here)
            def _(source=source, target=target, k=k):
                copy = pltpu.make_async_copy(source, target, sems.at[3 + k])
                copy.start()
                copy.wait()

    last_on = pltpu.make_async_copy(far_ref, far_all_ref.at[ndp - 1], sems.at[6])
    last_on.start()
    for copy in copies:
        copy.wait()
    left = jnp.concatenate(
        [ref[i * tokens : (i + 1) * tokens] for ref in (near_ref, far_ref) for i in range(3)], axis=1
    )
    for dx in range(ncol):
        start = pl.multiple_of(wrapped(col - dx, ncol) * depth, depth)
        right = jnp.concatenate([held_w[k, i, pl.ds(start, depth), :] for k in range(2) for i in range(3)], axis=1)
        total = held_part[dx] + lax.dot_general(
            left, right, (((1,), (1,)), ((), ())), preferred_element_type=F32
        )
        for block in range(tokens // rows):
            out_refs[block * ncol + dx][...] = total[block * rows : (block + 1) * rows].astype(BF16)
    handed_on.wait()
    last_on.wait()


def weight_grad_body(scale, *refs):
    (x0_ref, x1_ref), near_refs, far_ref, mixed_refs, refs = refs[:2], refs[2:6], refs[6], refs[7:11], refs[11:]
    out_ref, mixed_ref, long_ref, short_ref, held, held_mixed = refs
    nblocks, ncol, rows, depth = x0_ref.shape
    _, ndp, _, width = held.shape
    tokens = nblocks * rows
    i = pl.program_id(0)
    z, col = lax.axis_index("dp"), lax.axis_index("col")

    @pl.when(i == 0)
    def _():
        groups = long_ref.shape[0] // ndp
        for k, ahead in enumerate((0, -1, 1, 2)):
            owner = wrapped(z + ahead, ndp)
            held[0, owner] = near_refs[k][...]
            held[1, owner, : 3 * tokens] = far_ref[k]
        for back in range(ndp):
            held_mixed[wrapped(z - back, ndp)] = mixed_refs[back][...]
        for owner in range(ndp):
            lanes = slice(owner * width, (owner + 1) * width)
            mixed_ref[:, lanes] = held_mixed[owner]
            small = held[0, owner, 3 * tokens :].astype(F32)
            long_ref[owner * groups : (owner + 1) * groups] = small[:groups]
            nshort, three, _ = short_ref.shape
            for j in range(nshort):
                short_ref[j, :, lanes] = small[groups + three * j : groups + three * (j + 1)]

    at = pl.ds(pl.multiple_of(i * tokens, 16), tokens)
    gm = jnp.concatenate(
        [jnp.concatenate([held[k, owner, at, :] for owner in range(ndp)], axis=1) for k in range(2)], axis=0
    )
    for dx in range(ncol):
        start = pl.multiple_of(wrapped(col - dx, ncol) * depth, depth)
        x = jnp.concatenate(
            [x_ref[:, dx].reshape(tokens, depth) for x_ref in (x0_ref, x1_ref)], axis=0
        )
        out_ref[0, pl.ds(start, depth), :] = scale * lax.dot_general(
            x, gm, (((0,), (0,)), ((), ())), preferred_element_type=F32
        )


def delayed(values, count):
    row = lax.broadcasted_iota(jnp.int32, values.shape, 0)
    return jnp.where(row >= count, pltpu.roll(values, count, 0), 0.0)


def advanced(values, count):
    rows = values.shape[0]
    row = lax.broadcasted_iota(jnp.int32, values.shape, 0)
    return jnp.where(row < rows - count, pltpu.roll(values, rows - count, 0), 0.0)


def middle_body(scale, nshort, nrow, *refs):
    sums, refs = (refs[:3], refs[3:6]), refs[6:]
    (sf_ref, causal_ref, anti_ref), refs = refs[:3], refs[3:]
    *refs, m_ref, gm_ref, mixed_ref, go_ref = refs
    ndp = len(refs) // 2 - 1
    go_refs, (near_ref, other_ref), mixed_refs = refs[:ndp], refs[ndp : ndp + 2], refs[ndp + 2 :]
    tokens, width = go_ref.shape
    for behind, piece in enumerate(go_refs):
        at = wrapped(lax.axis_index("dp") - behind, ndp) * (tokens // ndp)
        go_ref[pl.ds(pl.multiple_of(at, 16), tokens // ndp)] = piece[...]
    row = lax.axis_index("row")
    nblocks = nrow // 2
    rows = tokens // nrow

    def places():
        for chunk, start in enumerate((row, row + 1 - 2 * lax.rem(row, 2))):
            for block in range(nblocks):
                at = tokens_of(wrapped(start - 2 * block, nrow), nrow) * rows
                for i in range(3):
                    yield chunk, (i * nblocks + block) * rows, pl.multiple_of(i * tokens + at, 16)

    for chunk, place, at in places():
        held = [ref[place : place + rows].astype(F32) for ref in sums[chunk]]
        m_ref[pl.ds(at, rows)] = held[0] + held[1] + held[2]
    groups, block, span = causal_ref.shape
    members = width // groups
    nspans = tokens // block
    lane = lax.broadcasted_iota(jnp.int32, (block, width), 1) // members
    lanes = lax.broadcasted_iota(jnp.int32, (block, 2 * width), 1) % width // members

    def past(i, j):
        held = m_ref[i * tokens : (i + 1) * tokens]
        return held if j == 0 else delayed(held, j)

    def taps(j, i):
        return sf_ref[3 * j + i : 3 * j + i + 1, :]

    feats = [sum(taps(j, i) * past(i, j) for j in range(nshort)) for i in range(3)]
    product = (feats[1] * feats[2]).astype(BF16)
    zero = jnp.zeros((block, width), BF16)
    p_blocks = [zero] + [product[b * block : (b + 1) * block] for b in range(nspans)]
    p_pairs = [jnp.concatenate(p_blocks[b : b + 2], axis=0) for b in range(nspans)]

    def filtered(band_ref, pairs):
        bands = band_ref[...].reshape(groups * block, span)
        out = []
        for b in range(0, nspans, 2):
            both = jnp.dot(bands, jnp.concatenate(pairs[b : b + 2], axis=1), preferred_element_type=F32)
            for h in range(2):
                part = both[:, h * width : (h + 1) * width]
                picked = part[:block]
                for g in range(1, groups):
                    picked = jnp.where(lane == g, part[g * block : (g + 1) * block], picked)
                out.append(picked)
        return jnp.concatenate(out, axis=0)

    conv = filtered(causal_ref, p_pairs)
    upstream = go_ref[...].astype(F32)
    mixed_ref[...] = (feats[0] * conv).astype(BF16)
    for ahead, out_ref in enumerate(mixed_refs):
        at = pl.multiple_of(wrapped(lax.axis_index("dp") + ahead, ndp) * (tokens // ndp), 16)
        out_ref[...] = mixed_ref[pl.ds(at, tokens // ndp)]
    grad_conv = (upstream * feats[0]).astype(BF16)
    c_blocks = [grad_conv[b * block : (b + 1) * block] for b in range(nspans)] + [zero]
    c_pairs = [jnp.concatenate(c_blocks[b : b + 2], axis=0) for b in range(nspans)]
    grad_product = filtered(anti_ref, c_pairs)

    corr = jnp.zeros((groups * block, span), F32)
    for b in range(0, nspans, 2):
        left = jnp.concatenate(c_blocks[b : b + 2], axis=1)
        stacked = jnp.concatenate(
            [jnp.where(lanes == g, left, jnp.zeros_like(left)) for g in range(groups)], axis=0
        )
        right = jnp.concatenate(p_pairs[b : b + 2], axis=1)
        corr += lax.dot_general(stacked, right, (((1,), (1,)), ((), ())), preferred_element_type=F32)
    turn = lax.broadcasted_iota(jnp.int32, (8, span), 0)
    sums = []
    for g in range(groups):
        part = corr[g * block : (g + 1) * block]
        count = block
        while count > 8:
            count //= 2
            part = part[:count] + pltpu.roll(part[count:], span - count, 1)
        for bit in (1, 2, 4):
            part = jnp.where((turn & bit) != 0, pltpu.roll(part, span - bit, 1), part)
        sums.append(jnp.sum(part, axis=0, keepdims=True))
    by_lag = jnp.concatenate(sums, axis=0)
    by_lag = (scale * pltpu.roll(by_lag, span - 1, 1)[:, :block]).astype(BF16)
    ahead = lax.broadcasted_iota(jnp.int32, (block, block), 0)
    back = lax.broadcasted_iota(jnp.int32, (block, block), 1)
    turned = jnp.where(ahead + back == block - 1, 1.0, 0.0).astype(BF16)
    by_lag = jnp.dot(by_lag, turned, preferred_element_type=F32)

    grad_feats = [upstream * conv, grad_product * feats[2], grad_product * feats[1]]
    short_rows = []
    for j in range(nshort):
        for i in range(3):
            short_rows.append(scale * jnp.sum(grad_feats[i] * past(i, j), axis=0, keepdims=True))
    for i in range(3):
        total = taps(0, i) * grad_feats[i]
        for j in range(1, nshort):
            total += taps(j, i) * advanced(grad_feats[i], j)
        gm_ref[i * tokens : (i + 1) * tokens] = total.astype(BF16)
    for chunk, place, at in places():
        (near_ref, other_ref)[chunk][place : place + rows] = gm_ref[pl.ds(at, rows)]
    tail = near_ref.shape[0] - 3 * tokens // 2 - groups - 3 * nshort
    small = jnp.concatenate([by_lag] + short_rows + [jnp.zeros((tail, width), F32)], axis=0)
    near_ref[3 * tokens // 2 :] = small.astype(BF16)


def shift(count, across):
    ndp, nrow = lax.axis_size("dp"), lax.axis_size("row")
    return [
        (a * nrow + r, (a + count) % ndp * nrow + (r + 1 - 2 * (r % 2) if across else r))
        for a in range(ndp)
        for r in range(nrow)
    ]


def first_hop(far):
    ndp = lax.axis_size("dp")
    return (
        lax.ppermute(far, "dp", [(a, a + 1) for a in range(ndp // 2)]),
        lax.ppermute(far, "dp", [(a, a - 1) for a in range(ndp // 2, ndp)]),
    )


def second_hop(own, right, left, from_left, from_right, across):
    rightward = lax.ppermute(right + from_left, ("dp", "row"), shift(1, across))
    leftward = lax.ppermute(left + from_right, ("dp", "row"), shift(-1, across))
    here = lax.ppermute(own, ("dp", "row"), shift(0, across)) if across else own
    return here, rightward, leftward


def gather_over_line(own, across):
    ndp = lax.axis_size("dp")
    before = lax.ppermute(own, ("dp", "row"), shift(1, across))
    after = lax.ppermute(own, ("dp", "row"), shift(-1, across))
    here = lax.ppermute(own, ("dp", "row"), shift(0, across)) if across else own
    far_before = lax.ppermute(before, "dp", [(a - 1, a) for a in range(ndp // 2, ndp)])
    far_after = lax.ppermute(after, "dp", [(a + 1, a) for a in range(ndp // 2)])
    return here, before, after, far_before, far_after


def move_activations(tokens, in_weight, short_filter, long_filter, grad_out):
    ndp, nrow, ncol = (lax.axis_size(a) for a in ("dp", "row", "col"))
    z = lax.axis_index("dp")
    rows, dcol = tokens.shape
    local = grad_out.shape[1]
    nshort = short_filter.shape[0]
    ngroups, ntaps = long_filter.shape
    seq = rows * ndp
    width, groups = local // ndp, ngroups // ndp
    drow = in_weight.shape[0]
    scale = float(seq) ** -0.5
    nblocks = nrow // 2
    chunk = nblocks * rows
    swap = [(tokens_of(b, nrow) * nrow + a, a * nrow + b) for a in range(ndp) for b in range(nrow)]
    swap_back = [(b, a) for a, b in swap]
    partner = [(a, a + 1 - 2 * (a % 2)) for a in range(nrow)]
    places = [(dy, dx) for dy in range(nblocks) for dx in range(ncol)]

    def offset(dy, dx):
        return [
            (a * ncol + b, (a + 2 * dy) % nrow * ncol + (b + dx) % ncol) for a in range(nrow) for b in range(ncol)
        ]

    w = jnp.transpose(in_weight, (1, 0, 2))
    moved = lax.ppermute(tokens, ("dp", "row"), swap)
    partner_w = lax.ppermute(w, "row", partner)
    upstream = [*kernel_call(split_body, [shaped((rows, width), BF16)] * ndp)(grad_out)]
    turn = [[(a, (a + ahead) % ndp) for a in range(ndp)] for ahead in range(ndp)]
    upstream[2] = lax.ppermute(upstream[2], "dp", turn[2])
    moved, partner_w, upstream = lax.optimization_barrier((moved, partner_w, upstream))
    near = [moved] + [lax.ppermute(moved, ("row", "col"), offset(*p)) for p in places[1:]]
    for ahead in (1, 3):
        upstream[ahead] = lax.ppermute(upstream[ahead], "dp", turn[ahead])
    upstream[1::2], near[1:] = lax.optimization_barrier((upstream[1::2], near[1:]))
    x0 = jnp.stack(near).reshape(nblocks, ncol, rows, dcol)

    sf = lax.dynamic_slice_in_dim(short_filter, z * width, width, 2).reshape(3 * nshort, width)
    lf = lax.dynamic_slice_in_dim(long_filter, z * groups, groups, 0).astype(F32)
    zeros = functools.partial(jnp.zeros, dtype=F32)
    bases = jnp.concatenate(
        [
            jnp.concatenate([zeros((groups, 1)), lf[:, ::-1], zeros((groups, ntaps - 1))], axis=1),
            jnp.concatenate([lf, zeros((groups, ntaps))], axis=1),
        ],
        axis=0,
    )
    bands = kernel_call(bands_body, shaped((2 * groups, ntaps, 2 * ntaps), BF16))(bases)

    mm_flops = seq * drow * 3 * local
    mm_bytes = seq * drow + 6 * drow * local + 3 * seq * local
    parts = kernel_call(
        project_body,
        [shaped((3, chunk, width), BF16)] * (2 * ndp),
        grid=(3,),
        in_specs=[pl.BlockSpec((nblocks, ncol, rows, dcol), lambda i: (0, 0, 0, 0))]
        + [pl.BlockSpec((1, drow, local), lambda i: (i, 0, 0))] * 2,
        out_specs=[pl.BlockSpec((1, chunk, width), lambda i: (i, 0, 0))] * (2 * ndp),
        scratch=[pltpu.VMEM((ndp, chunk, width), BF16)],
        flops=2 * mm_flops,
        nbytes=2 * mm_bytes,
    )(x0, w, partner_w)
    parts = [p.reshape(3 * chunk, width) for p in parts]
    x1 = lax.ppermute(x0, "row", partner)
    sums = []
    for across in (False, True):
        own, right, far, left = parts[ndp * across :][:ndp]
        from_left, from_right = first_hop(far)
        if not across:
            x1, from_left = lax.optimization_barrier((x1, from_left))
        sums += second_hop(own, right, left, from_left, from_right, across)

    extra = -(-(groups + 3 * nshort) // 16) * 16
    half = pl.BlockSpec((groups, ntaps, 2 * ntaps), lambda i: (0, 0, 0))
    other = pl.BlockSpec((groups, ntaps, 2 * ntaps), lambda i: (1, 0, 0))
    whole = lambda *shape: pl.BlockSpec(shape, lambda i: (0,) * len(shape))
    grad_near, grad_other, *mixed = kernel_call(
        functools.partial(middle_body, scale, nshort, nrow),
        [shaped((3 * chunk + extra, width), BF16), shaped((3 * chunk, width), BF16)]
        + [shaped((rows, width), BF16)] * ndp,
        grid=(1,),
        in_specs=[whole(3 * chunk, width)] * 6
        + [whole(3 * nshort, width), half, other]
        + [whole(rows, width)] * ndp,
        out_specs=[whole(3 * chunk + extra, width), whole(3 * chunk, width)] + [whole(rows, width)] * ndp,
        scratch=[
            pltpu.VMEM((3 * seq, width), F32),
            pltpu.VMEM((3 * seq, width), BF16),
            pltpu.VMEM((seq, width), BF16),
            pltpu.VMEM((seq, width), BF16),
        ],
        flops=3 * 2 * groups * ntaps * 2 * ntaps * width * (seq // ntaps),
        nbytes=2 * width * seq * 14,
        vmem=MOST_VMEM_BYTES,
    )(*sums, sf, bands, bands, *upstream)
    for ahead in range(1, ndp):
        mixed[ahead] = lax.ppermute(mixed[ahead], "dp", turn[ahead])
    *near, near_far_before, near_far_after = gather_over_line(grad_near, False)
    *far, far_far_before, far_far_after = gather_over_line(grad_other, True)
    mixed[2:], near_far_before = lax.optimization_barrier((mixed[2:], near_far_before))
    part, far_three = kernel_call(
        first_grad_body,
        [shaped((ncol, chunk, dcol), F32), shaped((3, 3 * chunk, width), BF16)],
        scratch=[pltpu.VMEM((ndp, 3 * chunk, width), BF16)],
        flops=2 * mm_flops,
        nbytes=2 * mm_bytes,
    )(*near, *far, w, partner_w)
    everywhere = pl.BlockSpec(memory_space=pl.ANY)
    in_vmem = pl.BlockSpec(memory_space=pltpu.VMEM)
    near_last, far_all, *blocks = kernel_call(
        functools.partial(second_grad_body, ndp),
        [shaped(grad_near.shape, BF16), shaped((ndp, *grad_other.shape), BF16)]
        + [shaped((rows, dcol), BF16)] * len(places),
        grid=(),
        in_specs=[everywhere] * 8,
        out_specs=[in_vmem, everywhere] + [in_vmem] * len(places),
        scratch=[
            pltpu.VMEM((2, 3, drow, width), BF16),
            pltpu.VMEM((ncol, chunk, dcol), F32),
            pltpu.VMEM(grad_other.shape, BF16),
            pltpu.SemaphoreType.DMA((7,)),
        ],
        flops=mm_flops // 2,
        nbytes=mm_bytes // 2,
        vmem=MOST_VMEM_BYTES,
    )(part, far_three, near_far_before, near_far_after, far_far_before, far_far_after, w, partner_w)
    arrivals = [
        lax.ppermute(sent, ("row", "col"), [(b, a) for a, b in offset(*p)])
        for p, sent in zip(places[1:], blocks[1:])
    ]
    far_all = lax.ppermute(far_all, "row", partner)
    arrived = sum((a.astype(F32) for a in arrivals), blocks[0].astype(F32)).astype(BF16)
    arrived, far_all, mixed[1] = lax.optimization_barrier((arrived, far_all, mixed[1]))
    grad_in = lax.ppermute(arrived, ("dp", "row"), swap_back)

    grad_weight, mixed, grad_long, grad_short = kernel_call(
        functools.partial(weight_grad_body, scale),
        [
            shaped((3, drow, local), F32),
            shaped((rows, local), BF16),
            shaped((ngroups, ntaps), F32),
            shaped((nshort, 3, local), F32),
        ],
        grid=(3,),
        in_specs=[whole(nblocks, ncol, rows, dcol)] * 2
        + [whole(*grad_near.shape)] * 4
        + [whole(*far_all.shape)]
        + [whole(rows, width)] * ndp,
        out_specs=[
            pl.BlockSpec((1, drow, local), lambda i: (i, 0, 0)),
            whole(rows, local),
            whole(ngroups, ntaps),
            whole(nshort, 3, local),
        ],
        scratch=[
            pltpu.VMEM((2, ndp, 3 * chunk + extra, width), BF16),
            pltpu.VMEM((ndp, rows, width), BF16),
        ],
        flops=2 * mm_flops,
        nbytes=2 * mm_bytes,
        vmem=MOST_VMEM_BYTES,
    )(x0, x1, *near, near_last, far_all, *mixed)
    grad_weight = jnp.transpose(grad_weight, (1, 0, 2))
    return (mixed, grad_in, grad_weight, grad_long, grad_short)


def from_behind(block, axis, distance):
    devices = range(lax.axis_size(axis))
    route = [(i - distance, i) for i in devices if i - distance in devices]
    return lax.ppermute(block, axis, route)


def toeplitz(leading, rows, span):
    groups = leading.shape[0]
    width = rows + span
    seed_row = jnp.concatenate(
        [leading, jnp.zeros((groups, width - leading.shape[1]), leading.dtype)], axis=1
    )
    tiled = jnp.tile(seed_row, (1, rows))
    skewed = tiled[:, : rows * (width - 1)].reshape(groups, rows, width - 1)
    return skewed[:, :, :span]


def to_groups(values, ngroups, members):
    count = values.shape[0]
    return values.reshape(count, ngroups, members).transpose(1, 2, 0)


def from_groups(values):
    groups, members, count = values.shape
    return values.transpose(2, 0, 1).reshape(count, groups * members)


def move_weights(tokens, in_weight, short_filter, long_filter, grad_out):
    rows = tokens.shape[0]
    local = grad_out.shape[1]
    nshort = short_filter.shape[0]
    ntaps = long_filter.shape[1]
    ngroups = long_filter.shape[0]
    members = local // ngroups
    margin = ntaps - 1
    span = rows + margin
    scale = float(rows * lax.axis_size("dp")) ** (-0.5)
    whole = lax.all_gather(tokens, ("row", "col"), axis=1, tiled=True)
    full_w = lax.all_gather(in_weight, "dp", axis=0, tiled=True)
    mixed_in = jnp.einsum("sd,dic->sic", whole, full_w, preferred_element_type=jnp.float32).astype(
        jnp.bfloat16
    )
    before = from_behind(mixed_in[rows - margin - nshort + 1 :], "dp", 1)
    extended = jnp.concatenate([before, mixed_in], axis=0).astype(jnp.float32)
    long_feats = jnp.zeros((span, 3, local), jnp.float32)
    for j in range(nshort):
        long_feats = (
            long_feats + short_filter[j][None] * extended[nshort - 1 - j : nshort - 1 - j + span]
        )
    product_ext = (long_feats[:, 1] * long_feats[:, 2]).astype(jnp.bfloat16)
    feats = long_feats[margin:]
    short_rows = extended[margin:]
    product_cols = to_groups(product_ext, ngroups, members)
    causal = toeplitz(long_filter[:, ::-1], rows, span)
    conv = from_groups(
        jnp.einsum("gst,gct->gcs", causal, product_cols, preferred_element_type=jnp.float32)
    )
    mixed = (feats[:, 0] * conv).astype(jnp.bfloat16)
    upstream = grad_out.astype(jnp.float32)
    grad_query = upstream * conv
    grad_conv = (upstream * feats[:, 0]).astype(jnp.bfloat16)
    after = from_behind(grad_conv[:margin], "dp", -1)
    grad_ext = jnp.concatenate([grad_conv, after], axis=0)
    anti = toeplitz(long_filter, rows, span)
    grad_product = from_groups(
        jnp.einsum(
            "gst,gct->gcs",
            anti,
            to_groups(grad_ext, ngroups, members),
            preferred_element_type=jnp.float32,
        )
    )
    reversed_cols = jnp.concatenate(
        [product_cols[:, :, ::-1], jnp.zeros((ngroups, members, rows), product_cols.dtype)], axis=2
    )
    width = span + rows
    pairs = jnp.einsum(
        "gcs,gcu->gsu",
        to_groups(grad_conv, ngroups, members),
        reversed_cols,
        preferred_element_type=jnp.float32,
    )
    diagonal = pairs.reshape(ngroups, rows * width)[:, : rows * (width - 1)].reshape(
        ngroups, rows, width - 1
    )
    filter_part = jnp.sum(diagonal[:, :, rows - 1 : rows - 1 + ntaps], axis=1)
    grad_feats = jnp.stack(
        [grad_query, grad_product * feats[:, 2], grad_product * feats[:, 1]], axis=1
    )
    later = from_behind(grad_feats[: nshort - 1], "dp", -1)
    feats_ext = jnp.concatenate([grad_feats, later], axis=0)
    grad_acc = jnp.zeros((rows, 3, local), jnp.float32)
    for j in range(nshort):
        grad_acc = grad_acc + short_filter[j][None] * feats_ext[j : j + rows]
    grad_mixed = grad_acc.astype(jnp.bfloat16)
    short_part = jnp.stack(
        [
            jnp.sum(grad_feats * short_rows[nshort - 1 - j : nshort - 1 - j + rows], axis=0)
            for j in range(nshort)
        ]
    )
    filter_total, short_total = (
        lax.psum(filter_part.astype(jnp.bfloat16), "dp").astype(jnp.float32),
        lax.psum(short_part.astype(jnp.bfloat16), "dp").astype(jnp.float32),
    )
    grad_long = filter_total * scale
    grad_short = short_total * scale
    partial_in = jnp.einsum("sic,dic->sd", grad_mixed, full_w, preferred_element_type=jnp.float32)
    summed_in = lax.psum_scatter(
        partial_in.astype(jnp.bfloat16), ("row", "col"), scatter_dimension=1, tiled=True
    )
    weight_term = (
        jnp.einsum("sd,sic->dic", whole, grad_mixed, preferred_element_type=jnp.float32) * scale
    )
    grad_weight = lax.psum_scatter(
        weight_term.astype(jnp.bfloat16), "dp", scatter_dimension=0, tiled=True
    ).astype(jnp.float32)
    return (mixed, summed_in, grad_weight, grad_long, grad_short)


def fits_whole_sequences(mesh, tokens, in_weight, short_filter, long_filter, grad_out):
    ndp, nrow, ncol = (mesh.shape[a] for a in ("dp", "row", "col"))
    seq, channels = grad_out.shape
    groups, ntaps = long_filter.shape
    local = channels // (nrow * ncol)
    width, rows = local // ndp, seq // ndp
    return (
        seq < tokens.shape[1]
        and ndp == nrow == 4
        and ncol * (tokens.shape[1] // (nrow * ncol)) == in_weight.shape[0] // ndp
        and ntaps == width == 128
        and seq % (2 * ntaps) == 0
        and rows % 16 == 0
        and groups % (8 * ndp * nrow * ncol) == 0
    )


def solution(mesh):
    placed = (
        P("dp", ("row", "col")),
        P("dp", None, ("row", "col")),
        P(None, None, ("row", "col")),
        P(("row", "col"), None),
        P("dp", ("row", "col")),
    )
    gives = (
        P("dp", ("row", "col")),
        P("dp", ("row", "col")),
        P("dp", None, ("row", "col")),
        P(("row", "col"), None),
        P(None, None, ("row", "col")),
    )

    def run(*arrays):
        plan = move_activations if fits_whole_sequences(mesh, *arrays) else move_weights
        return jax.shard_map(
            plan, mesh=mesh, in_specs=placed, out_specs=gives, check_vma=False
        )(*arrays)

    return run
```

```python
import functools

import jax
import jax.numpy as jnp
from jax import lax
from jax.experimental import pallas as pl
from jax.experimental.pallas import tpu as pltpu
from jax.sharding import PartitionSpec as P

VMEM_BYTES = 48 * 2**20
MOST_VMEM_BYTES = 62 * 2**20
F32 = jnp.float32
BF16 = jnp.bfloat16


def kernel_call(body, outs, grid=(), in_specs=None, out_specs=None, scratch=(), flops=0, nbytes=0, vmem=VMEM_BYTES):
    kwargs = {}
    if in_specs is not None:
        kwargs = dict(grid=grid, in_specs=in_specs, out_specs=out_specs)
    return pl.pallas_call(
        body,
        out_shape=outs,
        scratch_shapes=scratch,
        compiler_params=pltpu.CompilerParams(vmem_limit_bytes=vmem),
        cost_estimate=pl.CostEstimate(flops=flops, bytes_accessed=nbytes, transcendentals=0),
        **kwargs,
    )


def shaped(shape, dtype):
    return jax.ShapeDtypeStruct(shape, dtype)


def bands_body(base_ref, out_ref):
    groups, wide = base_ref.shape
    rows = out_ref.shape[1]
    row = lax.broadcasted_iota(jnp.int32, (8, wide), 0)
    for g in range(groups):
        band = jnp.broadcast_to(base_ref[g : g + 1, :], (8, wide))
        for bit in (1, 2, 4):
            band = jnp.where((row & bit) != 0, pltpu.roll(band, bit, 1), band)
        count = 8
        while count < rows:
            band = jnp.concatenate([band, pltpu.roll(band, count, 1)], axis=0)
            count *= 2
        out_ref[g] = band.astype(out_ref.dtype)


def tokens_of(row, nrow):
    return row % 2 * (nrow // 2) + row // 2


def wrapped(value, size):
    return lax.rem(value + 2 * size, size)


def split_body(all_ref, *out_refs):
    width = out_refs[0].shape[1]
    for ahead, out_ref in enumerate(out_refs):
        at = wrapped(lax.axis_index("dp") + ahead, len(out_refs)) * width
        out_ref[...] = all_ref[:, pl.ds(pl.multiple_of(at, width), width)]


def project_body(x_ref, w_ref, *refs):
    *out_refs, held = refs
    z, col = lax.axis_index("dp"), lax.axis_index("col")
    nblocks, ncol, rows, depth = x_ref.shape
    width = held.shape[2]
    total = jnp.zeros((nblocks * rows, w_ref.shape[2]), F32)
    for dx in range(ncol):
        start = pl.multiple_of(wrapped(col - dx, ncol) * depth, depth)
        total += jnp.dot(
            x_ref[:, dx].reshape(nblocks * rows, depth),
            w_ref[0, pl.ds(start, depth), :],
            preferred_element_type=F32,
        )
    for owner in range(len(out_refs)):
        held[owner] = total[:, owner * width : (owner + 1) * width].astype(BF16)
    for ahead, out_ref in enumerate(out_refs):
        out_ref[0] = held[wrapped(z + ahead, len(out_refs))]


def first_grad_body(near, near_before, near_after, far, far_before, far_after, w_ref, partner_w_ref, out_ref, far_ref, held):
    ndp, _, width = held.shape
    ncol, tokens, depth = out_ref.shape
    z, col = lax.axis_index("dp"), lax.axis_index("col")
    far_ref[0], far_ref[1], far_ref[2] = far[...], far_before[...], far_after[...]
    for pieces, weights, first in (
        ((near, near_before, near_after), w_ref, True),
        ((far, far_before, far_after), partner_w_ref, False),
    ):
        held[wrapped(z + ndp // 2, ndp)] = jnp.zeros(held.shape[1:], BF16)
        for ahead, piece in zip((0, -1, 1), pieces):
            held[wrapped(z + ahead, ndp)] = piece[: 3 * tokens]
        for dx in range(ncol):
            start = pl.multiple_of(wrapped(col - dx, ncol) * depth, depth)
            total = jnp.zeros((tokens, depth), F32) if first else out_ref[dx]
            for i in range(3):
                rows = slice(i * tokens, (i + 1) * tokens)
                total += lax.dot_general(
                    jnp.concatenate([held[owner, rows] for owner in range(ndp)], axis=1),
                    weights[i, pl.ds(start, depth), :],
                    (((1,), (1,)), ((), ())),
                    preferred_element_type=F32,
                )
            out_ref[dx] = total


def second_grad_body(ndp, part_ref, *refs):
    arrived, weights, refs = (refs[:2], refs[2:4]), refs[4:6], refs[6:]
    (near_ref, far_ref), refs = refs[:2], refs[2:]
    *out_refs, held_w, held_part, sems = refs
    ncol, tokens, depth = held_part.shape
    rows = out_refs[0].shape[0]
    width = near_ref.shape[1]
    z, col = lax.axis_index("dp"), lax.axis_index("col")
    lanes = pl.ds(pl.multiple_of(wrapped(z + ndp // 2, ndp) * width, width), width)
    copies = [
        pltpu.make_async_copy(w_ref.at[:, :, lanes], held_w.at[k], sems.at[k]) for k, w_ref in enumerate(weights)
    ]
    copies.append(pltpu.make_async_copy(part_ref, held_part, sems.at[2]))
    for copy in copies:
        copy.start()
    for k, (pair, target) in enumerate(zip(arrived, (near_ref, far_ref))):
        for source, here in zip(pair, (z >= ndp // 2, z < ndp // 2)):

            @pl.when(here)
            def _(source=source, target=target, k=k):
                copy = pltpu.make_async_copy(source, target, sems.at[3 + k])
                copy.start()
                copy.wait()

    for copy in copies:
        copy.wait()
    left = jnp.concatenate(
        [ref[i * tokens : (i + 1) * tokens] for ref in (near_ref, far_ref) for i in range(3)], axis=1
    )
    for dx in range(ncol):
        start = pl.multiple_of(wrapped(col - dx, ncol) * depth, depth)
        right = jnp.concatenate([held_w[k, i, pl.ds(start, depth), :] for k in range(2) for i in range(3)], axis=1)
        total = held_part[dx] + lax.dot_general(
            left, right, (((1,), (1,)), ((), ())), preferred_element_type=F32
        )
        for block in range(tokens // rows):
            out_refs[block * ncol + dx][...] = total[block * rows : (block + 1) * rows].astype(BF16)


def weight_grad_body(scale, *refs):
    (x0_ref, x1_ref), near_refs, (far_ref, far_last_ref), mixed_refs, refs = (
        refs[:2],
        refs[2:6],
        refs[6:8],
        refs[8:12],
        refs[12:],
    )
    out_ref, mixed_ref, long_ref, short_ref, held, held_mixed = refs
    nblocks, ncol, rows, depth = x0_ref.shape
    _, ndp, _, width = held.shape
    tokens = nblocks * rows
    i = pl.program_id(0)
    z, col = lax.axis_index("dp"), lax.axis_index("col")

    @pl.when(i == 0)
    def _():
        groups = long_ref.shape[0] // ndp
        for k, ahead in enumerate((0, -1, 1, 2)):
            owner = wrapped(z + ahead, ndp)
            held[0, owner] = near_refs[k][...]
            held[1, owner, : 3 * tokens] = far_ref[k] if k < 3 else far_last_ref[...]
        for back in range(ndp):
            held_mixed[wrapped(z - back, ndp)] = mixed_refs[back][...]
        for owner in range(ndp):
            lanes = slice(owner * width, (owner + 1) * width)
            mixed_ref[:, lanes] = held_mixed[owner]
            small = held[0, owner, 3 * tokens :].astype(F32)
            long_ref[owner * groups : (owner + 1) * groups] = small[:groups]
            nshort, three, _ = short_ref.shape
            for j in range(nshort):
                short_ref[j, :, lanes] = small[groups + three * j : groups + three * (j + 1)]

    at = pl.ds(pl.multiple_of(i * tokens, 16), tokens)
    gm = jnp.concatenate(
        [jnp.concatenate([held[k, owner, at, :] for owner in range(ndp)], axis=1) for k in range(2)], axis=0
    )
    for dx in range(ncol):
        start = pl.multiple_of(wrapped(col - dx, ncol) * depth, depth)
        x = jnp.concatenate(
            [x_ref[:, dx].reshape(tokens, depth) for x_ref in (x0_ref, x1_ref)], axis=0
        )
        out_ref[0, pl.ds(start, depth), :] = scale * lax.dot_general(
            x, gm, (((0,), (0,)), ((), ())), preferred_element_type=F32
        )


def delayed(values, count):
    row = lax.broadcasted_iota(jnp.int32, values.shape, 0)
    return jnp.where(row >= count, pltpu.roll(values, count, 0), 0.0)


def advanced(values, count):
    rows = values.shape[0]
    row = lax.broadcasted_iota(jnp.int32, values.shape, 0)
    return jnp.where(row < rows - count, pltpu.roll(values, rows - count, 0), 0.0)


def middle_body(scale, nshort, nrow, *refs):
    sums, refs = (refs[:3], refs[3:6]), refs[6:]
    (sf_ref, causal_ref, anti_ref), refs = refs[:3], refs[3:]
    *refs, m_ref, gm_ref, mixed_ref, go_ref = refs
    ndp = len(refs) // 2 - 1
    go_refs, (near_ref, other_ref), mixed_refs = refs[:ndp], refs[ndp : ndp + 2], refs[ndp + 2 :]
    tokens, width = go_ref.shape
    for behind, piece in enumerate(go_refs):
        at = wrapped(lax.axis_index("dp") - behind, ndp) * (tokens // ndp)
        go_ref[pl.ds(pl.multiple_of(at, 16), tokens // ndp)] = piece[...]
    row = lax.axis_index("row")
    nblocks = nrow // 2
    rows = tokens // nrow

    def places():
        for chunk, start in enumerate((row, row + 1 - 2 * lax.rem(row, 2))):
            for block in range(nblocks):
                at = tokens_of(wrapped(start - 2 * block, nrow), nrow) * rows
                for i in range(3):
                    yield chunk, (i * nblocks + block) * rows, pl.multiple_of(i * tokens + at, 16)

    for chunk, place, at in places():
        held = [ref[place : place + rows].astype(F32) for ref in sums[chunk]]
        m_ref[pl.ds(at, rows)] = held[0] + held[1] + held[2]
    groups, block, span = causal_ref.shape
    members = width // groups
    nspans = tokens // block
    lane = lax.broadcasted_iota(jnp.int32, (block, width), 1) // members
    lanes = lax.broadcasted_iota(jnp.int32, (block, 2 * width), 1) % width // members

    def past(i, j):
        held = m_ref[i * tokens : (i + 1) * tokens]
        return held if j == 0 else delayed(held, j)

    def taps(j, i):
        return sf_ref[3 * j + i : 3 * j + i + 1, :]

    feats = [sum(taps(j, i) * past(i, j) for j in range(nshort)) for i in range(3)]
    product = (feats[1] * feats[2]).astype(BF16)
    zero = jnp.zeros((block, width), BF16)
    p_blocks = [zero] + [product[b * block : (b + 1) * block] for b in range(nspans)]
    p_pairs = [jnp.concatenate(p_blocks[b : b + 2], axis=0) for b in range(nspans)]

    def filtered(band_ref, pairs):
        bands = band_ref[...].reshape(groups * block, span)
        out = []
        for b in range(0, nspans, 2):
            both = jnp.dot(bands, jnp.concatenate(pairs[b : b + 2], axis=1), preferred_element_type=F32)
            for h in range(2):
                part = both[:, h * width : (h + 1) * width]
                picked = part[:block]
                for g in range(1, groups):
                    picked = jnp.where(lane == g, part[g * block : (g + 1) * block], picked)
                out.append(picked)
        return jnp.concatenate(out, axis=0)

    conv = filtered(causal_ref, p_pairs)
    upstream = go_ref[...].astype(F32)
    mixed_ref[...] = (feats[0] * conv).astype(BF16)
    for ahead, out_ref in enumerate(mixed_refs):
        at = pl.multiple_of(wrapped(lax.axis_index("dp") + ahead, ndp) * (tokens // ndp), 16)
        out_ref[...] = mixed_ref[pl.ds(at, tokens // ndp)]
    grad_conv = (upstream * feats[0]).astype(BF16)
    c_blocks = [grad_conv[b * block : (b + 1) * block] for b in range(nspans)] + [zero]
    c_pairs = [jnp.concatenate(c_blocks[b : b + 2], axis=0) for b in range(nspans)]
    grad_product = filtered(anti_ref, c_pairs)

    corr = jnp.zeros((groups * block, span), F32)
    for b in range(0, nspans, 2):
        left = jnp.concatenate(c_blocks[b : b + 2], axis=1)
        stacked = jnp.concatenate(
            [jnp.where(lanes == g, left, jnp.zeros_like(left)) for g in range(groups)], axis=0
        )
        right = jnp.concatenate(p_pairs[b : b + 2], axis=1)
        corr += lax.dot_general(stacked, right, (((1,), (1,)), ((), ())), preferred_element_type=F32)
    turn = lax.broadcasted_iota(jnp.int32, (8, span), 0)
    sums = []
    for g in range(groups):
        part = corr[g * block : (g + 1) * block]
        count = block
        while count > 8:
            count //= 2
            part = part[:count] + pltpu.roll(part[count:], span - count, 1)
        for bit in (1, 2, 4):
            part = jnp.where((turn & bit) != 0, pltpu.roll(part, span - bit, 1), part)
        sums.append(jnp.sum(part, axis=0, keepdims=True))
    by_lag = jnp.concatenate(sums, axis=0)
    by_lag = (scale * pltpu.roll(by_lag, span - 1, 1)[:, :block]).astype(BF16)
    ahead = lax.broadcasted_iota(jnp.int32, (block, block), 0)
    back = lax.broadcasted_iota(jnp.int32, (block, block), 1)
    turned = jnp.where(ahead + back == block - 1, 1.0, 0.0).astype(BF16)
    by_lag = jnp.dot(by_lag, turned, preferred_element_type=F32)

    grad_feats = [upstream * conv, grad_product * feats[2], grad_product * feats[1]]
    short_rows = []
    for j in range(nshort):
        for i in range(3):
            short_rows.append(scale * jnp.sum(grad_feats[i] * past(i, j), axis=0, keepdims=True))
    for i in range(3):
        total = taps(0, i) * grad_feats[i]
        for j in range(1, nshort):
            total += taps(j, i) * advanced(grad_feats[i], j)
        gm_ref[i * tokens : (i + 1) * tokens] = total.astype(BF16)
    for chunk, place, at in places():
        (near_ref, other_ref)[chunk][place : place + rows] = gm_ref[pl.ds(at, rows)]
    tail = near_ref.shape[0] - 3 * tokens // 2 - groups - 3 * nshort
    small = jnp.concatenate([by_lag] + short_rows + [jnp.zeros((tail, width), F32)], axis=0)
    near_ref[3 * tokens // 2 :] = small.astype(BF16)


def sum_over_line(own, right, far, left):
    ndp = lax.axis_size("dp")
    from_left = lax.ppermute(far, "dp", [(a, a + 1) for a in range(ndp // 2)])
    from_right = lax.ppermute(far, "dp", [(a, a - 1) for a in range(ndp // 2, ndp)])
    rightward = lax.ppermute(right + from_left, "dp", [(a, (a + 1) % ndp) for a in range(ndp)])
    leftward = lax.ppermute(left + from_right, "dp", [(a, (a - 1) % ndp) for a in range(ndp)])
    return own, rightward, leftward


def gather_over_line(own, across):
    ndp, nrow = lax.axis_size("dp"), lax.axis_size("row")

    def shift(count):
        return [
            (a * nrow + r, (a + count) % ndp * nrow + (r + 1 - 2 * (r % 2) if across else r))
            for a in range(ndp)
            for r in range(nrow)
        ]

    before = lax.ppermute(own, ("dp", "row"), shift(1))
    after = lax.ppermute(own, ("dp", "row"), shift(-1))
    here = lax.ppermute(own, ("dp", "row"), shift(0)) if across else own
    far_before = lax.ppermute(before, "dp", [(a - 1, a) for a in range(ndp // 2, ndp)])
    far_after = lax.ppermute(after, "dp", [(a + 1, a) for a in range(ndp // 2)])
    return here, before, after, far_before, far_after


def move_activations(tokens, in_weight, short_filter, long_filter, grad_out):
    ndp, nrow, ncol = (lax.axis_size(a) for a in ("dp", "row", "col"))
    z = lax.axis_index("dp")
    rows, dcol = tokens.shape
    local = grad_out.shape[1]
    nshort = short_filter.shape[0]
    ngroups, ntaps = long_filter.shape
    seq = rows * ndp
    width, groups = local // ndp, ngroups // ndp
    drow = in_weight.shape[0]
    scale = float(seq) ** -0.5
    nblocks = nrow // 2
    chunk = nblocks * rows
    swap = [(tokens_of(b, nrow) * nrow + a, a * nrow + b) for a in range(ndp) for b in range(nrow)]
    swap_back = [(b, a) for a, b in swap]
    partner = [(a, a + 1 - 2 * (a % 2)) for a in range(nrow)]
    places = [(dy, dx) for dy in range(nblocks) for dx in range(ncol)]

    def offset(dy, dx):
        return [
            (a * ncol + b, (a + 2 * dy) % nrow * ncol + (b + dx) % ncol) for a in range(nrow) for b in range(ncol)
        ]

    w = jnp.transpose(in_weight, (1, 0, 2))
    moved = lax.ppermute(tokens, ("dp", "row"), swap)
    turn = [[(a, (a + ahead) % ndp) for a in range(ndp)] for ahead in range(ndp)]
    upstream = [*kernel_call(split_body, [shaped((rows, width), BF16)] * ndp)(grad_out)]
    upstream[2] = lax.ppermute(upstream[2], "dp", turn[2])
    moved, upstream = lax.optimization_barrier((moved, upstream))
    near = [moved] + [lax.ppermute(moved, ("row", "col"), offset(*p)) for p in places[1:]]
    for ahead in (1, 3):
        upstream[ahead] = lax.ppermute(upstream[ahead], "dp", turn[ahead])
    upstream[1::2], near[1:] = lax.optimization_barrier((upstream[1::2], near[1:]))
    x0 = jnp.stack(near).reshape(nblocks, ncol, rows, dcol)
    x1 = lax.ppermute(x0, "row", partner)

    sf = lax.dynamic_slice_in_dim(short_filter, z * width, width, 2).reshape(3 * nshort, width)
    lf = lax.dynamic_slice_in_dim(long_filter, z * groups, groups, 0).astype(F32)
    zeros = functools.partial(jnp.zeros, dtype=F32)
    bases = jnp.concatenate(
        [
            jnp.concatenate([zeros((groups, 1)), lf[:, ::-1], zeros((groups, ntaps - 1))], axis=1),
            jnp.concatenate([lf, zeros((groups, ntaps))], axis=1),
        ],
        axis=0,
    )
    bands = kernel_call(bands_body, shaped((2 * groups, ntaps, 2 * ntaps), BF16))(bases)

    mm_flops = seq * drow * 3 * local
    mm_bytes = seq * drow + 6 * drow * local + 3 * seq * local
    sums = []
    for x in (x0, x1):
        parts = kernel_call(
            project_body,
            [shaped((3, chunk, width), BF16)] * ndp,
            grid=(3,),
            in_specs=[
                pl.BlockSpec((nblocks, ncol, rows, dcol), lambda i: (0, 0, 0, 0)),
                pl.BlockSpec((1, drow, local), lambda i: (i, 0, 0)),
            ],
            out_specs=[pl.BlockSpec((1, chunk, width), lambda i: (i, 0, 0))] * ndp,
            scratch=[pltpu.VMEM((ndp, chunk, width), BF16)],
            flops=mm_flops,
            nbytes=mm_bytes,
        )(x, w)
        sums += sum_over_line(*(p.reshape(3 * chunk, width) for p in parts))

    extra = -(-(groups + 3 * nshort) // 16) * 16
    half = pl.BlockSpec((groups, ntaps, 2 * ntaps), lambda i: (0, 0, 0))
    other = pl.BlockSpec((groups, ntaps, 2 * ntaps), lambda i: (1, 0, 0))
    whole = lambda *shape: pl.BlockSpec(shape, lambda i: (0,) * len(shape))
    grad_near, grad_other, *mixed = kernel_call(
        functools.partial(middle_body, scale, nshort, nrow),
        [shaped((3 * chunk + extra, width), BF16), shaped((3 * chunk, width), BF16)]
        + [shaped((rows, width), BF16)] * ndp,
        grid=(1,),
        in_specs=[whole(3 * chunk, width)] * 6
        + [whole(3 * nshort, width), half, other]
        + [whole(rows, width)] * ndp,
        out_specs=[whole(3 * chunk + extra, width), whole(3 * chunk, width)] + [whole(rows, width)] * ndp,
        scratch=[
            pltpu.VMEM((3 * seq, width), F32),
            pltpu.VMEM((3 * seq, width), BF16),
            pltpu.VMEM((seq, width), BF16),
            pltpu.VMEM((seq, width), BF16),
        ],
        flops=3 * 2 * groups * ntaps * 2 * ntaps * width * (seq // ntaps),
        nbytes=2 * width * seq * 14,
        vmem=MOST_VMEM_BYTES,
    )(*sums, sf, bands, bands, *upstream)
    mixed = [mixed[0]] + [
        lax.ppermute(part, "dp", [(a, (a + ahead) % ndp) for a in range(ndp)])
        for ahead, part in enumerate(mixed)
        if ahead
    ]
    *near, near_far_before, near_far_after = gather_over_line(grad_near, False)
    *far, far_far_before, far_far_after = gather_over_line(grad_other, True)
    partner_w = lax.ppermute(w, "row", partner)
    part, far_three = kernel_call(
        first_grad_body,
        [shaped((ncol, chunk, dcol), F32), shaped((3, 3 * chunk, width), BF16)],
        scratch=[pltpu.VMEM((ndp, 3 * chunk, width), BF16)],
        flops=2 * mm_flops,
        nbytes=2 * mm_bytes,
    )(*near, *far, w, partner_w)
    everywhere = pl.BlockSpec(memory_space=pl.ANY)
    in_vmem = pl.BlockSpec(memory_space=pltpu.VMEM)
    near_last, far_last, *blocks = kernel_call(
        functools.partial(second_grad_body, ndp),
        [shaped(grad_near.shape, BF16), shaped(grad_other.shape, BF16)]
        + [shaped((rows, dcol), BF16)] * len(places),
        grid=(),
        in_specs=[everywhere] * 7,
        out_specs=[in_vmem] * (2 + len(places)),
        scratch=[
            pltpu.VMEM((2, 3, drow, width), BF16),
            pltpu.VMEM((ncol, chunk, dcol), F32),
            pltpu.SemaphoreType.DMA((5,)),
        ],
        flops=mm_flops // 2,
        nbytes=mm_bytes // 2,
        vmem=MOST_VMEM_BYTES,
    )(part, near_far_before, near_far_after, far_far_before, far_far_after, w, partner_w)
    far_three, far_last = lax.optimization_barrier((far_three, far_last))
    far_three, far_last = (lax.ppermute(part, "row", partner) for part in (far_three, far_last))
    arrivals = [
        lax.ppermute(sent, ("row", "col"), [(b, a) for a, b in offset(*p)])
        for p, sent in zip(places[1:], blocks[1:])
    ]
    arrived = sum((a.astype(F32) for a in arrivals), blocks[0].astype(F32)).astype(BF16)
    arrived, far_three, far_last, *mixed = lax.optimization_barrier((arrived, far_three, far_last, *mixed))
    grad_in = lax.ppermute(arrived, ("dp", "row"), swap_back)

    grad_weight, mixed, grad_long, grad_short = kernel_call(
        functools.partial(weight_grad_body, scale),
        [
            shaped((3, drow, local), F32),
            shaped((rows, local), BF16),
            shaped((ngroups, ntaps), F32),
            shaped((nshort, 3, local), F32),
        ],
        grid=(3,),
        in_specs=[whole(nblocks, ncol, rows, dcol)] * 2
        + [whole(*grad_near.shape)] * 4
        + [whole(*far_three.shape), whole(*far_last.shape)]
        + [whole(rows, width)] * ndp,
        out_specs=[
            pl.BlockSpec((1, drow, local), lambda i: (i, 0, 0)),
            whole(rows, local),
            whole(ngroups, ntaps),
            whole(nshort, 3, local),
        ],
        scratch=[
            pltpu.VMEM((2, ndp, 3 * chunk + extra, width), BF16),
            pltpu.VMEM((ndp, rows, width), BF16),
        ],
        flops=2 * mm_flops,
        nbytes=2 * mm_bytes,
        vmem=MOST_VMEM_BYTES,
    )(x0, x1, *near, near_last, far_three, far_last, *mixed)
    grad_weight = jnp.transpose(grad_weight, (1, 0, 2))
    return (mixed, grad_in, grad_weight, grad_long, grad_short)


def from_behind(block, axis, distance):
    devices = range(lax.axis_size(axis))
    route = [(i - distance, i) for i in devices if i - distance in devices]
    return lax.ppermute(block, axis, route)


def toeplitz(leading, rows, span):
    groups = leading.shape[0]
    width = rows + span
    seed_row = jnp.concatenate(
        [leading, jnp.zeros((groups, width - leading.shape[1]), leading.dtype)], axis=1
    )
    tiled = jnp.tile(seed_row, (1, rows))
    skewed = tiled[:, : rows * (width - 1)].reshape(groups, rows, width - 1)
    return skewed[:, :, :span]


def to_groups(values, ngroups, members):
    count = values.shape[0]
    return values.reshape(count, ngroups, members).transpose(1, 2, 0)


def from_groups(values):
    groups, members, count = values.shape
    return values.transpose(2, 0, 1).reshape(count, groups * members)


def move_weights(tokens, in_weight, short_filter, long_filter, grad_out):
    rows = tokens.shape[0]
    local = grad_out.shape[1]
    nshort = short_filter.shape[0]
    ntaps = long_filter.shape[1]
    ngroups = long_filter.shape[0]
    members = local // ngroups
    margin = ntaps - 1
    span = rows + margin
    scale = float(rows * lax.axis_size("dp")) ** (-0.5)
    whole = lax.all_gather(tokens, ("row", "col"), axis=1, tiled=True)
    full_w = lax.all_gather(in_weight, "dp", axis=0, tiled=True)
    mixed_in = jnp.einsum("sd,dic->sic", whole, full_w, preferred_element_type=jnp.float32).astype(
        jnp.bfloat16
    )
    before = from_behind(mixed_in[rows - margin - nshort + 1 :], "dp", 1)
    extended = jnp.concatenate([before, mixed_in], axis=0).astype(jnp.float32)
    long_feats = jnp.zeros((span, 3, local), jnp.float32)
    for j in range(nshort):
        long_feats = (
            long_feats + short_filter[j][None] * extended[nshort - 1 - j : nshort - 1 - j + span]
        )
    product_ext = (long_feats[:, 1] * long_feats[:, 2]).astype(jnp.bfloat16)
    feats = long_feats[margin:]
    short_rows = extended[margin:]
    product_cols = to_groups(product_ext, ngroups, members)
    causal = toeplitz(long_filter[:, ::-1], rows, span)
    conv = from_groups(
        jnp.einsum("gst,gct->gcs", causal, product_cols, preferred_element_type=jnp.float32)
    )
    mixed = (feats[:, 0] * conv).astype(jnp.bfloat16)
    upstream = grad_out.astype(jnp.float32)
    grad_query = upstream * conv
    grad_conv = (upstream * feats[:, 0]).astype(jnp.bfloat16)
    after = from_behind(grad_conv[:margin], "dp", -1)
    grad_ext = jnp.concatenate([grad_conv, after], axis=0)
    anti = toeplitz(long_filter, rows, span)
    grad_product = from_groups(
        jnp.einsum(
            "gst,gct->gcs",
            anti,
            to_groups(grad_ext, ngroups, members),
            preferred_element_type=jnp.float32,
        )
    )
    reversed_cols = jnp.concatenate(
        [product_cols[:, :, ::-1], jnp.zeros((ngroups, members, rows), product_cols.dtype)], axis=2
    )
    width = span + rows
    pairs = jnp.einsum(
        "gcs,gcu->gsu",
        to_groups(grad_conv, ngroups, members),
        reversed_cols,
        preferred_element_type=jnp.float32,
    )
    diagonal = pairs.reshape(ngroups, rows * width)[:, : rows * (width - 1)].reshape(
        ngroups, rows, width - 1
    )
    filter_part = jnp.sum(diagonal[:, :, rows - 1 : rows - 1 + ntaps], axis=1)
    grad_feats = jnp.stack(
        [grad_query, grad_product * feats[:, 2], grad_product * feats[:, 1]], axis=1
    )
    later = from_behind(grad_feats[: nshort - 1], "dp", -1)
    feats_ext = jnp.concatenate([grad_feats, later], axis=0)
    grad_acc = jnp.zeros((rows, 3, local), jnp.float32)
    for j in range(nshort):
        grad_acc = grad_acc + short_filter[j][None] * feats_ext[j : j + rows]
    grad_mixed = grad_acc.astype(jnp.bfloat16)
    short_part = jnp.stack(
        [
            jnp.sum(grad_feats * short_rows[nshort - 1 - j : nshort - 1 - j + rows], axis=0)
            for j in range(nshort)
        ]
    )
    filter_total, short_total = (
        lax.psum(filter_part.astype(jnp.bfloat16), "dp").astype(jnp.float32),
        lax.psum(short_part.astype(jnp.bfloat16), "dp").astype(jnp.float32),
    )
    grad_long = filter_total * scale
    grad_short = short_total * scale
    partial_in = jnp.einsum("sic,dic->sd", grad_mixed, full_w, preferred_element_type=jnp.float32)
    summed_in = lax.psum_scatter(
        partial_in.astype(jnp.bfloat16), ("row", "col"), scatter_dimension=1, tiled=True
    )
    weight_term = (
        jnp.einsum("sd,sic->dic", whole, grad_mixed, preferred_element_type=jnp.float32) * scale
    )
    grad_weight = lax.psum_scatter(
        weight_term.astype(jnp.bfloat16), "dp", scatter_dimension=0, tiled=True
    ).astype(jnp.float32)
    return (mixed, summed_in, grad_weight, grad_long, grad_short)


def fits_whole_sequences(mesh, tokens, in_weight, short_filter, long_filter, grad_out):
    ndp, nrow, ncol = (mesh.shape[a] for a in ("dp", "row", "col"))
    seq, channels = grad_out.shape
    groups, ntaps = long_filter.shape
    local = channels // (nrow * ncol)
    width, rows = local // ndp, seq // ndp
    return (
        seq < tokens.shape[1]
        and ndp == nrow == 4
        and ncol * (tokens.shape[1] // (nrow * ncol)) == in_weight.shape[0] // ndp
        and ntaps == width == 128
        and seq % (2 * ntaps) == 0
        and rows % 16 == 0
        and groups % (8 * ndp * nrow * ncol) == 0
    )


def solution(mesh):
    placed = (
        P("dp", ("row", "col")),
        P("dp", None, ("row", "col")),
        P(None, None, ("row", "col")),
        P(("row", "col"), None),
        P("dp", ("row", "col")),
    )
    gives = (
        P("dp", ("row", "col")),
        P("dp", ("row", "col")),
        P("dp", None, ("row", "col")),
        P(("row", "col"), None),
        P(None, None, ("row", "col")),
    )

    def run(*arrays):
        plan = move_activations if fits_whole_sequences(mesh, *arrays) else move_weights
        return jax.shard_map(
            plan, mesh=mesh, in_specs=placed, out_specs=gives, check_vma=False
        )(*arrays)

    return run
```

```python
import functools

import jax
import jax.numpy as jnp
from jax import lax
from jax.experimental import pallas as pl
from jax.experimental.pallas import tpu as pltpu
from jax.sharding import PartitionSpec as P

VMEM_BYTES = 48 * 2**20
MOST_VMEM_BYTES = 62 * 2**20
F32 = jnp.float32
BF16 = jnp.bfloat16


def kernel_call(body, outs, grid=(), in_specs=None, out_specs=None, scratch=(), flops=0, nbytes=0, vmem=VMEM_BYTES):
    kwargs = {}
    if in_specs is not None:
        kwargs = dict(grid=grid, in_specs=in_specs, out_specs=out_specs)
    return pl.pallas_call(
        body,
        out_shape=outs,
        scratch_shapes=scratch,
        compiler_params=pltpu.CompilerParams(vmem_limit_bytes=vmem),
        cost_estimate=pl.CostEstimate(flops=flops, bytes_accessed=nbytes, transcendentals=0),
        **kwargs,
    )


def shaped(shape, dtype):
    return jax.ShapeDtypeStruct(shape, dtype)


def bands_body(base_ref, out_ref):
    groups, wide = base_ref.shape
    rows = out_ref.shape[1]
    row = lax.broadcasted_iota(jnp.int32, (8, wide), 0)
    for g in range(groups):
        band = jnp.broadcast_to(base_ref[g : g + 1, :], (8, wide))
        for bit in (1, 2, 4):
            band = jnp.where((row & bit) != 0, pltpu.roll(band, bit, 1), band)
        count = 8
        while count < rows:
            band = jnp.concatenate([band, pltpu.roll(band, count, 1)], axis=0)
            count *= 2
        out_ref[g] = band.astype(out_ref.dtype)


def tokens_of(row, nrow):
    return row % 2 * (nrow // 2) + row // 2


def wrapped(value, size):
    return lax.rem(value + 2 * size, size)


def split_body(all_ref, *out_refs):
    width = out_refs[0].shape[1]
    for ahead, out_ref in enumerate(out_refs):
        at = wrapped(lax.axis_index("dp") + ahead, len(out_refs)) * width
        out_ref[...] = all_ref[:, pl.ds(pl.multiple_of(at, width), width)]


def project_body(x_ref, w_ref, *refs):
    *out_refs, held = refs
    z, col = lax.axis_index("dp"), lax.axis_index("col")
    nblocks, ncol, rows, depth = x_ref.shape
    width = held.shape[2]
    total = jnp.zeros((nblocks * rows, w_ref.shape[2]), F32)
    for dx in range(ncol):
        start = pl.multiple_of(wrapped(col - dx, ncol) * depth, depth)
        total += jnp.dot(
            x_ref[:, dx].reshape(nblocks * rows, depth),
            w_ref[0, pl.ds(start, depth), :],
            preferred_element_type=F32,
        )
    for owner in range(len(out_refs)):
        held[owner] = total[:, owner * width : (owner + 1) * width].astype(BF16)
    for ahead, out_ref in enumerate(out_refs):
        out_ref[0] = held[wrapped(z + ahead, len(out_refs))]


def first_grad_body(near, near_before, near_after, far, far_before, far_after, w_ref, partner_w_ref, out_ref, far_ref, held):
    ndp, _, width = held.shape
    ncol, tokens, depth = out_ref.shape
    z, col = lax.axis_index("dp"), lax.axis_index("col")
    far_ref[0], far_ref[1], far_ref[2] = far[...], far_before[...], far_after[...]
    for pieces, weights, first in (
        ((near, near_before, near_after), w_ref, True),
        ((far, far_before, far_after), partner_w_ref, False),
    ):
        held[wrapped(z + ndp // 2, ndp)] = jnp.zeros(held.shape[1:], BF16)
        for ahead, piece in zip((0, -1, 1), pieces):
            held[wrapped(z + ahead, ndp)] = piece[: 3 * tokens]
        for dx in range(ncol):
            start = pl.multiple_of(wrapped(col - dx, ncol) * depth, depth)
            total = jnp.zeros((tokens, depth), F32) if first else out_ref[dx]
            for i in range(3):
                rows = slice(i * tokens, (i + 1) * tokens)
                total += lax.dot_general(
                    jnp.concatenate([held[owner, rows] for owner in range(ndp)], axis=1),
                    weights[i, pl.ds(start, depth), :],
                    (((1,), (1,)), ((), ())),
                    preferred_element_type=F32,
                )
            out_ref[dx] = total


def second_grad_body(ndp, part_ref, *refs):
    arrived, weights, refs = (refs[:2], refs[2:4]), refs[4:6], refs[6:]
    (near_ref, far_ref), refs = refs[:2], refs[2:]
    *out_refs, held_w, held_part, sems = refs
    ncol, tokens, depth = held_part.shape
    rows = out_refs[0].shape[0]
    width = near_ref.shape[1]
    z, col = lax.axis_index("dp"), lax.axis_index("col")
    lanes = pl.ds(pl.multiple_of(wrapped(z + ndp // 2, ndp) * width, width), width)
    copies = [
        pltpu.make_async_copy(w_ref.at[:, :, lanes], held_w.at[k], sems.at[k]) for k, w_ref in enumerate(weights)
    ]
    copies.append(pltpu.make_async_copy(part_ref, held_part, sems.at[2]))
    for copy in copies:
        copy.start()
    for k, (pair, target) in enumerate(zip(arrived, (near_ref, far_ref))):
        for source, here in zip(pair, (z >= ndp // 2, z < ndp // 2)):

            @pl.when(here)
            def _(source=source, target=target, k=k):
                copy = pltpu.make_async_copy(source, target, sems.at[3 + k])
                copy.start()
                copy.wait()

    for copy in copies:
        copy.wait()
    left = jnp.concatenate(
        [ref[i * tokens : (i + 1) * tokens] for ref in (near_ref, far_ref) for i in range(3)], axis=1
    )
    for dx in range(ncol):
        start = pl.multiple_of(wrapped(col - dx, ncol) * depth, depth)
        right = jnp.concatenate([held_w[k, i, pl.ds(start, depth), :] for k in range(2) for i in range(3)], axis=1)
        total = held_part[dx] + lax.dot_general(
            left, right, (((1,), (1,)), ((), ())), preferred_element_type=F32
        )
        for block in range(tokens // rows):
            out_refs[block * ncol + dx][...] = total[block * rows : (block + 1) * rows].astype(BF16)


def weight_grad_body(scale, *refs):
    (x0_ref, x1_ref), near_refs, (far_ref, far_last_ref), mixed_refs, refs = (
        refs[:2],
        refs[2:6],
        refs[6:8],
        refs[8:12],
        refs[12:],
    )
    out_ref, mixed_ref, long_ref, short_ref, held, held_mixed = refs
    nblocks, ncol, rows, depth = x0_ref.shape
    _, ndp, _, width = held.shape
    tokens = nblocks * rows
    i = pl.program_id(0)
    z, col = lax.axis_index("dp"), lax.axis_index("col")

    @pl.when(i == 0)
    def _():
        groups = long_ref.shape[0] // ndp
        for k, ahead in enumerate((0, -1, 1, 2)):
            owner = wrapped(z + ahead, ndp)
            held[0, owner] = near_refs[k][...]
            held[1, owner, : 3 * tokens] = far_ref[k] if k < 3 else far_last_ref[...]
        for back in range(ndp):
            held_mixed[wrapped(z - back, ndp)] = mixed_refs[back][...]
        for owner in range(ndp):
            lanes = slice(owner * width, (owner + 1) * width)
            mixed_ref[:, lanes] = held_mixed[owner]
            small = held[0, owner, 3 * tokens :].astype(F32)
            long_ref[owner * groups : (owner + 1) * groups] = small[:groups]
            nshort, three, _ = short_ref.shape
            for j in range(nshort):
                short_ref[j, :, lanes] = small[groups + three * j : groups + three * (j + 1)]

    at = pl.ds(pl.multiple_of(i * tokens, 16), tokens)
    gm = jnp.concatenate(
        [jnp.concatenate([held[k, owner, at, :] for owner in range(ndp)], axis=1) for k in range(2)], axis=0
    )
    for dx in range(ncol):
        start = pl.multiple_of(wrapped(col - dx, ncol) * depth, depth)
        x = jnp.concatenate(
            [x_ref[:, dx].reshape(tokens, depth) for x_ref in (x0_ref, x1_ref)], axis=0
        )
        out_ref[0, pl.ds(start, depth), :] = scale * lax.dot_general(
            x, gm, (((0,), (0,)), ((), ())), preferred_element_type=F32
        )


def delayed(values, count):
    row = lax.broadcasted_iota(jnp.int32, values.shape, 0)
    return jnp.where(row >= count, pltpu.roll(values, count, 0), 0.0)


def advanced(values, count):
    rows = values.shape[0]
    row = lax.broadcasted_iota(jnp.int32, values.shape, 0)
    return jnp.where(row < rows - count, pltpu.roll(values, rows - count, 0), 0.0)


def middle_body(scale, nshort, nrow, *refs):
    sums, refs = (refs[:3], refs[3:6]), refs[6:]
    (sf_ref, causal_ref, anti_ref), refs = refs[:3], refs[3:]
    *refs, m_ref, gm_ref, mixed_ref, go_ref = refs
    ndp = len(refs) // 2 - 1
    go_refs, (near_ref, other_ref), mixed_refs = refs[:ndp], refs[ndp : ndp + 2], refs[ndp + 2 :]
    tokens, width = go_ref.shape
    for behind, piece in enumerate(go_refs):
        at = wrapped(lax.axis_index("dp") - behind, ndp) * (tokens // ndp)
        go_ref[pl.ds(pl.multiple_of(at, 16), tokens // ndp)] = piece[...]
    row = lax.axis_index("row")
    nblocks = nrow // 2
    rows = tokens // nrow

    def places():
        for chunk, start in enumerate((row, row + 1 - 2 * lax.rem(row, 2))):
            for block in range(nblocks):
                at = tokens_of(wrapped(start - 2 * block, nrow), nrow) * rows
                for i in range(3):
                    yield chunk, (i * nblocks + block) * rows, pl.multiple_of(i * tokens + at, 16)

    for chunk, place, at in places():
        held = [ref[place : place + rows].astype(F32) for ref in sums[chunk]]
        m_ref[pl.ds(at, rows)] = held[0] + held[1] + held[2]
    groups, block, span = causal_ref.shape
    members = width // groups
    nspans = tokens // block
    lane = lax.broadcasted_iota(jnp.int32, (block, width), 1) // members
    lanes = lax.broadcasted_iota(jnp.int32, (block, 2 * width), 1) % width // members

    def past(i, j):
        held = m_ref[i * tokens : (i + 1) * tokens]
        return held if j == 0 else delayed(held, j)

    def taps(j, i):
        return sf_ref[3 * j + i : 3 * j + i + 1, :]

    feats = [sum(taps(j, i) * past(i, j) for j in range(nshort)) for i in range(3)]
    product = (feats[1] * feats[2]).astype(BF16)
    zero = jnp.zeros((block, width), BF16)
    p_blocks = [zero] + [product[b * block : (b + 1) * block] for b in range(nspans)]
    p_pairs = [jnp.concatenate(p_blocks[b : b + 2], axis=0) for b in range(nspans)]

    def filtered(band_ref, pairs):
        bands = band_ref[...].reshape(groups * block, span)
        out = []
        for b in range(0, nspans, 2):
            both = jnp.dot(bands, jnp.concatenate(pairs[b : b + 2], axis=1), preferred_element_type=F32)
            for h in range(2):
                part = both[:, h * width : (h + 1) * width]
                picked = part[:block]
                for g in range(1, groups):
                    picked = jnp.where(lane == g, part[g * block : (g + 1) * block], picked)
                out.append(picked)
        return jnp.concatenate(out, axis=0)

    conv = filtered(causal_ref, p_pairs)
    upstream = go_ref[...].astype(F32)
    mixed_ref[...] = (feats[0] * conv).astype(BF16)
    for ahead, out_ref in enumerate(mixed_refs):
        at = pl.multiple_of(wrapped(lax.axis_index("dp") + ahead, ndp) * (tokens // ndp), 16)
        out_ref[...] = mixed_ref[pl.ds(at, tokens // ndp)]
    grad_conv = (upstream * feats[0]).astype(BF16)
    c_blocks = [grad_conv[b * block : (b + 1) * block] for b in range(nspans)] + [zero]
    c_pairs = [jnp.concatenate(c_blocks[b : b + 2], axis=0) for b in range(nspans)]
    grad_product = filtered(anti_ref, c_pairs)

    corr = jnp.zeros((groups * block, span), F32)
    for b in range(0, nspans, 2):
        left = jnp.concatenate(c_blocks[b : b + 2], axis=1)
        stacked = jnp.concatenate(
            [jnp.where(lanes == g, left, jnp.zeros_like(left)) for g in range(groups)], axis=0
        )
        right = jnp.concatenate(p_pairs[b : b + 2], axis=1)
        corr += lax.dot_general(stacked, right, (((1,), (1,)), ((), ())), preferred_element_type=F32)
    turn = lax.broadcasted_iota(jnp.int32, (8, span), 0)
    sums = []
    for g in range(groups):
        part = corr[g * block : (g + 1) * block]
        count = block
        while count > 8:
            count //= 2
            part = part[:count] + pltpu.roll(part[count:], span - count, 1)
        for bit in (1, 2, 4):
            part = jnp.where((turn & bit) != 0, pltpu.roll(part, span - bit, 1), part)
        sums.append(jnp.sum(part, axis=0, keepdims=True))
    by_lag = jnp.concatenate(sums, axis=0)
    by_lag = (scale * pltpu.roll(by_lag, span - 1, 1)[:, :block]).astype(BF16)
    ahead = lax.broadcasted_iota(jnp.int32, (block, block), 0)
    back = lax.broadcasted_iota(jnp.int32, (block, block), 1)
    turned = jnp.where(ahead + back == block - 1, 1.0, 0.0).astype(BF16)
    by_lag = jnp.dot(by_lag, turned, preferred_element_type=F32)

    grad_feats = [upstream * conv, grad_product * feats[2], grad_product * feats[1]]
    short_rows = []
    for j in range(nshort):
        for i in range(3):
            short_rows.append(scale * jnp.sum(grad_feats[i] * past(i, j), axis=0, keepdims=True))
    for i in range(3):
        total = taps(0, i) * grad_feats[i]
        for j in range(1, nshort):
            total += taps(j, i) * advanced(grad_feats[i], j)
        gm_ref[i * tokens : (i + 1) * tokens] = total.astype(BF16)
    for chunk, place, at in places():
        (near_ref, other_ref)[chunk][place : place + rows] = gm_ref[pl.ds(at, rows)]
    tail = near_ref.shape[0] - 3 * tokens // 2 - groups - 3 * nshort
    small = jnp.concatenate([by_lag] + short_rows + [jnp.zeros((tail, width), F32)], axis=0)
    near_ref[3 * tokens // 2 :] = small.astype(BF16)


def sum_over_line(own, right, far, left):
    ndp = lax.axis_size("dp")
    from_left = lax.ppermute(far, "dp", [(a, a + 1) for a in range(ndp // 2)])
    from_right = lax.ppermute(far, "dp", [(a, a - 1) for a in range(ndp // 2, ndp)])
    rightward = lax.ppermute(right + from_left, "dp", [(a, (a + 1) % ndp) for a in range(ndp)])
    leftward = lax.ppermute(left + from_right, "dp", [(a, (a - 1) % ndp) for a in range(ndp)])
    return own, rightward, leftward


def gather_over_line(own, across):
    ndp, nrow = lax.axis_size("dp"), lax.axis_size("row")

    def shift(count):
        return [
            (a * nrow + r, (a + count) % ndp * nrow + (r + 1 - 2 * (r % 2) if across else r))
            for a in range(ndp)
            for r in range(nrow)
        ]

    before = lax.ppermute(own, ("dp", "row"), shift(1))
    after = lax.ppermute(own, ("dp", "row"), shift(-1))
    here = lax.ppermute(own, ("dp", "row"), shift(0)) if across else own
    far_before = lax.ppermute(before, "dp", [(a - 1, a) for a in range(ndp // 2, ndp)])
    far_after = lax.ppermute(after, "dp", [(a + 1, a) for a in range(ndp // 2)])
    return here, before, after, far_before, far_after


def move_activations(tokens, in_weight, short_filter, long_filter, grad_out):
    ndp, nrow, ncol = (lax.axis_size(a) for a in ("dp", "row", "col"))
    z = lax.axis_index("dp")
    rows, dcol = tokens.shape
    local = grad_out.shape[1]
    nshort = short_filter.shape[0]
    ngroups, ntaps = long_filter.shape
    seq = rows * ndp
    width, groups = local // ndp, ngroups // ndp
    drow = in_weight.shape[0]
    scale = float(seq) ** -0.5
    nblocks = nrow // 2
    chunk = nblocks * rows
    swap = [(tokens_of(b, nrow) * nrow + a, a * nrow + b) for a in range(ndp) for b in range(nrow)]
    swap_back = [(b, a) for a, b in swap]
    partner = [(a, a + 1 - 2 * (a % 2)) for a in range(nrow)]
    places = [(dy, dx) for dy in range(nblocks) for dx in range(ncol)]

    def offset(dy, dx):
        return [
            (a * ncol + b, (a + 2 * dy) % nrow * ncol + (b + dx) % ncol) for a in range(nrow) for b in range(ncol)
        ]

    w = jnp.transpose(in_weight, (1, 0, 2))
    moved = lax.ppermute(tokens, ("dp", "row"), swap)
    turn = [[(a, (a + ahead) % ndp) for a in range(ndp)] for ahead in range(ndp)]
    upstream = [*kernel_call(split_body, [shaped((rows, width), BF16)] * ndp)(grad_out)]
    moved, upstream = lax.optimization_barrier((moved, upstream))
    near = [moved] + [lax.ppermute(moved, ("row", "col"), offset(*p)) for p in places[1:]]
    for ahead in (1, 3):
        upstream[ahead] = lax.ppermute(upstream[ahead], "dp", turn[ahead])
    upstream[1::2], near[1:] = lax.optimization_barrier((upstream[1::2], near[1:]))
    x0 = jnp.stack(near).reshape(nblocks, ncol, rows, dcol)
    x1 = lax.ppermute(x0, "row", partner)
    upstream[2] = lax.ppermute(upstream[2], "dp", turn[2])
    upstream[2], x1 = lax.optimization_barrier((upstream[2], x1))

    sf = lax.dynamic_slice_in_dim(short_filter, z * width, width, 2).reshape(3 * nshort, width)
    lf = lax.dynamic_slice_in_dim(long_filter, z * groups, groups, 0).astype(F32)
    zeros = functools.partial(jnp.zeros, dtype=F32)
    bases = jnp.concatenate(
        [
            jnp.concatenate([zeros((groups, 1)), lf[:, ::-1], zeros((groups, ntaps - 1))], axis=1),
            jnp.concatenate([lf, zeros((groups, ntaps))], axis=1),
        ],
        axis=0,
    )
    bands = kernel_call(bands_body, shaped((2 * groups, ntaps, 2 * ntaps), BF16))(bases)

    mm_flops = seq * drow * 3 * local
    mm_bytes = seq * drow + 6 * drow * local + 3 * seq * local
    sums = []
    for x in (x0, x1):
        parts = kernel_call(
            project_body,
            [shaped((3, chunk, width), BF16)] * ndp,
            grid=(3,),
            in_specs=[
                pl.BlockSpec((nblocks, ncol, rows, dcol), lambda i: (0, 0, 0, 0)),
                pl.BlockSpec((1, drow, local), lambda i: (i, 0, 0)),
            ],
            out_specs=[pl.BlockSpec((1, chunk, width), lambda i: (i, 0, 0))] * ndp,
            scratch=[pltpu.VMEM((ndp, chunk, width), BF16)],
            flops=mm_flops,
            nbytes=mm_bytes,
        )(x, w)
        sums += sum_over_line(*(p.reshape(3 * chunk, width) for p in parts))

    extra = -(-(groups + 3 * nshort) // 16) * 16
    half = pl.BlockSpec((groups, ntaps, 2 * ntaps), lambda i: (0, 0, 0))
    other = pl.BlockSpec((groups, ntaps, 2 * ntaps), lambda i: (1, 0, 0))
    whole = lambda *shape: pl.BlockSpec(shape, lambda i: (0,) * len(shape))
    grad_near, grad_other, *mixed = kernel_call(
        functools.partial(middle_body, scale, nshort, nrow),
        [shaped((3 * chunk + extra, width), BF16), shaped((3 * chunk, width), BF16)]
        + [shaped((rows, width), BF16)] * ndp,
        grid=(1,),
        in_specs=[whole(3 * chunk, width)] * 6
        + [whole(3 * nshort, width), half, other]
        + [whole(rows, width)] * ndp,
        out_specs=[whole(3 * chunk + extra, width), whole(3 * chunk, width)] + [whole(rows, width)] * ndp,
        scratch=[
            pltpu.VMEM((3 * seq, width), F32),
            pltpu.VMEM((3 * seq, width), BF16),
            pltpu.VMEM((seq, width), BF16),
            pltpu.VMEM((seq, width), BF16),
        ],
        flops=3 * 2 * groups * ntaps * 2 * ntaps * width * (seq // ntaps),
        nbytes=2 * width * seq * 14,
        vmem=MOST_VMEM_BYTES,
    )(*sums, sf, bands, bands, *upstream)
    mixed = [mixed[0]] + [
        lax.ppermute(part, "dp", [(a, (a + ahead) % ndp) for a in range(ndp)])
        for ahead, part in enumerate(mixed)
        if ahead
    ]
    *near, near_far_before, near_far_after = gather_over_line(grad_near, False)
    *far, far_far_before, far_far_after = gather_over_line(grad_other, True)
    partner_w = lax.ppermute(w, "row", partner)
    part, far_three = kernel_call(
        first_grad_body,
        [shaped((ncol, chunk, dcol), F32), shaped((3, 3 * chunk, width), BF16)],
        scratch=[pltpu.VMEM((ndp, 3 * chunk, width), BF16)],
        flops=2 * mm_flops,
        nbytes=2 * mm_bytes,
    )(*near, *far, w, partner_w)
    everywhere = pl.BlockSpec(memory_space=pl.ANY)
    in_vmem = pl.BlockSpec(memory_space=pltpu.VMEM)
    near_last, far_last, *blocks = kernel_call(
        functools.partial(second_grad_body, ndp),
        [shaped(grad_near.shape, BF16), shaped(grad_other.shape, BF16)]
        + [shaped((rows, dcol), BF16)] * len(places),
        grid=(),
        in_specs=[everywhere] * 7,
        out_specs=[in_vmem] * (2 + len(places)),
        scratch=[
            pltpu.VMEM((2, 3, drow, width), BF16),
            pltpu.VMEM((ncol, chunk, dcol), F32),
            pltpu.SemaphoreType.DMA((5,)),
        ],
        flops=mm_flops // 2,
        nbytes=mm_bytes // 2,
        vmem=MOST_VMEM_BYTES,
    )(part, near_far_before, near_far_after, far_far_before, far_far_after, w, partner_w)
    far_three, far_last, mixed[1:] = lax.optimization_barrier((far_three, far_last, mixed[1:]))
    far_three, far_last = (lax.ppermute(part, "row", partner) for part in (far_three, far_last))
    arrivals = [
        lax.ppermute(sent, ("row", "col"), [(b, a) for a, b in offset(*p)])
        for p, sent in zip(places[1:], blocks[1:])
    ]
    arrived = sum((a.astype(F32) for a in arrivals), blocks[0].astype(F32)).astype(BF16)
    arrived, far_three, far_last = lax.optimization_barrier((arrived, far_three, far_last))
    grad_in = lax.ppermute(arrived, ("dp", "row"), swap_back)

    grad_weight, mixed, grad_long, grad_short = kernel_call(
        functools.partial(weight_grad_body, scale),
        [
            shaped((3, drow, local), F32),
            shaped((rows, local), BF16),
            shaped((ngroups, ntaps), F32),
            shaped((nshort, 3, local), F32),
        ],
        grid=(3,),
        in_specs=[whole(nblocks, ncol, rows, dcol)] * 2
        + [whole(*grad_near.shape)] * 4
        + [whole(*far_three.shape), whole(*far_last.shape)]
        + [whole(rows, width)] * ndp,
        out_specs=[
            pl.BlockSpec((1, drow, local), lambda i: (i, 0, 0)),
            whole(rows, local),
            whole(ngroups, ntaps),
            whole(nshort, 3, local),
        ],
        scratch=[
            pltpu.VMEM((2, ndp, 3 * chunk + extra, width), BF16),
            pltpu.VMEM((ndp, rows, width), BF16),
        ],
        flops=2 * mm_flops,
        nbytes=2 * mm_bytes,
        vmem=MOST_VMEM_BYTES,
    )(x0, x1, *near, near_last, far_three, far_last, *mixed)
    grad_weight = jnp.transpose(grad_weight, (1, 0, 2))
    return (mixed, grad_in, grad_weight, grad_long, grad_short)


def from_behind(block, axis, distance):
    devices = range(lax.axis_size(axis))
    route = [(i - distance, i) for i in devices if i - distance in devices]
    return lax.ppermute(block, axis, route)


def toeplitz(leading, rows, span):
    groups = leading.shape[0]
    width = rows + span
    seed_row = jnp.concatenate(
        [leading, jnp.zeros((groups, width - leading.shape[1]), leading.dtype)], axis=1
    )
    tiled = jnp.tile(seed_row, (1, rows))
    skewed = tiled[:, : rows * (width - 1)].reshape(groups, rows, width - 1)
    return skewed[:, :, :span]


def to_groups(values, ngroups, members):
    count = values.shape[0]
    return values.reshape(count, ngroups, members).transpose(1, 2, 0)


def from_groups(values):
    groups, members, count = values.shape
    return values.transpose(2, 0, 1).reshape(count, groups * members)


def move_weights(tokens, in_weight, short_filter, long_filter, grad_out):
    rows = tokens.shape[0]
    local = grad_out.shape[1]
    nshort = short_filter.shape[0]
    ntaps = long_filter.shape[1]
    ngroups = long_filter.shape[0]
    members = local // ngroups
    margin = ntaps - 1
    span = rows + margin
    scale = float(rows * lax.axis_size("dp")) ** (-0.5)
    whole = lax.all_gather(tokens, ("row", "col"), axis=1, tiled=True)
    full_w = lax.all_gather(in_weight, "dp", axis=0, tiled=True)
    mixed_in = jnp.einsum("sd,dic->sic", whole, full_w, preferred_element_type=jnp.float32).astype(
        jnp.bfloat16
    )
    before = from_behind(mixed_in[rows - margin - nshort + 1 :], "dp", 1)
    extended = jnp.concatenate([before, mixed_in], axis=0).astype(jnp.float32)
    long_feats = jnp.zeros((span, 3, local), jnp.float32)
    for j in range(nshort):
        long_feats = (
            long_feats + short_filter[j][None] * extended[nshort - 1 - j : nshort - 1 - j + span]
        )
    product_ext = (long_feats[:, 1] * long_feats[:, 2]).astype(jnp.bfloat16)
    feats = long_feats[margin:]
    short_rows = extended[margin:]
    product_cols = to_groups(product_ext, ngroups, members)
    causal = toeplitz(long_filter[:, ::-1], rows, span)
    conv = from_groups(
        jnp.einsum("gst,gct->gcs", causal, product_cols, preferred_element_type=jnp.float32)
    )
    mixed = (feats[:, 0] * conv).astype(jnp.bfloat16)
    upstream = grad_out.astype(jnp.float32)
    grad_query = upstream * conv
    grad_conv = (upstream * feats[:, 0]).astype(jnp.bfloat16)
    after = from_behind(grad_conv[:margin], "dp", -1)
    grad_ext = jnp.concatenate([grad_conv, after], axis=0)
    anti = toeplitz(long_filter, rows, span)
    grad_product = from_groups(
        jnp.einsum(
            "gst,gct->gcs",
            anti,
            to_groups(grad_ext, ngroups, members),
            preferred_element_type=jnp.float32,
        )
    )
    reversed_cols = jnp.concatenate(
        [product_cols[:, :, ::-1], jnp.zeros((ngroups, members, rows), product_cols.dtype)], axis=2
    )
    width = span + rows
    pairs = jnp.einsum(
        "gcs,gcu->gsu",
        to_groups(grad_conv, ngroups, members),
        reversed_cols,
        preferred_element_type=jnp.float32,
    )
    diagonal = pairs.reshape(ngroups, rows * width)[:, : rows * (width - 1)].reshape(
        ngroups, rows, width - 1
    )
    filter_part = jnp.sum(diagonal[:, :, rows - 1 : rows - 1 + ntaps], axis=1)
    grad_feats = jnp.stack(
        [grad_query, grad_product * feats[:, 2], grad_product * feats[:, 1]], axis=1
    )
    later = from_behind(grad_feats[: nshort - 1], "dp", -1)
    feats_ext = jnp.concatenate([grad_feats, later], axis=0)
    grad_acc = jnp.zeros((rows, 3, local), jnp.float32)
    for j in range(nshort):
        grad_acc = grad_acc + short_filter[j][None] * feats_ext[j : j + rows]
    grad_mixed = grad_acc.astype(jnp.bfloat16)
    short_part = jnp.stack(
        [
            jnp.sum(grad_feats * short_rows[nshort - 1 - j : nshort - 1 - j + rows], axis=0)
            for j in range(nshort)
        ]
    )
    filter_total, short_total = (
        lax.psum(filter_part.astype(jnp.bfloat16), "dp").astype(jnp.float32),
        lax.psum(short_part.astype(jnp.bfloat16), "dp").astype(jnp.float32),
    )
    grad_long = filter_total * scale
    grad_short = short_total * scale
    partial_in = jnp.einsum("sic,dic->sd", grad_mixed, full_w, preferred_element_type=jnp.float32)
    summed_in = lax.psum_scatter(
        partial_in.astype(jnp.bfloat16), ("row", "col"), scatter_dimension=1, tiled=True
    )
    weight_term = (
        jnp.einsum("sd,sic->dic", whole, grad_mixed, preferred_element_type=jnp.float32) * scale
    )
    grad_weight = lax.psum_scatter(
        weight_term.astype(jnp.bfloat16), "dp", scatter_dimension=0, tiled=True
    ).astype(jnp.float32)
    return (mixed, summed_in, grad_weight, grad_long, grad_short)


def fits_whole_sequences(mesh, tokens, in_weight, short_filter, long_filter, grad_out):
    ndp, nrow, ncol = (mesh.shape[a] for a in ("dp", "row", "col"))
    seq, channels = grad_out.shape
    groups, ntaps = long_filter.shape
    local = channels // (nrow * ncol)
    width, rows = local // ndp, seq // ndp
    return (
        seq < tokens.shape[1]
        and ndp == nrow == 4
        and ncol * (tokens.shape[1] // (nrow * ncol)) == in_weight.shape[0] // ndp
        and ntaps == width == 128
        and seq % (2 * ntaps) == 0
        and rows % 16 == 0
        and groups % (8 * ndp * nrow * ncol) == 0
    )


def solution(mesh):
    placed = (
        P("dp", ("row", "col")),
        P("dp", None, ("row", "col")),
        P(None, None, ("row", "col")),
        P(("row", "col"), None),
        P("dp", ("row", "col")),
    )
    gives = (
        P("dp", ("row", "col")),
        P("dp", ("row", "col")),
        P("dp", None, ("row", "col")),
        P(("row", "col"), None),
        P(None, None, ("row", "col")),
    )

    def run(*arrays):
        plan = move_activations if fits_whole_sequences(mesh, *arrays) else move_weights
        return jax.shard_map(
            plan, mesh=mesh, in_specs=placed, out_specs=gives, check_vma=False
        )(*arrays)

    return run
```

```python
import functools

import jax
import jax.numpy as jnp
from jax import lax
from jax.experimental import pallas as pl
from jax.experimental.pallas import tpu as pltpu
from jax.sharding import PartitionSpec as P

VMEM_BYTES = 48 * 2**20
MOST_VMEM_BYTES = 62 * 2**20
F32 = jnp.float32
BF16 = jnp.bfloat16


def kernel_call(body, outs, grid=(), in_specs=None, out_specs=None, scratch=(), flops=0, nbytes=0, vmem=VMEM_BYTES):
    kwargs = {}
    if in_specs is not None:
        kwargs = dict(grid=grid, in_specs=in_specs, out_specs=out_specs)
    return pl.pallas_call(
        body,
        out_shape=outs,
        scratch_shapes=scratch,
        compiler_params=pltpu.CompilerParams(vmem_limit_bytes=vmem),
        cost_estimate=pl.CostEstimate(flops=flops, bytes_accessed=nbytes, transcendentals=0),
        **kwargs,
    )


def shaped(shape, dtype):
    return jax.ShapeDtypeStruct(shape, dtype)


def bands_body(base_ref, out_ref):
    groups, wide = base_ref.shape
    rows = out_ref.shape[1]
    row = lax.broadcasted_iota(jnp.int32, (8, wide), 0)
    for g in range(groups):
        band = jnp.broadcast_to(base_ref[g : g + 1, :], (8, wide))
        for bit in (1, 2, 4):
            band = jnp.where((row & bit) != 0, pltpu.roll(band, bit, 1), band)
        count = 8
        while count < rows:
            band = jnp.concatenate([band, pltpu.roll(band, count, 1)], axis=0)
            count *= 2
        out_ref[g] = band.astype(out_ref.dtype)


def tokens_of(row, nrow):
    return row % 2 * (nrow // 2) + row // 2


def wrapped(value, size):
    return lax.rem(value + 2 * size, size)


def split_body(all_ref, *out_refs):
    width = out_refs[0].shape[1]
    for ahead, out_ref in enumerate(out_refs):
        at = wrapped(lax.axis_index("dp") + ahead, len(out_refs)) * width
        out_ref[...] = all_ref[:, pl.ds(pl.multiple_of(at, width), width)]


def project_body(x_ref, w_ref, *refs):
    *out_refs, held = refs
    z, col = lax.axis_index("dp"), lax.axis_index("col")
    nblocks, ncol, rows, depth = x_ref.shape
    width = held.shape[2]
    total = jnp.zeros((nblocks * rows, w_ref.shape[2]), F32)
    for dx in range(ncol):
        start = pl.multiple_of(wrapped(col - dx, ncol) * depth, depth)
        total += jnp.dot(
            x_ref[:, dx].reshape(nblocks * rows, depth),
            w_ref[0, pl.ds(start, depth), :],
            preferred_element_type=F32,
        )
    for owner in range(len(out_refs)):
        held[owner] = total[:, owner * width : (owner + 1) * width].astype(BF16)
    for ahead, out_ref in enumerate(out_refs):
        out_ref[0] = held[wrapped(z + ahead, len(out_refs))]


def first_grad_body(near, near_before, near_after, far, far_before, far_after, w_ref, partner_w_ref, out_ref, far_ref, held):
    ndp, _, width = held.shape
    ncol, tokens, depth = out_ref.shape
    z, col = lax.axis_index("dp"), lax.axis_index("col")
    far_ref[0], far_ref[1], far_ref[2] = far[...], far_before[...], far_after[...]
    for pieces, weights, first in (
        ((near, near_before, near_after), w_ref, True),
        ((far, far_before, far_after), partner_w_ref, False),
    ):
        held[wrapped(z + ndp // 2, ndp)] = jnp.zeros(held.shape[1:], BF16)
        for ahead, piece in zip((0, -1, 1), pieces):
            held[wrapped(z + ahead, ndp)] = piece[: 3 * tokens]
        for dx in range(ncol):
            start = pl.multiple_of(wrapped(col - dx, ncol) * depth, depth)
            total = jnp.zeros((tokens, depth), F32) if first else out_ref[dx]
            for i in range(3):
                rows = slice(i * tokens, (i + 1) * tokens)
                total += lax.dot_general(
                    jnp.concatenate([held[owner, rows] for owner in range(ndp)], axis=1),
                    weights[i, pl.ds(start, depth), :],
                    (((1,), (1,)), ((), ())),
                    preferred_element_type=F32,
                )
            out_ref[dx] = total


def second_grad_body(ndp, part_ref, *refs):
    arrived, weights, refs = (refs[:2], refs[2:4]), refs[4:6], refs[6:]
    (near_ref, far_ref), refs = refs[:2], refs[2:]
    *out_refs, held_w, held_part, sems = refs
    ncol, tokens, depth = held_part.shape
    rows = out_refs[0].shape[0]
    width = near_ref.shape[1]
    z, col = lax.axis_index("dp"), lax.axis_index("col")
    lanes = pl.ds(pl.multiple_of(wrapped(z + ndp // 2, ndp) * width, width), width)
    copies = [
        pltpu.make_async_copy(w_ref.at[:, :, lanes], held_w.at[k], sems.at[k]) for k, w_ref in enumerate(weights)
    ]
    copies.append(pltpu.make_async_copy(part_ref, held_part, sems.at[2]))
    for copy in copies:
        copy.start()
    for k, (pair, target) in enumerate(zip(arrived, (near_ref, far_ref))):
        for source, here in zip(pair, (z >= ndp // 2, z < ndp // 2)):

            @pl.when(here)
            def _(source=source, target=target, k=k):
                copy = pltpu.make_async_copy(source, target, sems.at[3 + k])
                copy.start()
                copy.wait()

    for copy in copies:
        copy.wait()
    left = jnp.concatenate(
        [ref[i * tokens : (i + 1) * tokens] for ref in (near_ref, far_ref) for i in range(3)], axis=1
    )
    for dx in range(ncol):
        start = pl.multiple_of(wrapped(col - dx, ncol) * depth, depth)
        right = jnp.concatenate([held_w[k, i, pl.ds(start, depth), :] for k in range(2) for i in range(3)], axis=1)
        total = held_part[dx] + lax.dot_general(
            left, right, (((1,), (1,)), ((), ())), preferred_element_type=F32
        )
        for block in range(tokens // rows):
            out_refs[block * ncol + dx][...] = total[block * rows : (block + 1) * rows].astype(BF16)


def weight_grad_body(scale, *refs):
    (x0_ref, x1_ref), near_refs, (far_ref, far_last_ref), mixed_refs, refs = (
        refs[:2],
        refs[2:6],
        refs[6:8],
        refs[8:12],
        refs[12:],
    )
    out_ref, mixed_ref, long_ref, short_ref, held, held_mixed = refs
    nblocks, ncol, rows, depth = x0_ref.shape
    _, ndp, _, width = held.shape
    tokens = nblocks * rows
    i = pl.program_id(0)
    z, col = lax.axis_index("dp"), lax.axis_index("col")

    @pl.when(i == 0)
    def _():
        groups = long_ref.shape[0] // ndp
        for k, ahead in enumerate((0, -1, 1, 2)):
            owner = wrapped(z + ahead, ndp)
            held[0, owner] = near_refs[k][...]
            held[1, owner, : 3 * tokens] = far_ref[k] if k < 3 else far_last_ref[...]
        for back in range(ndp):
            held_mixed[wrapped(z - back, ndp)] = mixed_refs[back][...]
        for owner in range(ndp):
            lanes = slice(owner * width, (owner + 1) * width)
            mixed_ref[:, lanes] = held_mixed[owner]
            small = held[0, owner, 3 * tokens :].astype(F32)
            long_ref[owner * groups : (owner + 1) * groups] = small[:groups]
            nshort, three, _ = short_ref.shape
            for j in range(nshort):
                short_ref[j, :, lanes] = small[groups + three * j : groups + three * (j + 1)]

    at = pl.ds(pl.multiple_of(i * tokens, 16), tokens)
    gm = jnp.concatenate(
        [jnp.concatenate([held[k, owner, at, :] for owner in range(ndp)], axis=1) for k in range(2)], axis=0
    )
    for dx in range(ncol):
        start = pl.multiple_of(wrapped(col - dx, ncol) * depth, depth)
        x = jnp.concatenate(
            [x_ref[:, dx].reshape(tokens, depth) for x_ref in (x0_ref, x1_ref)], axis=0
        )
        out_ref[0, pl.ds(start, depth), :] = scale * lax.dot_general(
            x, gm, (((0,), (0,)), ((), ())), preferred_element_type=F32
        )


def delayed(values, count):
    row = lax.broadcasted_iota(jnp.int32, values.shape, 0)
    return jnp.where(row >= count, pltpu.roll(values, count, 0), 0.0)


def advanced(values, count):
    rows = values.shape[0]
    row = lax.broadcasted_iota(jnp.int32, values.shape, 0)
    return jnp.where(row < rows - count, pltpu.roll(values, rows - count, 0), 0.0)


def middle_body(scale, nshort, nrow, *refs):
    sums, refs = (refs[:3], refs[3:6]), refs[6:]
    (sf_ref, causal_ref, anti_ref), refs = refs[:3], refs[3:]
    *refs, m_ref, gm_ref, mixed_ref, go_ref = refs
    ndp = len(refs) // 2 - 1
    go_refs, (near_ref, other_ref), mixed_refs = refs[:ndp], refs[ndp : ndp + 2], refs[ndp + 2 :]
    tokens, width = go_ref.shape
    for behind, piece in enumerate(go_refs):
        at = wrapped(lax.axis_index("dp") - behind, ndp) * (tokens // ndp)
        go_ref[pl.ds(pl.multiple_of(at, 16), tokens // ndp)] = piece[...]
    row = lax.axis_index("row")
    nblocks = nrow // 2
    rows = tokens // nrow

    def places():
        for chunk, start in enumerate((row, row + 1 - 2 * lax.rem(row, 2))):
            for block in range(nblocks):
                at = tokens_of(wrapped(start - 2 * block, nrow), nrow) * rows
                for i in range(3):
                    yield chunk, (i * nblocks + block) * rows, pl.multiple_of(i * tokens + at, 16)

    for chunk, place, at in places():
        held = [ref[place : place + rows].astype(F32) for ref in sums[chunk]]
        m_ref[pl.ds(at, rows)] = held[0] + held[1] + held[2]
    groups, block, span = causal_ref.shape
    members = width // groups
    nspans = tokens // block
    lane = lax.broadcasted_iota(jnp.int32, (block, width), 1) // members
    lanes = lax.broadcasted_iota(jnp.int32, (block, 2 * width), 1) % width // members

    def past(i, j):
        held = m_ref[i * tokens : (i + 1) * tokens]
        return held if j == 0 else delayed(held, j)

    def taps(j, i):
        return sf_ref[3 * j + i : 3 * j + i + 1, :]

    feats = [sum(taps(j, i) * past(i, j) for j in range(nshort)) for i in range(3)]
    product = (feats[1] * feats[2]).astype(BF16)
    zero = jnp.zeros((block, width), BF16)
    p_blocks = [zero] + [product[b * block : (b + 1) * block] for b in range(nspans)]
    p_pairs = [jnp.concatenate(p_blocks[b : b + 2], axis=0) for b in range(nspans)]

    def filtered(band_ref, pairs):
        bands = band_ref[...].reshape(groups * block, span)
        out = []
        for b in range(0, nspans, 2):
            both = jnp.dot(bands, jnp.concatenate(pairs[b : b + 2], axis=1), preferred_element_type=F32)
            for h in range(2):
                part = both[:, h * width : (h + 1) * width]
                picked = part[:block]
                for g in range(1, groups):
                    picked = jnp.where(lane == g, part[g * block : (g + 1) * block], picked)
                out.append(picked)
        return jnp.concatenate(out, axis=0)

    conv = filtered(causal_ref, p_pairs)
    upstream = go_ref[...].astype(F32)
    mixed_ref[...] = (feats[0] * conv).astype(BF16)
    for ahead, out_ref in enumerate(mixed_refs):
        at = pl.multiple_of(wrapped(lax.axis_index("dp") + ahead, ndp) * (tokens // ndp), 16)
        out_ref[...] = mixed_ref[pl.ds(at, tokens // ndp)]
    grad_conv = (upstream * feats[0]).astype(BF16)
    c_blocks = [grad_conv[b * block : (b + 1) * block] for b in range(nspans)] + [zero]
    c_pairs = [jnp.concatenate(c_blocks[b : b + 2], axis=0) for b in range(nspans)]
    grad_product = filtered(anti_ref, c_pairs)

    corr = jnp.zeros((groups * block, span), F32)
    for b in range(0, nspans, 2):
        left = jnp.concatenate(c_blocks[b : b + 2], axis=1)
        stacked = jnp.concatenate(
            [jnp.where(lanes == g, left, jnp.zeros_like(left)) for g in range(groups)], axis=0
        )
        right = jnp.concatenate(p_pairs[b : b + 2], axis=1)
        corr += lax.dot_general(stacked, right, (((1,), (1,)), ((), ())), preferred_element_type=F32)
    turn = lax.broadcasted_iota(jnp.int32, (8, span), 0)
    sums = []
    for g in range(groups):
        part = corr[g * block : (g + 1) * block]
        count = block
        while count > 8:
            count //= 2
            part = part[:count] + pltpu.roll(part[count:], span - count, 1)
        for bit in (1, 2, 4):
            part = jnp.where((turn & bit) != 0, pltpu.roll(part, span - bit, 1), part)
        sums.append(jnp.sum(part, axis=0, keepdims=True))
    by_lag = jnp.concatenate(sums, axis=0)
    by_lag = (scale * pltpu.roll(by_lag, span - 1, 1)[:, :block]).astype(BF16)
    ahead = lax.broadcasted_iota(jnp.int32, (block, block), 0)
    back = lax.broadcasted_iota(jnp.int32, (block, block), 1)
    turned = jnp.where(ahead + back == block - 1, 1.0, 0.0).astype(BF16)
    by_lag = jnp.dot(by_lag, turned, preferred_element_type=F32)

    grad_feats = [upstream * conv, grad_product * feats[2], grad_product * feats[1]]
    short_rows = []
    for j in range(nshort):
        for i in range(3):
            short_rows.append(scale * jnp.sum(grad_feats[i] * past(i, j), axis=0, keepdims=True))
    for i in range(3):
        total = taps(0, i) * grad_feats[i]
        for j in range(1, nshort):
            total += taps(j, i) * advanced(grad_feats[i], j)
        gm_ref[i * tokens : (i + 1) * tokens] = total.astype(BF16)
    for chunk, place, at in places():
        (near_ref, other_ref)[chunk][place : place + rows] = gm_ref[pl.ds(at, rows)]
    tail = near_ref.shape[0] - 3 * tokens // 2 - groups - 3 * nshort
    small = jnp.concatenate([by_lag] + short_rows + [jnp.zeros((tail, width), F32)], axis=0)
    near_ref[3 * tokens // 2 :] = small.astype(BF16)


def first_hop(far):
    ndp = lax.axis_size("dp")
    return (
        lax.ppermute(far, "dp", [(a, a + 1) for a in range(ndp // 2)]),
        lax.ppermute(far, "dp", [(a, a - 1) for a in range(ndp // 2, ndp)]),
    )


def second_hop(right, left, from_left, from_right):
    ndp = lax.axis_size("dp")
    rightward = lax.ppermute(right + from_left, "dp", [(a, (a + 1) % ndp) for a in range(ndp)])
    leftward = lax.ppermute(left + from_right, "dp", [(a, (a - 1) % ndp) for a in range(ndp)])
    return rightward, leftward


def gather_over_line(own, across):
    ndp, nrow = lax.axis_size("dp"), lax.axis_size("row")

    def shift(count):
        return [
            (a * nrow + r, (a + count) % ndp * nrow + (r + 1 - 2 * (r % 2) if across else r))
            for a in range(ndp)
            for r in range(nrow)
        ]

    before = lax.ppermute(own, ("dp", "row"), shift(1))
    after = lax.ppermute(own, ("dp", "row"), shift(-1))
    here = lax.ppermute(own, ("dp", "row"), shift(0)) if across else own
    far_before = lax.ppermute(before, "dp", [(a - 1, a) for a in range(ndp // 2, ndp)])
    far_after = lax.ppermute(after, "dp", [(a + 1, a) for a in range(ndp // 2)])
    return here, before, after, far_before, far_after


def move_activations(tokens, in_weight, short_filter, long_filter, grad_out):
    ndp, nrow, ncol = (lax.axis_size(a) for a in ("dp", "row", "col"))
    z = lax.axis_index("dp")
    rows, dcol = tokens.shape
    local = grad_out.shape[1]
    nshort = short_filter.shape[0]
    ngroups, ntaps = long_filter.shape
    seq = rows * ndp
    width, groups = local // ndp, ngroups // ndp
    drow = in_weight.shape[0]
    scale = float(seq) ** -0.5
    nblocks = nrow // 2
    chunk = nblocks * rows
    swap = [(tokens_of(b, nrow) * nrow + a, a * nrow + b) for a in range(ndp) for b in range(nrow)]
    swap_back = [(b, a) for a, b in swap]
    partner = [(a, a + 1 - 2 * (a % 2)) for a in range(nrow)]
    places = [(dy, dx) for dy in range(nblocks) for dx in range(ncol)]

    def offset(dy, dx):
        return [
            (a * ncol + b, (a + 2 * dy) % nrow * ncol + (b + dx) % ncol) for a in range(nrow) for b in range(ncol)
        ]

    w = jnp.transpose(in_weight, (1, 0, 2))
    moved = lax.ppermute(tokens, ("dp", "row"), swap)
    turn = [[(a, (a + ahead) % ndp) for a in range(ndp)] for ahead in range(ndp)]
    upstream = [*kernel_call(split_body, [shaped((rows, width), BF16)] * ndp)(grad_out)]
    upstream[1] = lax.ppermute(upstream[1], "dp", turn[1])
    moved, upstream = lax.optimization_barrier((moved, upstream))
    near = [moved] + [lax.ppermute(moved, ("row", "col"), offset(*p)) for p in places[1:]]
    upstream[3] = lax.ppermute(upstream[3], "dp", turn[3])
    partner_w = lax.ppermute(w, "row", partner)
    upstream[3], near[1:], partner_w = lax.optimization_barrier((upstream[3], near[1:], partner_w))
    x0 = jnp.stack(near).reshape(nblocks, ncol, rows, dcol)
    x1 = lax.ppermute(x0, "row", partner)

    sf = lax.dynamic_slice_in_dim(short_filter, z * width, width, 2).reshape(3 * nshort, width)
    lf = lax.dynamic_slice_in_dim(long_filter, z * groups, groups, 0).astype(F32)
    zeros = functools.partial(jnp.zeros, dtype=F32)
    bases = jnp.concatenate(
        [
            jnp.concatenate([zeros((groups, 1)), lf[:, ::-1], zeros((groups, ntaps - 1))], axis=1),
            jnp.concatenate([lf, zeros((groups, ntaps))], axis=1),
        ],
        axis=0,
    )
    bands = kernel_call(bands_body, shaped((2 * groups, ntaps, 2 * ntaps), BF16))(bases)

    mm_flops = seq * drow * 3 * local
    mm_bytes = seq * drow + 6 * drow * local + 3 * seq * local
    sums = []
    for x in (x0, x1):
        parts = kernel_call(
            project_body,
            [shaped((3, chunk, width), BF16)] * ndp,
            grid=(3,),
            in_specs=[
                pl.BlockSpec((nblocks, ncol, rows, dcol), lambda i: (0, 0, 0, 0)),
                pl.BlockSpec((1, drow, local), lambda i: (i, 0, 0)),
            ],
            out_specs=[pl.BlockSpec((1, chunk, width), lambda i: (i, 0, 0))] * ndp,
            scratch=[pltpu.VMEM((ndp, chunk, width), BF16)],
            flops=mm_flops,
            nbytes=mm_bytes,
        )(x, w)
        own, right, far, left = (p.reshape(3 * chunk, width) for p in parts)
        passed = first_hop(far)
        sums += [own, *second_hop(right, left, *passed)]
    passed, upstream[2] = lax.optimization_barrier((passed, upstream[2]))
    upstream[2] = lax.ppermute(upstream[2], "dp", turn[2])

    extra = -(-(groups + 3 * nshort) // 16) * 16
    half = pl.BlockSpec((groups, ntaps, 2 * ntaps), lambda i: (0, 0, 0))
    other = pl.BlockSpec((groups, ntaps, 2 * ntaps), lambda i: (1, 0, 0))
    whole = lambda *shape: pl.BlockSpec(shape, lambda i: (0,) * len(shape))
    grad_near, grad_other, *mixed = kernel_call(
        functools.partial(middle_body, scale, nshort, nrow),
        [shaped((3 * chunk + extra, width), BF16), shaped((3 * chunk, width), BF16)]
        + [shaped((rows, width), BF16)] * ndp,
        grid=(1,),
        in_specs=[whole(3 * chunk, width)] * 6
        + [whole(3 * nshort, width), half, other]
        + [whole(rows, width)] * ndp,
        out_specs=[whole(3 * chunk + extra, width), whole(3 * chunk, width)] + [whole(rows, width)] * ndp,
        scratch=[
            pltpu.VMEM((3 * seq, width), F32),
            pltpu.VMEM((3 * seq, width), BF16),
            pltpu.VMEM((seq, width), BF16),
            pltpu.VMEM((seq, width), BF16),
        ],
        flops=3 * 2 * groups * ntaps * 2 * ntaps * width * (seq // ntaps),
        nbytes=2 * width * seq * 14,
        vmem=MOST_VMEM_BYTES,
    )(*sums, sf, bands, bands, *upstream)
    *near, near_far_before, near_far_after = gather_over_line(grad_near, False)
    *far, far_far_before, far_far_after = gather_over_line(grad_other, True)
    part, far_three = kernel_call(
        first_grad_body,
        [shaped((ncol, chunk, dcol), F32), shaped((3, 3 * chunk, width), BF16)],
        scratch=[pltpu.VMEM((ndp, 3 * chunk, width), BF16)],
        flops=2 * mm_flops,
        nbytes=2 * mm_bytes,
    )(*near, *far, w, partner_w)
    part, mixed = lax.optimization_barrier((part, mixed))
    for ahead in range(1, ndp):
        mixed[ahead] = lax.ppermute(mixed[ahead], "dp", turn[ahead])
    everywhere = pl.BlockSpec(memory_space=pl.ANY)
    in_vmem = pl.BlockSpec(memory_space=pltpu.VMEM)
    near_last, far_last, *blocks = kernel_call(
        functools.partial(second_grad_body, ndp),
        [shaped(grad_near.shape, BF16), shaped(grad_other.shape, BF16)]
        + [shaped((rows, dcol), BF16)] * len(places),
        grid=(),
        in_specs=[everywhere] * 7,
        out_specs=[in_vmem] * (2 + len(places)),
        scratch=[
            pltpu.VMEM((2, 3, drow, width), BF16),
            pltpu.VMEM((ncol, chunk, dcol), F32),
            pltpu.SemaphoreType.DMA((5,)),
        ],
        flops=mm_flops // 2,
        nbytes=mm_bytes // 2,
        vmem=MOST_VMEM_BYTES,
    )(part, near_far_before, near_far_after, far_far_before, far_far_after, w, partner_w)
    far_three, far_last, mixed[1:] = lax.optimization_barrier((far_three, far_last, mixed[1:]))
    far_three, far_last = (lax.ppermute(part, "row", partner) for part in (far_three, far_last))
    arrivals = [
        lax.ppermute(sent, ("row", "col"), [(b, a) for a, b in offset(*p)])
        for p, sent in zip(places[1:], blocks[1:])
    ]
    arrived = sum((a.astype(F32) for a in arrivals), blocks[0].astype(F32)).astype(BF16)
    arrived, far_three, far_last = lax.optimization_barrier((arrived, far_three, far_last))
    grad_in = lax.ppermute(arrived, ("dp", "row"), swap_back)

    grad_weight, mixed, grad_long, grad_short = kernel_call(
        functools.partial(weight_grad_body, scale),
        [
            shaped((3, drow, local), F32),
            shaped((rows, local), BF16),
            shaped((ngroups, ntaps), F32),
            shaped((nshort, 3, local), F32),
        ],
        grid=(3,),
        in_specs=[whole(nblocks, ncol, rows, dcol)] * 2
        + [whole(*grad_near.shape)] * 4
        + [whole(*far_three.shape), whole(*far_last.shape)]
        + [whole(rows, width)] * ndp,
        out_specs=[
            pl.BlockSpec((1, drow, local), lambda i: (i, 0, 0)),
            whole(rows, local),
            whole(ngroups, ntaps),
            whole(nshort, 3, local),
        ],
        scratch=[
            pltpu.VMEM((2, ndp, 3 * chunk + extra, width), BF16),
            pltpu.VMEM((ndp, rows, width), BF16),
        ],
        flops=2 * mm_flops,
        nbytes=2 * mm_bytes,
        vmem=MOST_VMEM_BYTES,
    )(x0, x1, *near, near_last, far_three, far_last, *mixed)
    grad_weight = jnp.transpose(grad_weight, (1, 0, 2))
    return (mixed, grad_in, grad_weight, grad_long, grad_short)


def from_behind(block, axis, distance):
    devices = range(lax.axis_size(axis))
    route = [(i - distance, i) for i in devices if i - distance in devices]
    return lax.ppermute(block, axis, route)


def toeplitz(leading, rows, span):
    groups = leading.shape[0]
    width = rows + span
    seed_row = jnp.concatenate(
        [leading, jnp.zeros((groups, width - leading.shape[1]), leading.dtype)], axis=1
    )
    tiled = jnp.tile(seed_row, (1, rows))
    skewed = tiled[:, : rows * (width - 1)].reshape(groups, rows, width - 1)
    return skewed[:, :, :span]


def to_groups(values, ngroups, members):
    count = values.shape[0]
    return values.reshape(count, ngroups, members).transpose(1, 2, 0)


def from_groups(values):
    groups, members, count = values.shape
    return values.transpose(2, 0, 1).reshape(count, groups * members)


def move_weights(tokens, in_weight, short_filter, long_filter, grad_out):
    rows = tokens.shape[0]
    local = grad_out.shape[1]
    nshort = short_filter.shape[0]
    ntaps = long_filter.shape[1]
    ngroups = long_filter.shape[0]
    members = local // ngroups
    margin = ntaps - 1
    span = rows + margin
    scale = float(rows * lax.axis_size("dp")) ** (-0.5)
    whole = lax.all_gather(tokens, ("row", "col"), axis=1, tiled=True)
    full_w = lax.all_gather(in_weight, "dp", axis=0, tiled=True)
    mixed_in = jnp.einsum("sd,dic->sic", whole, full_w, preferred_element_type=jnp.float32).astype(
        jnp.bfloat16
    )
    before = from_behind(mixed_in[rows - margin - nshort + 1 :], "dp", 1)
    extended = jnp.concatenate([before, mixed_in], axis=0).astype(jnp.float32)
    long_feats = jnp.zeros((span, 3, local), jnp.float32)
    for j in range(nshort):
        long_feats = (
            long_feats + short_filter[j][None] * extended[nshort - 1 - j : nshort - 1 - j + span]
        )
    product_ext = (long_feats[:, 1] * long_feats[:, 2]).astype(jnp.bfloat16)
    feats = long_feats[margin:]
    short_rows = extended[margin:]
    product_cols = to_groups(product_ext, ngroups, members)
    causal = toeplitz(long_filter[:, ::-1], rows, span)
    conv = from_groups(
        jnp.einsum("gst,gct->gcs", causal, product_cols, preferred_element_type=jnp.float32)
    )
    mixed = (feats[:, 0] * conv).astype(jnp.bfloat16)
    upstream = grad_out.astype(jnp.float32)
    grad_query = upstream * conv
    grad_conv = (upstream * feats[:, 0]).astype(jnp.bfloat16)
    after = from_behind(grad_conv[:margin], "dp", -1)
    grad_ext = jnp.concatenate([grad_conv, after], axis=0)
    anti = toeplitz(long_filter, rows, span)
    grad_product = from_groups(
        jnp.einsum(
            "gst,gct->gcs",
            anti,
            to_groups(grad_ext, ngroups, members),
            preferred_element_type=jnp.float32,
        )
    )
    reversed_cols = jnp.concatenate(
        [product_cols[:, :, ::-1], jnp.zeros((ngroups, members, rows), product_cols.dtype)], axis=2
    )
    width = span + rows
    pairs = jnp.einsum(
        "gcs,gcu->gsu",
        to_groups(grad_conv, ngroups, members),
        reversed_cols,
        preferred_element_type=jnp.float32,
    )
    diagonal = pairs.reshape(ngroups, rows * width)[:, : rows * (width - 1)].reshape(
        ngroups, rows, width - 1
    )
    filter_part = jnp.sum(diagonal[:, :, rows - 1 : rows - 1 + ntaps], axis=1)
    grad_feats = jnp.stack(
        [grad_query, grad_product * feats[:, 2], grad_product * feats[:, 1]], axis=1
    )
    later = from_behind(grad_feats[: nshort - 1], "dp", -1)
    feats_ext = jnp.concatenate([grad_feats, later], axis=0)
    grad_acc = jnp.zeros((rows, 3, local), jnp.float32)
    for j in range(nshort):
        grad_acc = grad_acc + short_filter[j][None] * feats_ext[j : j + rows]
    grad_mixed = grad_acc.astype(jnp.bfloat16)
    short_part = jnp.stack(
        [
            jnp.sum(grad_feats * short_rows[nshort - 1 - j : nshort - 1 - j + rows], axis=0)
            for j in range(nshort)
        ]
    )
    filter_total, short_total = (
        lax.psum(filter_part.astype(jnp.bfloat16), "dp").astype(jnp.float32),
        lax.psum(short_part.astype(jnp.bfloat16), "dp").astype(jnp.float32),
    )
    grad_long = filter_total * scale
    grad_short = short_total * scale
    partial_in = jnp.einsum("sic,dic->sd", grad_mixed, full_w, preferred_element_type=jnp.float32)
    summed_in = lax.psum_scatter(
        partial_in.astype(jnp.bfloat16), ("row", "col"), scatter_dimension=1, tiled=True
    )
    weight_term = (
        jnp.einsum("sd,sic->dic", whole, grad_mixed, preferred_element_type=jnp.float32) * scale
    )
    grad_weight = lax.psum_scatter(
        weight_term.astype(jnp.bfloat16), "dp", scatter_dimension=0, tiled=True
    ).astype(jnp.float32)
    return (mixed, summed_in, grad_weight, grad_long, grad_short)


def fits_whole_sequences(mesh, tokens, in_weight, short_filter, long_filter, grad_out):
    ndp, nrow, ncol = (mesh.shape[a] for a in ("dp", "row", "col"))
    seq, channels = grad_out.shape
    groups, ntaps = long_filter.shape
    local = channels // (nrow * ncol)
    width, rows = local // ndp, seq // ndp
    return (
        seq < tokens.shape[1]
        and ndp == nrow == 4
        and ncol * (tokens.shape[1] // (nrow * ncol)) == in_weight.shape[0] // ndp
        and ntaps == width == 128
        and seq % (2 * ntaps) == 0
        and rows % 16 == 0
        and groups % (8 * ndp * nrow * ncol) == 0
    )


def solution(mesh):
    placed = (
        P("dp", ("row", "col")),
        P("dp", None, ("row", "col")),
        P(None, None, ("row", "col")),
        P(("row", "col"), None),
        P("dp", ("row", "col")),
    )
    gives = (
        P("dp", ("row", "col")),
        P("dp", ("row", "col")),
        P("dp", None, ("row", "col")),
        P(("row", "col"), None),
        P(None, None, ("row", "col")),
    )

    def run(*arrays):
        plan = move_activations if fits_whole_sequences(mesh, *arrays) else move_weights
        return jax.shard_map(
            plan, mesh=mesh, in_specs=placed, out_specs=gives, check_vma=False
        )(*arrays)

    return run
```

```python
import functools

import jax
import jax.numpy as jnp
from jax import lax
from jax.experimental import pallas as pl
from jax.experimental.pallas import tpu as pltpu
from jax.sharding import PartitionSpec as P

VMEM_BYTES = 48 * 2**20
MOST_VMEM_BYTES = 62 * 2**20
F32 = jnp.float32
BF16 = jnp.bfloat16


def kernel_call(body, outs, grid=(), in_specs=None, out_specs=None, scratch=(), flops=0, nbytes=0, vmem=VMEM_BYTES):
    kwargs = {}
    if in_specs is not None:
        kwargs = dict(grid=grid, in_specs=in_specs, out_specs=out_specs)
    return pl.pallas_call(
        body,
        out_shape=outs,
        scratch_shapes=scratch,
        compiler_params=pltpu.CompilerParams(vmem_limit_bytes=vmem),
        cost_estimate=pl.CostEstimate(flops=flops, bytes_accessed=nbytes, transcendentals=0),
        **kwargs,
    )


def shaped(shape, dtype):
    return jax.ShapeDtypeStruct(shape, dtype)


def bands_body(base_ref, out_ref):
    groups, wide = base_ref.shape
    rows = out_ref.shape[1]
    row = lax.broadcasted_iota(jnp.int32, (8, wide), 0)
    for g in range(groups):
        band = jnp.broadcast_to(base_ref[g : g + 1, :], (8, wide))
        for bit in (1, 2, 4):
            band = jnp.where((row & bit) != 0, pltpu.roll(band, bit, 1), band)
        count = 8
        while count < rows:
            band = jnp.concatenate([band, pltpu.roll(band, count, 1)], axis=0)
            count *= 2
        out_ref[g] = band.astype(out_ref.dtype)


def tokens_of(row, nrow):
    return row % 2 * (nrow // 2) + row // 2


def wrapped(value, size):
    return lax.rem(value + 2 * size, size)


def split_body(all_ref, *out_refs):
    width = out_refs[0].shape[1]
    for ahead, out_ref in enumerate(out_refs):
        at = wrapped(lax.axis_index("dp") + ahead, len(out_refs)) * width
        out_ref[...] = all_ref[:, pl.ds(pl.multiple_of(at, width), width)]


def project_body(x_ref, w_ref, *refs):
    *out_refs, held = refs
    z, col = lax.axis_index("dp"), lax.axis_index("col")
    nblocks, ncol, rows, depth = x_ref.shape
    width = held.shape[2]
    total = jnp.zeros((nblocks * rows, w_ref.shape[2]), F32)
    for dx in range(ncol):
        start = pl.multiple_of(wrapped(col - dx, ncol) * depth, depth)
        total += jnp.dot(
            x_ref[:, dx].reshape(nblocks * rows, depth),
            w_ref[0, pl.ds(start, depth), :],
            preferred_element_type=F32,
        )
    for owner in range(len(out_refs)):
        held[owner] = total[:, owner * width : (owner + 1) * width].astype(BF16)
    for ahead, out_ref in enumerate(out_refs):
        out_ref[0] = held[wrapped(z + ahead, len(out_refs))]


def first_grad_body(near, near_before, near_after, far, far_before, far_after, w_ref, partner_w_ref, out_ref, far_ref, held):
    ndp, _, width = held.shape
    ncol, tokens, depth = out_ref.shape
    z, col = lax.axis_index("dp"), lax.axis_index("col")
    far_ref[0], far_ref[1], far_ref[2] = far[...], far_before[...], far_after[...]
    for pieces, weights, first in (
        ((near, near_before, near_after), w_ref, True),
        ((far, far_before, far_after), partner_w_ref, False),
    ):
        held[wrapped(z + ndp // 2, ndp)] = jnp.zeros(held.shape[1:], BF16)
        for ahead, piece in zip((0, -1, 1), pieces):
            held[wrapped(z + ahead, ndp)] = piece[: 3 * tokens]
        for dx in range(ncol):
            start = pl.multiple_of(wrapped(col - dx, ncol) * depth, depth)
            total = jnp.zeros((tokens, depth), F32) if first else out_ref[dx]
            for i in range(3):
                rows = slice(i * tokens, (i + 1) * tokens)
                total += lax.dot_general(
                    jnp.concatenate([held[owner, rows] for owner in range(ndp)], axis=1),
                    weights[i, pl.ds(start, depth), :],
                    (((1,), (1,)), ((), ())),
                    preferred_element_type=F32,
                )
            out_ref[dx] = total


def second_grad_body(ndp, part_ref, *refs):
    arrived, weights, refs = (refs[:2], refs[2:4]), refs[4:6], refs[6:]
    (near_ref, far_ref), refs = refs[:2], refs[2:]
    *out_refs, held_w, held_part, sems = refs
    ncol, tokens, depth = held_part.shape
    rows = out_refs[0].shape[0]
    width = near_ref.shape[1]
    z, col = lax.axis_index("dp"), lax.axis_index("col")
    lanes = pl.ds(pl.multiple_of(wrapped(z + ndp // 2, ndp) * width, width), width)
    copies = [
        pltpu.make_async_copy(w_ref.at[:, :, lanes], held_w.at[k], sems.at[k]) for k, w_ref in enumerate(weights)
    ]
    copies.append(pltpu.make_async_copy(part_ref, held_part, sems.at[2]))
    for copy in copies:
        copy.start()
    for k, (pair, target) in enumerate(zip(arrived, (near_ref, far_ref))):
        for source, here in zip(pair, (z >= ndp // 2, z < ndp // 2)):

            @pl.when(here)
            def _(source=source, target=target, k=k):
                copy = pltpu.make_async_copy(source, target, sems.at[3 + k])
                copy.start()
                copy.wait()

    for copy in copies:
        copy.wait()
    left = jnp.concatenate(
        [ref[i * tokens : (i + 1) * tokens] for ref in (near_ref, far_ref) for i in range(3)], axis=1
    )
    for dx in range(ncol):
        start = pl.multiple_of(wrapped(col - dx, ncol) * depth, depth)
        right = jnp.concatenate([held_w[k, i, pl.ds(start, depth), :] for k in range(2) for i in range(3)], axis=1)
        total = held_part[dx] + lax.dot_general(
            left, right, (((1,), (1,)), ((), ())), preferred_element_type=F32
        )
        for block in range(tokens // rows):
            out_refs[block * ncol + dx][...] = total[block * rows : (block + 1) * rows].astype(BF16)


def weight_grad_body(scale, *refs):
    (x0_ref, x1_ref), near_refs, (far_ref, far_last_ref), mixed_refs, refs = (
        refs[:2],
        refs[2:6],
        refs[6:8],
        refs[8:12],
        refs[12:],
    )
    out_ref, mixed_ref, long_ref, short_ref, held, held_mixed = refs
    nblocks, ncol, rows, depth = x0_ref.shape
    _, ndp, _, width = held.shape
    tokens = nblocks * rows
    i = pl.program_id(0)
    z, col = lax.axis_index("dp"), lax.axis_index("col")

    @pl.when(i == 0)
    def _():
        groups = long_ref.shape[0] // ndp
        for k, ahead in enumerate((0, -1, 1, 2)):
            owner = wrapped(z + ahead, ndp)
            held[0, owner] = near_refs[k][...]
            held[1, owner, : 3 * tokens] = far_ref[k] if k < 3 else far_last_ref[...]
        for back in range(ndp):
            held_mixed[wrapped(z - back, ndp)] = mixed_refs[back][...]
        for owner in range(ndp):
            lanes = slice(owner * width, (owner + 1) * width)
            mixed_ref[:, lanes] = held_mixed[owner]
            small = held[0, owner, 3 * tokens :].astype(F32)
            long_ref[owner * groups : (owner + 1) * groups] = small[:groups]
            nshort, three, _ = short_ref.shape
            for j in range(nshort):
                short_ref[j, :, lanes] = small[groups + three * j : groups + three * (j + 1)]

    at = pl.ds(pl.multiple_of(i * tokens, 16), tokens)
    gm = jnp.concatenate(
        [jnp.concatenate([held[k, owner, at, :] for owner in range(ndp)], axis=1) for k in range(2)], axis=0
    )
    for dx in range(ncol):
        start = pl.multiple_of(wrapped(col - dx, ncol) * depth, depth)
        x = jnp.concatenate(
            [x_ref[:, dx].reshape(tokens, depth) for x_ref in (x0_ref, x1_ref)], axis=0
        )
        out_ref[0, pl.ds(start, depth), :] = scale * lax.dot_general(
            x, gm, (((0,), (0,)), ((), ())), preferred_element_type=F32
        )


def delayed(values, count):
    row = lax.broadcasted_iota(jnp.int32, values.shape, 0)
    return jnp.where(row >= count, pltpu.roll(values, count, 0), 0.0)


def advanced(values, count):
    rows = values.shape[0]
    row = lax.broadcasted_iota(jnp.int32, values.shape, 0)
    return jnp.where(row < rows - count, pltpu.roll(values, rows - count, 0), 0.0)


def middle_body(scale, nshort, nrow, *refs):
    sums, refs = (refs[:3], refs[3:6]), refs[6:]
    (sf_ref, causal_ref, anti_ref), refs = refs[:3], refs[3:]
    *refs, m_ref, gm_ref, mixed_ref, go_ref = refs
    ndp = len(refs) // 2 - 1
    go_refs, (near_ref, other_ref), mixed_refs = refs[:ndp], refs[ndp : ndp + 2], refs[ndp + 2 :]
    tokens, width = go_ref.shape
    for behind, piece in enumerate(go_refs):
        at = wrapped(lax.axis_index("dp") - behind, ndp) * (tokens // ndp)
        go_ref[pl.ds(pl.multiple_of(at, 16), tokens // ndp)] = piece[...]
    row = lax.axis_index("row")
    nblocks = nrow // 2
    rows = tokens // nrow

    def places():
        for chunk, start in enumerate((row, row + 1 - 2 * lax.rem(row, 2))):
            for block in range(nblocks):
                at = tokens_of(wrapped(start - 2 * block, nrow), nrow) * rows
                for i in range(3):
                    yield chunk, (i * nblocks + block) * rows, pl.multiple_of(i * tokens + at, 16)

    for chunk, place, at in places():
        held = [ref[place : place + rows].astype(F32) for ref in sums[chunk]]
        m_ref[pl.ds(at, rows)] = held[0] + held[1] + held[2]
    groups, block, span = causal_ref.shape
    members = width // groups
    nspans = tokens // block
    lane = lax.broadcasted_iota(jnp.int32, (block, width), 1) // members
    lanes = lax.broadcasted_iota(jnp.int32, (block, 2 * width), 1) % width // members

    def past(i, j):
        held = m_ref[i * tokens : (i + 1) * tokens]
        return held if j == 0 else delayed(held, j)

    def taps(j, i):
        return sf_ref[3 * j + i : 3 * j + i + 1, :]

    feats = [sum(taps(j, i) * past(i, j) for j in range(nshort)) for i in range(3)]
    product = (feats[1] * feats[2]).astype(BF16)
    zero = jnp.zeros((block, width), BF16)
    p_blocks = [zero] + [product[b * block : (b + 1) * block] for b in range(nspans)]
    p_pairs = [jnp.concatenate(p_blocks[b : b + 2], axis=0) for b in range(nspans)]

    def filtered(band_ref, pairs):
        bands = band_ref[...].reshape(groups * block, span)
        out = []
        for b in range(0, nspans, 2):
            both = jnp.dot(bands, jnp.concatenate(pairs[b : b + 2], axis=1), preferred_element_type=F32)
            for h in range(2):
                part = both[:, h * width : (h + 1) * width]
                picked = part[:block]
                for g in range(1, groups):
                    picked = jnp.where(lane == g, part[g * block : (g + 1) * block], picked)
                out.append(picked)
        return jnp.concatenate(out, axis=0)

    conv = filtered(causal_ref, p_pairs)
    upstream = go_ref[...].astype(F32)
    mixed_ref[...] = (feats[0] * conv).astype(BF16)
    for ahead, out_ref in enumerate(mixed_refs):
        at = pl.multiple_of(wrapped(lax.axis_index("dp") + ahead, ndp) * (tokens // ndp), 16)
        out_ref[...] = mixed_ref[pl.ds(at, tokens // ndp)]
    grad_conv = (upstream * feats[0]).astype(BF16)
    c_blocks = [grad_conv[b * block : (b + 1) * block] for b in range(nspans)] + [zero]
    c_pairs = [jnp.concatenate(c_blocks[b : b + 2], axis=0) for b in range(nspans)]
    grad_product = filtered(anti_ref, c_pairs)

    corr = jnp.zeros((groups * block, span), F32)
    for b in range(0, nspans, 2):
        left = jnp.concatenate(c_blocks[b : b + 2], axis=1)
        stacked = jnp.concatenate(
            [jnp.where(lanes == g, left, jnp.zeros_like(left)) for g in range(groups)], axis=0
        )
        right = jnp.concatenate(p_pairs[b : b + 2], axis=1)
        corr += lax.dot_general(stacked, right, (((1,), (1,)), ((), ())), preferred_element_type=F32)
    turn = lax.broadcasted_iota(jnp.int32, (8, span), 0)
    sums = []
    for g in range(groups):
        part = corr[g * block : (g + 1) * block]
        count = block
        while count > 8:
            count //= 2
            part = part[:count] + pltpu.roll(part[count:], span - count, 1)
        for bit in (1, 2, 4):
            part = jnp.where((turn & bit) != 0, pltpu.roll(part, span - bit, 1), part)
        sums.append(jnp.sum(part, axis=0, keepdims=True))
    by_lag = jnp.concatenate(sums, axis=0)
    by_lag = (scale * pltpu.roll(by_lag, span - 1, 1)[:, :block]).astype(BF16)
    ahead = lax.broadcasted_iota(jnp.int32, (block, block), 0)
    back = lax.broadcasted_iota(jnp.int32, (block, block), 1)
    turned = jnp.where(ahead + back == block - 1, 1.0, 0.0).astype(BF16)
    by_lag = jnp.dot(by_lag, turned, preferred_element_type=F32)

    grad_feats = [upstream * conv, grad_product * feats[2], grad_product * feats[1]]
    short_rows = []
    for j in range(nshort):
        for i in range(3):
            short_rows.append(scale * jnp.sum(grad_feats[i] * past(i, j), axis=0, keepdims=True))
    for i in range(3):
        total = taps(0, i) * grad_feats[i]
        for j in range(1, nshort):
            total += taps(j, i) * advanced(grad_feats[i], j)
        gm_ref[i * tokens : (i + 1) * tokens] = total.astype(BF16)
    for chunk, place, at in places():
        (near_ref, other_ref)[chunk][place : place + rows] = gm_ref[pl.ds(at, rows)]
    tail = near_ref.shape[0] - 3 * tokens // 2 - groups - 3 * nshort
    small = jnp.concatenate([by_lag] + short_rows + [jnp.zeros((tail, width), F32)], axis=0)
    near_ref[3 * tokens // 2 :] = small.astype(BF16)


def sum_over_line(own, right, far, left):
    ndp = lax.axis_size("dp")
    from_left = lax.ppermute(far, "dp", [(a, a + 1) for a in range(ndp // 2)])
    from_right = lax.ppermute(far, "dp", [(a, a - 1) for a in range(ndp // 2, ndp)])
    rightward = lax.ppermute(right + from_left, "dp", [(a, (a + 1) % ndp) for a in range(ndp)])
    leftward = lax.ppermute(left + from_right, "dp", [(a, (a - 1) % ndp) for a in range(ndp)])
    return own, rightward, leftward


def gather_over_line(own, across):
    ndp, nrow = lax.axis_size("dp"), lax.axis_size("row")

    def shift(count):
        return [
            (a * nrow + r, (a + count) % ndp * nrow + (r + 1 - 2 * (r % 2) if across else r))
            for a in range(ndp)
            for r in range(nrow)
        ]

    before = lax.ppermute(own, ("dp", "row"), shift(1))
    after = lax.ppermute(own, ("dp", "row"), shift(-1))
    here = lax.ppermute(own, ("dp", "row"), shift(0)) if across else own
    far_before = lax.ppermute(before, "dp", [(a - 1, a) for a in range(ndp // 2, ndp)])
    far_after = lax.ppermute(after, "dp", [(a + 1, a) for a in range(ndp // 2)])
    return here, before, after, far_before, far_after


def move_activations(tokens, in_weight, short_filter, long_filter, grad_out):
    ndp, nrow, ncol = (lax.axis_size(a) for a in ("dp", "row", "col"))
    z = lax.axis_index("dp")
    rows, dcol = tokens.shape
    local = grad_out.shape[1]
    nshort = short_filter.shape[0]
    ngroups, ntaps = long_filter.shape
    seq = rows * ndp
    width, groups = local // ndp, ngroups // ndp
    drow = in_weight.shape[0]
    scale = float(seq) ** -0.5
    nblocks = nrow // 2
    chunk = nblocks * rows
    swap = [(tokens_of(b, nrow) * nrow + a, a * nrow + b) for a in range(ndp) for b in range(nrow)]
    swap_back = [(b, a) for a, b in swap]
    partner = [(a, a + 1 - 2 * (a % 2)) for a in range(nrow)]
    places = [(dy, dx) for dy in range(nblocks) for dx in range(ncol)]

    def offset(dy, dx):
        return [
            (a * ncol + b, (a + 2 * dy) % nrow * ncol + (b + dx) % ncol) for a in range(nrow) for b in range(ncol)
        ]

    w = jnp.transpose(in_weight, (1, 0, 2))
    moved = lax.ppermute(tokens, ("dp", "row"), swap)
    turn = [[(a, (a + ahead) % ndp) for a in range(ndp)] for ahead in range(ndp)]
    upstream = [*kernel_call(split_body, [shaped((rows, width), BF16)] * ndp)(grad_out)]
    upstream[1] = lax.ppermute(upstream[1], "dp", turn[1])
    moved, upstream = lax.optimization_barrier((moved, upstream))
    near = [moved] + [lax.ppermute(moved, ("row", "col"), offset(*p)) for p in places[1:]]
    for ahead in range(2, ndp):
        upstream[ahead] = lax.ppermute(upstream[ahead], "dp", turn[ahead])
    upstream[2:], near[1:] = lax.optimization_barrier((upstream[2:], near[1:]))
    x0 = jnp.stack(near).reshape(nblocks, ncol, rows, dcol)
    x1 = lax.ppermute(x0, "row", partner)

    sf = lax.dynamic_slice_in_dim(short_filter, z * width, width, 2).reshape(3 * nshort, width)
    lf = lax.dynamic_slice_in_dim(long_filter, z * groups, groups, 0).astype(F32)
    zeros = functools.partial(jnp.zeros, dtype=F32)
    bases = jnp.concatenate(
        [
            jnp.concatenate([zeros((groups, 1)), lf[:, ::-1], zeros((groups, ntaps - 1))], axis=1),
            jnp.concatenate([lf, zeros((groups, ntaps))], axis=1),
        ],
        axis=0,
    )
    bands = kernel_call(bands_body, shaped((2 * groups, ntaps, 2 * ntaps), BF16))(bases)

    mm_flops = seq * drow * 3 * local
    mm_bytes = seq * drow + 6 * drow * local + 3 * seq * local
    sums = []
    for x in (x0, x1):
        parts = kernel_call(
            project_body,
            [shaped((3, chunk, width), BF16)] * ndp,
            grid=(3,),
            in_specs=[
                pl.BlockSpec((nblocks, ncol, rows, dcol), lambda i: (0, 0, 0, 0)),
                pl.BlockSpec((1, drow, local), lambda i: (i, 0, 0)),
            ],
            out_specs=[pl.BlockSpec((1, chunk, width), lambda i: (i, 0, 0))] * ndp,
            scratch=[pltpu.VMEM((ndp, chunk, width), BF16)],
            flops=mm_flops,
            nbytes=mm_bytes,
        )(x, w)
        sums += sum_over_line(*(p.reshape(3 * chunk, width) for p in parts))

    extra = -(-(groups + 3 * nshort) // 16) * 16
    half = pl.BlockSpec((groups, ntaps, 2 * ntaps), lambda i: (0, 0, 0))
    other = pl.BlockSpec((groups, ntaps, 2 * ntaps), lambda i: (1, 0, 0))
    whole = lambda *shape: pl.BlockSpec(shape, lambda i: (0,) * len(shape))
    grad_near, grad_other, *mixed = kernel_call(
        functools.partial(middle_body, scale, nshort, nrow),
        [shaped((3 * chunk + extra, width), BF16), shaped((3 * chunk, width), BF16)]
        + [shaped((rows, width), BF16)] * ndp,
        grid=(1,),
        in_specs=[whole(3 * chunk, width)] * 6
        + [whole(3 * nshort, width), half, other]
        + [whole(rows, width)] * ndp,
        out_specs=[whole(3 * chunk + extra, width), whole(3 * chunk, width)] + [whole(rows, width)] * ndp,
        scratch=[
            pltpu.VMEM((3 * seq, width), F32),
            pltpu.VMEM((3 * seq, width), BF16),
            pltpu.VMEM((seq, width), BF16),
            pltpu.VMEM((seq, width), BF16),
        ],
        flops=3 * 2 * groups * ntaps * 2 * ntaps * width * (seq // ntaps),
        nbytes=2 * width * seq * 14,
        vmem=MOST_VMEM_BYTES,
    )(*sums, sf, bands, bands, *upstream)
    mixed = [mixed[0]] + [
        lax.ppermute(part, "dp", [(a, (a + ahead) % ndp) for a in range(ndp)])
        for ahead, part in enumerate(mixed)
        if ahead
    ]
    *near, near_far_before, near_far_after = gather_over_line(grad_near, False)
    *far, far_far_before, far_far_after = gather_over_line(grad_other, True)
    partner_w = lax.ppermute(w, "row", partner)
    part, far_three = kernel_call(
        first_grad_body,
        [shaped((ncol, chunk, dcol), F32), shaped((3, 3 * chunk, width), BF16)],
        scratch=[pltpu.VMEM((ndp, 3 * chunk, width), BF16)],
        flops=2 * mm_flops,
        nbytes=2 * mm_bytes,
    )(*near, *far, w, partner_w)
    everywhere = pl.BlockSpec(memory_space=pl.ANY)
    in_vmem = pl.BlockSpec(memory_space=pltpu.VMEM)
    near_last, far_last, *blocks = kernel_call(
        functools.partial(second_grad_body, ndp),
        [shaped(grad_near.shape, BF16), shaped(grad_other.shape, BF16)]
        + [shaped((rows, dcol), BF16)] * len(places),
        grid=(),
        in_specs=[everywhere] * 7,
        out_specs=[in_vmem] * (2 + len(places)),
        scratch=[
            pltpu.VMEM((2, 3, drow, width), BF16),
            pltpu.VMEM((ncol, chunk, dcol), F32),
            pltpu.SemaphoreType.DMA((5,)),
        ],
        flops=mm_flops // 2,
        nbytes=mm_bytes // 2,
        vmem=MOST_VMEM_BYTES,
    )(part, near_far_before, near_far_after, far_far_before, far_far_after, w, partner_w)
    far_three, far_last, mixed[1:] = lax.optimization_barrier((far_three, far_last, mixed[1:]))
    far_three, far_last = (lax.ppermute(part, "row", partner) for part in (far_three, far_last))
    arrivals = [
        lax.ppermute(sent, ("row", "col"), [(b, a) for a, b in offset(*p)])
        for p, sent in zip(places[1:], blocks[1:])
    ]
    arrived = sum((a.astype(F32) for a in arrivals), blocks[0].astype(F32)).astype(BF16)
    arrived, far_three, far_last = lax.optimization_barrier((arrived, far_three, far_last))
    grad_in = lax.ppermute(arrived, ("dp", "row"), swap_back)

    grad_weight, mixed, grad_long, grad_short = kernel_call(
        functools.partial(weight_grad_body, scale),
        [
            shaped((3, drow, local), F32),
            shaped((rows, local), BF16),
            shaped((ngroups, ntaps), F32),
            shaped((nshort, 3, local), F32),
        ],
        grid=(3,),
        in_specs=[whole(nblocks, ncol, rows, dcol)] * 2
        + [whole(*grad_near.shape)] * 4
        + [whole(*far_three.shape), whole(*far_last.shape)]
        + [whole(rows, width)] * ndp,
        out_specs=[
            pl.BlockSpec((1, drow, local), lambda i: (i, 0, 0)),
            whole(rows, local),
            whole(ngroups, ntaps),
            whole(nshort, 3, local),
        ],
        scratch=[
            pltpu.VMEM((2, ndp, 3 * chunk + extra, width), BF16),
            pltpu.VMEM((ndp, rows, width), BF16),
        ],
        flops=2 * mm_flops,
        nbytes=2 * mm_bytes,
        vmem=MOST_VMEM_BYTES,
    )(x0, x1, *near, near_last, far_three, far_last, *mixed)
    grad_weight = jnp.transpose(grad_weight, (1, 0, 2))
    return (mixed, grad_in, grad_weight, grad_long, grad_short)


def from_behind(block, axis, distance):
    devices = range(lax.axis_size(axis))
    route = [(i - distance, i) for i in devices if i - distance in devices]
    return lax.ppermute(block, axis, route)


def toeplitz(leading, rows, span):
    groups = leading.shape[0]
    width = rows + span
    seed_row = jnp.concatenate(
        [leading, jnp.zeros((groups, width - leading.shape[1]), leading.dtype)], axis=1
    )
    tiled = jnp.tile(seed_row, (1, rows))
    skewed = tiled[:, : rows * (width - 1)].reshape(groups, rows, width - 1)
    return skewed[:, :, :span]


def to_groups(values, ngroups, members):
    count = values.shape[0]
    return values.reshape(count, ngroups, members).transpose(1, 2, 0)


def from_groups(values):
    groups, members, count = values.shape
    return values.transpose(2, 0, 1).reshape(count, groups * members)


def move_weights(tokens, in_weight, short_filter, long_filter, grad_out):
    rows = tokens.shape[0]
    local = grad_out.shape[1]
    nshort = short_filter.shape[0]
    ntaps = long_filter.shape[1]
    ngroups = long_filter.shape[0]
    members = local // ngroups
    margin = ntaps - 1
    span = rows + margin
    scale = float(rows * lax.axis_size("dp")) ** (-0.5)
    whole = lax.all_gather(tokens, ("row", "col"), axis=1, tiled=True)
    full_w = lax.all_gather(in_weight, "dp", axis=0, tiled=True)
    mixed_in = jnp.einsum("sd,dic->sic", whole, full_w, preferred_element_type=jnp.float32).astype(
        jnp.bfloat16
    )
    before = from_behind(mixed_in[rows - margin - nshort + 1 :], "dp", 1)
    extended = jnp.concatenate([before, mixed_in], axis=0).astype(jnp.float32)
    long_feats = jnp.zeros((span, 3, local), jnp.float32)
    for j in range(nshort):
        long_feats = (
            long_feats + short_filter[j][None] * extended[nshort - 1 - j : nshort - 1 - j + span]
        )
    product_ext = (long_feats[:, 1] * long_feats[:, 2]).astype(jnp.bfloat16)
    feats = long_feats[margin:]
    short_rows = extended[margin:]
    product_cols = to_groups(product_ext, ngroups, members)
    causal = toeplitz(long_filter[:, ::-1], rows, span)
    conv = from_groups(
        jnp.einsum("gst,gct->gcs", causal, product_cols, preferred_element_type=jnp.float32)
    )
    mixed = (feats[:, 0] * conv).astype(jnp.bfloat16)
    upstream = grad_out.astype(jnp.float32)
    grad_query = upstream * conv
    grad_conv = (upstream * feats[:, 0]).astype(jnp.bfloat16)
    after = from_behind(grad_conv[:margin], "dp", -1)
    grad_ext = jnp.concatenate([grad_conv, after], axis=0)
    anti = toeplitz(long_filter, rows, span)
    grad_product = from_groups(
        jnp.einsum(
            "gst,gct->gcs",
            anti,
            to_groups(grad_ext, ngroups, members),
            preferred_element_type=jnp.float32,
        )
    )
    reversed_cols = jnp.concatenate(
        [product_cols[:, :, ::-1], jnp.zeros((ngroups, members, rows), product_cols.dtype)], axis=2
    )
    width = span + rows
    pairs = jnp.einsum(
        "gcs,gcu->gsu",
        to_groups(grad_conv, ngroups, members),
        reversed_cols,
        preferred_element_type=jnp.float32,
    )
    diagonal = pairs.reshape(ngroups, rows * width)[:, : rows * (width - 1)].reshape(
        ngroups, rows, width - 1
    )
    filter_part = jnp.sum(diagonal[:, :, rows - 1 : rows - 1 + ntaps], axis=1)
    grad_feats = jnp.stack(
        [grad_query, grad_product * feats[:, 2], grad_product * feats[:, 1]], axis=1
    )
    later = from_behind(grad_feats[: nshort - 1], "dp", -1)
    feats_ext = jnp.concatenate([grad_feats, later], axis=0)
    grad_acc = jnp.zeros((rows, 3, local), jnp.float32)
    for j in range(nshort):
        grad_acc = grad_acc + short_filter[j][None] * feats_ext[j : j + rows]
    grad_mixed = grad_acc.astype(jnp.bfloat16)
    short_part = jnp.stack(
        [
            jnp.sum(grad_feats * short_rows[nshort - 1 - j : nshort - 1 - j + rows], axis=0)
            for j in range(nshort)
        ]
    )
    filter_total, short_total = (
        lax.psum(filter_part.astype(jnp.bfloat16), "dp").astype(jnp.float32),
        lax.psum(short_part.astype(jnp.bfloat16), "dp").astype(jnp.float32),
    )
    grad_long = filter_total * scale
    grad_short = short_total * scale
    partial_in = jnp.einsum("sic,dic->sd", grad_mixed, full_w, preferred_element_type=jnp.float32)
    summed_in = lax.psum_scatter(
        partial_in.astype(jnp.bfloat16), ("row", "col"), scatter_dimension=1, tiled=True
    )
    weight_term = (
        jnp.einsum("sd,sic->dic", whole, grad_mixed, preferred_element_type=jnp.float32) * scale
    )
    grad_weight = lax.psum_scatter(
        weight_term.astype(jnp.bfloat16), "dp", scatter_dimension=0, tiled=True
    ).astype(jnp.float32)
    return (mixed, summed_in, grad_weight, grad_long, grad_short)


def fits_whole_sequences(mesh, tokens, in_weight, short_filter, long_filter, grad_out):
    ndp, nrow, ncol = (mesh.shape[a] for a in ("dp", "row", "col"))
    seq, channels = grad_out.shape
    groups, ntaps = long_filter.shape
    local = channels // (nrow * ncol)
    width, rows = local // ndp, seq // ndp
    return (
        seq < tokens.shape[1]
        and ndp == nrow == 4
        and ncol * (tokens.shape[1] // (nrow * ncol)) == in_weight.shape[0] // ndp
        and ntaps == width == 128
        and seq % (2 * ntaps) == 0
        and rows % 16 == 0
        and groups % (8 * ndp * nrow * ncol) == 0
    )


def solution(mesh):
    placed = (
        P("dp", ("row", "col")),
        P("dp", None, ("row", "col")),
        P(None, None, ("row", "col")),
        P(("row", "col"), None),
        P("dp", ("row", "col")),
    )
    gives = (
        P("dp", ("row", "col")),
        P("dp", ("row", "col")),
        P("dp", None, ("row", "col")),
        P(("row", "col"), None),
        P(None, None, ("row", "col")),
    )

    def run(*arrays):
        plan = move_activations if fits_whole_sequences(mesh, *arrays) else move_weights
        return jax.shard_map(
            plan, mesh=mesh, in_specs=placed, out_specs=gives, check_vma=False
        )(*arrays)

    return run
```

```python
import functools

import jax
import jax.numpy as jnp
from jax import lax
from jax.experimental import pallas as pl
from jax.experimental.pallas import tpu as pltpu
from jax.sharding import PartitionSpec as P

VMEM_BYTES = 48 * 2**20
MOST_VMEM_BYTES = 62 * 2**20
F32 = jnp.float32
BF16 = jnp.bfloat16


def kernel_call(body, outs, grid=(), in_specs=None, out_specs=None, scratch=(), flops=0, nbytes=0, vmem=VMEM_BYTES):
    kwargs = {}
    if in_specs is not None:
        kwargs = dict(grid=grid, in_specs=in_specs, out_specs=out_specs)
    return pl.pallas_call(
        body,
        out_shape=outs,
        scratch_shapes=scratch,
        compiler_params=pltpu.CompilerParams(vmem_limit_bytes=vmem),
        cost_estimate=pl.CostEstimate(flops=flops, bytes_accessed=nbytes, transcendentals=0),
        **kwargs,
    )


def shaped(shape, dtype):
    return jax.ShapeDtypeStruct(shape, dtype)


def bands_body(base_ref, out_ref):
    groups, wide = base_ref.shape
    rows = out_ref.shape[1]
    row = lax.broadcasted_iota(jnp.int32, (8, wide), 0)
    for g in range(groups):
        band = jnp.broadcast_to(base_ref[g : g + 1, :], (8, wide))
        for bit in (1, 2, 4):
            band = jnp.where((row & bit) != 0, pltpu.roll(band, bit, 1), band)
        count = 8
        while count < rows:
            band = jnp.concatenate([band, pltpu.roll(band, count, 1)], axis=0)
            count *= 2
        out_ref[g] = band.astype(out_ref.dtype)


def tokens_of(row, nrow):
    return row % 2 * (nrow // 2) + row // 2


def wrapped(value, size):
    return lax.rem(value + 2 * size, size)


def split_body(all_ref, *out_refs):
    width = out_refs[0].shape[1]
    for ahead, out_ref in enumerate(out_refs):
        at = wrapped(lax.axis_index("dp") + ahead, len(out_refs)) * width
        out_ref[...] = all_ref[:, pl.ds(pl.multiple_of(at, width), width)]


def project_body(x_ref, w_ref, *refs):
    *out_refs, held = refs
    z, col = lax.axis_index("dp"), lax.axis_index("col")
    nblocks, ncol, rows, depth = x_ref.shape
    width = held.shape[2]
    total = jnp.zeros((nblocks * rows, w_ref.shape[2]), F32)
    for dx in range(ncol):
        start = pl.multiple_of(wrapped(col - dx, ncol) * depth, depth)
        total += jnp.dot(
            x_ref[:, dx].reshape(nblocks * rows, depth),
            w_ref[0, pl.ds(start, depth), :],
            preferred_element_type=F32,
        )
    for owner in range(len(out_refs)):
        held[owner] = total[:, owner * width : (owner + 1) * width].astype(BF16)
    for ahead, out_ref in enumerate(out_refs):
        out_ref[0] = held[wrapped(z + ahead, len(out_refs))]


def far_columns_body(w_ref, out_ref, sem):
    ndp = lax.axis_size("dp")
    width = out_ref.shape[2]
    start = wrapped(lax.axis_index("dp") + ndp // 2, ndp) * width
    copy = pltpu.make_async_copy(w_ref.at[:, :, pl.ds(pl.multiple_of(start, width), width)], out_ref, sem)
    copy.start()
    copy.wait()


def first_grad_body(own, before, after, w_ref, out_ref, held):
    ndp, _, width = held.shape
    ncol, tokens, depth = out_ref.shape
    z, col = lax.axis_index("dp"), lax.axis_index("col")
    held[wrapped(z + ndp // 2, ndp)] = jnp.zeros(held.shape[1:], BF16)
    for ahead, piece in zip((0, -1, 1), (own, before, after)):
        held[wrapped(z + ahead, ndp)] = piece[: 3 * tokens]
    for dx in range(ncol):
        start = pl.multiple_of(wrapped(col - dx, ncol) * depth, depth)
        total = jnp.zeros((tokens, depth), F32)
        for i in range(3):
            rows = slice(i * tokens, (i + 1) * tokens)
            total += lax.dot_general(
                jnp.concatenate([held[owner, rows] for owner in range(ndp)], axis=1),
                w_ref[i, pl.ds(start, depth), :],
                (((1,), (1,)), ((), ())),
                preferred_element_type=F32,
            )
        out_ref[dx] = total.astype(out_ref.dtype)


def second_grad_body(ndp, *refs):
    arrived, sources, refs = (refs[:2], refs[2:4]), refs[4:8], refs[8:]
    (near_ref, far_ref), refs = refs[:2], refs[2:]
    *out_refs, held_w, held_partner_w, held_part, held_partner, sems = refs
    held = (held_w, held_partner_w, held_part, held_partner)
    ncol, tokens, depth = held_part.shape
    rows = out_refs[0].shape[0]
    z, col = lax.axis_index("dp"), lax.axis_index("col")
    copies = [pltpu.make_async_copy(a, b, sems.at[k]) for k, (a, b) in enumerate(zip(sources, held))]
    for copy in copies:
        copy.start()
    for k, (pair, target) in enumerate(zip(arrived, (near_ref, far_ref))):
        for source, here in zip(pair, (z >= ndp // 2, z < ndp // 2)):

            @pl.when(here)
            def _(source=source, target=target, k=k):
                copy = pltpu.make_async_copy(source, target, sems.at[4 + k])
                copy.start()
                copy.wait()

    for copy in copies:
        copy.wait()
    left = jnp.concatenate(
        [ref[i * tokens : (i + 1) * tokens] for ref in (near_ref, far_ref) for i in range(3)], axis=1
    )
    for dx in range(ncol):
        start = pl.multiple_of(wrapped(col - dx, ncol) * depth, depth)
        right = jnp.concatenate(
            [w_ref[i, pl.ds(start, depth), :] for w_ref in (held_w, held_partner_w) for i in range(3)], axis=1
        )
        total = held_part[dx] + held_partner[dx].astype(F32)
        total += lax.dot_general(left, right, (((1,), (1,)), ((), ())), preferred_element_type=F32)
        for block in range(tokens // rows):
            out_refs[block * ncol + dx][...] = total[block * rows : (block + 1) * rows].astype(BF16)


def weight_grad_body(scale, *refs):
    (x0_ref, x1_ref), near_refs, other_refs, mixed_refs, refs = refs[:2], refs[2:6], refs[6:10], refs[10:14], refs[14:]
    out_ref, mixed_ref, long_ref, short_ref, held, held_mixed = refs
    nblocks, ncol, rows, depth = x0_ref.shape
    _, ndp, _, width = held.shape
    tokens = nblocks * rows
    i = pl.program_id(0)
    z, col = lax.axis_index("dp"), lax.axis_index("col")

    @pl.when(i == 0)
    def _():
        groups = long_ref.shape[0] // ndp
        for k, ahead in enumerate((0, -1, 1, 2)):
            owner = wrapped(z + ahead, ndp)
            held[0, owner] = near_refs[k][...]
            held[1, owner, : 3 * tokens] = other_refs[k][...]
        for back in range(ndp):
            held_mixed[wrapped(z - back, ndp)] = mixed_refs[back][...]
        for owner in range(ndp):
            lanes = slice(owner * width, (owner + 1) * width)
            mixed_ref[:, lanes] = held_mixed[owner]
            small = held[0, owner, 3 * tokens :].astype(F32)
            long_ref[owner * groups : (owner + 1) * groups] = small[:groups]
            nshort, three, _ = short_ref.shape
            for j in range(nshort):
                short_ref[j, :, lanes] = small[groups + three * j : groups + three * (j + 1)]

    at = pl.ds(pl.multiple_of(i * tokens, 16), tokens)
    gm = jnp.concatenate(
        [jnp.concatenate([held[k, owner, at, :] for owner in range(ndp)], axis=1) for k in range(2)], axis=0
    )
    for dx in range(ncol):
        start = pl.multiple_of(wrapped(col - dx, ncol) * depth, depth)
        x = jnp.concatenate(
            [x_ref[:, dx].reshape(tokens, depth) for x_ref in (x0_ref, x1_ref)], axis=0
        )
        out_ref[0, pl.ds(start, depth), :] = scale * lax.dot_general(
            x, gm, (((0,), (0,)), ((), ())), preferred_element_type=F32
        )


def delayed(values, count):
    row = lax.broadcasted_iota(jnp.int32, values.shape, 0)
    return jnp.where(row >= count, pltpu.roll(values, count, 0), 0.0)


def advanced(values, count):
    rows = values.shape[0]
    row = lax.broadcasted_iota(jnp.int32, values.shape, 0)
    return jnp.where(row < rows - count, pltpu.roll(values, rows - count, 0), 0.0)


def middle_body(scale, nshort, nrow, *refs):
    sums, refs = (refs[:3], refs[3:6]), refs[6:]
    (sf_ref, causal_ref, anti_ref), refs = refs[:3], refs[3:]
    *refs, m_ref, gm_ref, mixed_ref, go_ref = refs
    ndp = len(refs) // 2 - 1
    go_refs, (near_ref, other_ref), mixed_refs = refs[:ndp], refs[ndp : ndp + 2], refs[ndp + 2 :]
    tokens, width = go_ref.shape
    for behind, piece in enumerate(go_refs):
        at = wrapped(lax.axis_index("dp") - behind, ndp) * (tokens // ndp)
        go_ref[pl.ds(pl.multiple_of(at, 16), tokens // ndp)] = piece[...]
    row = lax.axis_index("row")
    nblocks = nrow // 2
    rows = tokens // nrow

    def places():
        for chunk, start in enumerate((row, row + 1 - 2 * lax.rem(row, 2))):
            for block in range(nblocks):
                at = tokens_of(wrapped(start - 2 * block, nrow), nrow) * rows
                for i in range(3):
                    yield chunk, (i * nblocks + block) * rows, pl.multiple_of(i * tokens + at, 16)

    for chunk, place, at in places():
        held = [ref[place : place + rows].astype(F32) for ref in sums[chunk]]
        m_ref[pl.ds(at, rows)] = held[0] + held[1] + held[2]
    groups, block, span = causal_ref.shape
    members = width // groups
    nspans = tokens // block
    lane = lax.broadcasted_iota(jnp.int32, (block, width), 1) // members
    lanes = lax.broadcasted_iota(jnp.int32, (block, 2 * width), 1) % width // members

    def past(i, j):
        held = m_ref[i * tokens : (i + 1) * tokens]
        return held if j == 0 else delayed(held, j)

    def taps(j, i):
        return sf_ref[3 * j + i : 3 * j + i + 1, :]

    feats = [sum(taps(j, i) * past(i, j) for j in range(nshort)) for i in range(3)]
    product = (feats[1] * feats[2]).astype(BF16)
    zero = jnp.zeros((block, width), BF16)
    p_blocks = [zero] + [product[b * block : (b + 1) * block] for b in range(nspans)]
    p_pairs = [jnp.concatenate(p_blocks[b : b + 2], axis=0) for b in range(nspans)]

    def filtered(band_ref, pairs):
        bands = band_ref[...].reshape(groups * block, span)
        out = []
        for b in range(0, nspans, 2):
            both = jnp.dot(bands, jnp.concatenate(pairs[b : b + 2], axis=1), preferred_element_type=F32)
            for h in range(2):
                part = both[:, h * width : (h + 1) * width]
                picked = part[:block]
                for g in range(1, groups):
                    picked = jnp.where(lane == g, part[g * block : (g + 1) * block], picked)
                out.append(picked)
        return jnp.concatenate(out, axis=0)

    conv = filtered(causal_ref, p_pairs)
    upstream = go_ref[...].astype(F32)
    mixed_ref[...] = (feats[0] * conv).astype(BF16)
    for ahead, out_ref in enumerate(mixed_refs):
        at = pl.multiple_of(wrapped(lax.axis_index("dp") + ahead, ndp) * (tokens // ndp), 16)
        out_ref[...] = mixed_ref[pl.ds(at, tokens // ndp)]
    grad_conv = (upstream * feats[0]).astype(BF16)
    c_blocks = [grad_conv[b * block : (b + 1) * block] for b in range(nspans)] + [zero]
    c_pairs = [jnp.concatenate(c_blocks[b : b + 2], axis=0) for b in range(nspans)]
    grad_product = filtered(anti_ref, c_pairs)

    corr = jnp.zeros((groups * block, span), F32)
    for b in range(0, nspans, 2):
        left = jnp.concatenate(c_blocks[b : b + 2], axis=1)
        stacked = jnp.concatenate(
            [jnp.where(lanes == g, left, jnp.zeros_like(left)) for g in range(groups)], axis=0
        )
        right = jnp.concatenate(p_pairs[b : b + 2], axis=1)
        corr += lax.dot_general(stacked, right, (((1,), (1,)), ((), ())), preferred_element_type=F32)
    turn = lax.broadcasted_iota(jnp.int32, (8, span), 0)
    sums = []
    for g in range(groups):
        part = corr[g * block : (g + 1) * block]
        count = block
        while count > 8:
            count //= 2
            part = part[:count] + pltpu.roll(part[count:], span - count, 1)
        for bit in (1, 2, 4):
            part = jnp.where((turn & bit) != 0, pltpu.roll(part, span - bit, 1), part)
        sums.append(jnp.sum(part, axis=0, keepdims=True))
    by_lag = jnp.concatenate(sums, axis=0)
    by_lag = (scale * pltpu.roll(by_lag, span - 1, 1)[:, :block]).astype(BF16)
    ahead = lax.broadcasted_iota(jnp.int32, (block, block), 0)
    back = lax.broadcasted_iota(jnp.int32, (block, block), 1)
    turned = jnp.where(ahead + back == block - 1, 1.0, 0.0).astype(BF16)
    by_lag = jnp.dot(by_lag, turned, preferred_element_type=F32)

    grad_feats = [upstream * conv, grad_product * feats[2], grad_product * feats[1]]
    short_rows = []
    for j in range(nshort):
        for i in range(3):
            short_rows.append(scale * jnp.sum(grad_feats[i] * past(i, j), axis=0, keepdims=True))
    for i in range(3):
        total = taps(0, i) * grad_feats[i]
        for j in range(1, nshort):
            total += taps(j, i) * advanced(grad_feats[i], j)
        gm_ref[i * tokens : (i + 1) * tokens] = total.astype(BF16)
    for chunk, place, at in places():
        (near_ref, other_ref)[chunk][place : place + rows] = gm_ref[pl.ds(at, rows)]
    tail = near_ref.shape[0] - 3 * tokens // 2 - groups - 3 * nshort
    small = jnp.concatenate([by_lag] + short_rows + [jnp.zeros((tail, width), F32)], axis=0)
    near_ref[3 * tokens // 2 :] = small.astype(BF16)


def first_hop(far):
    ndp = lax.axis_size("dp")
    return (
        lax.ppermute(far, "dp", [(a, a + 1) for a in range(ndp // 2)]),
        lax.ppermute(far, "dp", [(a, a - 1) for a in range(ndp // 2, ndp)]),
    )


def second_hop(right, left, from_left, from_right):
    ndp = lax.axis_size("dp")
    rightward = lax.ppermute(right + from_left, "dp", [(a, (a + 1) % ndp) for a in range(ndp)])
    leftward = lax.ppermute(left + from_right, "dp", [(a, (a - 1) % ndp) for a in range(ndp)])
    return rightward, leftward


def gather_over_line(own, across):
    ndp, nrow = lax.axis_size("dp"), lax.axis_size("row")

    def pairs(dps, count, across):
        return [
            (a * nrow + r, (a + count) % ndp * nrow + (r + 1 - 2 * (r % 2) if across else r))
            for a in dps
            for r in range(nrow)
        ]

    before = lax.ppermute(own, ("dp", "row"), pairs(range(ndp), 1, False))
    after = lax.ppermute(own, ("dp", "row"), pairs(range(ndp), -1, False))
    far_before = lax.ppermute(before, ("dp", "row"), pairs(range(ndp // 2 - 1, ndp - 1), 1, across))
    far_after = lax.ppermute(after, ("dp", "row"), pairs(range(1, ndp // 2 + 1), -1, across))
    return own, before, after, far_before, far_after


def move_activations(tokens, in_weight, short_filter, long_filter, grad_out):
    ndp, nrow, ncol = (lax.axis_size(a) for a in ("dp", "row", "col"))
    z = lax.axis_index("dp")
    rows, dcol = tokens.shape
    local = grad_out.shape[1]
    nshort = short_filter.shape[0]
    ngroups, ntaps = long_filter.shape
    seq = rows * ndp
    width, groups = local // ndp, ngroups // ndp
    drow = in_weight.shape[0]
    scale = float(seq) ** -0.5
    nblocks = nrow // 2
    chunk = nblocks * rows
    swap = [(tokens_of(b, nrow) * nrow + a, a * nrow + b) for a in range(ndp) for b in range(nrow)]
    swap_back = [(b, a) for a, b in swap]
    partner = [(a, a + 1 - 2 * (a % 2)) for a in range(nrow)]
    places = [(dy, dx) for dy in range(nblocks) for dx in range(ncol)]

    def offset(dy, dx):
        return [
            (a * ncol + b, (a + 2 * dy) % nrow * ncol + (b + dx) % ncol) for a in range(nrow) for b in range(ncol)
        ]

    w = jnp.transpose(in_weight, (1, 0, 2))
    moved = lax.ppermute(tokens, ("dp", "row"), swap)
    far_w = kernel_call(
        far_columns_body,
        shaped((3, drow, width), BF16),
        in_specs=[pl.BlockSpec(memory_space=pl.ANY)],
        out_specs=pl.BlockSpec(memory_space=pltpu.VMEM),
        scratch=[pltpu.SemaphoreType.DMA],
    )(w)
    turn = [[(a, (a + ahead) % ndp) for a in range(ndp)] for ahead in range(ndp)]
    upstream = [*kernel_call(split_body, [shaped((rows, width), BF16)] * ndp)(grad_out)]
    upstream[1] = lax.ppermute(upstream[1], "dp", turn[1])
    moved, upstream, far_w = lax.optimization_barrier((moved, upstream, far_w))
    near = [moved] + [lax.ppermute(moved, ("row", "col"), offset(*p)) for p in places[1:]]
    for ahead in range(2, ndp):
        upstream[ahead] = lax.ppermute(upstream[ahead], "dp", turn[ahead])
    upstream[2:], near[1:] = lax.optimization_barrier((upstream[2:], near[1:]))
    x0 = jnp.stack(near).reshape(nblocks, ncol, rows, dcol)
    x1 = lax.ppermute(x0, "row", partner)

    sf = lax.dynamic_slice_in_dim(short_filter, z * width, width, 2).reshape(3 * nshort, width)
    lf = lax.dynamic_slice_in_dim(long_filter, z * groups, groups, 0).astype(F32)
    zeros = functools.partial(jnp.zeros, dtype=F32)
    bases = jnp.concatenate(
        [
            jnp.concatenate([zeros((groups, 1)), lf[:, ::-1], zeros((groups, ntaps - 1))], axis=1),
            jnp.concatenate([lf, zeros((groups, ntaps))], axis=1),
        ],
        axis=0,
    )
    bands = kernel_call(bands_body, shaped((2 * groups, ntaps, 2 * ntaps), BF16))(bases)

    mm_flops = seq * drow * 3 * local
    mm_bytes = seq * drow + 6 * drow * local + 3 * seq * local
    shares, passed, sums = [], [], []
    for x in (x0, x1):
        parts = kernel_call(
            project_body,
            [shaped((3, chunk, width), BF16)] * ndp,
            grid=(3,),
            in_specs=[
                pl.BlockSpec((nblocks, ncol, rows, dcol), lambda i: (0, 0, 0, 0)),
                pl.BlockSpec((1, drow, local), lambda i: (i, 0, 0)),
            ],
            out_specs=[pl.BlockSpec((1, chunk, width), lambda i: (i, 0, 0))] * ndp,
            scratch=[pltpu.VMEM((ndp, chunk, width), BF16)],
            flops=mm_flops,
            nbytes=mm_bytes,
        )(x, w)
        shares.append([p.reshape(3 * chunk, width) for p in parts])
        passed.append(first_hop(shares[-1][2]))
    passed[0], shares[1] = lax.optimization_barrier((passed[0], shares[1]))
    for (own, right, _, left), came in zip(shares, passed):
        sums += [own, *second_hop(right, left, *came)]

    partner_far_w = lax.ppermute(far_w, "row", partner)
    sums, partner_far_w = lax.optimization_barrier((sums, partner_far_w))
    extra = -(-(groups + 3 * nshort) // 16) * 16
    half = pl.BlockSpec((groups, ntaps, 2 * ntaps), lambda i: (0, 0, 0))
    other = pl.BlockSpec((groups, ntaps, 2 * ntaps), lambda i: (1, 0, 0))
    whole = lambda *shape: pl.BlockSpec(shape, lambda i: (0,) * len(shape))
    grad_near, grad_other, *mixed = kernel_call(
        functools.partial(middle_body, scale, nshort, nrow),
        [shaped((3 * chunk + extra, width), BF16), shaped((3 * chunk, width), BF16)]
        + [shaped((rows, width), BF16)] * ndp,
        grid=(1,),
        in_specs=[whole(3 * chunk, width)] * 6
        + [whole(3 * nshort, width), half, other]
        + [whole(rows, width)] * ndp,
        out_specs=[whole(3 * chunk + extra, width), whole(3 * chunk, width)] + [whole(rows, width)] * ndp,
        scratch=[
            pltpu.VMEM((3 * seq, width), F32),
            pltpu.VMEM((3 * seq, width), BF16),
            pltpu.VMEM((seq, width), BF16),
            pltpu.VMEM((seq, width), BF16),
        ],
        flops=3 * 2 * groups * ntaps * 2 * ntaps * width * (seq // ntaps),
        nbytes=2 * width * seq * 14,
        vmem=MOST_VMEM_BYTES,
    )(*sums, sf, bands, bands, *upstream)
    *near, near_far_before, near_far_after = gather_over_line(grad_near, False)
    *far, far_far_before, far_far_after = gather_over_line(grad_other, True)
    near, far = lax.optimization_barrier((near, far))
    parts = [
        kernel_call(
            first_grad_body,
            shaped((ncol, chunk, dcol), dtype),
            scratch=[pltpu.VMEM((ndp, 3 * chunk, width), BF16)],
            flops=mm_flops,
            nbytes=mm_bytes,
        )(*pieces, w)
        for pieces, dtype in ((far, BF16), (near, F32))
    ]
    for ahead in range(1, ndp):
        mixed[ahead] = lax.ppermute(mixed[ahead], "dp", turn[ahead])
    from_partner = lax.ppermute(parts[0], "row", partner)
    everywhere = pl.BlockSpec(memory_space=pl.ANY)
    in_vmem = pl.BlockSpec(memory_space=pltpu.VMEM)
    near_last, far_last, *blocks = kernel_call(
        functools.partial(second_grad_body, ndp),
        [shaped(grad_near.shape, BF16), shaped(grad_other.shape, BF16)]
        + [shaped((rows, dcol), BF16)] * len(places),
        in_specs=[everywhere] * 8,
        out_specs=[in_vmem] * (2 + len(places)),
        scratch=[
            pltpu.VMEM(far_w.shape, BF16),
            pltpu.VMEM(far_w.shape, BF16),
            pltpu.VMEM((ncol, chunk, dcol), F32),
            pltpu.VMEM((ncol, chunk, dcol), BF16),
            pltpu.SemaphoreType.DMA((6,)),
        ],
        flops=mm_flops // 2,
        nbytes=mm_bytes // 2,
        vmem=MOST_VMEM_BYTES,
    )(near_far_before, near_far_after, far_far_before, far_far_after, far_w, partner_far_w, parts[1], from_partner)
    blocks[1], mixed[1:] = lax.optimization_barrier((blocks[1], mixed[1:]))
    far_last = lax.ppermute(far_last, "row", partner)
    arrivals = [
        lax.ppermute(sent, ("row", "col"), [(b, a) for a, b in offset(*p)])
        for p, sent in zip(places[1:], blocks[1:])
    ]
    arrived = sum((a.astype(F32) for a in arrivals), blocks[0].astype(F32)).astype(BF16)
    arrived, far_last = lax.optimization_barrier((arrived, far_last))
    grad_in = lax.ppermute(arrived, ("dp", "row"), swap_back)

    grad_weight, mixed, grad_long, grad_short = kernel_call(
        functools.partial(weight_grad_body, scale),
        [
            shaped((3, drow, local), F32),
            shaped((rows, local), BF16),
            shaped((ngroups, ntaps), F32),
            shaped((nshort, 3, local), F32),
        ],
        grid=(3,),
        in_specs=[whole(nblocks, ncol, rows, dcol)] * 2
        + [whole(*grad_near.shape)] * 4
        + [whole(*grad_other.shape)] * 4
        + [whole(rows, width)] * ndp,
        out_specs=[
            pl.BlockSpec((1, drow, local), lambda i: (i, 0, 0)),
            whole(rows, local),
            whole(ngroups, ntaps),
            whole(nshort, 3, local),
        ],
        scratch=[
            pltpu.VMEM((2, ndp, 3 * chunk + extra, width), BF16),
            pltpu.VMEM((ndp, rows, width), BF16),
        ],
        flops=2 * mm_flops,
        nbytes=2 * mm_bytes,
        vmem=MOST_VMEM_BYTES,
    )(x0, x1, *near, near_last, *far, far_last, *mixed)
    grad_weight = jnp.transpose(grad_weight, (1, 0, 2))
    return (mixed, grad_in, grad_weight, grad_long, grad_short)


def from_behind(block, axis, distance):
    devices = range(lax.axis_size(axis))
    route = [(i - distance, i) for i in devices if i - distance in devices]
    return lax.ppermute(block, axis, route)


def toeplitz(leading, rows, span):
    groups = leading.shape[0]
    width = rows + span
    seed_row = jnp.concatenate(
        [leading, jnp.zeros((groups, width - leading.shape[1]), leading.dtype)], axis=1
    )
    tiled = jnp.tile(seed_row, (1, rows))
    skewed = tiled[:, : rows * (width - 1)].reshape(groups, rows, width - 1)
    return skewed[:, :, :span]


def to_groups(values, ngroups, members):
    count = values.shape[0]
    return values.reshape(count, ngroups, members).transpose(1, 2, 0)


def from_groups(values):
    groups, members, count = values.shape
    return values.transpose(2, 0, 1).reshape(count, groups * members)


def move_weights(tokens, in_weight, short_filter, long_filter, grad_out):
    rows = tokens.shape[0]
    local = grad_out.shape[1]
    nshort = short_filter.shape[0]
    ntaps = long_filter.shape[1]
    ngroups = long_filter.shape[0]
    members = local // ngroups
    margin = ntaps - 1
    span = rows + margin
    scale = float(rows * lax.axis_size("dp")) ** (-0.5)
    whole = lax.all_gather(tokens, ("row", "col"), axis=1, tiled=True)
    full_w = lax.all_gather(in_weight, "dp", axis=0, tiled=True)
    mixed_in = jnp.einsum("sd,dic->sic", whole, full_w, preferred_element_type=jnp.float32).astype(
        jnp.bfloat16
    )
    before = from_behind(mixed_in[rows - margin - nshort + 1 :], "dp", 1)
    extended = jnp.concatenate([before, mixed_in], axis=0).astype(jnp.float32)
    long_feats = jnp.zeros((span, 3, local), jnp.float32)
    for j in range(nshort):
        long_feats = (
            long_feats + short_filter[j][None] * extended[nshort - 1 - j : nshort - 1 - j + span]
        )
    product_ext = (long_feats[:, 1] * long_feats[:, 2]).astype(jnp.bfloat16)
    feats = long_feats[margin:]
    short_rows = extended[margin:]
    product_cols = to_groups(product_ext, ngroups, members)
    causal = toeplitz(long_filter[:, ::-1], rows, span)
    conv = from_groups(
        jnp.einsum("gst,gct->gcs", causal, product_cols, preferred_element_type=jnp.float32)
    )
    mixed = (feats[:, 0] * conv).astype(jnp.bfloat16)
    upstream = grad_out.astype(jnp.float32)
    grad_query = upstream * conv
    grad_conv = (upstream * feats[:, 0]).astype(jnp.bfloat16)
    after = from_behind(grad_conv[:margin], "dp", -1)
    grad_ext = jnp.concatenate([grad_conv, after], axis=0)
    anti = toeplitz(long_filter, rows, span)
    grad_product = from_groups(
        jnp.einsum(
            "gst,gct->gcs",
            anti,
            to_groups(grad_ext, ngroups, members),
            preferred_element_type=jnp.float32,
        )
    )
    reversed_cols = jnp.concatenate(
        [product_cols[:, :, ::-1], jnp.zeros((ngroups, members, rows), product_cols.dtype)], axis=2
    )
    width = span + rows
    pairs = jnp.einsum(
        "gcs,gcu->gsu",
        to_groups(grad_conv, ngroups, members),
        reversed_cols,
        preferred_element_type=jnp.float32,
    )
    diagonal = pairs.reshape(ngroups, rows * width)[:, : rows * (width - 1)].reshape(
        ngroups, rows, width - 1
    )
    filter_part = jnp.sum(diagonal[:, :, rows - 1 : rows - 1 + ntaps], axis=1)
    grad_feats = jnp.stack(
        [grad_query, grad_product * feats[:, 2], grad_product * feats[:, 1]], axis=1
    )
    later = from_behind(grad_feats[: nshort - 1], "dp", -1)
    feats_ext = jnp.concatenate([grad_feats, later], axis=0)
    grad_acc = jnp.zeros((rows, 3, local), jnp.float32)
    for j in range(nshort):
        grad_acc = grad_acc + short_filter[j][None] * feats_ext[j : j + rows]
    grad_mixed = grad_acc.astype(jnp.bfloat16)
    short_part = jnp.stack(
        [
            jnp.sum(grad_feats * short_rows[nshort - 1 - j : nshort - 1 - j + rows], axis=0)
            for j in range(nshort)
        ]
    )
    filter_total, short_total = (
        lax.psum(filter_part.astype(jnp.bfloat16), "dp").astype(jnp.float32),
        lax.psum(short_part.astype(jnp.bfloat16), "dp").astype(jnp.float32),
    )
    grad_long = filter_total * scale
    grad_short = short_total * scale
    partial_in = jnp.einsum("sic,dic->sd", grad_mixed, full_w, preferred_element_type=jnp.float32)
    summed_in = lax.psum_scatter(
        partial_in.astype(jnp.bfloat16), ("row", "col"), scatter_dimension=1, tiled=True
    )
    weight_term = (
        jnp.einsum("sd,sic->dic", whole, grad_mixed, preferred_element_type=jnp.float32) * scale
    )
    grad_weight = lax.psum_scatter(
        weight_term.astype(jnp.bfloat16), "dp", scatter_dimension=0, tiled=True
    ).astype(jnp.float32)
    return (mixed, summed_in, grad_weight, grad_long, grad_short)


def fits_whole_sequences(mesh, tokens, in_weight, short_filter, long_filter, grad_out):
    ndp, nrow, ncol = (mesh.shape[a] for a in ("dp", "row", "col"))
    seq, channels = grad_out.shape
    groups, ntaps = long_filter.shape
    local = channels // (nrow * ncol)
    width, rows = local // ndp, seq // ndp
    return (
        seq < tokens.shape[1]
        and ndp == nrow == 4
        and ncol * (tokens.shape[1] // (nrow * ncol)) == in_weight.shape[0] // ndp
        and ntaps == width == 128
        and seq % (2 * ntaps) == 0
        and rows % 16 == 0
        and groups % (8 * ndp * nrow * ncol) == 0
    )


def solution(mesh):
    placed = (
        P("dp", ("row", "col")),
        P("dp", None, ("row", "col")),
        P(None, None, ("row", "col")),
        P(("row", "col"), None),
        P("dp", ("row", "col")),
    )
    gives = (
        P("dp", ("row", "col")),
        P("dp", ("row", "col")),
        P("dp", None, ("row", "col")),
        P(("row", "col"), None),
        P(None, None, ("row", "col")),
    )

    def run(*arrays):
        plan = move_activations if fits_whole_sequences(mesh, *arrays) else move_weights
        return jax.shard_map(
            plan, mesh=mesh, in_specs=placed, out_specs=gives, check_vma=False
        )(*arrays)

    return run
```

```python
import functools

import jax
import jax.numpy as jnp
from jax import lax
from jax.experimental import pallas as pl
from jax.experimental.pallas import tpu as pltpu
from jax.sharding import PartitionSpec as P

VMEM_BYTES = 48 * 2**20
MOST_VMEM_BYTES = 62 * 2**20
F32 = jnp.float32
BF16 = jnp.bfloat16


def kernel_call(body, outs, grid=(), in_specs=None, out_specs=None, scratch=(), flops=0, nbytes=0, vmem=VMEM_BYTES):
    kwargs = {}
    if in_specs is not None:
        kwargs = dict(grid=grid, in_specs=in_specs, out_specs=out_specs)
    return pl.pallas_call(
        body,
        out_shape=outs,
        scratch_shapes=scratch,
        compiler_params=pltpu.CompilerParams(vmem_limit_bytes=vmem),
        cost_estimate=pl.CostEstimate(flops=flops, bytes_accessed=nbytes, transcendentals=0),
        **kwargs,
    )


def shaped(shape, dtype):
    return jax.ShapeDtypeStruct(shape, dtype)


def bands_body(base_ref, out_ref):
    groups, wide = base_ref.shape
    rows = out_ref.shape[1]
    row = lax.broadcasted_iota(jnp.int32, (8, wide), 0)
    for g in range(groups):
        band = jnp.broadcast_to(base_ref[g : g + 1, :], (8, wide))
        for bit in (1, 2, 4):
            band = jnp.where((row & bit) != 0, pltpu.roll(band, bit, 1), band)
        count = 8
        while count < rows:
            band = jnp.concatenate([band, pltpu.roll(band, count, 1)], axis=0)
            count *= 2
        out_ref[g] = band.astype(out_ref.dtype)


def tokens_of(row, nrow):
    return row % 2 * (nrow // 2) + row // 2


def wrapped(value, size):
    return lax.rem(value + 2 * size, size)


def split_body(all_ref, *out_refs):
    width = out_refs[0].shape[1]
    for ahead, out_ref in enumerate(out_refs):
        at = wrapped(lax.axis_index("dp") + ahead, len(out_refs)) * width
        out_ref[...] = all_ref[:, pl.ds(pl.multiple_of(at, width), width)]


def project_body(x_ref, w_ref, *refs):
    *out_refs, held = refs
    z, col = lax.axis_index("dp"), lax.axis_index("col")
    nblocks, ncol, rows, depth = x_ref.shape
    width = held.shape[2]
    total = jnp.zeros((nblocks * rows, w_ref.shape[2]), F32)
    for dx in range(ncol):
        start = pl.multiple_of(wrapped(col - dx, ncol) * depth, depth)
        total += jnp.dot(
            x_ref[:, dx].reshape(nblocks * rows, depth),
            w_ref[0, pl.ds(start, depth), :],
            preferred_element_type=F32,
        )
    for owner in range(len(out_refs)):
        held[owner] = total[:, owner * width : (owner + 1) * width].astype(BF16)
    for ahead, out_ref in enumerate(out_refs):
        out_ref[0] = held[wrapped(z + ahead, len(out_refs))]


def far_columns_body(w_ref, out_ref, sem):
    ndp = lax.axis_size("dp")
    width = out_ref.shape[2]
    start = wrapped(lax.axis_index("dp") + ndp // 2, ndp) * width
    copy = pltpu.make_async_copy(w_ref.at[:, :, pl.ds(pl.multiple_of(start, width), width)], out_ref, sem)
    copy.start()
    copy.wait()


def first_grad_body(near, near_before, near_after, far, far_before, far_after, w_ref, partner_w_ref, out_ref, far_ref, held):
    ndp, _, width = held.shape
    ncol, tokens, depth = out_ref.shape
    z, col = lax.axis_index("dp"), lax.axis_index("col")
    far_ref[0], far_ref[1] = far_before[...], far_after[...]
    for pieces, weights, first in (
        ((near, near_before, near_after), w_ref, True),
        ((far, far_before, far_after), partner_w_ref, False),
    ):
        held[wrapped(z + ndp // 2, ndp)] = jnp.zeros(held.shape[1:], BF16)
        for ahead, piece in zip((0, -1, 1), pieces):
            held[wrapped(z + ahead, ndp)] = piece[: 3 * tokens]
        for dx in range(ncol):
            start = pl.multiple_of(wrapped(col - dx, ncol) * depth, depth)
            total = jnp.zeros((tokens, depth), F32) if first else out_ref[dx]
            for i in range(3):
                rows = slice(i * tokens, (i + 1) * tokens)
                total += lax.dot_general(
                    jnp.concatenate([held[owner, rows] for owner in range(ndp)], axis=1),
                    weights[i, pl.ds(start, depth), :],
                    (((1,), (1,)), ((), ())),
                    preferred_element_type=F32,
                )
            out_ref[dx] = total


def second_grad_body(ndp, part_ref, *refs):
    arrived, (w_ref, partner_w_ref), refs = (refs[:2], refs[2:4]), refs[4:6], refs[6:]
    (near_ref, far_ref), refs = refs[:2], refs[2:]
    *out_refs, held_w, held_part, sems = refs
    ncol, tokens, depth = held_part.shape
    rows = out_refs[0].shape[0]
    width = near_ref.shape[1]
    z, col = lax.axis_index("dp"), lax.axis_index("col")
    lanes = pl.ds(pl.multiple_of(wrapped(z + ndp // 2, ndp) * width, width), width)
    copies = [
        pltpu.make_async_copy(w_ref, held_w.at[0], sems.at[0]),
        pltpu.make_async_copy(partner_w_ref.at[:, :, lanes], held_w.at[1], sems.at[1]),
    ]
    copies.append(pltpu.make_async_copy(part_ref, held_part, sems.at[2]))
    for copy in copies:
        copy.start()
    for k, (pair, target) in enumerate(zip(arrived, (near_ref, far_ref))):
        for source, here in zip(pair, (z >= ndp // 2, z < ndp // 2)):

            @pl.when(here)
            def _(source=source, target=target, k=k):
                copy = pltpu.make_async_copy(source, target, sems.at[3 + k])
                copy.start()
                copy.wait()

    for copy in copies:
        copy.wait()
    left = jnp.concatenate(
        [ref[i * tokens : (i + 1) * tokens] for ref in (near_ref, far_ref) for i in range(3)], axis=1
    )
    for dx in range(ncol):
        start = pl.multiple_of(wrapped(col - dx, ncol) * depth, depth)
        right = jnp.concatenate([held_w[k, i, pl.ds(start, depth), :] for k in range(2) for i in range(3)], axis=1)
        total = held_part[dx] + lax.dot_general(
            left, right, (((1,), (1,)), ((), ())), preferred_element_type=F32
        )
        for block in range(tokens // rows):
            out_refs[block * ncol + dx][...] = total[block * rows : (block + 1) * rows].astype(BF16)


def weight_grad_body(scale, *refs):
    (x0_ref, x1_ref), near_refs, other_refs, mixed_refs, refs = refs[:2], refs[2:6], refs[6:9], refs[9:13], refs[13:]
    own_ref, two_ref, last_ref = other_refs
    other = (own_ref, two_ref.at[0], two_ref.at[1], last_ref)
    out_ref, mixed_ref, long_ref, short_ref, held, held_mixed = refs
    nblocks, ncol, rows, depth = x0_ref.shape
    _, ndp, _, width = held.shape
    tokens = nblocks * rows
    i = pl.program_id(0)
    z, col = lax.axis_index("dp"), lax.axis_index("col")

    @pl.when(i == 0)
    def _():
        groups = long_ref.shape[0] // ndp
        for k, ahead in enumerate((0, -1, 1, 2)):
            owner = wrapped(z + ahead, ndp)
            held[0, owner] = near_refs[k][...]
            held[1, owner, : 3 * tokens] = other[k][...]
        for back in range(ndp):
            held_mixed[wrapped(z - back, ndp)] = mixed_refs[back][...]
        for owner in range(ndp):
            lanes = slice(owner * width, (owner + 1) * width)
            mixed_ref[:, lanes] = held_mixed[owner]
            small = held[0, owner, 3 * tokens :].astype(F32)
            long_ref[owner * groups : (owner + 1) * groups] = small[:groups]
            nshort, three, _ = short_ref.shape
            for j in range(nshort):
                short_ref[j, :, lanes] = small[groups + three * j : groups + three * (j + 1)]

    at = pl.ds(pl.multiple_of(i * tokens, 16), tokens)
    gm = jnp.concatenate(
        [jnp.concatenate([held[k, owner, at, :] for owner in range(ndp)], axis=1) for k in range(2)], axis=0
    )
    for dx in range(ncol):
        start = pl.multiple_of(wrapped(col - dx, ncol) * depth, depth)
        x = jnp.concatenate(
            [x_ref[:, dx].reshape(tokens, depth) for x_ref in (x0_ref, x1_ref)], axis=0
        )
        out_ref[0, pl.ds(start, depth), :] = scale * lax.dot_general(
            x, gm, (((0,), (0,)), ((), ())), preferred_element_type=F32
        )


def delayed(values, count):
    row = lax.broadcasted_iota(jnp.int32, values.shape, 0)
    return jnp.where(row >= count, pltpu.roll(values, count, 0), 0.0)


def advanced(values, count):
    rows = values.shape[0]
    row = lax.broadcasted_iota(jnp.int32, values.shape, 0)
    return jnp.where(row < rows - count, pltpu.roll(values, rows - count, 0), 0.0)


def middle_body(scale, nshort, nrow, *refs):
    sums, refs = (refs[:3], refs[3:6]), refs[6:]
    (sf_ref, causal_ref, anti_ref), refs = refs[:3], refs[3:]
    *refs, m_ref, gm_ref, mixed_ref, go_ref = refs
    ndp = len(refs) // 2 - 1
    go_refs, (near_ref, other_ref), mixed_refs = refs[:ndp], refs[ndp : ndp + 2], refs[ndp + 2 :]
    tokens, width = go_ref.shape
    for behind, piece in enumerate(go_refs):
        at = wrapped(lax.axis_index("dp") - behind, ndp) * (tokens // ndp)
        go_ref[pl.ds(pl.multiple_of(at, 16), tokens // ndp)] = piece[...]
    row = lax.axis_index("row")
    nblocks = nrow // 2
    rows = tokens // nrow

    def places():
        for chunk, start in enumerate((row, row + 1 - 2 * lax.rem(row, 2))):
            for block in range(nblocks):
                at = tokens_of(wrapped(start - 2 * block, nrow), nrow) * rows
                for i in range(3):
                    yield chunk, (i * nblocks + block) * rows, pl.multiple_of(i * tokens + at, 16)

    for chunk, place, at in places():
        held = [ref[place : place + rows].astype(F32) for ref in sums[chunk]]
        m_ref[pl.ds(at, rows)] = held[0] + held[1] + held[2]
    groups, block, span = causal_ref.shape
    members = width // groups
    nspans = tokens // block
    lane = lax.broadcasted_iota(jnp.int32, (block, width), 1) // members
    lanes = lax.broadcasted_iota(jnp.int32, (block, 2 * width), 1) % width // members

    def past(i, j):
        held = m_ref[i * tokens : (i + 1) * tokens]
        return held if j == 0 else delayed(held, j)

    def taps(j, i):
        return sf_ref[3 * j + i : 3 * j + i + 1, :]

    feats = [sum(taps(j, i) * past(i, j) for j in range(nshort)) for i in range(3)]
    product = (feats[1] * feats[2]).astype(BF16)
    zero = jnp.zeros((block, width), BF16)
    p_blocks = [zero] + [product[b * block : (b + 1) * block] for b in range(nspans)]
    p_pairs = [jnp.concatenate(p_blocks[b : b + 2], axis=0) for b in range(nspans)]

    def filtered(band_ref, pairs):
        bands = band_ref[...].reshape(groups * block, span)
        out = []
        for b in range(0, nspans, 2):
            both = jnp.dot(bands, jnp.concatenate(pairs[b : b + 2], axis=1), preferred_element_type=F32)
            for h in range(2):
                part = both[:, h * width : (h + 1) * width]
                picked = part[:block]
                for g in range(1, groups):
                    picked = jnp.where(lane == g, part[g * block : (g + 1) * block], picked)
                out.append(picked)
        return jnp.concatenate(out, axis=0)

    conv = filtered(causal_ref, p_pairs)
    upstream = go_ref[...].astype(F32)
    mixed_ref[...] = (feats[0] * conv).astype(BF16)
    for ahead, out_ref in enumerate(mixed_refs):
        at = pl.multiple_of(wrapped(lax.axis_index("dp") + ahead, ndp) * (tokens // ndp), 16)
        out_ref[...] = mixed_ref[pl.ds(at, tokens // ndp)]
    grad_conv = (upstream * feats[0]).astype(BF16)
    c_blocks = [grad_conv[b * block : (b + 1) * block] for b in range(nspans)] + [zero]
    c_pairs = [jnp.concatenate(c_blocks[b : b + 2], axis=0) for b in range(nspans)]
    grad_product = filtered(anti_ref, c_pairs)

    corr = jnp.zeros((groups * block, span), F32)
    for b in range(0, nspans, 2):
        left = jnp.concatenate(c_blocks[b : b + 2], axis=1)
        stacked = jnp.concatenate(
            [jnp.where(lanes == g, left, jnp.zeros_like(left)) for g in range(groups)], axis=0
        )
        right = jnp.concatenate(p_pairs[b : b + 2], axis=1)
        corr += lax.dot_general(stacked, right, (((1,), (1,)), ((), ())), preferred_element_type=F32)
    turn = lax.broadcasted_iota(jnp.int32, (8, span), 0)
    sums = []
    for g in range(groups):
        part = corr[g * block : (g + 1) * block]
        count = block
        while count > 8:
            count //= 2
            part = part[:count] + pltpu.roll(part[count:], span - count, 1)
        for bit in (1, 2, 4):
            part = jnp.where((turn & bit) != 0, pltpu.roll(part, span - bit, 1), part)
        sums.append(jnp.sum(part, axis=0, keepdims=True))
    by_lag = jnp.concatenate(sums, axis=0)
    by_lag = (scale * pltpu.roll(by_lag, span - 1, 1)[:, :block]).astype(BF16)
    ahead = lax.broadcasted_iota(jnp.int32, (block, block), 0)
    back = lax.broadcasted_iota(jnp.int32, (block, block), 1)
    turned = jnp.where(ahead + back == block - 1, 1.0, 0.0).astype(BF16)
    by_lag = jnp.dot(by_lag, turned, preferred_element_type=F32)

    grad_feats = [upstream * conv, grad_product * feats[2], grad_product * feats[1]]
    short_rows = []
    for j in range(nshort):
        for i in range(3):
            short_rows.append(scale * jnp.sum(grad_feats[i] * past(i, j), axis=0, keepdims=True))
    for i in range(3):
        total = taps(0, i) * grad_feats[i]
        for j in range(1, nshort):
            total += taps(j, i) * advanced(grad_feats[i], j)
        gm_ref[i * tokens : (i + 1) * tokens] = total.astype(BF16)
    for chunk, place, at in places():
        (near_ref, other_ref)[chunk][place : place + rows] = gm_ref[pl.ds(at, rows)]
    tail = near_ref.shape[0] - 3 * tokens // 2 - groups - 3 * nshort
    small = jnp.concatenate([by_lag] + short_rows + [jnp.zeros((tail, width), F32)], axis=0)
    near_ref[3 * tokens // 2 :] = small.astype(BF16)


def sum_over_line(own, right, far, left):
    ndp = lax.axis_size("dp")
    from_left = lax.ppermute(far, "dp", [(a, a + 1) for a in range(ndp // 2)])
    from_right = lax.ppermute(far, "dp", [(a, a - 1) for a in range(ndp // 2, ndp)])
    rightward = lax.ppermute(right + from_left, "dp", [(a, (a + 1) % ndp) for a in range(ndp)])
    leftward = lax.ppermute(left + from_right, "dp", [(a, (a - 1) % ndp) for a in range(ndp)])
    return own, rightward, leftward


def gather_over_line(own, across):
    ndp, nrow = lax.axis_size("dp"), lax.axis_size("row")

    def shift(count):
        return [
            (a * nrow + r, (a + count) % ndp * nrow + (r + 1 - 2 * (r % 2) if across else r))
            for a in range(ndp)
            for r in range(nrow)
        ]

    before = lax.ppermute(own, ("dp", "row"), shift(1))
    after = lax.ppermute(own, ("dp", "row"), shift(-1))
    here = lax.ppermute(own, ("dp", "row"), shift(0)) if across else own
    far_before = lax.ppermute(before, "dp", [(a - 1, a) for a in range(ndp // 2, ndp)])
    far_after = lax.ppermute(after, "dp", [(a + 1, a) for a in range(ndp // 2)])
    return here, before, after, far_before, far_after


def move_activations(tokens, in_weight, short_filter, long_filter, grad_out):
    ndp, nrow, ncol = (lax.axis_size(a) for a in ("dp", "row", "col"))
    z = lax.axis_index("dp")
    rows, dcol = tokens.shape
    local = grad_out.shape[1]
    nshort = short_filter.shape[0]
    ngroups, ntaps = long_filter.shape
    seq = rows * ndp
    width, groups = local // ndp, ngroups // ndp
    drow = in_weight.shape[0]
    scale = float(seq) ** -0.5
    nblocks = nrow // 2
    chunk = nblocks * rows
    swap = [(tokens_of(b, nrow) * nrow + a, a * nrow + b) for a in range(ndp) for b in range(nrow)]
    swap_back = [(b, a) for a, b in swap]
    partner = [(a, a + 1 - 2 * (a % 2)) for a in range(nrow)]
    places = [(dy, dx) for dy in range(nblocks) for dx in range(ncol)]

    def offset(dy, dx):
        return [
            (a * ncol + b, (a + 2 * dy) % nrow * ncol + (b + dx) % ncol) for a in range(nrow) for b in range(ncol)
        ]

    w = jnp.transpose(in_weight, (1, 0, 2))
    moved = lax.ppermute(tokens, ("dp", "row"), swap)
    far_w = kernel_call(
        far_columns_body,
        shaped((3, drow, width), BF16),
        in_specs=[pl.BlockSpec(memory_space=pl.ANY)],
        out_specs=pl.BlockSpec(memory_space=pltpu.VMEM),
        scratch=[pltpu.SemaphoreType.DMA],
    )(w)
    turn = [[(a, (a + ahead) % ndp) for a in range(ndp)] for ahead in range(ndp)]
    upstream = [*kernel_call(split_body, [shaped((rows, width), BF16)] * ndp)(grad_out)]
    moved, upstream, far_w = lax.optimization_barrier((moved, upstream, far_w))
    near = [moved] + [lax.ppermute(moved, ("row", "col"), offset(*p)) for p in places[1:]]
    for ahead in (1, 3):
        upstream[ahead] = lax.ppermute(upstream[ahead], "dp", turn[ahead])
    upstream[1::2], near[1:] = lax.optimization_barrier((upstream[1::2], near[1:]))
    x0 = jnp.stack(near).reshape(nblocks, ncol, rows, dcol)
    x1 = lax.ppermute(x0, "row", partner)
    upstream[2] = lax.ppermute(upstream[2], "dp", turn[2])
    upstream[2], x1 = lax.optimization_barrier((upstream[2], x1))

    sf = lax.dynamic_slice_in_dim(short_filter, z * width, width, 2).reshape(3 * nshort, width)
    lf = lax.dynamic_slice_in_dim(long_filter, z * groups, groups, 0).astype(F32)
    zeros = functools.partial(jnp.zeros, dtype=F32)
    bases = jnp.concatenate(
        [
            jnp.concatenate([zeros((groups, 1)), lf[:, ::-1], zeros((groups, ntaps - 1))], axis=1),
            jnp.concatenate([lf, zeros((groups, ntaps))], axis=1),
        ],
        axis=0,
    )
    bands = kernel_call(bands_body, shaped((2 * groups, ntaps, 2 * ntaps), BF16))(bases)

    mm_flops = seq * drow * 3 * local
    mm_bytes = seq * drow + 6 * drow * local + 3 * seq * local
    sums = []
    for x in (x0, x1):
        parts = kernel_call(
            project_body,
            [shaped((3, chunk, width), BF16)] * ndp,
            grid=(3,),
            in_specs=[
                pl.BlockSpec((nblocks, ncol, rows, dcol), lambda i: (0, 0, 0, 0)),
                pl.BlockSpec((1, drow, local), lambda i: (i, 0, 0)),
            ],
            out_specs=[pl.BlockSpec((1, chunk, width), lambda i: (i, 0, 0))] * ndp,
            scratch=[pltpu.VMEM((ndp, chunk, width), BF16)],
            flops=mm_flops,
            nbytes=mm_bytes,
        )(x, w)
        sums += sum_over_line(*(p.reshape(3 * chunk, width) for p in parts))

    extra = -(-(groups + 3 * nshort) // 16) * 16
    half = pl.BlockSpec((groups, ntaps, 2 * ntaps), lambda i: (0, 0, 0))
    other = pl.BlockSpec((groups, ntaps, 2 * ntaps), lambda i: (1, 0, 0))
    whole = lambda *shape: pl.BlockSpec(shape, lambda i: (0,) * len(shape))
    grad_near, grad_other, *mixed = kernel_call(
        functools.partial(middle_body, scale, nshort, nrow),
        [shaped((3 * chunk + extra, width), BF16), shaped((3 * chunk, width), BF16)]
        + [shaped((rows, width), BF16)] * ndp,
        grid=(1,),
        in_specs=[whole(3 * chunk, width)] * 6
        + [whole(3 * nshort, width), half, other]
        + [whole(rows, width)] * ndp,
        out_specs=[whole(3 * chunk + extra, width), whole(3 * chunk, width)] + [whole(rows, width)] * ndp,
        scratch=[
            pltpu.VMEM((3 * seq, width), F32),
            pltpu.VMEM((3 * seq, width), BF16),
            pltpu.VMEM((seq, width), BF16),
            pltpu.VMEM((seq, width), BF16),
        ],
        flops=3 * 2 * groups * ntaps * 2 * ntaps * width * (seq // ntaps),
        nbytes=2 * width * seq * 14,
        vmem=MOST_VMEM_BYTES,
    )(*sums, sf, bands, bands, *upstream)
    mixed = [mixed[0]] + [
        lax.ppermute(part, "dp", [(a, (a + ahead) % ndp) for a in range(ndp)])
        for ahead, part in enumerate(mixed)
        if ahead
    ]
    *near, near_far_before, near_far_after = gather_over_line(grad_near, False)
    *far, far_far_before, far_far_after = gather_over_line(grad_other, True)
    partner_w = lax.ppermute(w, "row", partner)
    part, far_two = kernel_call(
        first_grad_body,
        [shaped((ncol, chunk, dcol), F32), shaped((2, 3 * chunk, width), BF16)],
        scratch=[pltpu.VMEM((ndp, 3 * chunk, width), BF16)],
        flops=2 * mm_flops,
        nbytes=2 * mm_bytes,
    )(*near, *far, w, partner_w)
    everywhere = pl.BlockSpec(memory_space=pl.ANY)
    in_vmem = pl.BlockSpec(memory_space=pltpu.VMEM)
    near_last, far_last, *blocks = kernel_call(
        functools.partial(second_grad_body, ndp),
        [shaped(grad_near.shape, BF16), shaped(grad_other.shape, BF16)]
        + [shaped((rows, dcol), BF16)] * len(places),
        grid=(),
        in_specs=[everywhere] * 7,
        out_specs=[in_vmem] * (2 + len(places)),
        scratch=[
            pltpu.VMEM((2, 3, drow, width), BF16),
            pltpu.VMEM((ncol, chunk, dcol), F32),
            pltpu.SemaphoreType.DMA((5,)),
        ],
        flops=mm_flops // 2,
        nbytes=mm_bytes // 2,
        vmem=MOST_VMEM_BYTES,
    )(part, near_far_before, near_far_after, far_far_before, far_far_after, far_w, partner_w)
    far_two, far_last, mixed[1:] = lax.optimization_barrier((far_two, far_last, mixed[1:]))
    far_two, far_last = (lax.ppermute(part, "row", partner) for part in (far_two, far_last))
    arrivals = [
        lax.ppermute(sent, ("row", "col"), [(b, a) for a, b in offset(*p)])
        for p, sent in zip(places[1:], blocks[1:])
    ]
    arrived = sum((a.astype(F32) for a in arrivals), blocks[0].astype(F32)).astype(BF16)
    arrived, far_two, far_last = lax.optimization_barrier((arrived, far_two, far_last))
    grad_in = lax.ppermute(arrived, ("dp", "row"), swap_back)

    grad_weight, mixed, grad_long, grad_short = kernel_call(
        functools.partial(weight_grad_body, scale),
        [
            shaped((3, drow, local), F32),
            shaped((rows, local), BF16),
            shaped((ngroups, ntaps), F32),
            shaped((nshort, 3, local), F32),
        ],
        grid=(3,),
        in_specs=[whole(nblocks, ncol, rows, dcol)] * 2
        + [whole(*grad_near.shape)] * 4
        + [whole(*grad_other.shape), whole(*far_two.shape), whole(*far_last.shape)]
        + [whole(rows, width)] * ndp,
        out_specs=[
            pl.BlockSpec((1, drow, local), lambda i: (i, 0, 0)),
            whole(rows, local),
            whole(ngroups, ntaps),
            whole(nshort, 3, local),
        ],
        scratch=[
            pltpu.VMEM((2, ndp, 3 * chunk + extra, width), BF16),
            pltpu.VMEM((ndp, rows, width), BF16),
        ],
        flops=2 * mm_flops,
        nbytes=2 * mm_bytes,
        vmem=MOST_VMEM_BYTES,
    )(x0, x1, *near, near_last, grad_other, far_two, far_last, *mixed)
    grad_weight = jnp.transpose(grad_weight, (1, 0, 2))
    return (mixed, grad_in, grad_weight, grad_long, grad_short)


def from_behind(block, axis, distance):
    devices = range(lax.axis_size(axis))
    route = [(i - distance, i) for i in devices if i - distance in devices]
    return lax.ppermute(block, axis, route)


def toeplitz(leading, rows, span):
    groups = leading.shape[0]
    width = rows + span
    seed_row = jnp.concatenate(
        [leading, jnp.zeros((groups, width - leading.shape[1]), leading.dtype)], axis=1
    )
    tiled = jnp.tile(seed_row, (1, rows))
    skewed = tiled[:, : rows * (width - 1)].reshape(groups, rows, width - 1)
    return skewed[:, :, :span]


def to_groups(values, ngroups, members):
    count = values.shape[0]
    return values.reshape(count, ngroups, members).transpose(1, 2, 0)


def from_groups(values):
    groups, members, count = values.shape
    return values.transpose(2, 0, 1).reshape(count, groups * members)


def move_weights(tokens, in_weight, short_filter, long_filter, grad_out):
    rows = tokens.shape[0]
    local = grad_out.shape[1]
    nshort = short_filter.shape[0]
    ntaps = long_filter.shape[1]
    ngroups = long_filter.shape[0]
    members = local // ngroups
    margin = ntaps - 1
    span = rows + margin
    scale = float(rows * lax.axis_size("dp")) ** (-0.5)
    whole = lax.all_gather(tokens, ("row", "col"), axis=1, tiled=True)
    full_w = lax.all_gather(in_weight, "dp", axis=0, tiled=True)
    mixed_in = jnp.einsum("sd,dic->sic", whole, full_w, preferred_element_type=jnp.float32).astype(
        jnp.bfloat16
    )
    before = from_behind(mixed_in[rows - margin - nshort + 1 :], "dp", 1)
    extended = jnp.concatenate([before, mixed_in], axis=0).astype(jnp.float32)
    long_feats = jnp.zeros((span, 3, local), jnp.float32)
    for j in range(nshort):
        long_feats = (
            long_feats + short_filter[j][None] * extended[nshort - 1 - j : nshort - 1 - j + span]
        )
    product_ext = (long_feats[:, 1] * long_feats[:, 2]).astype(jnp.bfloat16)
    feats = long_feats[margin:]
    short_rows = extended[margin:]
    product_cols = to_groups(product_ext, ngroups, members)
    causal = toeplitz(long_filter[:, ::-1], rows, span)
    conv = from_groups(
        jnp.einsum("gst,gct->gcs", causal, product_cols, preferred_element_type=jnp.float32)
    )
    mixed = (feats[:, 0] * conv).astype(jnp.bfloat16)
    upstream = grad_out.astype(jnp.float32)
    grad_query = upstream * conv
    grad_conv = (upstream * feats[:, 0]).astype(jnp.bfloat16)
    after = from_behind(grad_conv[:margin], "dp", -1)
    grad_ext = jnp.concatenate([grad_conv, after], axis=0)
    anti = toeplitz(long_filter, rows, span)
    grad_product = from_groups(
        jnp.einsum(
            "gst,gct->gcs",
            anti,
            to_groups(grad_ext, ngroups, members),
            preferred_element_type=jnp.float32,
        )
    )
    reversed_cols = jnp.concatenate(
        [product_cols[:, :, ::-1], jnp.zeros((ngroups, members, rows), product_cols.dtype)], axis=2
    )
    width = span + rows
    pairs = jnp.einsum(
        "gcs,gcu->gsu",
        to_groups(grad_conv, ngroups, members),
        reversed_cols,
        preferred_element_type=jnp.float32,
    )
    diagonal = pairs.reshape(ngroups, rows * width)[:, : rows * (width - 1)].reshape(
        ngroups, rows, width - 1
    )
    filter_part = jnp.sum(diagonal[:, :, rows - 1 : rows - 1 + ntaps], axis=1)
    grad_feats = jnp.stack(
        [grad_query, grad_product * feats[:, 2], grad_product * feats[:, 1]], axis=1
    )
    later = from_behind(grad_feats[: nshort - 1], "dp", -1)
    feats_ext = jnp.concatenate([grad_feats, later], axis=0)
    grad_acc = jnp.zeros((rows, 3, local), jnp.float32)
    for j in range(nshort):
        grad_acc = grad_acc + short_filter[j][None] * feats_ext[j : j + rows]
    grad_mixed = grad_acc.astype(jnp.bfloat16)
    short_part = jnp.stack(
        [
            jnp.sum(grad_feats * short_rows[nshort - 1 - j : nshort - 1 - j + rows], axis=0)
            for j in range(nshort)
        ]
    )
    filter_total, short_total = (
        lax.psum(filter_part.astype(jnp.bfloat16), "dp").astype(jnp.float32),
        lax.psum(short_part.astype(jnp.bfloat16), "dp").astype(jnp.float32),
    )
    grad_long = filter_total * scale
    grad_short = short_total * scale
    partial_in = jnp.einsum("sic,dic->sd", grad_mixed, full_w, preferred_element_type=jnp.float32)
    summed_in = lax.psum_scatter(
        partial_in.astype(jnp.bfloat16), ("row", "col"), scatter_dimension=1, tiled=True
    )
    weight_term = (
        jnp.einsum("sd,sic->dic", whole, grad_mixed, preferred_element_type=jnp.float32) * scale
    )
    grad_weight = lax.psum_scatter(
        weight_term.astype(jnp.bfloat16), "dp", scatter_dimension=0, tiled=True
    ).astype(jnp.float32)
    return (mixed, summed_in, grad_weight, grad_long, grad_short)


def fits_whole_sequences(mesh, tokens, in_weight, short_filter, long_filter, grad_out):
    ndp, nrow, ncol = (mesh.shape[a] for a in ("dp", "row", "col"))
    seq, channels = grad_out.shape
    groups, ntaps = long_filter.shape
    local = channels // (nrow * ncol)
    width, rows = local // ndp, seq // ndp
    return (
        seq < tokens.shape[1]
        and ndp == nrow == 4
        and ncol * (tokens.shape[1] // (nrow * ncol)) == in_weight.shape[0] // ndp
        and ntaps == width == 128
        and seq % (2 * ntaps) == 0
        and rows % 16 == 0
        and groups % (8 * ndp * nrow * ncol) == 0
    )


def solution(mesh):
    placed = (
        P("dp", ("row", "col")),
        P("dp", None, ("row", "col")),
        P(None, None, ("row", "col")),
        P(("row", "col"), None),
        P("dp", ("row", "col")),
    )
    gives = (
        P("dp", ("row", "col")),
        P("dp", ("row", "col")),
        P("dp", None, ("row", "col")),
        P(("row", "col"), None),
        P(None, None, ("row", "col")),
    )

    def run(*arrays):
        plan = move_activations if fits_whole_sequences(mesh, *arrays) else move_weights
        return jax.shard_map(
            plan, mesh=mesh, in_specs=placed, out_specs=gives, check_vma=False
        )(*arrays)

    return run
```

```python
import functools

import jax
import jax.numpy as jnp
from jax import lax
from jax.experimental import pallas as pl
from jax.experimental.pallas import tpu as pltpu
from jax.sharding import PartitionSpec as P

VMEM_BYTES = 48 * 2**20
MOST_VMEM_BYTES = 62 * 2**20
F32 = jnp.float32
BF16 = jnp.bfloat16


def kernel_call(body, outs, grid=(), in_specs=None, out_specs=None, scratch=(), flops=0, nbytes=0, vmem=VMEM_BYTES):
    kwargs = {}
    if in_specs is not None:
        kwargs = dict(grid=grid, in_specs=in_specs, out_specs=out_specs)
    return pl.pallas_call(
        body,
        out_shape=outs,
        scratch_shapes=scratch,
        compiler_params=pltpu.CompilerParams(vmem_limit_bytes=vmem),
        cost_estimate=pl.CostEstimate(flops=flops, bytes_accessed=nbytes, transcendentals=0),
        **kwargs,
    )


def shaped(shape, dtype):
    return jax.ShapeDtypeStruct(shape, dtype)


def bands_body(base_ref, out_ref):
    groups, wide = base_ref.shape
    rows = out_ref.shape[1]
    row = lax.broadcasted_iota(jnp.int32, (8, wide), 0)
    for g in range(groups):
        band = jnp.broadcast_to(base_ref[g : g + 1, :], (8, wide))
        for bit in (1, 2, 4):
            band = jnp.where((row & bit) != 0, pltpu.roll(band, bit, 1), band)
        count = 8
        while count < rows:
            band = jnp.concatenate([band, pltpu.roll(band, count, 1)], axis=0)
            count *= 2
        out_ref[g] = band.astype(out_ref.dtype)


def tokens_of(row, nrow):
    return row % 2 * (nrow // 2) + row // 2


def wrapped(value, size):
    return lax.rem(value + 2 * size, size)


def split_body(all_ref, *out_refs):
    width = out_refs[0].shape[1]
    for ahead, out_ref in enumerate(out_refs):
        at = wrapped(lax.axis_index("dp") + ahead, len(out_refs)) * width
        out_ref[...] = all_ref[:, pl.ds(pl.multiple_of(at, width), width)]


def project_body(x_ref, w_ref, *refs):
    *out_refs, held = refs
    z, col = lax.axis_index("dp"), lax.axis_index("col")
    nblocks, ncol, rows, depth = x_ref.shape
    width = held.shape[2]
    total = jnp.zeros((nblocks * rows, w_ref.shape[2]), F32)
    for dx in range(ncol):
        start = pl.multiple_of(wrapped(col - dx, ncol) * depth, depth)
        total += jnp.dot(
            x_ref[:, dx].reshape(nblocks * rows, depth),
            w_ref[0, pl.ds(start, depth), :],
            preferred_element_type=F32,
        )
    for owner in range(len(out_refs)):
        held[owner] = total[:, owner * width : (owner + 1) * width].astype(BF16)
    for ahead, out_ref in enumerate(out_refs):
        out_ref[0] = held[wrapped(z + ahead, len(out_refs))]


def far_columns_body(w_ref, out_ref, sem):
    ndp = lax.axis_size("dp")
    width = out_ref.shape[2]
    start = wrapped(lax.axis_index("dp") + ndp // 2, ndp) * width
    copy = pltpu.make_async_copy(w_ref.at[:, :, pl.ds(pl.multiple_of(start, width), width)], out_ref, sem)
    copy.start()
    copy.wait()


def first_grad_body(
    near, near_before, near_after, far, far_before, far_after, w_ref, partner_w_ref, out_ref, far_ref, held, held_w, sems
):
    _, ndp, _, width = held.shape
    ncol, tokens, depth = out_ref.shape
    z, col = lax.axis_index("dp"), lax.axis_index("col")
    copies = []
    for dx in range(ncol):
        start = pl.multiple_of(wrapped(col - dx, ncol) * depth, depth)
        for k, weights in enumerate((w_ref, partner_w_ref)):
            copy = pltpu.make_async_copy(weights.at[:, pl.ds(start, depth)], held_w.at[k, dx], sems.at[k, dx])
            copy.start()
            copies.append(copy)
    far_ref[0], far_ref[1] = far_before[...], far_after[...]
    for k, pieces in enumerate(((near, near_before, near_after), (far, far_before, far_after))):
        held[k, wrapped(z + ndp // 2, ndp)] = jnp.zeros(held.shape[2:], BF16)
        for ahead, piece in zip((0, -1, 1), pieces):
            held[k, wrapped(z + ahead, ndp)] = piece[: 3 * tokens]
    for dx in range(ncol):
        total = jnp.zeros((tokens, depth), F32)
        for k in range(2):
            copies[2 * dx + k].wait()
            for i in range(3):
                rows = slice(i * tokens, (i + 1) * tokens)
                total += lax.dot_general(
                    jnp.concatenate([held[k, owner, rows] for owner in range(ndp)], axis=1),
                    held_w[k, dx, i],
                    (((1,), (1,)), ((), ())),
                    preferred_element_type=F32,
                )
        out_ref[dx] = total.astype(BF16)


def second_grad_body(ndp, part_ref, *refs):
    arrived, (w_ref, partner_w_ref), refs = (refs[:2], refs[2:4]), refs[4:6], refs[6:]
    (near_ref, far_ref), refs = refs[:2], refs[2:]
    *out_refs, held_w, held_part, sems = refs
    ncol, tokens, depth = held_part.shape
    rows = out_refs[0].shape[0]
    width = near_ref.shape[1]
    z, col = lax.axis_index("dp"), lax.axis_index("col")
    lanes = pl.ds(pl.multiple_of(wrapped(z + ndp // 2, ndp) * width, width), width)
    copies = [
        pltpu.make_async_copy(w_ref, held_w.at[0], sems.at[0]),
        pltpu.make_async_copy(partner_w_ref.at[:, :, lanes], held_w.at[1], sems.at[1]),
    ]
    copies.append(pltpu.make_async_copy(part_ref, held_part, sems.at[2]))
    for copy in copies:
        copy.start()
    for k, (pair, target) in enumerate(zip(arrived, (near_ref, far_ref))):
        for source, here in zip(pair, (z >= ndp // 2, z < ndp // 2)):

            @pl.when(here)
            def _(source=source, target=target, k=k):
                copy = pltpu.make_async_copy(source, target, sems.at[3 + k])
                copy.start()
                copy.wait()

    for copy in copies:
        copy.wait()
    left = jnp.concatenate(
        [ref[i * tokens : (i + 1) * tokens] for ref in (near_ref, far_ref) for i in range(3)], axis=1
    )
    for dx in range(ncol):
        start = pl.multiple_of(wrapped(col - dx, ncol) * depth, depth)
        right = jnp.concatenate([held_w[k, i, pl.ds(start, depth), :] for k in range(2) for i in range(3)], axis=1)
        total = held_part[dx].astype(F32) + lax.dot_general(
            left, right, (((1,), (1,)), ((), ())), preferred_element_type=F32
        )
        for block in range(tokens // rows):
            out_refs[block * ncol + dx][...] = total[block * rows : (block + 1) * rows].astype(BF16)


def weight_grad_body(scale, *refs):
    (x0_ref, x1_ref), near_refs, other_refs, mixed_refs, refs = refs[:2], refs[2:6], refs[6:9], refs[9:13], refs[13:]
    own_ref, two_ref, last_ref = other_refs
    other = (own_ref, two_ref.at[0], two_ref.at[1], last_ref)
    out_ref, mixed_ref, long_ref, short_ref, held, held_mixed = refs
    nblocks, ncol, rows, depth = x0_ref.shape
    _, ndp, _, width = held.shape
    tokens = nblocks * rows
    i = pl.program_id(0)
    z, col = lax.axis_index("dp"), lax.axis_index("col")

    @pl.when(i == 0)
    def _():
        groups = long_ref.shape[0] // ndp
        for k, ahead in enumerate((0, -1, 1, 2)):
            owner = wrapped(z + ahead, ndp)
            held[0, owner] = near_refs[k][...]
            held[1, owner, : 3 * tokens] = other[k][...]
        for back in range(ndp):
            held_mixed[wrapped(z - back, ndp)] = mixed_refs[back][...]
        for owner in range(ndp):
            lanes = slice(owner * width, (owner + 1) * width)
            mixed_ref[:, lanes] = held_mixed[owner]
            small = held[0, owner, 3 * tokens :].astype(F32)
            long_ref[owner * groups : (owner + 1) * groups] = small[:groups]
            nshort, three, _ = short_ref.shape
            for j in range(nshort):
                short_ref[j, :, lanes] = small[groups + three * j : groups + three * (j + 1)]

    at = pl.ds(pl.multiple_of(i * tokens, 16), tokens)
    gm = jnp.concatenate(
        [jnp.concatenate([held[k, owner, at, :] for owner in range(ndp)], axis=1) for k in range(2)], axis=0
    )
    for dx in range(ncol):
        start = pl.multiple_of(wrapped(col - dx, ncol) * depth, depth)
        x = jnp.concatenate(
            [x_ref[:, dx].reshape(tokens, depth) for x_ref in (x0_ref, x1_ref)], axis=0
        )
        out_ref[0, pl.ds(start, depth), :] = scale * lax.dot_general(
            x, gm, (((0,), (0,)), ((), ())), preferred_element_type=F32
        )


def delayed(values, count):
    row = lax.broadcasted_iota(jnp.int32, values.shape, 0)
    return jnp.where(row >= count, pltpu.roll(values, count, 0), 0.0)


def advanced(values, count):
    rows = values.shape[0]
    row = lax.broadcasted_iota(jnp.int32, values.shape, 0)
    return jnp.where(row < rows - count, pltpu.roll(values, rows - count, 0), 0.0)


def middle_body(scale, nshort, nrow, *refs):
    sums, refs = (refs[:3], refs[3:6]), refs[6:]
    (sf_ref, causal_ref, anti_ref), refs = refs[:3], refs[3:]
    *refs, m_ref, gm_ref, mixed_ref, go_ref = refs
    ndp = len(refs) // 2 - 1
    go_refs, (near_ref, other_ref), mixed_refs = refs[:ndp], refs[ndp : ndp + 2], refs[ndp + 2 :]
    tokens, width = go_ref.shape
    for behind, piece in enumerate(go_refs):
        at = wrapped(lax.axis_index("dp") - behind, ndp) * (tokens // ndp)
        go_ref[pl.ds(pl.multiple_of(at, 16), tokens // ndp)] = piece[...]
    row = lax.axis_index("row")
    nblocks = nrow // 2
    rows = tokens // nrow

    def places():
        for chunk, start in enumerate((row, row + 1 - 2 * lax.rem(row, 2))):
            for block in range(nblocks):
                at = tokens_of(wrapped(start - 2 * block, nrow), nrow) * rows
                for i in range(3):
                    yield chunk, (i * nblocks + block) * rows, pl.multiple_of(i * tokens + at, 16)

    for chunk, place, at in places():
        held = [ref[place : place + rows].astype(F32) for ref in sums[chunk]]
        m_ref[pl.ds(at, rows)] = held[0] + held[1] + held[2]
    groups, block, span = causal_ref.shape
    members = width // groups
    nspans = tokens // block
    lane = lax.broadcasted_iota(jnp.int32, (block, width), 1) // members
    lanes = lax.broadcasted_iota(jnp.int32, (block, 2 * width), 1) % width // members

    def past(i, j):
        held = m_ref[i * tokens : (i + 1) * tokens]
        return held if j == 0 else delayed(held, j)

    def taps(j, i):
        return sf_ref[3 * j + i : 3 * j + i + 1, :]

    feats = [sum(taps(j, i) * past(i, j) for j in range(nshort)) for i in range(3)]
    product = (feats[1] * feats[2]).astype(BF16)
    zero = jnp.zeros((block, width), BF16)
    p_blocks = [zero] + [product[b * block : (b + 1) * block] for b in range(nspans)]
    p_pairs = [jnp.concatenate(p_blocks[b : b + 2], axis=0) for b in range(nspans)]

    def filtered(band_ref, pairs):
        bands = band_ref[...].reshape(groups * block, span)
        out = []
        for b in range(0, nspans, 2):
            both = jnp.dot(bands, jnp.concatenate(pairs[b : b + 2], axis=1), preferred_element_type=F32)
            for h in range(2):
                part = both[:, h * width : (h + 1) * width]
                picked = part[:block]
                for g in range(1, groups):
                    picked = jnp.where(lane == g, part[g * block : (g + 1) * block], picked)
                out.append(picked)
        return jnp.concatenate(out, axis=0)

    conv = filtered(causal_ref, p_pairs)
    upstream = go_ref[...].astype(F32)
    mixed_ref[...] = (feats[0] * conv).astype(BF16)
    for ahead, out_ref in enumerate(mixed_refs):
        at = pl.multiple_of(wrapped(lax.axis_index("dp") + ahead, ndp) * (tokens // ndp), 16)
        out_ref[...] = mixed_ref[pl.ds(at, tokens // ndp)]
    grad_conv = (upstream * feats[0]).astype(BF16)
    c_blocks = [grad_conv[b * block : (b + 1) * block] for b in range(nspans)] + [zero]
    c_pairs = [jnp.concatenate(c_blocks[b : b + 2], axis=0) for b in range(nspans)]
    grad_product = filtered(anti_ref, c_pairs)

    corr = jnp.zeros((groups * block, span), F32)
    for b in range(0, nspans, 2):
        left = jnp.concatenate(c_blocks[b : b + 2], axis=1)
        stacked = jnp.concatenate(
            [jnp.where(lanes == g, left, jnp.zeros_like(left)) for g in range(groups)], axis=0
        )
        right = jnp.concatenate(p_pairs[b : b + 2], axis=1)
        corr += lax.dot_general(stacked, right, (((1,), (1,)), ((), ())), preferred_element_type=F32)
    turn = lax.broadcasted_iota(jnp.int32, (8, span), 0)
    sums = []
    for g in range(groups):
        part = corr[g * block : (g + 1) * block]
        count = block
        while count > 8:
            count //= 2
            part = part[:count] + pltpu.roll(part[count:], span - count, 1)
        for bit in (1, 2, 4):
            part = jnp.where((turn & bit) != 0, pltpu.roll(part, span - bit, 1), part)
        sums.append(jnp.sum(part, axis=0, keepdims=True))
    by_lag = jnp.concatenate(sums, axis=0)
    by_lag = (scale * pltpu.roll(by_lag, span - 1, 1)[:, :block]).astype(BF16)
    ahead = lax.broadcasted_iota(jnp.int32, (block, block), 0)
    back = lax.broadcasted_iota(jnp.int32, (block, block), 1)
    turned = jnp.where(ahead + back == block - 1, 1.0, 0.0).astype(BF16)
    by_lag = jnp.dot(by_lag, turned, preferred_element_type=F32)

    grad_feats = [upstream * conv, grad_product * feats[2], grad_product * feats[1]]
    short_rows = []
    for j in range(nshort):
        for i in range(3):
            short_rows.append(scale * jnp.sum(grad_feats[i] * past(i, j), axis=0, keepdims=True))
    for i in range(3):
        total = taps(0, i) * grad_feats[i]
        for j in range(1, nshort):
            total += taps(j, i) * advanced(grad_feats[i], j)
        gm_ref[i * tokens : (i + 1) * tokens] = total.astype(BF16)
    for chunk, place, at in places():
        (near_ref, other_ref)[chunk][place : place + rows] = gm_ref[pl.ds(at, rows)]
    tail = near_ref.shape[0] - 3 * tokens // 2 - groups - 3 * nshort
    small = jnp.concatenate([by_lag] + short_rows + [jnp.zeros((tail, width), F32)], axis=0)
    near_ref[3 * tokens // 2 :] = small.astype(BF16)


def sum_over_line(own, right, far, left):
    ndp = lax.axis_size("dp")
    from_left = lax.ppermute(far, "dp", [(a, a + 1) for a in range(ndp // 2)])
    from_right = lax.ppermute(far, "dp", [(a, a - 1) for a in range(ndp // 2, ndp)])
    rightward = lax.ppermute(right + from_left, "dp", [(a, (a + 1) % ndp) for a in range(ndp)])
    leftward = lax.ppermute(left + from_right, "dp", [(a, (a - 1) % ndp) for a in range(ndp)])
    return own, rightward, leftward


def gather_over_line(own, across):
    ndp, nrow = lax.axis_size("dp"), lax.axis_size("row")

    def shift(count):
        return [
            (a * nrow + r, (a + count) % ndp * nrow + (r + 1 - 2 * (r % 2) if across else r))
            for a in range(ndp)
            for r in range(nrow)
        ]

    before = lax.ppermute(own, ("dp", "row"), shift(1))
    after = lax.ppermute(own, ("dp", "row"), shift(-1))
    here = lax.ppermute(own, ("dp", "row"), shift(0)) if across else own
    far_before = lax.ppermute(before, "dp", [(a - 1, a) for a in range(ndp // 2, ndp)])
    far_after = lax.ppermute(after, "dp", [(a + 1, a) for a in range(ndp // 2)])
    return here, before, after, far_before, far_after


def move_activations(tokens, in_weight, short_filter, long_filter, grad_out):
    ndp, nrow, ncol = (lax.axis_size(a) for a in ("dp", "row", "col"))
    z = lax.axis_index("dp")
    rows, dcol = tokens.shape
    local = grad_out.shape[1]
    nshort = short_filter.shape[0]
    ngroups, ntaps = long_filter.shape
    seq = rows * ndp
    width, groups = local // ndp, ngroups // ndp
    drow = in_weight.shape[0]
    scale = float(seq) ** -0.5
    nblocks = nrow // 2
    chunk = nblocks * rows
    swap = [(tokens_of(b, nrow) * nrow + a, a * nrow + b) for a in range(ndp) for b in range(nrow)]
    swap_back = [(b, a) for a, b in swap]
    partner = [(a, a + 1 - 2 * (a % 2)) for a in range(nrow)]
    places = [(dy, dx) for dy in range(nblocks) for dx in range(ncol)]

    def offset(dy, dx):
        return [
            (a * ncol + b, (a + 2 * dy) % nrow * ncol + (b + dx) % ncol) for a in range(nrow) for b in range(ncol)
        ]

    w = jnp.transpose(in_weight, (1, 0, 2))
    moved = lax.ppermute(tokens, ("dp", "row"), swap)
    far_w = kernel_call(
        far_columns_body,
        shaped((3, drow, width), BF16),
        in_specs=[pl.BlockSpec(memory_space=pl.ANY)],
        out_specs=pl.BlockSpec(memory_space=pltpu.VMEM),
        scratch=[pltpu.SemaphoreType.DMA],
    )(w)
    turn = [[(a, (a + ahead) % ndp) for a in range(ndp)] for ahead in range(ndp)]
    upstream = [*kernel_call(split_body, [shaped((rows, width), BF16)] * ndp)(grad_out)]
    moved, upstream, far_w = lax.optimization_barrier((moved, upstream, far_w))
    near = [moved] + [lax.ppermute(moved, ("row", "col"), offset(*p)) for p in places[1:]]
    for ahead in (1, 3):
        upstream[ahead] = lax.ppermute(upstream[ahead], "dp", turn[ahead])
    upstream[1::2], near[1:] = lax.optimization_barrier((upstream[1::2], near[1:]))
    x0 = jnp.stack(near).reshape(nblocks, ncol, rows, dcol)
    x1 = lax.ppermute(x0, "row", partner)
    upstream[2] = lax.ppermute(upstream[2], "dp", turn[2])
    upstream[2], x1 = lax.optimization_barrier((upstream[2], x1))

    sf = lax.dynamic_slice_in_dim(short_filter, z * width, width, 2).reshape(3 * nshort, width)
    lf = lax.dynamic_slice_in_dim(long_filter, z * groups, groups, 0).astype(F32)
    zeros = functools.partial(jnp.zeros, dtype=F32)
    bases = jnp.concatenate(
        [
            jnp.concatenate([zeros((groups, 1)), lf[:, ::-1], zeros((groups, ntaps - 1))], axis=1),
            jnp.concatenate([lf, zeros((groups, ntaps))], axis=1),
        ],
        axis=0,
    )
    bands = kernel_call(bands_body, shaped((2 * groups, ntaps, 2 * ntaps), BF16))(bases)

    mm_flops = seq * drow * 3 * local
    mm_bytes = seq * drow + 6 * drow * local + 3 * seq * local
    sums = []
    for x in (x0, x1):
        parts = kernel_call(
            project_body,
            [shaped((3, chunk, width), BF16)] * ndp,
            grid=(3,),
            in_specs=[
                pl.BlockSpec((nblocks, ncol, rows, dcol), lambda i: (0, 0, 0, 0)),
                pl.BlockSpec((1, drow, local), lambda i: (i, 0, 0)),
            ],
            out_specs=[pl.BlockSpec((1, chunk, width), lambda i: (i, 0, 0))] * ndp,
            scratch=[pltpu.VMEM((ndp, chunk, width), BF16)],
            flops=mm_flops,
            nbytes=mm_bytes,
        )(x, w)
        sums += sum_over_line(*(p.reshape(3 * chunk, width) for p in parts))

    extra = -(-(groups + 3 * nshort) // 16) * 16
    half = pl.BlockSpec((groups, ntaps, 2 * ntaps), lambda i: (0, 0, 0))
    other = pl.BlockSpec((groups, ntaps, 2 * ntaps), lambda i: (1, 0, 0))
    whole = lambda *shape: pl.BlockSpec(shape, lambda i: (0,) * len(shape))
    grad_near, grad_other, *mixed = kernel_call(
        functools.partial(middle_body, scale, nshort, nrow),
        [shaped((3 * chunk + extra, width), BF16), shaped((3 * chunk, width), BF16)]
        + [shaped((rows, width), BF16)] * ndp,
        grid=(1,),
        in_specs=[whole(3 * chunk, width)] * 6
        + [whole(3 * nshort, width), half, other]
        + [whole(rows, width)] * ndp,
        out_specs=[whole(3 * chunk + extra, width), whole(3 * chunk, width)] + [whole(rows, width)] * ndp,
        scratch=[
            pltpu.VMEM((3 * seq, width), F32),
            pltpu.VMEM((3 * seq, width), BF16),
            pltpu.VMEM((seq, width), BF16),
            pltpu.VMEM((seq, width), BF16),
        ],
        flops=3 * 2 * groups * ntaps * 2 * ntaps * width * (seq // ntaps),
        nbytes=2 * width * seq * 14,
        vmem=MOST_VMEM_BYTES,
    )(*sums, sf, bands, bands, *upstream)
    mixed = [mixed[0]] + [
        lax.ppermute(part, "dp", [(a, (a + ahead) % ndp) for a in range(ndp)])
        for ahead, part in enumerate(mixed)
        if ahead
    ]
    *near, near_far_before, near_far_after = gather_over_line(grad_near, False)
    *far, far_far_before, far_far_after = gather_over_line(grad_other, True)
    partner_w = lax.ppermute(w, "row", partner)
    everywhere = pl.BlockSpec(memory_space=pl.ANY)
    in_vmem = pl.BlockSpec(memory_space=pltpu.VMEM)
    part, far_two = kernel_call(
        first_grad_body,
        [shaped((ncol, chunk, dcol), BF16), shaped((2, 3 * chunk, width), BF16)],
        in_specs=[in_vmem] * 6 + [everywhere] * 2,
        out_specs=[in_vmem] * 2,
        scratch=[
            pltpu.VMEM((2, ndp, 3 * chunk, width), BF16),
            pltpu.VMEM((2, ncol, 3, dcol, local), BF16),
            pltpu.SemaphoreType.DMA((2, ncol)),
        ],
        flops=2 * mm_flops,
        nbytes=2 * mm_bytes,
    )(*near, *far, w, partner_w)
    near_last, far_last, *blocks = kernel_call(
        functools.partial(second_grad_body, ndp),
        [shaped(grad_near.shape, BF16), shaped(grad_other.shape, BF16)]
        + [shaped((rows, dcol), BF16)] * len(places),
        grid=(),
        in_specs=[everywhere] * 7,
        out_specs=[in_vmem] * (2 + len(places)),
        scratch=[
            pltpu.VMEM((2, 3, drow, width), BF16),
            pltpu.VMEM((ncol, chunk, dcol), BF16),
            pltpu.SemaphoreType.DMA((5,)),
        ],
        flops=mm_flops // 2,
        nbytes=mm_bytes // 2,
        vmem=MOST_VMEM_BYTES,
    )(part, near_far_before, near_far_after, far_far_before, far_far_after, far_w, partner_w)
    far_two, far_last, mixed[1:] = lax.optimization_barrier((far_two, far_last, mixed[1:]))
    far_two, far_last = (lax.ppermute(part, "row", partner) for part in (far_two, far_last))
    arrivals = [
        lax.ppermute(sent, ("row", "col"), [(b, a) for a, b in offset(*p)])
        for p, sent in zip(places[1:], blocks[1:])
    ]
    arrived = sum((a.astype(F32) for a in arrivals), blocks[0].astype(F32)).astype(BF16)
    arrived, far_two, far_last = lax.optimization_barrier((arrived, far_two, far_last))
    grad_in = lax.ppermute(arrived, ("dp", "row"), swap_back)

    grad_weight, mixed, grad_long, grad_short = kernel_call(
        functools.partial(weight_grad_body, scale),
        [
            shaped((3, drow, local), F32),
            shaped((rows, local), BF16),
            shaped((ngroups, ntaps), F32),
            shaped((nshort, 3, local), F32),
        ],
        grid=(3,),
        in_specs=[whole(nblocks, ncol, rows, dcol)] * 2
        + [whole(*grad_near.shape)] * 4
        + [whole(*grad_other.shape), whole(*far_two.shape), whole(*far_last.shape)]
        + [whole(rows, width)] * ndp,
        out_specs=[
            pl.BlockSpec((1, drow, local), lambda i: (i, 0, 0)),
            whole(rows, local),
            whole(ngroups, ntaps),
            whole(nshort, 3, local),
        ],
        scratch=[
            pltpu.VMEM((2, ndp, 3 * chunk + extra, width), BF16),
            pltpu.VMEM((ndp, rows, width), BF16),
        ],
        flops=2 * mm_flops,
        nbytes=2 * mm_bytes,
        vmem=MOST_VMEM_BYTES,
    )(x0, x1, *near, near_last, grad_other, far_two, far_last, *mixed)
    grad_weight = jnp.transpose(grad_weight, (1, 0, 2))
    return (mixed, grad_in, grad_weight, grad_long, grad_short)


def from_behind(block, axis, distance):
    devices = range(lax.axis_size(axis))
    route = [(i - distance, i) for i in devices if i - distance in devices]
    return lax.ppermute(block, axis, route)


def toeplitz(leading, rows, span):
    groups = leading.shape[0]
    width = rows + span
    seed_row = jnp.concatenate(
        [leading, jnp.zeros((groups, width - leading.shape[1]), leading.dtype)], axis=1
    )
    tiled = jnp.tile(seed_row, (1, rows))
    skewed = tiled[:, : rows * (width - 1)].reshape(groups, rows, width - 1)
    return skewed[:, :, :span]


def to_groups(values, ngroups, members):
    count = values.shape[0]
    return values.reshape(count, ngroups, members).transpose(1, 2, 0)


def from_groups(values):
    groups, members, count = values.shape
    return values.transpose(2, 0, 1).reshape(count, groups * members)


def move_weights(tokens, in_weight, short_filter, long_filter, grad_out):
    rows = tokens.shape[0]
    local = grad_out.shape[1]
    nshort = short_filter.shape[0]
    ntaps = long_filter.shape[1]
    ngroups = long_filter.shape[0]
    members = local // ngroups
    margin = ntaps - 1
    span = rows + margin
    scale = float(rows * lax.axis_size("dp")) ** (-0.5)
    whole = lax.all_gather(tokens, ("row", "col"), axis=1, tiled=True)
    full_w = lax.all_gather(in_weight, "dp", axis=0, tiled=True)
    mixed_in = jnp.einsum("sd,dic->sic", whole, full_w, preferred_element_type=jnp.float32).astype(
        jnp.bfloat16
    )
    before = from_behind(mixed_in[rows - margin - nshort + 1 :], "dp", 1)
    extended = jnp.concatenate([before, mixed_in], axis=0).astype(jnp.float32)
    long_feats = jnp.zeros((span, 3, local), jnp.float32)
    for j in range(nshort):
        long_feats = (
            long_feats + short_filter[j][None] * extended[nshort - 1 - j : nshort - 1 - j + span]
        )
    product_ext = (long_feats[:, 1] * long_feats[:, 2]).astype(jnp.bfloat16)
    feats = long_feats[margin:]
    short_rows = extended[margin:]
    product_cols = to_groups(product_ext, ngroups, members)
    causal = toeplitz(long_filter[:, ::-1], rows, span)
    conv = from_groups(
        jnp.einsum("gst,gct->gcs", causal, product_cols, preferred_element_type=jnp.float32)
    )
    mixed = (feats[:, 0] * conv).astype(jnp.bfloat16)
    upstream = grad_out.astype(jnp.float32)
    grad_query = upstream * conv
    grad_conv = (upstream * feats[:, 0]).astype(jnp.bfloat16)
    after = from_behind(grad_conv[:margin], "dp", -1)
    grad_ext = jnp.concatenate([grad_conv, after], axis=0)
    anti = toeplitz(long_filter, rows, span)
    grad_product = from_groups(
        jnp.einsum(
            "gst,gct->gcs",
            anti,
            to_groups(grad_ext, ngroups, members),
            preferred_element_type=jnp.float32,
        )
    )
    reversed_cols = jnp.concatenate(
        [product_cols[:, :, ::-1], jnp.zeros((ngroups, members, rows), product_cols.dtype)], axis=2
    )
    width = span + rows
    pairs = jnp.einsum(
        "gcs,gcu->gsu",
        to_groups(grad_conv, ngroups, members),
        reversed_cols,
        preferred_element_type=jnp.float32,
    )
    diagonal = pairs.reshape(ngroups, rows * width)[:, : rows * (width - 1)].reshape(
        ngroups, rows, width - 1
    )
    filter_part = jnp.sum(diagonal[:, :, rows - 1 : rows - 1 + ntaps], axis=1)
    grad_feats = jnp.stack(
        [grad_query, grad_product * feats[:, 2], grad_product * feats[:, 1]], axis=1
    )
    later = from_behind(grad_feats[: nshort - 1], "dp", -1)
    feats_ext = jnp.concatenate([grad_feats, later], axis=0)
    grad_acc = jnp.zeros((rows, 3, local), jnp.float32)
    for j in range(nshort):
        grad_acc = grad_acc + short_filter[j][None] * feats_ext[j : j + rows]
    grad_mixed = grad_acc.astype(jnp.bfloat16)
    short_part = jnp.stack(
        [
            jnp.sum(grad_feats * short_rows[nshort - 1 - j : nshort - 1 - j + rows], axis=0)
            for j in range(nshort)
        ]
    )
    filter_total, short_total = (
        lax.psum(filter_part.astype(jnp.bfloat16), "dp").astype(jnp.float32),
        lax.psum(short_part.astype(jnp.bfloat16), "dp").astype(jnp.float32),
    )
    grad_long = filter_total * scale
    grad_short = short_total * scale
    partial_in = jnp.einsum("sic,dic->sd", grad_mixed, full_w, preferred_element_type=jnp.float32)
    summed_in = lax.psum_scatter(
        partial_in.astype(jnp.bfloat16), ("row", "col"), scatter_dimension=1, tiled=True
    )
    weight_term = (
        jnp.einsum("sd,sic->dic", whole, grad_mixed, preferred_element_type=jnp.float32) * scale
    )
    grad_weight = lax.psum_scatter(
        weight_term.astype(jnp.bfloat16), "dp", scatter_dimension=0, tiled=True
    ).astype(jnp.float32)
    return (mixed, summed_in, grad_weight, grad_long, grad_short)


def fits_whole_sequences(mesh, tokens, in_weight, short_filter, long_filter, grad_out):
    ndp, nrow, ncol = (mesh.shape[a] for a in ("dp", "row", "col"))
    seq, channels = grad_out.shape
    groups, ntaps = long_filter.shape
    local = channels // (nrow * ncol)
    width, rows = local // ndp, seq // ndp
    return (
        seq < tokens.shape[1]
        and ndp == nrow == 4
        and ncol * (tokens.shape[1] // (nrow * ncol)) == in_weight.shape[0] // ndp
        and ntaps == width == 128
        and seq % (2 * ntaps) == 0
        and rows % 16 == 0
        and groups % (8 * ndp * nrow * ncol) == 0
    )


def solution(mesh):
    placed = (
        P("dp", ("row", "col")),
        P("dp", None, ("row", "col")),
        P(None, None, ("row", "col")),
        P(("row", "col"), None),
        P("dp", ("row", "col")),
    )
    gives = (
        P("dp", ("row", "col")),
        P("dp", ("row", "col")),
        P("dp", None, ("row", "col")),
        P(("row", "col"), None),
        P(None, None, ("row", "col")),
    )

    def run(*arrays):
        plan = move_activations if fits_whole_sequences(mesh, *arrays) else move_weights
        return jax.shard_map(
            plan, mesh=mesh, in_specs=placed, out_specs=gives, check_vma=False
        )(*arrays)

    return run
```

```python
import functools

import jax
import jax.numpy as jnp
from jax import lax
from jax.experimental import pallas as pl
from jax.experimental.pallas import tpu as pltpu
from jax.sharding import PartitionSpec as P

VMEM_BYTES = 48 * 2**20
MOST_VMEM_BYTES = 62 * 2**20
F32 = jnp.float32
BF16 = jnp.bfloat16


def kernel_call(body, outs, grid=(), in_specs=None, out_specs=None, scratch=(), flops=0, nbytes=0, vmem=VMEM_BYTES):
    kwargs = {}
    if in_specs is not None:
        kwargs = dict(grid=grid, in_specs=in_specs, out_specs=out_specs)
    return pl.pallas_call(
        body,
        out_shape=outs,
        scratch_shapes=scratch,
        compiler_params=pltpu.CompilerParams(vmem_limit_bytes=vmem),
        cost_estimate=pl.CostEstimate(flops=flops, bytes_accessed=nbytes, transcendentals=0),
        **kwargs,
    )


def shaped(shape, dtype):
    return jax.ShapeDtypeStruct(shape, dtype)


def bands_body(base_ref, out_ref):
    groups, wide = base_ref.shape
    rows = out_ref.shape[1]
    row = lax.broadcasted_iota(jnp.int32, (8, wide), 0)
    for g in range(groups):
        band = jnp.broadcast_to(base_ref[g : g + 1, :], (8, wide))
        for bit in (1, 2, 4):
            band = jnp.where((row & bit) != 0, pltpu.roll(band, bit, 1), band)
        count = 8
        while count < rows:
            band = jnp.concatenate([band, pltpu.roll(band, count, 1)], axis=0)
            count *= 2
        out_ref[g] = band.astype(out_ref.dtype)


def tokens_of(row, nrow):
    return row % 2 * (nrow // 2) + row // 2


def wrapped(value, size):
    return lax.rem(value + 2 * size, size)


def split_body(all_ref, *out_refs):
    width = out_refs[0].shape[1]
    for ahead, out_ref in enumerate(out_refs):
        at = wrapped(lax.axis_index("dp") + ahead, len(out_refs)) * width
        out_ref[...] = all_ref[:, pl.ds(pl.multiple_of(at, width), width)]


def project_body(x_ref, w_ref, *refs):
    *out_refs, held = refs
    z, col = lax.axis_index("dp"), lax.axis_index("col")
    nblocks, ncol, rows, depth = x_ref.shape
    width = held.shape[2]
    total = jnp.zeros((nblocks * rows, w_ref.shape[2]), F32)
    for dx in range(ncol):
        start = pl.multiple_of(wrapped(col - dx, ncol) * depth, depth)
        total += jnp.dot(
            x_ref[:, dx].reshape(nblocks * rows, depth),
            w_ref[0, pl.ds(start, depth), :],
            preferred_element_type=F32,
        )
    for owner in range(len(out_refs)):
        held[owner] = total[:, owner * width : (owner + 1) * width].astype(BF16)
    for ahead, out_ref in enumerate(out_refs):
        out_ref[0] = held[wrapped(z + ahead, len(out_refs))]


def far_columns_body(w_ref, out_ref, sem):
    ndp = lax.axis_size("dp")
    width = out_ref.shape[2]
    start = wrapped(lax.axis_index("dp") + ndp // 2, ndp) * width
    copy = pltpu.make_async_copy(w_ref.at[:, :, pl.ds(pl.multiple_of(start, width), width)], out_ref, sem)
    copy.start()
    copy.wait()


def first_grad_body(
    near, near_before, near_after, far, far_before, far_after, w_ref, partner_w_ref, out_ref, far_ref, held, held_w, sems
):
    _, ndp, _, width = held.shape
    ncol, tokens, depth = out_ref.shape
    z, col = lax.axis_index("dp"), lax.axis_index("col")
    copies = []
    for dx in range(ncol):
        start = pl.multiple_of(wrapped(col - dx, ncol) * depth, depth)
        for k, weights in enumerate((w_ref, partner_w_ref)):
            copy = pltpu.make_async_copy(weights.at[:, pl.ds(start, depth)], held_w.at[k, dx], sems.at[k, dx])
            copy.start()
            copies.append(copy)
    far_ref[0], far_ref[1] = far_before[...], far_after[...]
    for k, pieces in enumerate(((near, near_before, near_after), (far, far_before, far_after))):
        held[k, wrapped(z + ndp // 2, ndp)] = jnp.zeros(held.shape[2:], BF16)
        for ahead, piece in zip((0, -1, 1), pieces):
            held[k, wrapped(z + ahead, ndp)] = piece[: 3 * tokens]
    for dx in range(ncol):
        total = jnp.zeros((tokens, depth), F32)
        for k in range(2):
            copies[2 * dx + k].wait()
            for i in range(3):
                rows = slice(i * tokens, (i + 1) * tokens)
                total += lax.dot_general(
                    jnp.concatenate([held[k, owner, rows] for owner in range(ndp)], axis=1),
                    held_w[k, dx, i],
                    (((1,), (1,)), ((), ())),
                    preferred_element_type=F32,
                )
        out_ref[dx] = total.astype(BF16)


def second_grad_body(ndp, part_ref, *refs):
    arrived, (w_ref, partner_w_ref), refs = (refs[:2], refs[2:4]), refs[4:6], refs[6:]
    (near_ref, far_ref), refs = refs[:2], refs[2:]
    *out_refs, held_w, held_part, sems = refs
    ncol, tokens, depth = held_part.shape
    rows = out_refs[0].shape[0]
    width = near_ref.shape[1]
    z, col = lax.axis_index("dp"), lax.axis_index("col")
    lanes = pl.ds(pl.multiple_of(wrapped(z + ndp // 2, ndp) * width, width), width)
    copies = [
        pltpu.make_async_copy(w_ref, held_w.at[0], sems.at[0]),
        pltpu.make_async_copy(partner_w_ref.at[:, :, lanes], held_w.at[1], sems.at[1]),
    ]
    copies.append(pltpu.make_async_copy(part_ref, held_part, sems.at[2]))
    for copy in copies:
        copy.start()
    for k, (pair, target) in enumerate(zip(arrived, (near_ref, far_ref))):
        for source, here in zip(pair, (z >= ndp // 2, z < ndp // 2)):

            @pl.when(here)
            def _(source=source, target=target, k=k):
                copy = pltpu.make_async_copy(source, target, sems.at[3 + k])
                copy.start()
                copy.wait()

    for copy in copies:
        copy.wait()
    left = jnp.concatenate(
        [ref[i * tokens : (i + 1) * tokens] for ref in (near_ref, far_ref) for i in range(3)], axis=1
    )
    for dx in range(ncol):
        start = pl.multiple_of(wrapped(col - dx, ncol) * depth, depth)
        right = jnp.concatenate([held_w[k, i, pl.ds(start, depth), :] for k in range(2) for i in range(3)], axis=1)
        total = held_part[dx].astype(F32) + lax.dot_general(
            left, right, (((1,), (1,)), ((), ())), preferred_element_type=F32
        )
        for block in range(tokens // rows):
            out_refs[block * ncol + dx][...] = total[block * rows : (block + 1) * rows].astype(BF16)


def weight_products(x_ref, held, at, ncol):
    ndp = held.shape[0]
    nblocks, _, rows, depth = x_ref.shape
    col = lax.axis_index("col")
    gm = jnp.concatenate([held[owner, at, :] for owner in range(ndp)], axis=1)
    for dx in range(ncol):
        start = pl.multiple_of(wrapped(col - dx, ncol) * depth, depth)
        x = x_ref[:, dx].reshape(nblocks * rows, depth)
        yield pl.ds(start, depth), lax.dot_general(x, gm, (((0,), (0,)), ((), ())), preferred_element_type=F32)


def own_weight_grad_body(x_ref, *refs):
    pieces, (out_ref, long_ref, short_ref, held) = refs[:4], refs[4:]
    ndp, _, width = held.shape
    tokens = x_ref.shape[0] * x_ref.shape[2]
    z = lax.axis_index("dp")

    @pl.when(pl.program_id(0) == 0)
    def _():
        groups = long_ref.shape[0] // ndp
        nshort, three, _ = short_ref.shape
        for piece, ahead in zip(pieces, (0, -1, 1, 2)):
            held[wrapped(z + ahead, ndp)] = piece[...]
        for owner in range(ndp):
            lanes = slice(owner * width, (owner + 1) * width)
            small = held[owner, 3 * tokens :].astype(F32)
            long_ref[owner * groups : (owner + 1) * groups] = small[:groups]
            for j in range(nshort):
                short_ref[j, :, lanes] = small[groups + three * j : groups + three * (j + 1)]

    at = pl.ds(pl.multiple_of(pl.program_id(0) * tokens, 16), tokens)
    for place, product in weight_products(x_ref, held, at, x_ref.shape[1]):
        out_ref[0, place, :] = product.astype(BF16)


def weight_grad_body(scale, x_ref, part_ref, *refs):
    (own_ref, two_ref, last_ref), mixed_refs, refs = refs[:3], refs[3:7], refs[7:]
    out_ref, mixed_ref, held, held_mixed = refs
    ndp, _, width = held.shape
    tokens = x_ref.shape[0] * x_ref.shape[2]
    z = lax.axis_index("dp")

    @pl.when(pl.program_id(0) == 0)
    def _():
        for piece, ahead in zip((own_ref, two_ref.at[0], two_ref.at[1], last_ref), (0, -1, 1, 2)):
            held[wrapped(z + ahead, ndp)] = piece[...]
        for back in range(ndp):
            held_mixed[wrapped(z - back, ndp)] = mixed_refs[back][...]
        for owner in range(ndp):
            mixed_ref[:, owner * width : (owner + 1) * width] = held_mixed[owner]

    at = pl.ds(pl.multiple_of(pl.program_id(0) * tokens, 16), tokens)
    for place, product in weight_products(x_ref, held, at, x_ref.shape[1]):
        out_ref[0, place, :] = scale * (part_ref[0, place, :].astype(F32) + product)


def delayed(values, count):
    row = lax.broadcasted_iota(jnp.int32, values.shape, 0)
    return jnp.where(row >= count, pltpu.roll(values, count, 0), 0.0)


def advanced(values, count):
    rows = values.shape[0]
    row = lax.broadcasted_iota(jnp.int32, values.shape, 0)
    return jnp.where(row < rows - count, pltpu.roll(values, rows - count, 0), 0.0)


def middle_body(scale, nshort, nrow, *refs):
    sums, refs = (refs[:3], refs[3:6]), refs[6:]
    (sf_ref, causal_ref, anti_ref), refs = refs[:3], refs[3:]
    *refs, m_ref, gm_ref, mixed_ref, go_ref = refs
    ndp = len(refs) // 2 - 1
    go_refs, (near_ref, other_ref), mixed_refs = refs[:ndp], refs[ndp : ndp + 2], refs[ndp + 2 :]
    tokens, width = go_ref.shape
    for behind, piece in enumerate(go_refs):
        at = wrapped(lax.axis_index("dp") - behind, ndp) * (tokens // ndp)
        go_ref[pl.ds(pl.multiple_of(at, 16), tokens // ndp)] = piece[...]
    row = lax.axis_index("row")
    nblocks = nrow // 2
    rows = tokens // nrow

    def places():
        for chunk, start in enumerate((row, row + 1 - 2 * lax.rem(row, 2))):
            for block in range(nblocks):
                at = tokens_of(wrapped(start - 2 * block, nrow), nrow) * rows
                for i in range(3):
                    yield chunk, (i * nblocks + block) * rows, pl.multiple_of(i * tokens + at, 16)

    for chunk, place, at in places():
        held = [ref[place : place + rows].astype(F32) for ref in sums[chunk]]
        m_ref[pl.ds(at, rows)] = held[0] + held[1] + held[2]
    groups, block, span = causal_ref.shape
    members = width // groups
    nspans = tokens // block
    lane = lax.broadcasted_iota(jnp.int32, (block, width), 1) // members
    lanes = lax.broadcasted_iota(jnp.int32, (block, 2 * width), 1) % width // members

    def past(i, j):
        held = m_ref[i * tokens : (i + 1) * tokens]
        return held if j == 0 else delayed(held, j)

    def taps(j, i):
        return sf_ref[3 * j + i : 3 * j + i + 1, :]

    feats = [sum(taps(j, i) * past(i, j) for j in range(nshort)) for i in range(3)]
    product = (feats[1] * feats[2]).astype(BF16)
    zero = jnp.zeros((block, width), BF16)
    p_blocks = [zero] + [product[b * block : (b + 1) * block] for b in range(nspans)]
    p_pairs = [jnp.concatenate(p_blocks[b : b + 2], axis=0) for b in range(nspans)]

    def filtered(band_ref, pairs):
        bands = band_ref[...].reshape(groups * block, span)
        out = []
        for b in range(0, nspans, 2):
            both = jnp.dot(bands, jnp.concatenate(pairs[b : b + 2], axis=1), preferred_element_type=F32)
            for h in range(2):
                part = both[:, h * width : (h + 1) * width]
                picked = part[:block]
                for g in range(1, groups):
                    picked = jnp.where(lane == g, part[g * block : (g + 1) * block], picked)
                out.append(picked)
        return jnp.concatenate(out, axis=0)

    conv = filtered(causal_ref, p_pairs)
    upstream = go_ref[...].astype(F32)
    mixed_ref[...] = (feats[0] * conv).astype(BF16)
    for ahead, out_ref in enumerate(mixed_refs):
        at = pl.multiple_of(wrapped(lax.axis_index("dp") + ahead, ndp) * (tokens // ndp), 16)
        out_ref[...] = mixed_ref[pl.ds(at, tokens // ndp)]
    grad_conv = (upstream * feats[0]).astype(BF16)
    c_blocks = [grad_conv[b * block : (b + 1) * block] for b in range(nspans)] + [zero]
    c_pairs = [jnp.concatenate(c_blocks[b : b + 2], axis=0) for b in range(nspans)]
    grad_product = filtered(anti_ref, c_pairs)

    corr = jnp.zeros((groups * block, span), F32)
    for b in range(0, nspans, 2):
        left = jnp.concatenate(c_blocks[b : b + 2], axis=1)
        stacked = jnp.concatenate(
            [jnp.where(lanes == g, left, jnp.zeros_like(left)) for g in range(groups)], axis=0
        )
        right = jnp.concatenate(p_pairs[b : b + 2], axis=1)
        corr += lax.dot_general(stacked, right, (((1,), (1,)), ((), ())), preferred_element_type=F32)
    turn = lax.broadcasted_iota(jnp.int32, (8, span), 0)
    sums = []
    for g in range(groups):
        part = corr[g * block : (g + 1) * block]
        count = block
        while count > 8:
            count //= 2
            part = part[:count] + pltpu.roll(part[count:], span - count, 1)
        for bit in (1, 2, 4):
            part = jnp.where((turn & bit) != 0, pltpu.roll(part, span - bit, 1), part)
        sums.append(jnp.sum(part, axis=0, keepdims=True))
    by_lag = jnp.concatenate(sums, axis=0)
    by_lag = (scale * pltpu.roll(by_lag, span - 1, 1)[:, :block]).astype(BF16)
    ahead = lax.broadcasted_iota(jnp.int32, (block, block), 0)
    back = lax.broadcasted_iota(jnp.int32, (block, block), 1)
    turned = jnp.where(ahead + back == block - 1, 1.0, 0.0).astype(BF16)
    by_lag = jnp.dot(by_lag, turned, preferred_element_type=F32)

    grad_feats = [upstream * conv, grad_product * feats[2], grad_product * feats[1]]
    short_rows = []
    for j in range(nshort):
        for i in range(3):
            short_rows.append(scale * jnp.sum(grad_feats[i] * past(i, j), axis=0, keepdims=True))
    for i in range(3):
        total = taps(0, i) * grad_feats[i]
        for j in range(1, nshort):
            total += taps(j, i) * advanced(grad_feats[i], j)
        gm_ref[i * tokens : (i + 1) * tokens] = total.astype(BF16)
    for chunk, place, at in places():
        (near_ref, other_ref)[chunk][place : place + rows] = gm_ref[pl.ds(at, rows)]
    tail = near_ref.shape[0] - 3 * tokens // 2 - groups - 3 * nshort
    small = jnp.concatenate([by_lag] + short_rows + [jnp.zeros((tail, width), F32)], axis=0)
    near_ref[3 * tokens // 2 :] = small.astype(BF16)


def sum_over_line(own, right, far, left):
    ndp = lax.axis_size("dp")
    from_left = lax.ppermute(far, "dp", [(a, a + 1) for a in range(ndp // 2)])
    from_right = lax.ppermute(far, "dp", [(a, a - 1) for a in range(ndp // 2, ndp)])
    rightward = lax.ppermute(right + from_left, "dp", [(a, (a + 1) % ndp) for a in range(ndp)])
    leftward = lax.ppermute(left + from_right, "dp", [(a, (a - 1) % ndp) for a in range(ndp)])
    return own, rightward, leftward


def gather_over_line(own, across):
    ndp, nrow = lax.axis_size("dp"), lax.axis_size("row")

    def shift(count):
        return [
            (a * nrow + r, (a + count) % ndp * nrow + (r + 1 - 2 * (r % 2) if across else r))
            for a in range(ndp)
            for r in range(nrow)
        ]

    before = lax.ppermute(own, ("dp", "row"), shift(1))
    after = lax.ppermute(own, ("dp", "row"), shift(-1))
    here = lax.ppermute(own, ("dp", "row"), shift(0)) if across else own
    far_before = lax.ppermute(before, "dp", [(a - 1, a) for a in range(ndp // 2, ndp)])
    far_after = lax.ppermute(after, "dp", [(a + 1, a) for a in range(ndp // 2)])
    return here, before, after, far_before, far_after


def move_activations(tokens, in_weight, short_filter, long_filter, grad_out):
    ndp, nrow, ncol = (lax.axis_size(a) for a in ("dp", "row", "col"))
    z = lax.axis_index("dp")
    rows, dcol = tokens.shape
    local = grad_out.shape[1]
    nshort = short_filter.shape[0]
    ngroups, ntaps = long_filter.shape
    seq = rows * ndp
    width, groups = local // ndp, ngroups // ndp
    drow = in_weight.shape[0]
    scale = float(seq) ** -0.5
    nblocks = nrow // 2
    chunk = nblocks * rows
    swap = [(tokens_of(b, nrow) * nrow + a, a * nrow + b) for a in range(ndp) for b in range(nrow)]
    swap_back = [(b, a) for a, b in swap]
    partner = [(a, a + 1 - 2 * (a % 2)) for a in range(nrow)]
    places = [(dy, dx) for dy in range(nblocks) for dx in range(ncol)]

    def offset(dy, dx):
        return [
            (a * ncol + b, (a + 2 * dy) % nrow * ncol + (b + dx) % ncol) for a in range(nrow) for b in range(ncol)
        ]

    w = jnp.transpose(in_weight, (1, 0, 2))
    moved = lax.ppermute(tokens, ("dp", "row"), swap)
    far_w = kernel_call(
        far_columns_body,
        shaped((3, drow, width), BF16),
        in_specs=[pl.BlockSpec(memory_space=pl.ANY)],
        out_specs=pl.BlockSpec(memory_space=pltpu.VMEM),
        scratch=[pltpu.SemaphoreType.DMA],
    )(w)
    turn = [[(a, (a + ahead) % ndp) for a in range(ndp)] for ahead in range(ndp)]
    upstream = [*kernel_call(split_body, [shaped((rows, width), BF16)] * ndp)(grad_out)]
    moved, upstream, far_w = lax.optimization_barrier((moved, upstream, far_w))
    near = [moved] + [lax.ppermute(moved, ("row", "col"), offset(*p)) for p in places[1:]]
    for ahead in (1, 3):
        upstream[ahead] = lax.ppermute(upstream[ahead], "dp", turn[ahead])
    upstream[1::2], near[1:] = lax.optimization_barrier((upstream[1::2], near[1:]))
    x0 = jnp.stack(near).reshape(nblocks, ncol, rows, dcol)
    x1 = lax.ppermute(x0, "row", partner)
    upstream[2] = lax.ppermute(upstream[2], "dp", turn[2])
    upstream[2], x1 = lax.optimization_barrier((upstream[2], x1))

    sf = lax.dynamic_slice_in_dim(short_filter, z * width, width, 2).reshape(3 * nshort, width)
    lf = lax.dynamic_slice_in_dim(long_filter, z * groups, groups, 0).astype(F32)
    zeros = functools.partial(jnp.zeros, dtype=F32)
    bases = jnp.concatenate(
        [
            jnp.concatenate([zeros((groups, 1)), lf[:, ::-1], zeros((groups, ntaps - 1))], axis=1),
            jnp.concatenate([lf, zeros((groups, ntaps))], axis=1),
        ],
        axis=0,
    )
    bands = kernel_call(bands_body, shaped((2 * groups, ntaps, 2 * ntaps), BF16))(bases)

    mm_flops = seq * drow * 3 * local
    mm_bytes = seq * drow + 6 * drow * local + 3 * seq * local
    sums = []
    for x in (x0, x1):
        parts = kernel_call(
            project_body,
            [shaped((3, chunk, width), BF16)] * ndp,
            grid=(3,),
            in_specs=[
                pl.BlockSpec((nblocks, ncol, rows, dcol), lambda i: (0, 0, 0, 0)),
                pl.BlockSpec((1, drow, local), lambda i: (i, 0, 0)),
            ],
            out_specs=[pl.BlockSpec((1, chunk, width), lambda i: (i, 0, 0))] * ndp,
            scratch=[pltpu.VMEM((ndp, chunk, width), BF16)],
            flops=mm_flops,
            nbytes=mm_bytes,
        )(x, w)
        sums += sum_over_line(*(p.reshape(3 * chunk, width) for p in parts))

    extra = -(-(groups + 3 * nshort) // 16) * 16
    half = pl.BlockSpec((groups, ntaps, 2 * ntaps), lambda i: (0, 0, 0))
    other = pl.BlockSpec((groups, ntaps, 2 * ntaps), lambda i: (1, 0, 0))
    whole = lambda *shape: pl.BlockSpec(shape, lambda i: (0,) * len(shape))
    grad_near, grad_other, *mixed = kernel_call(
        functools.partial(middle_body, scale, nshort, nrow),
        [shaped((3 * chunk + extra, width), BF16), shaped((3 * chunk, width), BF16)]
        + [shaped((rows, width), BF16)] * ndp,
        grid=(1,),
        in_specs=[whole(3 * chunk, width)] * 6
        + [whole(3 * nshort, width), half, other]
        + [whole(rows, width)] * ndp,
        out_specs=[whole(3 * chunk + extra, width), whole(3 * chunk, width)] + [whole(rows, width)] * ndp,
        scratch=[
            pltpu.VMEM((3 * seq, width), F32),
            pltpu.VMEM((3 * seq, width), BF16),
            pltpu.VMEM((seq, width), BF16),
            pltpu.VMEM((seq, width), BF16),
        ],
        flops=3 * 2 * groups * ntaps * 2 * ntaps * width * (seq // ntaps),
        nbytes=2 * width * seq * 14,
        vmem=MOST_VMEM_BYTES,
    )(*sums, sf, bands, bands, *upstream)
    mixed = [mixed[0]] + [
        lax.ppermute(part, "dp", [(a, (a + ahead) % ndp) for a in range(ndp)])
        for ahead, part in enumerate(mixed)
        if ahead
    ]
    *near, near_far_before, near_far_after = gather_over_line(grad_near, False)
    *far, far_far_before, far_far_after = gather_over_line(grad_other, True)
    partner_w = lax.ppermute(w, "row", partner)
    everywhere = pl.BlockSpec(memory_space=pl.ANY)
    in_vmem = pl.BlockSpec(memory_space=pltpu.VMEM)
    part, far_two = kernel_call(
        first_grad_body,
        [shaped((ncol, chunk, dcol), BF16), shaped((2, 3 * chunk, width), BF16)],
        in_specs=[in_vmem] * 6 + [everywhere] * 2,
        out_specs=[in_vmem] * 2,
        scratch=[
            pltpu.VMEM((2, ndp, 3 * chunk, width), BF16),
            pltpu.VMEM((2, ncol, 3, dcol, local), BF16),
            pltpu.SemaphoreType.DMA((2, ncol)),
        ],
        flops=2 * mm_flops,
        nbytes=2 * mm_bytes,
    )(*near, *far, w, partner_w)
    near_last, far_last, *blocks = kernel_call(
        functools.partial(second_grad_body, ndp),
        [shaped(grad_near.shape, BF16), shaped(grad_other.shape, BF16)]
        + [shaped((rows, dcol), BF16)] * len(places),
        grid=(),
        in_specs=[everywhere] * 7,
        out_specs=[in_vmem] * (2 + len(places)),
        scratch=[
            pltpu.VMEM((2, 3, drow, width), BF16),
            pltpu.VMEM((ncol, chunk, dcol), BF16),
            pltpu.SemaphoreType.DMA((5,)),
        ],
        flops=mm_flops // 2,
        nbytes=mm_bytes // 2,
        vmem=MOST_VMEM_BYTES,
    )(part, near_far_before, near_far_after, far_far_before, far_far_after, far_w, partner_w)
    far_two, far_last, mixed[1:] = lax.optimization_barrier((far_two, far_last, mixed[1:]))
    far_two, far_last = (lax.ppermute(part, "row", partner) for part in (far_two, far_last))
    arrivals = [
        lax.ppermute(sent, ("row", "col"), [(b, a) for a, b in offset(*p)])
        for p, sent in zip(places[1:], blocks[1:])
    ]
    arrived = sum((a.astype(F32) for a in arrivals), blocks[0].astype(F32)).astype(BF16)
    one_of_three = pl.BlockSpec((1, drow, local), lambda i: (i, 0, 0))
    own_part, grad_long, grad_short = kernel_call(
        own_weight_grad_body,
        [shaped((3, drow, local), BF16), shaped((ngroups, ntaps), F32), shaped((nshort, 3, local), F32)],
        grid=(3,),
        in_specs=[whole(nblocks, ncol, rows, dcol)] + [whole(*grad_near.shape)] * 4,
        out_specs=[one_of_three, whole(ngroups, ntaps), whole(nshort, 3, local)],
        scratch=[pltpu.VMEM((ndp, 3 * chunk + extra, width), BF16)],
        flops=mm_flops,
        nbytes=mm_bytes,
        vmem=MOST_VMEM_BYTES,
    )(x0, *near, near_last)
    arrived, far_two, far_last, own_part = lax.optimization_barrier((arrived, far_two, far_last, own_part))
    grad_in = lax.ppermute(arrived, ("dp", "row"), swap_back)

    grad_weight, mixed = kernel_call(
        functools.partial(weight_grad_body, scale),
        [shaped((3, drow, local), F32), shaped((rows, local), BF16)],
        grid=(3,),
        in_specs=[whole(nblocks, ncol, rows, dcol), one_of_three]
        + [whole(*grad_other.shape), whole(*far_two.shape), whole(*far_last.shape)]
        + [whole(rows, width)] * ndp,
        out_specs=[one_of_three, whole(rows, local)],
        scratch=[pltpu.VMEM((ndp, 3 * chunk, width), BF16), pltpu.VMEM((ndp, rows, width), BF16)],
        flops=mm_flops,
        nbytes=mm_bytes,
        vmem=MOST_VMEM_BYTES,
    )(x1, own_part, grad_other, far_two, far_last, *mixed)
    grad_weight = jnp.transpose(grad_weight, (1, 0, 2))
    return (mixed, grad_in, grad_weight, grad_long, grad_short)


def from_behind(block, axis, distance):
    devices = range(lax.axis_size(axis))
    route = [(i - distance, i) for i in devices if i - distance in devices]
    return lax.ppermute(block, axis, route)


def toeplitz(leading, rows, span):
    groups = leading.shape[0]
    width = rows + span
    seed_row = jnp.concatenate(
        [leading, jnp.zeros((groups, width - leading.shape[1]), leading.dtype)], axis=1
    )
    tiled = jnp.tile(seed_row, (1, rows))
    skewed = tiled[:, : rows * (width - 1)].reshape(groups, rows, width - 1)
    return skewed[:, :, :span]


def to_groups(values, ngroups, members):
    count = values.shape[0]
    return values.reshape(count, ngroups, members).transpose(1, 2, 0)


def from_groups(values):
    groups, members, count = values.shape
    return values.transpose(2, 0, 1).reshape(count, groups * members)


def move_weights(tokens, in_weight, short_filter, long_filter, grad_out):
    rows = tokens.shape[0]
    local = grad_out.shape[1]
    nshort = short_filter.shape[0]
    ntaps = long_filter.shape[1]
    ngroups = long_filter.shape[0]
    members = local // ngroups
    margin = ntaps - 1
    span = rows + margin
    scale = float(rows * lax.axis_size("dp")) ** (-0.5)
    whole = lax.all_gather(tokens, ("row", "col"), axis=1, tiled=True)
    full_w = lax.all_gather(in_weight, "dp", axis=0, tiled=True)
    mixed_in = jnp.einsum("sd,dic->sic", whole, full_w, preferred_element_type=jnp.float32).astype(
        jnp.bfloat16
    )
    before = from_behind(mixed_in[rows - margin - nshort + 1 :], "dp", 1)
    extended = jnp.concatenate([before, mixed_in], axis=0).astype(jnp.float32)
    long_feats = jnp.zeros((span, 3, local), jnp.float32)
    for j in range(nshort):
        long_feats = (
            long_feats + short_filter[j][None] * extended[nshort - 1 - j : nshort - 1 - j + span]
        )
    product_ext = (long_feats[:, 1] * long_feats[:, 2]).astype(jnp.bfloat16)
    feats = long_feats[margin:]
    short_rows = extended[margin:]
    product_cols = to_groups(product_ext, ngroups, members)
    causal = toeplitz(long_filter[:, ::-1], rows, span)
    conv = from_groups(
        jnp.einsum("gst,gct->gcs", causal, product_cols, preferred_element_type=jnp.float32)
    )
    mixed = (feats[:, 0] * conv).astype(jnp.bfloat16)
    upstream = grad_out.astype(jnp.float32)
    grad_query = upstream * conv
    grad_conv = (upstream * feats[:, 0]).astype(jnp.bfloat16)
    after = from_behind(grad_conv[:margin], "dp", -1)
    grad_ext = jnp.concatenate([grad_conv, after], axis=0)
    anti = toeplitz(long_filter, rows, span)
    grad_product = from_groups(
        jnp.einsum(
            "gst,gct->gcs",
            anti,
            to_groups(grad_ext, ngroups, members),
            preferred_element_type=jnp.float32,
        )
    )
    reversed_cols = jnp.concatenate(
        [product_cols[:, :, ::-1], jnp.zeros((ngroups, members, rows), product_cols.dtype)], axis=2
    )
    width = span + rows
    pairs = jnp.einsum(
        "gcs,gcu->gsu",
        to_groups(grad_conv, ngroups, members),
        reversed_cols,
        preferred_element_type=jnp.float32,
    )
    diagonal = pairs.reshape(ngroups, rows * width)[:, : rows * (width - 1)].reshape(
        ngroups, rows, width - 1
    )
    filter_part = jnp.sum(diagonal[:, :, rows - 1 : rows - 1 + ntaps], axis=1)
    grad_feats = jnp.stack(
        [grad_query, grad_product * feats[:, 2], grad_product * feats[:, 1]], axis=1
    )
    later = from_behind(grad_feats[: nshort - 1], "dp", -1)
    feats_ext = jnp.concatenate([grad_feats, later], axis=0)
    grad_acc = jnp.zeros((rows, 3, local), jnp.float32)
    for j in range(nshort):
        grad_acc = grad_acc + short_filter[j][None] * feats_ext[j : j + rows]
    grad_mixed = grad_acc.astype(jnp.bfloat16)
    short_part = jnp.stack(
        [
            jnp.sum(grad_feats * short_rows[nshort - 1 - j : nshort - 1 - j + rows], axis=0)
            for j in range(nshort)
        ]
    )
    filter_total, short_total = (
        lax.psum(filter_part.astype(jnp.bfloat16), "dp").astype(jnp.float32),
        lax.psum(short_part.astype(jnp.bfloat16), "dp").astype(jnp.float32),
    )
    grad_long = filter_total * scale
    grad_short = short_total * scale
    partial_in = jnp.einsum("sic,dic->sd", grad_mixed, full_w, preferred_element_type=jnp.float32)
    summed_in = lax.psum_scatter(
        partial_in.astype(jnp.bfloat16), ("row", "col"), scatter_dimension=1, tiled=True
    )
    weight_term = (
        jnp.einsum("sd,sic->dic", whole, grad_mixed, preferred_element_type=jnp.float32) * scale
    )
    grad_weight = lax.psum_scatter(
        weight_term.astype(jnp.bfloat16), "dp", scatter_dimension=0, tiled=True
    ).astype(jnp.float32)
    return (mixed, summed_in, grad_weight, grad_long, grad_short)


def fits_whole_sequences(mesh, tokens, in_weight, short_filter, long_filter, grad_out):
    ndp, nrow, ncol = (mesh.shape[a] for a in ("dp", "row", "col"))
    seq, channels = grad_out.shape
    groups, ntaps = long_filter.shape
    local = channels // (nrow * ncol)
    width, rows = local // ndp, seq // ndp
    return (
        seq < tokens.shape[1]
        and ndp == nrow == 4
        and ncol * (tokens.shape[1] // (nrow * ncol)) == in_weight.shape[0] // ndp
        and ntaps == width == 128
        and seq % (2 * ntaps) == 0
        and rows % 16 == 0
        and groups % (8 * ndp * nrow * ncol) == 0
    )


def solution(mesh):
    placed = (
        P("dp", ("row", "col")),
        P("dp", None, ("row", "col")),
        P(None, None, ("row", "col")),
        P(("row", "col"), None),
        P("dp", ("row", "col")),
    )
    gives = (
        P("dp", ("row", "col")),
        P("dp", ("row", "col")),
        P("dp", None, ("row", "col")),
        P(("row", "col"), None),
        P(None, None, ("row", "col")),
    )

    def run(*arrays):
        plan = move_activations if fits_whole_sequences(mesh, *arrays) else move_weights
        return jax.shard_map(
            plan, mesh=mesh, in_specs=placed, out_specs=gives, check_vma=False
        )(*arrays)

    return run
```

```python
import functools

import jax
import jax.numpy as jnp
from jax import lax
from jax.experimental import pallas as pl
from jax.experimental.pallas import tpu as pltpu
from jax.sharding import PartitionSpec as P

VMEM_BYTES = 48 * 2**20
MOST_VMEM_BYTES = 62 * 2**20
F32 = jnp.float32
BF16 = jnp.bfloat16


def kernel_call(body, outs, grid=(), in_specs=None, out_specs=None, scratch=(), flops=0, nbytes=0, vmem=VMEM_BYTES):
    kwargs = {}
    if in_specs is not None:
        kwargs = dict(grid=grid, in_specs=in_specs, out_specs=out_specs)
    return pl.pallas_call(
        body,
        out_shape=outs,
        scratch_shapes=scratch,
        compiler_params=pltpu.CompilerParams(vmem_limit_bytes=vmem),
        cost_estimate=pl.CostEstimate(flops=flops, bytes_accessed=nbytes, transcendentals=0),
        **kwargs,
    )


def shaped(shape, dtype):
    return jax.ShapeDtypeStruct(shape, dtype)


def bands_body(base_ref, out_ref):
    groups, wide = base_ref.shape
    rows = out_ref.shape[1]
    row = lax.broadcasted_iota(jnp.int32, (8, wide), 0)
    for g in range(groups):
        band = jnp.broadcast_to(base_ref[g : g + 1, :], (8, wide))
        for bit in (1, 2, 4):
            band = jnp.where((row & bit) != 0, pltpu.roll(band, bit, 1), band)
        count = 8
        while count < rows:
            band = jnp.concatenate([band, pltpu.roll(band, count, 1)], axis=0)
            count *= 2
        out_ref[g] = band.astype(out_ref.dtype)


def tokens_of(row, nrow):
    return row % 2 * (nrow // 2) + row // 2


def wrapped(value, size):
    return lax.rem(value + 2 * size, size)


def split_body(all_ref, *out_refs):
    width = out_refs[0].shape[1]
    for ahead, out_ref in enumerate(out_refs):
        at = wrapped(lax.axis_index("dp") + ahead, len(out_refs)) * width
        out_ref[...] = all_ref[:, pl.ds(pl.multiple_of(at, width), width)]


def project_body(x_ref, w_ref, *refs):
    *out_refs, held = refs
    z, col = lax.axis_index("dp"), lax.axis_index("col")
    nblocks, ncol, rows, depth = x_ref.shape
    width = held.shape[2]
    total = jnp.zeros((nblocks * rows, w_ref.shape[2]), F32)
    for dx in range(ncol):
        start = pl.multiple_of(wrapped(col - dx, ncol) * depth, depth)
        total += jnp.dot(
            x_ref[:, dx].reshape(nblocks * rows, depth),
            w_ref[0, pl.ds(start, depth), :],
            preferred_element_type=F32,
        )
    for owner in range(len(out_refs)):
        held[owner] = total[:, owner * width : (owner + 1) * width].astype(BF16)
    for ahead, out_ref in enumerate(out_refs):
        out_ref[0] = held[wrapped(z + ahead, len(out_refs))]


def far_columns_body(w_ref, out_ref, sem):
    ndp = lax.axis_size("dp")
    width = out_ref.shape[2]
    start = wrapped(lax.axis_index("dp") + ndp // 2, ndp) * width
    copy = pltpu.make_async_copy(w_ref.at[:, :, pl.ds(pl.multiple_of(start, width), width)], out_ref, sem)
    copy.start()
    copy.wait()


def first_grad_body(
    near, near_before, near_after, far, far_before, far_after, w_ref, partner_w_ref, out_ref, far_ref, held, held_w, sems
):
    _, ndp, _, width = held.shape
    ncol, tokens, depth = out_ref.shape
    z, col = lax.axis_index("dp"), lax.axis_index("col")
    copies = []
    for dx in range(ncol):
        start = pl.multiple_of(wrapped(col - dx, ncol) * depth, depth)
        for k, weights in enumerate((w_ref, partner_w_ref)):
            copy = pltpu.make_async_copy(weights.at[:, pl.ds(start, depth)], held_w.at[k, dx], sems.at[k, dx])
            copy.start()
            copies.append(copy)
    far_ref[0], far_ref[1] = far_before[...], far_after[...]
    for k, pieces in enumerate(((near, near_before, near_after), (far, far_before, far_after))):
        held[k, wrapped(z + ndp // 2, ndp)] = jnp.zeros(held.shape[2:], BF16)
        for ahead, piece in zip((0, -1, 1), pieces):
            held[k, wrapped(z + ahead, ndp)] = piece[: 3 * tokens]
    for dx in range(ncol):
        total = jnp.zeros((tokens, depth), F32)
        for k in range(2):
            copies[2 * dx + k].wait()
            for i in range(3):
                rows = slice(i * tokens, (i + 1) * tokens)
                total += lax.dot_general(
                    jnp.concatenate([held[k, owner, rows] for owner in range(ndp)], axis=1),
                    held_w[k, dx, i],
                    (((1,), (1,)), ((), ())),
                    preferred_element_type=F32,
                )
        out_ref[dx] = total.astype(BF16)


def second_grad_body(ndp, part_ref, *refs):
    arrived, (w_ref, partner_w_ref), refs = (refs[:2], refs[2:4]), refs[4:6], refs[6:]
    (near_ref, far_ref), refs = refs[:2], refs[2:]
    *out_refs, held_w, held_part, sems = refs
    ncol, tokens, depth = held_part.shape
    rows = out_refs[0].shape[0]
    width = near_ref.shape[1]
    z, col = lax.axis_index("dp"), lax.axis_index("col")
    lanes = pl.ds(pl.multiple_of(wrapped(z + ndp // 2, ndp) * width, width), width)
    copies = [
        pltpu.make_async_copy(w_ref, held_w.at[0], sems.at[0]),
        pltpu.make_async_copy(partner_w_ref.at[:, :, lanes], held_w.at[1], sems.at[1]),
    ]
    copies.append(pltpu.make_async_copy(part_ref, held_part, sems.at[2]))
    for copy in copies:
        copy.start()
    for k, (pair, target) in enumerate(zip(arrived, (near_ref, far_ref))):
        for source, here in zip(pair, (z >= ndp // 2, z < ndp // 2)):

            @pl.when(here)
            def _(source=source, target=target, k=k):
                copy = pltpu.make_async_copy(source, target, sems.at[3 + k])
                copy.start()
                copy.wait()

    for copy in copies:
        copy.wait()
    left = jnp.concatenate(
        [ref[i * tokens : (i + 1) * tokens] for ref in (near_ref, far_ref) for i in range(3)], axis=1
    )
    for dx in range(ncol):
        start = pl.multiple_of(wrapped(col - dx, ncol) * depth, depth)
        right = jnp.concatenate([held_w[k, i, pl.ds(start, depth), :] for k in range(2) for i in range(3)], axis=1)
        total = held_part[dx].astype(F32) + lax.dot_general(
            left, right, (((1,), (1,)), ((), ())), preferred_element_type=F32
        )
        for block in range(tokens // rows):
            out_refs[block * ncol + dx][...] = total[block * rows : (block + 1) * rows].astype(BF16)


def weight_grad_body(scale, *refs):
    (x0_ref, x1_ref), near_refs, other_refs, mixed_refs, refs = refs[:2], refs[2:6], refs[6:9], refs[9:13], refs[13:]
    own_ref, two_ref, last_ref = other_refs
    other = (own_ref, two_ref.at[0], two_ref.at[1], last_ref)
    out_ref, mixed_ref, long_ref, short_ref, held, held_mixed = refs
    nblocks, ncol, rows, depth = x0_ref.shape
    _, ndp, _, width = held.shape
    tokens = nblocks * rows
    i = pl.program_id(0)
    z, col = lax.axis_index("dp"), lax.axis_index("col")

    @pl.when((i == 0) & (pl.program_id(1) == 0))
    def _():
        groups = long_ref.shape[0] // ndp
        for k, ahead in enumerate((0, -1, 1, 2)):
            owner = wrapped(z + ahead, ndp)
            held[0, owner] = near_refs[k][...]
            held[1, owner, : 3 * tokens] = other[k][...]
        for back in range(ndp):
            held_mixed[wrapped(z - back, ndp)] = mixed_refs[back][...]
        for owner in range(ndp):
            lanes = slice(owner * width, (owner + 1) * width)
            mixed_ref[:, lanes] = held_mixed[owner]
            small = held[0, owner, 3 * tokens :].astype(F32)
            long_ref[owner * groups : (owner + 1) * groups] = small[:groups]
            nshort, three, _ = short_ref.shape
            for j in range(nshort):
                short_ref[j, :, lanes] = small[groups + three * j : groups + three * (j + 1)]

    at = pl.ds(pl.multiple_of(i * tokens, 16), tokens)
    gm = jnp.concatenate(
        [jnp.concatenate([held[k, owner, at, :] for owner in range(ndp)], axis=1) for k in range(2)], axis=0
    )
    dx = wrapped(col - pl.program_id(1), ncol)
    x = jnp.concatenate([x_ref[:, dx].reshape(tokens, depth) for x_ref in (x0_ref, x1_ref)], axis=0)
    out_ref[0] = scale * lax.dot_general(x, gm, (((0,), (0,)), ((), ())), preferred_element_type=F32)


def delayed(values, count):
    row = lax.broadcasted_iota(jnp.int32, values.shape, 0)
    return jnp.where(row >= count, pltpu.roll(values, count, 0), 0.0)


def advanced(values, count):
    rows = values.shape[0]
    row = lax.broadcasted_iota(jnp.int32, values.shape, 0)
    return jnp.where(row < rows - count, pltpu.roll(values, rows - count, 0), 0.0)


def middle_body(scale, nshort, nrow, *refs):
    sums, refs = (refs[:3], refs[3:6]), refs[6:]
    (sf_ref, causal_ref, anti_ref), refs = refs[:3], refs[3:]
    *refs, m_ref, gm_ref, mixed_ref, go_ref = refs
    ndp = len(refs) // 2 - 1
    go_refs, (near_ref, other_ref), mixed_refs = refs[:ndp], refs[ndp : ndp + 2], refs[ndp + 2 :]
    tokens, width = go_ref.shape
    for behind, piece in enumerate(go_refs):
        at = wrapped(lax.axis_index("dp") - behind, ndp) * (tokens // ndp)
        go_ref[pl.ds(pl.multiple_of(at, 16), tokens // ndp)] = piece[...]
    row = lax.axis_index("row")
    nblocks = nrow // 2
    rows = tokens // nrow

    def places():
        for chunk, start in enumerate((row, row + 1 - 2 * lax.rem(row, 2))):
            for block in range(nblocks):
                at = tokens_of(wrapped(start - 2 * block, nrow), nrow) * rows
                for i in range(3):
                    yield chunk, (i * nblocks + block) * rows, pl.multiple_of(i * tokens + at, 16)

    for chunk, place, at in places():
        held = [ref[place : place + rows].astype(F32) for ref in sums[chunk]]
        m_ref[pl.ds(at, rows)] = held[0] + held[1] + held[2]
    groups, block, span = causal_ref.shape
    members = width // groups
    nspans = tokens // block
    lane = lax.broadcasted_iota(jnp.int32, (block, width), 1) // members
    lanes = lax.broadcasted_iota(jnp.int32, (block, 2 * width), 1) % width // members

    def past(i, j):
        held = m_ref[i * tokens : (i + 1) * tokens]
        return held if j == 0 else delayed(held, j)

    def taps(j, i):
        return sf_ref[3 * j + i : 3 * j + i + 1, :]

    feats = [sum(taps(j, i) * past(i, j) for j in range(nshort)) for i in range(3)]
    product = (feats[1] * feats[2]).astype(BF16)
    zero = jnp.zeros((block, width), BF16)
    p_blocks = [zero] + [product[b * block : (b + 1) * block] for b in range(nspans)]
    p_pairs = [jnp.concatenate(p_blocks[b : b + 2], axis=0) for b in range(nspans)]

    def filtered(band_ref, pairs):
        bands = band_ref[...].reshape(groups * block, span)
        out = []
        for b in range(0, nspans, 2):
            both = jnp.dot(bands, jnp.concatenate(pairs[b : b + 2], axis=1), preferred_element_type=F32)
            for h in range(2):
                part = both[:, h * width : (h + 1) * width]
                picked = part[:block]
                for g in range(1, groups):
                    picked = jnp.where(lane == g, part[g * block : (g + 1) * block], picked)
                out.append(picked)
        return jnp.concatenate(out, axis=0)

    conv = filtered(causal_ref, p_pairs)
    upstream = go_ref[...].astype(F32)
    mixed_ref[...] = (feats[0] * conv).astype(BF16)
    for ahead, out_ref in enumerate(mixed_refs):
        at = pl.multiple_of(wrapped(lax.axis_index("dp") + ahead, ndp) * (tokens // ndp), 16)
        out_ref[...] = mixed_ref[pl.ds(at, tokens // ndp)]
    grad_conv = (upstream * feats[0]).astype(BF16)
    c_blocks = [grad_conv[b * block : (b + 1) * block] for b in range(nspans)] + [zero]
    c_pairs = [jnp.concatenate(c_blocks[b : b + 2], axis=0) for b in range(nspans)]
    grad_product = filtered(anti_ref, c_pairs)

    corr = jnp.zeros((groups * block, span), F32)
    for b in range(0, nspans, 2):
        left = jnp.concatenate(c_blocks[b : b + 2], axis=1)
        stacked = jnp.concatenate(
            [jnp.where(lanes == g, left, jnp.zeros_like(left)) for g in range(groups)], axis=0
        )
        right = jnp.concatenate(p_pairs[b : b + 2], axis=1)
        corr += lax.dot_general(stacked, right, (((1,), (1,)), ((), ())), preferred_element_type=F32)
    turn = lax.broadcasted_iota(jnp.int32, (8, span), 0)
    sums = []
    for g in range(groups):
        part = corr[g * block : (g + 1) * block]
        count = block
        while count > 8:
            count //= 2
            part = part[:count] + pltpu.roll(part[count:], span - count, 1)
        for bit in (1, 2, 4):
            part = jnp.where((turn & bit) != 0, pltpu.roll(part, span - bit, 1), part)
        sums.append(jnp.sum(part, axis=0, keepdims=True))
    by_lag = jnp.concatenate(sums, axis=0)
    by_lag = (scale * pltpu.roll(by_lag, span - 1, 1)[:, :block]).astype(BF16)
    ahead = lax.broadcasted_iota(jnp.int32, (block, block), 0)
    back = lax.broadcasted_iota(jnp.int32, (block, block), 1)
    turned = jnp.where(ahead + back == block - 1, 1.0, 0.0).astype(BF16)
    by_lag = jnp.dot(by_lag, turned, preferred_element_type=F32)

    grad_feats = [upstream * conv, grad_product * feats[2], grad_product * feats[1]]
    short_rows = []
    for j in range(nshort):
        for i in range(3):
            short_rows.append(scale * jnp.sum(grad_feats[i] * past(i, j), axis=0, keepdims=True))
    for i in range(3):
        total = taps(0, i) * grad_feats[i]
        for j in range(1, nshort):
            total += taps(j, i) * advanced(grad_feats[i], j)
        gm_ref[i * tokens : (i + 1) * tokens] = total.astype(BF16)
    for chunk, place, at in places():
        (near_ref, other_ref)[chunk][place : place + rows] = gm_ref[pl.ds(at, rows)]
    tail = near_ref.shape[0] - 3 * tokens // 2 - groups - 3 * nshort
    small = jnp.concatenate([by_lag] + short_rows + [jnp.zeros((tail, width), F32)], axis=0)
    near_ref[3 * tokens // 2 :] = small.astype(BF16)


def first_hop(far):
    ndp = lax.axis_size("dp")
    return (
        lax.ppermute(far, "dp", [(a, a + 1) for a in range(ndp // 2)]),
        lax.ppermute(far, "dp", [(a, a - 1) for a in range(ndp // 2, ndp)]),
    )


def second_hop(right, left, from_left, from_right):
    ndp = lax.axis_size("dp")
    rightward = lax.ppermute(right + from_left, "dp", [(a, (a + 1) % ndp) for a in range(ndp)])
    leftward = lax.ppermute(left + from_right, "dp", [(a, (a - 1) % ndp) for a in range(ndp)])
    return rightward, leftward


def gather_over_line(own, across):
    ndp, nrow = lax.axis_size("dp"), lax.axis_size("row")

    def shift(count):
        return [
            (a * nrow + r, (a + count) % ndp * nrow + (r + 1 - 2 * (r % 2) if across else r))
            for a in range(ndp)
            for r in range(nrow)
        ]

    before = lax.ppermute(own, ("dp", "row"), shift(1))
    after = lax.ppermute(own, ("dp", "row"), shift(-1))
    here = lax.ppermute(own, ("dp", "row"), shift(0)) if across else own
    far_before = lax.ppermute(before, "dp", [(a - 1, a) for a in range(ndp // 2, ndp)])
    far_after = lax.ppermute(after, "dp", [(a + 1, a) for a in range(ndp // 2)])
    return here, before, after, far_before, far_after


def move_activations(tokens, in_weight, short_filter, long_filter, grad_out):
    ndp, nrow, ncol = (lax.axis_size(a) for a in ("dp", "row", "col"))
    z = lax.axis_index("dp")
    rows, dcol = tokens.shape
    local = grad_out.shape[1]
    nshort = short_filter.shape[0]
    ngroups, ntaps = long_filter.shape
    seq = rows * ndp
    width, groups = local // ndp, ngroups // ndp
    drow = in_weight.shape[0]
    scale = float(seq) ** -0.5
    nblocks = nrow // 2
    chunk = nblocks * rows
    swap = [(tokens_of(b, nrow) * nrow + a, a * nrow + b) for a in range(ndp) for b in range(nrow)]
    swap_back = [(b, a) for a, b in swap]
    partner = [(a, a + 1 - 2 * (a % 2)) for a in range(nrow)]
    places = [(dy, dx) for dy in range(nblocks) for dx in range(ncol)]

    def offset(dy, dx):
        return [
            (a * ncol + b, (a + 2 * dy) % nrow * ncol + (b + dx) % ncol) for a in range(nrow) for b in range(ncol)
        ]

    w = jnp.transpose(in_weight, (1, 0, 2))
    moved = lax.ppermute(tokens, ("dp", "row"), swap)
    far_w = kernel_call(
        far_columns_body,
        shaped((3, drow, width), BF16),
        in_specs=[pl.BlockSpec(memory_space=pl.ANY)],
        out_specs=pl.BlockSpec(memory_space=pltpu.VMEM),
        scratch=[pltpu.SemaphoreType.DMA],
    )(w)
    turn = [[(a, (a + ahead) % ndp) for a in range(ndp)] for ahead in range(ndp)]
    upstream = [*kernel_call(split_body, [shaped((rows, width), BF16)] * ndp)(grad_out)]
    moved, upstream, far_w = lax.optimization_barrier((moved, upstream, far_w))
    near = [moved] + [lax.ppermute(moved, ("row", "col"), offset(*p)) for p in places[1:]]
    for ahead in (1, 3):
        upstream[ahead] = lax.ppermute(upstream[ahead], "dp", turn[ahead])
    upstream[1::2], near[1:] = lax.optimization_barrier((upstream[1::2], near[1:]))
    x0 = jnp.stack(near).reshape(nblocks, ncol, rows, dcol)
    x1 = lax.ppermute(x0, "row", partner)
    upstream[2] = lax.ppermute(upstream[2], "dp", turn[2])

    sf = lax.dynamic_slice_in_dim(short_filter, z * width, width, 2).reshape(3 * nshort, width)
    lf = lax.dynamic_slice_in_dim(long_filter, z * groups, groups, 0).astype(F32)
    zeros = functools.partial(jnp.zeros, dtype=F32)
    bases = jnp.concatenate(
        [
            jnp.concatenate([zeros((groups, 1)), lf[:, ::-1], zeros((groups, ntaps - 1))], axis=1),
            jnp.concatenate([lf, zeros((groups, ntaps))], axis=1),
        ],
        axis=0,
    )
    bands = kernel_call(bands_body, shaped((2 * groups, ntaps, 2 * ntaps), BF16))(bases)

    mm_flops = seq * drow * 3 * local
    mm_bytes = seq * drow + 6 * drow * local + 3 * seq * local
    shares, passed, sums = [], [], []
    for x in (x0, x1):
        parts = kernel_call(
            project_body,
            [shaped((3, chunk, width), BF16)] * ndp,
            grid=(3,),
            in_specs=[
                pl.BlockSpec((nblocks, ncol, rows, dcol), lambda i: (0, 0, 0, 0)),
                pl.BlockSpec((1, drow, local), lambda i: (i, 0, 0)),
            ],
            out_specs=[pl.BlockSpec((1, chunk, width), lambda i: (i, 0, 0))] * ndp,
            scratch=[pltpu.VMEM((ndp, chunk, width), BF16)],
            flops=mm_flops,
            nbytes=mm_bytes,
        )(x, w)
        shares.append([p.reshape(3 * chunk, width) for p in parts])
        passed.append(first_hop(shares[-1][2]))
    passed[0], shares[1], upstream[2], later_w = lax.optimization_barrier((passed[0], shares[1], upstream[2], w))
    for (own, right, _, left), came in zip(shares, passed):
        sums += [own, *second_hop(right, left, *came)]

    extra = -(-(groups + 3 * nshort) // 16) * 16
    half = pl.BlockSpec((groups, ntaps, 2 * ntaps), lambda i: (0, 0, 0))
    other = pl.BlockSpec((groups, ntaps, 2 * ntaps), lambda i: (1, 0, 0))
    whole = lambda *shape: pl.BlockSpec(shape, lambda i: (0,) * len(shape))
    grad_near, grad_other, *mixed = kernel_call(
        functools.partial(middle_body, scale, nshort, nrow),
        [shaped((3 * chunk + extra, width), BF16), shaped((3 * chunk, width), BF16)]
        + [shaped((rows, width), BF16)] * ndp,
        grid=(1,),
        in_specs=[whole(3 * chunk, width)] * 6
        + [whole(3 * nshort, width), half, other]
        + [whole(rows, width)] * ndp,
        out_specs=[whole(3 * chunk + extra, width), whole(3 * chunk, width)] + [whole(rows, width)] * ndp,
        scratch=[
            pltpu.VMEM((3 * seq, width), F32),
            pltpu.VMEM((3 * seq, width), BF16),
            pltpu.VMEM((seq, width), BF16),
            pltpu.VMEM((seq, width), BF16),
        ],
        flops=3 * 2 * groups * ntaps * 2 * ntaps * width * (seq // ntaps),
        nbytes=2 * width * seq * 14,
        vmem=MOST_VMEM_BYTES,
    )(*sums, sf, bands, bands, *upstream)
    mixed = [mixed[0]] + [
        lax.ppermute(part, "dp", [(a, (a + ahead) % ndp) for a in range(ndp)])
        for ahead, part in enumerate(mixed)
        if ahead
    ]
    *near, near_far_before, near_far_after = gather_over_line(grad_near, False)
    *far, far_far_before, far_far_after = gather_over_line(grad_other, True)
    partner_w = lax.ppermute(later_w, "row", partner)
    everywhere = pl.BlockSpec(memory_space=pl.ANY)
    in_vmem = pl.BlockSpec(memory_space=pltpu.VMEM)
    part, far_two = kernel_call(
        first_grad_body,
        [shaped((ncol, chunk, dcol), BF16), shaped((2, 3 * chunk, width), BF16)],
        in_specs=[in_vmem] * 6 + [everywhere] * 2,
        out_specs=[in_vmem] * 2,
        scratch=[
            pltpu.VMEM((2, ndp, 3 * chunk, width), BF16),
            pltpu.VMEM((2, ncol, 3, dcol, local), BF16),
            pltpu.SemaphoreType.DMA((2, ncol)),
        ],
        flops=2 * mm_flops,
        nbytes=2 * mm_bytes,
    )(*near, *far, w, partner_w)
    near_last, far_last, *blocks = kernel_call(
        functools.partial(second_grad_body, ndp),
        [shaped(grad_near.shape, BF16), shaped(grad_other.shape, BF16)]
        + [shaped((rows, dcol), BF16)] * len(places),
        grid=(),
        in_specs=[everywhere] * 7,
        out_specs=[in_vmem] * (2 + len(places)),
        scratch=[
            pltpu.VMEM((2, 3, drow, width), BF16),
            pltpu.VMEM((ncol, chunk, dcol), BF16),
            pltpu.SemaphoreType.DMA((5,)),
        ],
        flops=mm_flops // 2,
        nbytes=mm_bytes // 2,
        vmem=MOST_VMEM_BYTES,
    )(part, near_far_before, near_far_after, far_far_before, far_far_after, far_w, partner_w)
    far_two, far_last, mixed[1:] = lax.optimization_barrier((far_two, far_last, mixed[1:]))
    far_two, far_last = (lax.ppermute(part, "row", partner) for part in (far_two, far_last))
    arrivals = [
        lax.ppermute(sent, ("row", "col"), [(b, a) for a, b in offset(*p)])
        for p, sent in zip(places[1:], blocks[1:])
    ]
    arrived = sum((a.astype(F32) for a in arrivals), blocks[0].astype(F32)).astype(BF16)
    arrived, far_two, far_last = lax.optimization_barrier((arrived, far_two, far_last))
    grad_in = lax.ppermute(arrived, ("dp", "row"), swap_back)

    each = lambda *shape: pl.BlockSpec(shape, lambda i, e: (0,) * len(shape))
    grad_weight, mixed, grad_long, grad_short = kernel_call(
        functools.partial(weight_grad_body, scale),
        [
            shaped((3, drow, local), F32),
            shaped((rows, local), BF16),
            shaped((ngroups, ntaps), F32),
            shaped((nshort, 3, local), F32),
        ],
        grid=(3, ncol),
        in_specs=[each(nblocks, ncol, rows, dcol)] * 2
        + [each(*grad_near.shape)] * 4
        + [each(*grad_other.shape), each(*far_two.shape), each(*far_last.shape)]
        + [each(rows, width)] * ndp,
        out_specs=[
            pl.BlockSpec((1, dcol, local), lambda i, e: (i, e, 0)),
            each(rows, local),
            each(ngroups, ntaps),
            each(nshort, 3, local),
        ],
        scratch=[
            pltpu.VMEM((2, ndp, 3 * chunk + extra, width), BF16),
            pltpu.VMEM((ndp, rows, width), BF16),
        ],
        flops=2 * mm_flops,
        nbytes=2 * mm_bytes,
        vmem=MOST_VMEM_BYTES,
    )(x0, x1, *near, near_last, grad_other, far_two, far_last, *mixed)
    grad_weight = jnp.transpose(grad_weight, (1, 0, 2))
    return (mixed, grad_in, grad_weight, grad_long, grad_short)


def from_behind(block, axis, distance):
    devices = range(lax.axis_size(axis))
    route = [(i - distance, i) for i in devices if i - distance in devices]
    return lax.ppermute(block, axis, route)


def toeplitz(leading, rows, span):
    groups = leading.shape[0]
    width = rows + span
    seed_row = jnp.concatenate(
        [leading, jnp.zeros((groups, width - leading.shape[1]), leading.dtype)], axis=1
    )
    tiled = jnp.tile(seed_row, (1, rows))
    skewed = tiled[:, : rows * (width - 1)].reshape(groups, rows, width - 1)
    return skewed[:, :, :span]


def to_groups(values, ngroups, members):
    count = values.shape[0]
    return values.reshape(count, ngroups, members).transpose(1, 2, 0)


def from_groups(values):
    groups, members, count = values.shape
    return values.transpose(2, 0, 1).reshape(count, groups * members)


def move_weights(tokens, in_weight, short_filter, long_filter, grad_out):
    rows = tokens.shape[0]
    local = grad_out.shape[1]
    nshort = short_filter.shape[0]
    ntaps = long_filter.shape[1]
    ngroups = long_filter.shape[0]
    members = local // ngroups
    margin = ntaps - 1
    span = rows + margin
    scale = float(rows * lax.axis_size("dp")) ** (-0.5)
    whole = lax.all_gather(tokens, ("row", "col"), axis=1, tiled=True)
    full_w = lax.all_gather(in_weight, "dp", axis=0, tiled=True)
    mixed_in = jnp.einsum("sd,dic->sic", whole, full_w, preferred_element_type=jnp.float32).astype(
        jnp.bfloat16
    )
    before = from_behind(mixed_in[rows - margin - nshort + 1 :], "dp", 1)
    extended = jnp.concatenate([before, mixed_in], axis=0).astype(jnp.float32)
    long_feats = jnp.zeros((span, 3, local), jnp.float32)
    for j in range(nshort):
        long_feats = (
            long_feats + short_filter[j][None] * extended[nshort - 1 - j : nshort - 1 - j + span]
        )
    product_ext = (long_feats[:, 1] * long_feats[:, 2]).astype(jnp.bfloat16)
    feats = long_feats[margin:]
    short_rows = extended[margin:]
    product_cols = to_groups(product_ext, ngroups, members)
    causal = toeplitz(long_filter[:, ::-1], rows, span)
    conv = from_groups(
        jnp.einsum("gst,gct->gcs", causal, product_cols, preferred_element_type=jnp.float32)
    )
    mixed = (feats[:, 0] * conv).astype(jnp.bfloat16)
    upstream = grad_out.astype(jnp.float32)
    grad_query = upstream * conv
    grad_conv = (upstream * feats[:, 0]).astype(jnp.bfloat16)
    after = from_behind(grad_conv[:margin], "dp", -1)
    grad_ext = jnp.concatenate([grad_conv, after], axis=0)
    anti = toeplitz(long_filter, rows, span)
    grad_product = from_groups(
        jnp.einsum(
            "gst,gct->gcs",
            anti,
            to_groups(grad_ext, ngroups, members),
            preferred_element_type=jnp.float32,
        )
    )
    reversed_cols = jnp.concatenate(
        [product_cols[:, :, ::-1], jnp.zeros((ngroups, members, rows), product_cols.dtype)], axis=2
    )
    width = span + rows
    pairs = jnp.einsum(
        "gcs,gcu->gsu",
        to_groups(grad_conv, ngroups, members),
        reversed_cols,
        preferred_element_type=jnp.float32,
    )
    diagonal = pairs.reshape(ngroups, rows * width)[:, : rows * (width - 1)].reshape(
        ngroups, rows, width - 1
    )
    filter_part = jnp.sum(diagonal[:, :, rows - 1 : rows - 1 + ntaps], axis=1)
    grad_feats = jnp.stack(
        [grad_query, grad_product * feats[:, 2], grad_product * feats[:, 1]], axis=1
    )
    later = from_behind(grad_feats[: nshort - 1], "dp", -1)
    feats_ext = jnp.concatenate([grad_feats, later], axis=0)
    grad_acc = jnp.zeros((rows, 3, local), jnp.float32)
    for j in range(nshort):
        grad_acc = grad_acc + short_filter[j][None] * feats_ext[j : j + rows]
    grad_mixed = grad_acc.astype(jnp.bfloat16)
    short_part = jnp.stack(
        [
            jnp.sum(grad_feats * short_rows[nshort - 1 - j : nshort - 1 - j + rows], axis=0)
            for j in range(nshort)
        ]
    )
    filter_total, short_total = (
        lax.psum(filter_part.astype(jnp.bfloat16), "dp").astype(jnp.float32),
        lax.psum(short_part.astype(jnp.bfloat16), "dp").astype(jnp.float32),
    )
    grad_long = filter_total * scale
    grad_short = short_total * scale
    partial_in = jnp.einsum("sic,dic->sd", grad_mixed, full_w, preferred_element_type=jnp.float32)
    summed_in = lax.psum_scatter(
        partial_in.astype(jnp.bfloat16), ("row", "col"), scatter_dimension=1, tiled=True
    )
    weight_term = (
        jnp.einsum("sd,sic->dic", whole, grad_mixed, preferred_element_type=jnp.float32) * scale
    )
    grad_weight = lax.psum_scatter(
        weight_term.astype(jnp.bfloat16), "dp", scatter_dimension=0, tiled=True
    ).astype(jnp.float32)
    return (mixed, summed_in, grad_weight, grad_long, grad_short)


def fits_whole_sequences(mesh, tokens, in_weight, short_filter, long_filter, grad_out):
    ndp, nrow, ncol = (mesh.shape[a] for a in ("dp", "row", "col"))
    seq, channels = grad_out.shape
    groups, ntaps = long_filter.shape
    local = channels // (nrow * ncol)
    width, rows = local // ndp, seq // ndp
    return (
        seq < tokens.shape[1]
        and ndp == nrow == 4
        and ncol * (tokens.shape[1] // (nrow * ncol)) == in_weight.shape[0] // ndp
        and ntaps == width == 128
        and seq % (2 * ntaps) == 0
        and rows % 16 == 0
        and groups % (8 * ndp * nrow * ncol) == 0
    )


def solution(mesh):
    placed = (
        P("dp", ("row", "col")),
        P("dp", None, ("row", "col")),
        P(None, None, ("row", "col")),
        P(("row", "col"), None),
        P("dp", ("row", "col")),
    )
    gives = (
        P("dp", ("row", "col")),
        P("dp", ("row", "col")),
        P("dp", None, ("row", "col")),
        P(("row", "col"), None),
        P(None, None, ("row", "col")),
    )

    def run(*arrays):
        plan = move_activations if fits_whole_sequences(mesh, *arrays) else move_weights
        return jax.shard_map(
            plan, mesh=mesh, in_specs=placed, out_specs=gives, check_vma=False
        )(*arrays)

    return run
```

```python
import functools

import jax
import jax.numpy as jnp
from jax import lax
from jax.experimental import pallas as pl
from jax.experimental.pallas import tpu as pltpu
from jax.sharding import PartitionSpec as P

VMEM_BYTES = 48 * 2**20
MOST_VMEM_BYTES = 62 * 2**20
F32 = jnp.float32
BF16 = jnp.bfloat16


def kernel_call(body, outs, grid=(), in_specs=None, out_specs=None, scratch=(), flops=0, nbytes=0, vmem=VMEM_BYTES):
    kwargs = {}
    if in_specs is not None:
        kwargs = dict(grid=grid, in_specs=in_specs, out_specs=out_specs)
    return pl.pallas_call(
        body,
        out_shape=outs,
        scratch_shapes=scratch,
        compiler_params=pltpu.CompilerParams(vmem_limit_bytes=vmem),
        cost_estimate=pl.CostEstimate(flops=flops, bytes_accessed=nbytes, transcendentals=0),
        **kwargs,
    )


def shaped(shape, dtype):
    return jax.ShapeDtypeStruct(shape, dtype)


def bands_body(base_ref, out_ref):
    groups, wide = base_ref.shape
    rows = out_ref.shape[1]
    row = lax.broadcasted_iota(jnp.int32, (8, wide), 0)
    for g in range(groups):
        band = jnp.broadcast_to(base_ref[g : g + 1, :], (8, wide))
        for bit in (1, 2, 4):
            band = jnp.where((row & bit) != 0, pltpu.roll(band, bit, 1), band)
        count = 8
        while count < rows:
            band = jnp.concatenate([band, pltpu.roll(band, count, 1)], axis=0)
            count *= 2
        out_ref[g] = band.astype(out_ref.dtype)


def tokens_of(row, nrow):
    return row % 2 * (nrow // 2) + row // 2


def wrapped(value, size):
    return lax.rem(value + 2 * size, size)


def split_body(all_ref, *out_refs):
    width = out_refs[0].shape[1]
    for ahead, out_ref in enumerate(out_refs):
        at = wrapped(lax.axis_index("dp") + ahead, len(out_refs)) * width
        out_ref[...] = all_ref[:, pl.ds(pl.multiple_of(at, width), width)]


def project_body(x_ref, w_ref, *refs):
    *out_refs, held = refs
    z, col = lax.axis_index("dp"), lax.axis_index("col")
    nblocks, ncol, rows, depth = x_ref.shape
    width = held.shape[2]
    total = jnp.zeros((nblocks * rows, w_ref.shape[2]), F32)
    for dx in range(ncol):
        start = pl.multiple_of(wrapped(col - dx, ncol) * depth, depth)
        total += jnp.dot(
            x_ref[:, dx].reshape(nblocks * rows, depth),
            w_ref[0, pl.ds(start, depth), :],
            preferred_element_type=F32,
        )
    for owner in range(len(out_refs)):
        held[owner] = total[:, owner * width : (owner + 1) * width].astype(BF16)
    for ahead, out_ref in enumerate(out_refs):
        out_ref[0] = held[wrapped(z + ahead, len(out_refs))]


def far_columns_body(w_ref, out_ref, sem):
    ndp = lax.axis_size("dp")
    width = out_ref.shape[2]
    start = wrapped(lax.axis_index("dp") + ndp // 2, ndp) * width
    copy = pltpu.make_async_copy(w_ref.at[:, :, pl.ds(pl.multiple_of(start, width), width)], out_ref, sem)
    copy.start()
    copy.wait()


def first_grad_body(
    near, near_before, near_after, far, far_before, far_after, w_ref, partner_w_ref, out_ref, far_ref, held, held_w, sems
):
    _, ndp, _, width = held.shape
    ncol, tokens, depth = out_ref.shape
    z, col = lax.axis_index("dp"), lax.axis_index("col")
    copies = []
    for dx in range(ncol):
        start = pl.multiple_of(wrapped(col - dx, ncol) * depth, depth)
        for k, weights in enumerate((w_ref, partner_w_ref)):
            copy = pltpu.make_async_copy(weights.at[:, pl.ds(start, depth)], held_w.at[k, dx], sems.at[k, dx])
            copy.start()
            copies.append(copy)
    far_ref[0], far_ref[1] = far_before[...], far_after[...]
    for k, pieces in enumerate(((near, near_before, near_after), (far, far_before, far_after))):
        held[k, wrapped(z + ndp // 2, ndp)] = jnp.zeros(held.shape[2:], BF16)
        for ahead, piece in zip((0, -1, 1), pieces):
            held[k, wrapped(z + ahead, ndp)] = piece[: 3 * tokens]
    for dx in range(ncol):
        total = jnp.zeros((tokens, depth), F32)
        for k in range(2):
            copies[2 * dx + k].wait()
            for i in range(3):
                rows = slice(i * tokens, (i + 1) * tokens)
                total += lax.dot_general(
                    jnp.concatenate([held[k, owner, rows] for owner in range(ndp)], axis=1),
                    held_w[k, dx, i],
                    (((1,), (1,)), ((), ())),
                    preferred_element_type=F32,
                )
        out_ref[dx] = total.astype(BF16)


def second_grad_body(ndp, part_ref, *refs):
    arrived, (w_ref, partner_w_ref), refs = (refs[:2], refs[2:4]), refs[4:6], refs[6:]
    (near_ref, far_ref), refs = refs[:2], refs[2:]
    *out_refs, held_w, held_part, sems = refs
    ncol, tokens, depth = held_part.shape
    rows = out_refs[0].shape[0]
    width = near_ref.shape[1]
    z, col = lax.axis_index("dp"), lax.axis_index("col")
    lanes = pl.ds(pl.multiple_of(wrapped(z + ndp // 2, ndp) * width, width), width)
    copies = [
        pltpu.make_async_copy(w_ref, held_w.at[0], sems.at[0]),
        pltpu.make_async_copy(partner_w_ref.at[:, :, lanes], held_w.at[1], sems.at[1]),
    ]
    copies.append(pltpu.make_async_copy(part_ref, held_part, sems.at[2]))
    for copy in copies:
        copy.start()
    for k, (pair, target) in enumerate(zip(arrived, (near_ref, far_ref))):
        for source, here in zip(pair, (z >= ndp // 2, z < ndp // 2)):

            @pl.when(here)
            def _(source=source, target=target, k=k):
                copy = pltpu.make_async_copy(source, target, sems.at[3 + k])
                copy.start()
                copy.wait()

    for copy in copies:
        copy.wait()
    left = jnp.concatenate(
        [ref[i * tokens : (i + 1) * tokens] for ref in (near_ref, far_ref) for i in range(3)], axis=1
    )
    for dx in range(ncol):
        start = pl.multiple_of(wrapped(col - dx, ncol) * depth, depth)
        right = jnp.concatenate([held_w[k, i, pl.ds(start, depth), :] for k in range(2) for i in range(3)], axis=1)
        total = held_part[dx].astype(F32) + lax.dot_general(
            left, right, (((1,), (1,)), ((), ())), preferred_element_type=F32
        )
        for block in range(tokens // rows):
            out_refs[block * ncol + dx][...] = total[block * rows : (block + 1) * rows].astype(BF16)


def transpose_body(x0_ref, x1_ref, out_ref):
    nblocks, ncol, rows, depth = x0_ref.shape
    tokens = nblocks * rows
    col = lax.axis_index("col")
    for dx in range(ncol):
        start = pl.multiple_of(wrapped(col - dx, ncol) * depth, depth)
        for k, x_ref in enumerate((x0_ref, x1_ref)):
            out_ref[pl.ds(start, depth), k * tokens : (k + 1) * tokens] = x_ref[:, dx].reshape(tokens, depth).T


def weight_grad_body(scale, *refs):
    xt_ref, near_refs, other_refs, mixed_refs, refs = refs[0], refs[1:5], refs[5:8], refs[8:12], refs[12:]
    own_ref, two_ref, last_ref = other_refs
    other = (own_ref, two_ref.at[0], two_ref.at[1], last_ref)
    out_ref, mixed_ref, long_ref, short_ref, held, held_mixed = refs
    _, ndp, _, width = held.shape
    tokens = xt_ref.shape[1] // 2
    i = pl.program_id(0)
    z = lax.axis_index("dp")

    @pl.when(i == 0)
    def _():
        groups = long_ref.shape[0] // ndp
        for k, ahead in enumerate((0, -1, 1, 2)):
            owner = wrapped(z + ahead, ndp)
            held[0, owner] = near_refs[k][...]
            held[1, owner, : 3 * tokens] = other[k][...]
        for back in range(ndp):
            held_mixed[wrapped(z - back, ndp)] = mixed_refs[back][...]
        for owner in range(ndp):
            lanes = slice(owner * width, (owner + 1) * width)
            mixed_ref[:, lanes] = held_mixed[owner]
            small = held[0, owner, 3 * tokens :].astype(F32)
            long_ref[owner * groups : (owner + 1) * groups] = small[:groups]
            nshort, three, _ = short_ref.shape
            for j in range(nshort):
                short_ref[j, :, lanes] = small[groups + three * j : groups + three * (j + 1)]

    at = pl.ds(pl.multiple_of(i * tokens, 16), tokens)
    gm = jnp.concatenate(
        [jnp.concatenate([held[k, owner, at, :] for owner in range(ndp)], axis=1) for k in range(2)], axis=0
    )
    out_ref[0] = scale * jnp.dot(xt_ref[...], gm, preferred_element_type=F32)


def delayed(values, count):
    row = lax.broadcasted_iota(jnp.int32, values.shape, 0)
    return jnp.where(row >= count, pltpu.roll(values, count, 0), 0.0)


def advanced(values, count):
    rows = values.shape[0]
    row = lax.broadcasted_iota(jnp.int32, values.shape, 0)
    return jnp.where(row < rows - count, pltpu.roll(values, rows - count, 0), 0.0)


def middle_body(scale, nshort, nrow, *refs):
    sums, refs = (refs[:3], refs[3:6]), refs[6:]
    (sf_ref, causal_ref, anti_ref), refs = refs[:3], refs[3:]
    *refs, m_ref, gm_ref, mixed_ref, go_ref = refs
    ndp = len(refs) // 2 - 1
    go_refs, (near_ref, other_ref), mixed_refs = refs[:ndp], refs[ndp : ndp + 2], refs[ndp + 2 :]
    tokens, width = go_ref.shape
    for behind, piece in enumerate(go_refs):
        at = wrapped(lax.axis_index("dp") - behind, ndp) * (tokens // ndp)
        go_ref[pl.ds(pl.multiple_of(at, 16), tokens // ndp)] = piece[...]
    row = lax.axis_index("row")
    nblocks = nrow // 2
    rows = tokens // nrow

    def places():
        for chunk, start in enumerate((row, row + 1 - 2 * lax.rem(row, 2))):
            for block in range(nblocks):
                at = tokens_of(wrapped(start - 2 * block, nrow), nrow) * rows
                for i in range(3):
                    yield chunk, (i * nblocks + block) * rows, pl.multiple_of(i * tokens + at, 16)

    for chunk, place, at in places():
        held = [ref[place : place + rows].astype(F32) for ref in sums[chunk]]
        m_ref[pl.ds(at, rows)] = held[0] + held[1] + held[2]
    groups, block, span = causal_ref.shape
    members = width // groups
    nspans = tokens // block
    lane = lax.broadcasted_iota(jnp.int32, (block, width), 1) // members
    lanes = lax.broadcasted_iota(jnp.int32, (block, 2 * width), 1) % width // members

    def past(i, j):
        held = m_ref[i * tokens : (i + 1) * tokens]
        return held if j == 0 else delayed(held, j)

    def taps(j, i):
        return sf_ref[3 * j + i : 3 * j + i + 1, :]

    feats = [sum(taps(j, i) * past(i, j) for j in range(nshort)) for i in range(3)]
    product = (feats[1] * feats[2]).astype(BF16)
    zero = jnp.zeros((block, width), BF16)
    p_blocks = [zero] + [product[b * block : (b + 1) * block] for b in range(nspans)]
    p_pairs = [jnp.concatenate(p_blocks[b : b + 2], axis=0) for b in range(nspans)]

    def filtered(band_ref, pairs):
        bands = band_ref[...].reshape(groups * block, span)
        out = []
        for b in range(0, nspans, 2):
            both = jnp.dot(bands, jnp.concatenate(pairs[b : b + 2], axis=1), preferred_element_type=F32)
            for h in range(2):
                part = both[:, h * width : (h + 1) * width]
                picked = part[:block]
                for g in range(1, groups):
                    picked = jnp.where(lane == g, part[g * block : (g + 1) * block], picked)
                out.append(picked)
        return jnp.concatenate(out, axis=0)

    conv = filtered(causal_ref, p_pairs)
    upstream = go_ref[...].astype(F32)
    mixed_ref[...] = (feats[0] * conv).astype(BF16)
    for ahead, out_ref in enumerate(mixed_refs):
        at = pl.multiple_of(wrapped(lax.axis_index("dp") + ahead, ndp) * (tokens // ndp), 16)
        out_ref[...] = mixed_ref[pl.ds(at, tokens // ndp)]
    grad_conv = (upstream * feats[0]).astype(BF16)
    c_blocks = [grad_conv[b * block : (b + 1) * block] for b in range(nspans)] + [zero]
    c_pairs = [jnp.concatenate(c_blocks[b : b + 2], axis=0) for b in range(nspans)]
    grad_product = filtered(anti_ref, c_pairs)

    corr = jnp.zeros((groups * block, span), F32)
    for b in range(0, nspans, 2):
        left = jnp.concatenate(c_blocks[b : b + 2], axis=1)
        stacked = jnp.concatenate(
            [jnp.where(lanes == g, left, jnp.zeros_like(left)) for g in range(groups)], axis=0
        )
        right = jnp.concatenate(p_pairs[b : b + 2], axis=1)
        corr += lax.dot_general(stacked, right, (((1,), (1,)), ((), ())), preferred_element_type=F32)
    turn = lax.broadcasted_iota(jnp.int32, (8, span), 0)
    sums = []
    for g in range(groups):
        part = corr[g * block : (g + 1) * block]
        count = block
        while count > 8:
            count //= 2
            part = part[:count] + pltpu.roll(part[count:], span - count, 1)
        for bit in (1, 2, 4):
            part = jnp.where((turn & bit) != 0, pltpu.roll(part, span - bit, 1), part)
        sums.append(jnp.sum(part, axis=0, keepdims=True))
    by_lag = jnp.concatenate(sums, axis=0)
    by_lag = (scale * pltpu.roll(by_lag, span - 1, 1)[:, :block]).astype(BF16)
    ahead = lax.broadcasted_iota(jnp.int32, (block, block), 0)
    back = lax.broadcasted_iota(jnp.int32, (block, block), 1)
    turned = jnp.where(ahead + back == block - 1, 1.0, 0.0).astype(BF16)
    by_lag = jnp.dot(by_lag, turned, preferred_element_type=F32)

    grad_feats = [upstream * conv, grad_product * feats[2], grad_product * feats[1]]
    short_rows = []
    for j in range(nshort):
        for i in range(3):
            short_rows.append(scale * jnp.sum(grad_feats[i] * past(i, j), axis=0, keepdims=True))
    for i in range(3):
        total = taps(0, i) * grad_feats[i]
        for j in range(1, nshort):
            total += taps(j, i) * advanced(grad_feats[i], j)
        gm_ref[i * tokens : (i + 1) * tokens] = total.astype(BF16)
    for chunk, place, at in places():
        (near_ref, other_ref)[chunk][place : place + rows] = gm_ref[pl.ds(at, rows)]
    tail = near_ref.shape[0] - 3 * tokens // 2 - groups - 3 * nshort
    small = jnp.concatenate([by_lag] + short_rows + [jnp.zeros((tail, width), F32)], axis=0)
    near_ref[3 * tokens // 2 :] = small.astype(BF16)


def sum_over_line(own, right, far, left):
    ndp = lax.axis_size("dp")
    from_left = lax.ppermute(far, "dp", [(a, a + 1) for a in range(ndp // 2)])
    from_right = lax.ppermute(far, "dp", [(a, a - 1) for a in range(ndp // 2, ndp)])
    rightward = lax.ppermute(right + from_left, "dp", [(a, (a + 1) % ndp) for a in range(ndp)])
    leftward = lax.ppermute(left + from_right, "dp", [(a, (a - 1) % ndp) for a in range(ndp)])
    return own, rightward, leftward


def gather_over_line(own, across):
    ndp, nrow = lax.axis_size("dp"), lax.axis_size("row")

    def shift(count):
        return [
            (a * nrow + r, (a + count) % ndp * nrow + (r + 1 - 2 * (r % 2) if across else r))
            for a in range(ndp)
            for r in range(nrow)
        ]

    before = lax.ppermute(own, ("dp", "row"), shift(1))
    after = lax.ppermute(own, ("dp", "row"), shift(-1))
    here = lax.ppermute(own, ("dp", "row"), shift(0)) if across else own
    far_before = lax.ppermute(before, "dp", [(a - 1, a) for a in range(ndp // 2, ndp)])
    far_after = lax.ppermute(after, "dp", [(a + 1, a) for a in range(ndp // 2)])
    return here, before, after, far_before, far_after


def move_activations(tokens, in_weight, short_filter, long_filter, grad_out):
    ndp, nrow, ncol = (lax.axis_size(a) for a in ("dp", "row", "col"))
    z = lax.axis_index("dp")
    rows, dcol = tokens.shape
    local = grad_out.shape[1]
    nshort = short_filter.shape[0]
    ngroups, ntaps = long_filter.shape
    seq = rows * ndp
    width, groups = local // ndp, ngroups // ndp
    drow = in_weight.shape[0]
    scale = float(seq) ** -0.5
    nblocks = nrow // 2
    chunk = nblocks * rows
    swap = [(tokens_of(b, nrow) * nrow + a, a * nrow + b) for a in range(ndp) for b in range(nrow)]
    swap_back = [(b, a) for a, b in swap]
    partner = [(a, a + 1 - 2 * (a % 2)) for a in range(nrow)]
    places = [(dy, dx) for dy in range(nblocks) for dx in range(ncol)]

    def offset(dy, dx):
        return [
            (a * ncol + b, (a + 2 * dy) % nrow * ncol + (b + dx) % ncol) for a in range(nrow) for b in range(ncol)
        ]

    w = jnp.transpose(in_weight, (1, 0, 2))
    moved = lax.ppermute(tokens, ("dp", "row"), swap)
    far_w = kernel_call(
        far_columns_body,
        shaped((3, drow, width), BF16),
        in_specs=[pl.BlockSpec(memory_space=pl.ANY)],
        out_specs=pl.BlockSpec(memory_space=pltpu.VMEM),
        scratch=[pltpu.SemaphoreType.DMA],
    )(w)
    turn = [[(a, (a + ahead) % ndp) for a in range(ndp)] for ahead in range(ndp)]
    upstream = [*kernel_call(split_body, [shaped((rows, width), BF16)] * ndp)(grad_out)]
    moved, upstream, far_w = lax.optimization_barrier((moved, upstream, far_w))
    near = [moved] + [lax.ppermute(moved, ("row", "col"), offset(*p)) for p in places[1:]]
    for ahead in (1, 3):
        upstream[ahead] = lax.ppermute(upstream[ahead], "dp", turn[ahead])
    upstream[1::2], near[1:] = lax.optimization_barrier((upstream[1::2], near[1:]))
    x0 = jnp.stack(near).reshape(nblocks, ncol, rows, dcol)
    x1 = lax.ppermute(x0, "row", partner)
    upstream[2] = lax.ppermute(upstream[2], "dp", turn[2])
    upstream[2], x1 = lax.optimization_barrier((upstream[2], x1))

    sf = lax.dynamic_slice_in_dim(short_filter, z * width, width, 2).reshape(3 * nshort, width)
    lf = lax.dynamic_slice_in_dim(long_filter, z * groups, groups, 0).astype(F32)
    zeros = functools.partial(jnp.zeros, dtype=F32)
    bases = jnp.concatenate(
        [
            jnp.concatenate([zeros((groups, 1)), lf[:, ::-1], zeros((groups, ntaps - 1))], axis=1),
            jnp.concatenate([lf, zeros((groups, ntaps))], axis=1),
        ],
        axis=0,
    )
    bands = kernel_call(bands_body, shaped((2 * groups, ntaps, 2 * ntaps), BF16))(bases)

    mm_flops = seq * drow * 3 * local
    mm_bytes = seq * drow + 6 * drow * local + 3 * seq * local
    sums = []
    for x in (x0, x1):
        parts = kernel_call(
            project_body,
            [shaped((3, chunk, width), BF16)] * ndp,
            grid=(3,),
            in_specs=[
                pl.BlockSpec((nblocks, ncol, rows, dcol), lambda i: (0, 0, 0, 0)),
                pl.BlockSpec((1, drow, local), lambda i: (i, 0, 0)),
            ],
            out_specs=[pl.BlockSpec((1, chunk, width), lambda i: (i, 0, 0))] * ndp,
            scratch=[pltpu.VMEM((ndp, chunk, width), BF16)],
            flops=mm_flops,
            nbytes=mm_bytes,
        )(x, w)
        sums += sum_over_line(*(p.reshape(3 * chunk, width) for p in parts))

    xt = kernel_call(transpose_body, shaped((drow, 2 * chunk), BF16))(x0, x1)
    sums, xt = lax.optimization_barrier((sums, xt))
    extra = -(-(groups + 3 * nshort) // 16) * 16
    half = pl.BlockSpec((groups, ntaps, 2 * ntaps), lambda i: (0, 0, 0))
    other = pl.BlockSpec((groups, ntaps, 2 * ntaps), lambda i: (1, 0, 0))
    whole = lambda *shape: pl.BlockSpec(shape, lambda i: (0,) * len(shape))
    grad_near, grad_other, *mixed = kernel_call(
        functools.partial(middle_body, scale, nshort, nrow),
        [shaped((3 * chunk + extra, width), BF16), shaped((3 * chunk, width), BF16)]
        + [shaped((rows, width), BF16)] * ndp,
        grid=(1,),
        in_specs=[whole(3 * chunk, width)] * 6
        + [whole(3 * nshort, width), half, other]
        + [whole(rows, width)] * ndp,
        out_specs=[whole(3 * chunk + extra, width), whole(3 * chunk, width)] + [whole(rows, width)] * ndp,
        scratch=[
            pltpu.VMEM((3 * seq, width), F32),
            pltpu.VMEM((3 * seq, width), BF16),
            pltpu.VMEM((seq, width), BF16),
            pltpu.VMEM((seq, width), BF16),
        ],
        flops=3 * 2 * groups * ntaps * 2 * ntaps * width * (seq // ntaps),
        nbytes=2 * width * seq * 14,
        vmem=MOST_VMEM_BYTES,
    )(*sums, sf, bands, bands, *upstream)
    mixed = [mixed[0]] + [
        lax.ppermute(part, "dp", [(a, (a + ahead) % ndp) for a in range(ndp)])
        for ahead, part in enumerate(mixed)
        if ahead
    ]
    *near, near_far_before, near_far_after = gather_over_line(grad_near, False)
    *far, far_far_before, far_far_after = gather_over_line(grad_other, True)
    partner_w = lax.ppermute(w, "row", partner)
    everywhere = pl.BlockSpec(memory_space=pl.ANY)
    in_vmem = pl.BlockSpec(memory_space=pltpu.VMEM)
    part, far_two = kernel_call(
        first_grad_body,
        [shaped((ncol, chunk, dcol), BF16), shaped((2, 3 * chunk, width), BF16)],
        in_specs=[in_vmem] * 6 + [everywhere] * 2,
        out_specs=[in_vmem] * 2,
        scratch=[
            pltpu.VMEM((2, ndp, 3 * chunk, width), BF16),
            pltpu.VMEM((2, ncol, 3, dcol, local), BF16),
            pltpu.SemaphoreType.DMA((2, ncol)),
        ],
        flops=2 * mm_flops,
        nbytes=2 * mm_bytes,
    )(*near, *far, w, partner_w)
    near_last, far_last, *blocks = kernel_call(
        functools.partial(second_grad_body, ndp),
        [shaped(grad_near.shape, BF16), shaped(grad_other.shape, BF16)]
        + [shaped((rows, dcol), BF16)] * len(places),
        grid=(),
        in_specs=[everywhere] * 7,
        out_specs=[in_vmem] * (2 + len(places)),
        scratch=[
            pltpu.VMEM((2, 3, drow, width), BF16),
            pltpu.VMEM((ncol, chunk, dcol), BF16),
            pltpu.SemaphoreType.DMA((5,)),
        ],
        flops=mm_flops // 2,
        nbytes=mm_bytes // 2,
        vmem=MOST_VMEM_BYTES,
    )(part, near_far_before, near_far_after, far_far_before, far_far_after, far_w, partner_w)
    far_two, far_last, mixed[1:] = lax.optimization_barrier((far_two, far_last, mixed[1:]))
    far_two, far_last = (lax.ppermute(part, "row", partner) for part in (far_two, far_last))
    arrivals = [
        lax.ppermute(sent, ("row", "col"), [(b, a) for a, b in offset(*p)])
        for p, sent in zip(places[1:], blocks[1:])
    ]
    arrived = sum((a.astype(F32) for a in arrivals), blocks[0].astype(F32)).astype(BF16)
    arrived, far_two, far_last = lax.optimization_barrier((arrived, far_two, far_last))
    grad_in = lax.ppermute(arrived, ("dp", "row"), swap_back)

    grad_weight, mixed, grad_long, grad_short = kernel_call(
        functools.partial(weight_grad_body, scale),
        [
            shaped((3, drow, local), F32),
            shaped((rows, local), BF16),
            shaped((ngroups, ntaps), F32),
            shaped((nshort, 3, local), F32),
        ],
        grid=(3,),
        in_specs=[whole(drow, 2 * chunk)]
        + [whole(*grad_near.shape)] * 4
        + [whole(*grad_other.shape), whole(*far_two.shape), whole(*far_last.shape)]
        + [whole(rows, width)] * ndp,
        out_specs=[
            pl.BlockSpec((1, drow, local), lambda i: (i, 0, 0)),
            whole(rows, local),
            whole(ngroups, ntaps),
            whole(nshort, 3, local),
        ],
        scratch=[
            pltpu.VMEM((2, ndp, 3 * chunk + extra, width), BF16),
            pltpu.VMEM((ndp, rows, width), BF16),
        ],
        flops=2 * mm_flops,
        nbytes=2 * mm_bytes,
        vmem=MOST_VMEM_BYTES,
    )(xt, *near, near_last, grad_other, far_two, far_last, *mixed)
    grad_weight = jnp.transpose(grad_weight, (1, 0, 2))
    return (mixed, grad_in, grad_weight, grad_long, grad_short)


def from_behind(block, axis, distance):
    devices = range(lax.axis_size(axis))
    route = [(i - distance, i) for i in devices if i - distance in devices]
    return lax.ppermute(block, axis, route)


def toeplitz(leading, rows, span):
    groups = leading.shape[0]
    width = rows + span
    seed_row = jnp.concatenate(
        [leading, jnp.zeros((groups, width - leading.shape[1]), leading.dtype)], axis=1
    )
    tiled = jnp.tile(seed_row, (1, rows))
    skewed = tiled[:, : rows * (width - 1)].reshape(groups, rows, width - 1)
    return skewed[:, :, :span]


def to_groups(values, ngroups, members):
    count = values.shape[0]
    return values.reshape(count, ngroups, members).transpose(1, 2, 0)


def from_groups(values):
    groups, members, count = values.shape
    return values.transpose(2, 0, 1).reshape(count, groups * members)


def move_weights(tokens, in_weight, short_filter, long_filter, grad_out):
    rows = tokens.shape[0]
    local = grad_out.shape[1]
    nshort = short_filter.shape[0]
    ntaps = long_filter.shape[1]
    ngroups = long_filter.shape[0]
    members = local // ngroups
    margin = ntaps - 1
    span = rows + margin
    scale = float(rows * lax.axis_size("dp")) ** (-0.5)
    whole = lax.all_gather(tokens, ("row", "col"), axis=1, tiled=True)
    full_w = lax.all_gather(in_weight, "dp", axis=0, tiled=True)
    mixed_in = jnp.einsum("sd,dic->sic", whole, full_w, preferred_element_type=jnp.float32).astype(
        jnp.bfloat16
    )
    before = from_behind(mixed_in[rows - margin - nshort + 1 :], "dp", 1)
    extended = jnp.concatenate([before, mixed_in], axis=0).astype(jnp.float32)
    long_feats = jnp.zeros((span, 3, local), jnp.float32)
    for j in range(nshort):
        long_feats = (
            long_feats + short_filter[j][None] * extended[nshort - 1 - j : nshort - 1 - j + span]
        )
    product_ext = (long_feats[:, 1] * long_feats[:, 2]).astype(jnp.bfloat16)
    feats = long_feats[margin:]
    short_rows = extended[margin:]
    product_cols = to_groups(product_ext, ngroups, members)
    causal = toeplitz(long_filter[:, ::-1], rows, span)
    conv = from_groups(
        jnp.einsum("gst,gct->gcs", causal, product_cols, preferred_element_type=jnp.float32)
    )
    mixed = (feats[:, 0] * conv).astype(jnp.bfloat16)
    upstream = grad_out.astype(jnp.float32)
    grad_query = upstream * conv
    grad_conv = (upstream * feats[:, 0]).astype(jnp.bfloat16)
    after = from_behind(grad_conv[:margin], "dp", -1)
    grad_ext = jnp.concatenate([grad_conv, after], axis=0)
    anti = toeplitz(long_filter, rows, span)
    grad_product = from_groups(
        jnp.einsum(
            "gst,gct->gcs",
            anti,
            to_groups(grad_ext, ngroups, members),
            preferred_element_type=jnp.float32,
        )
    )
    reversed_cols = jnp.concatenate(
        [product_cols[:, :, ::-1], jnp.zeros((ngroups, members, rows), product_cols.dtype)], axis=2
    )
    width = span + rows
    pairs = jnp.einsum(
        "gcs,gcu->gsu",
        to_groups(grad_conv, ngroups, members),
        reversed_cols,
        preferred_element_type=jnp.float32,
    )
    diagonal = pairs.reshape(ngroups, rows * width)[:, : rows * (width - 1)].reshape(
        ngroups, rows, width - 1
    )
    filter_part = jnp.sum(diagonal[:, :, rows - 1 : rows - 1 + ntaps], axis=1)
    grad_feats = jnp.stack(
        [grad_query, grad_product * feats[:, 2], grad_product * feats[:, 1]], axis=1
    )
    later = from_behind(grad_feats[: nshort - 1], "dp", -1)
    feats_ext = jnp.concatenate([grad_feats, later], axis=0)
    grad_acc = jnp.zeros((rows, 3, local), jnp.float32)
    for j in range(nshort):
        grad_acc = grad_acc + short_filter[j][None] * feats_ext[j : j + rows]
    grad_mixed = grad_acc.astype(jnp.bfloat16)
    short_part = jnp.stack(
        [
            jnp.sum(grad_feats * short_rows[nshort - 1 - j : nshort - 1 - j + rows], axis=0)
            for j in range(nshort)
        ]
    )
    filter_total, short_total = (
        lax.psum(filter_part.astype(jnp.bfloat16), "dp").astype(jnp.float32),
        lax.psum(short_part.astype(jnp.bfloat16), "dp").astype(jnp.float32),
    )
    grad_long = filter_total * scale
    grad_short = short_total * scale
    partial_in = jnp.einsum("sic,dic->sd", grad_mixed, full_w, preferred_element_type=jnp.float32)
    summed_in = lax.psum_scatter(
        partial_in.astype(jnp.bfloat16), ("row", "col"), scatter_dimension=1, tiled=True
    )
    weight_term = (
        jnp.einsum("sd,sic->dic", whole, grad_mixed, preferred_element_type=jnp.float32) * scale
    )
    grad_weight = lax.psum_scatter(
        weight_term.astype(jnp.bfloat16), "dp", scatter_dimension=0, tiled=True
    ).astype(jnp.float32)
    return (mixed, summed_in, grad_weight, grad_long, grad_short)


def fits_whole_sequences(mesh, tokens, in_weight, short_filter, long_filter, grad_out):
    ndp, nrow, ncol = (mesh.shape[a] for a in ("dp", "row", "col"))
    seq, channels = grad_out.shape
    groups, ntaps = long_filter.shape
    local = channels // (nrow * ncol)
    width, rows = local // ndp, seq // ndp
    return (
        seq < tokens.shape[1]
        and ndp == nrow == 4
        and ncol * (tokens.shape[1] // (nrow * ncol)) == in_weight.shape[0] // ndp
        and ntaps == width == 128
        and seq % (2 * ntaps) == 0
        and rows % 16 == 0
        and groups % (8 * ndp * nrow * ncol) == 0
    )


def solution(mesh):
    placed = (
        P("dp", ("row", "col")),
        P("dp", None, ("row", "col")),
        P(None, None, ("row", "col")),
        P(("row", "col"), None),
        P("dp", ("row", "col")),
    )
    gives = (
        P("dp", ("row", "col")),
        P("dp", ("row", "col")),
        P("dp", None, ("row", "col")),
        P(("row", "col"), None),
        P(None, None, ("row", "col")),
    )

    def run(*arrays):
        plan = move_activations if fits_whole_sequences(mesh, *arrays) else move_weights
        return jax.shard_map(
            plan, mesh=mesh, in_specs=placed, out_specs=gives, check_vma=False
        )(*arrays)

    return run
```

```python
import functools

import jax
import jax.numpy as jnp
from jax import lax
from jax.experimental import pallas as pl
from jax.experimental.pallas import tpu as pltpu
from jax.sharding import PartitionSpec as P

VMEM_BYTES = 48 * 2**20
MOST_VMEM_BYTES = 62 * 2**20
F32 = jnp.float32
BF16 = jnp.bfloat16


def kernel_call(body, outs, grid=(), in_specs=None, out_specs=None, scratch=(), flops=0, nbytes=0, vmem=VMEM_BYTES):
    kwargs = {}
    if in_specs is not None:
        kwargs = dict(grid=grid, in_specs=in_specs, out_specs=out_specs)
    return pl.pallas_call(
        body,
        out_shape=outs,
        scratch_shapes=scratch,
        compiler_params=pltpu.CompilerParams(vmem_limit_bytes=vmem),
        cost_estimate=pl.CostEstimate(flops=flops, bytes_accessed=nbytes, transcendentals=0),
        **kwargs,
    )


def shaped(shape, dtype):
    return jax.ShapeDtypeStruct(shape, dtype)


def bands_body(base_ref, out_ref):
    groups, wide = base_ref.shape
    rows = out_ref.shape[1]
    row = lax.broadcasted_iota(jnp.int32, (8, wide), 0)
    for g in range(groups):
        band = jnp.broadcast_to(base_ref[g : g + 1, :], (8, wide))
        for bit in (1, 2, 4):
            band = jnp.where((row & bit) != 0, pltpu.roll(band, bit, 1), band)
        count = 8
        while count < rows:
            band = jnp.concatenate([band, pltpu.roll(band, count, 1)], axis=0)
            count *= 2
        out_ref[g] = band.astype(out_ref.dtype)


def tokens_of(row, nrow):
    return row % 2 * (nrow // 2) + row // 2


def wrapped(value, size):
    return lax.rem(value + 2 * size, size)


def split_body(all_ref, *out_refs):
    width = out_refs[0].shape[1]
    for ahead, out_ref in enumerate(out_refs):
        at = wrapped(lax.axis_index("dp") + ahead, len(out_refs)) * width
        out_ref[...] = all_ref[:, pl.ds(pl.multiple_of(at, width), width)]


def project_body(x_ref, w_ref, *refs):
    *out_refs, held = refs
    z, col = lax.axis_index("dp"), lax.axis_index("col")
    nblocks, ncol, rows, depth = x_ref.shape
    width = held.shape[2]
    total = jnp.zeros((nblocks * rows, w_ref.shape[2]), F32)
    for dx in range(ncol):
        start = pl.multiple_of(wrapped(col - dx, ncol) * depth, depth)
        total += jnp.dot(
            x_ref[:, dx].reshape(nblocks * rows, depth),
            w_ref[0, pl.ds(start, depth), :],
            preferred_element_type=F32,
        )
    for owner in range(len(out_refs)):
        held[owner] = total[:, owner * width : (owner + 1) * width].astype(BF16)
    for ahead, out_ref in enumerate(out_refs):
        out_ref[0] = held[wrapped(z + ahead, len(out_refs))]


def far_columns_body(w_ref, out_ref, sem):
    ndp = lax.axis_size("dp")
    width = out_ref.shape[2]
    start = wrapped(lax.axis_index("dp") + ndp // 2, ndp) * width
    copy = pltpu.make_async_copy(w_ref.at[:, :, pl.ds(pl.multiple_of(start, width), width)], out_ref, sem)
    copy.start()
    copy.wait()


def first_grad_body(
    near, near_before, near_after, far, far_before, far_after, w_ref, partner_w_ref, out_ref, far_ref, held, held_w, sems
):
    _, ndp, _, width = held.shape
    ncol, tokens, depth = out_ref.shape
    z, col = lax.axis_index("dp"), lax.axis_index("col")
    copies = []
    for dx in range(ncol):
        start = pl.multiple_of(wrapped(col - dx, ncol) * depth, depth)
        for k, weights in enumerate((w_ref, partner_w_ref)):
            copy = pltpu.make_async_copy(weights.at[:, pl.ds(start, depth)], held_w.at[k, dx], sems.at[k, dx])
            copy.start()
            copies.append(copy)
    far_ref[0], far_ref[1] = far_before[...], far_after[...]
    for k, pieces in enumerate(((near, near_before, near_after), (far, far_before, far_after))):
        held[k, wrapped(z + ndp // 2, ndp)] = jnp.zeros(held.shape[2:], BF16)
        for ahead, piece in zip((0, -1, 1), pieces):
            held[k, wrapped(z + ahead, ndp)] = piece[: 3 * tokens]
    for dx in range(ncol):
        total = jnp.zeros((tokens, depth), F32)
        for k in range(2):
            copies[2 * dx + k].wait()
            for i in range(3):
                rows = slice(i * tokens, (i + 1) * tokens)
                total += lax.dot_general(
                    jnp.concatenate([held[k, owner, rows] for owner in range(ndp)], axis=1),
                    held_w[k, dx, i],
                    (((1,), (1,)), ((), ())),
                    preferred_element_type=F32,
                )
        out_ref[dx] = total.astype(BF16)


def second_grad_body(ndp, part_ref, *refs):
    arrived, (w_ref, partner_w_ref), refs = (refs[:2], refs[2:4]), refs[4:6], refs[6:]
    (near_ref, far_ref), refs = refs[:2], refs[2:]
    *out_refs, held_w, held_part, sems = refs
    ncol, tokens, depth = held_part.shape
    rows = out_refs[0].shape[0]
    width = near_ref.shape[1]
    z, col = lax.axis_index("dp"), lax.axis_index("col")
    lanes = pl.ds(pl.multiple_of(wrapped(z + ndp // 2, ndp) * width, width), width)
    copies = [
        pltpu.make_async_copy(w_ref, held_w.at[0], sems.at[0]),
        pltpu.make_async_copy(partner_w_ref.at[:, :, lanes], held_w.at[1], sems.at[1]),
    ]
    copies.append(pltpu.make_async_copy(part_ref, held_part, sems.at[2]))
    for copy in copies:
        copy.start()
    for k, (pair, target) in enumerate(zip(arrived, (near_ref, far_ref))):
        for source, here in zip(pair, (z >= ndp // 2, z < ndp // 2)):

            @pl.when(here)
            def _(source=source, target=target, k=k):
                copy = pltpu.make_async_copy(source, target, sems.at[3 + k])
                copy.start()
                copy.wait()

    for copy in copies:
        copy.wait()
    left = jnp.concatenate(
        [ref[i * tokens : (i + 1) * tokens] for ref in (near_ref, far_ref) for i in range(3)], axis=1
    )
    for dx in range(ncol):
        start = pl.multiple_of(wrapped(col - dx, ncol) * depth, depth)
        right = jnp.concatenate([held_w[k, i, pl.ds(start, depth), :] for k in range(2) for i in range(3)], axis=1)
        total = held_part[dx].astype(F32) + lax.dot_general(
            left, right, (((1,), (1,)), ((), ())), preferred_element_type=F32
        )
        for block in range(tokens // rows):
            out_refs[block * ncol + dx][...] = total[block * rows : (block + 1) * rows].astype(BF16)


def weight_grad_body(scale, *refs):
    (x0_ref, x1_ref), near_refs, other_refs, mixed_refs, refs = refs[:2], refs[2:6], refs[6:9], refs[9:13], refs[13:]
    own_ref, two_ref, last_ref = other_refs
    other = (own_ref, two_ref.at[0], two_ref.at[1], last_ref)
    out_ref, mixed_ref, long_ref, short_ref, held, held_mixed = refs
    nblocks, ncol, rows, depth = x0_ref.shape
    _, ndp, _, width = held.shape
    tokens = nblocks * rows
    i = pl.program_id(0)
    z, col = lax.axis_index("dp"), lax.axis_index("col")

    @pl.when(i == 0)
    def _():
        groups = long_ref.shape[0] // ndp
        for k, ahead in enumerate((0, -1, 1, 2)):
            owner = wrapped(z + ahead, ndp)
            held[0, owner] = near_refs[k][...]
            held[1, owner, : 3 * tokens] = other[k][...]
        for back in range(ndp):
            held_mixed[wrapped(z - back, ndp)] = mixed_refs[back][...]
        for owner in range(ndp):
            lanes = slice(owner * width, (owner + 1) * width)
            mixed_ref[:, lanes] = held_mixed[owner]
            small = held[0, owner, 3 * tokens :].astype(F32)
            long_ref[owner * groups : (owner + 1) * groups] = small[:groups]
            nshort, three, _ = short_ref.shape
            for j in range(nshort):
                short_ref[j, :, lanes] = small[groups + three * j : groups + three * (j + 1)]

    at = pl.ds(pl.multiple_of(i * tokens, 16), tokens)
    gm = jnp.concatenate(
        [jnp.concatenate([held[k, owner, at, :] for owner in range(ndp)], axis=1) for k in range(2)], axis=0
    )
    for dx in range(ncol):
        start = pl.multiple_of(wrapped(col - dx, ncol) * depth, depth)
        x = jnp.concatenate(
            [x_ref[:, dx].reshape(tokens, depth) for x_ref in (x0_ref, x1_ref)], axis=0
        )
        out_ref[0, pl.ds(start, depth), :] = scale * lax.dot_general(
            x, gm, (((0,), (0,)), ((), ())), preferred_element_type=F32
        )


def delayed(values, count):
    row = lax.broadcasted_iota(jnp.int32, values.shape, 0)
    return jnp.where(row >= count, pltpu.roll(values, count, 0), 0.0)


def advanced(values, count):
    rows = values.shape[0]
    row = lax.broadcasted_iota(jnp.int32, values.shape, 0)
    return jnp.where(row < rows - count, pltpu.roll(values, rows - count, 0), 0.0)


def middle_body(scale, nshort, nrow, *refs):
    sums, refs = (refs[:3], refs[3:6]), refs[6:]
    (sf_ref, causal_ref, anti_ref), refs = refs[:3], refs[3:]
    *refs, m_ref, gm_ref, mixed_ref, go_ref = refs
    ndp = len(refs) // 2 - 1
    go_refs, (near_ref, other_ref), mixed_refs = refs[:ndp], refs[ndp : ndp + 2], refs[ndp + 2 :]
    tokens, width = go_ref.shape
    for behind, piece in enumerate(go_refs):
        at = wrapped(lax.axis_index("dp") - behind, ndp) * (tokens // ndp)
        go_ref[pl.ds(pl.multiple_of(at, 16), tokens // ndp)] = piece[...]
    row = lax.axis_index("row")
    nblocks = nrow // 2
    rows = tokens // nrow

    def places():
        for chunk, start in enumerate((row, row + 1 - 2 * lax.rem(row, 2))):
            for block in range(nblocks):
                at = tokens_of(wrapped(start - 2 * block, nrow), nrow) * rows
                for i in range(3):
                    yield chunk, (i * nblocks + block) * rows, pl.multiple_of(i * tokens + at, 16)

    for chunk, place, at in places():
        held = [ref[place : place + rows].astype(F32) for ref in sums[chunk]]
        m_ref[pl.ds(at, rows)] = held[0] + held[1] + held[2]
    groups, block, span = causal_ref.shape
    members = width // groups
    nspans = tokens // block
    lane = lax.broadcasted_iota(jnp.int32, (block, width), 1) // members
    lanes = lax.broadcasted_iota(jnp.int32, (block, 2 * width), 1) % width // members

    def past(i, j):
        held = m_ref[i * tokens : (i + 1) * tokens]
        return held if j == 0 else delayed(held, j)

    def taps(j, i):
        return sf_ref[3 * j + i : 3 * j + i + 1, :]

    feats = [sum(taps(j, i) * past(i, j) for j in range(nshort)) for i in range(3)]
    product = (feats[1] * feats[2]).astype(BF16)
    zero = jnp.zeros((block, width), BF16)
    p_blocks = [zero] + [product[b * block : (b + 1) * block] for b in range(nspans)]
    p_pairs = [jnp.concatenate(p_blocks[b : b + 2], axis=0) for b in range(nspans)]

    def filtered(band_ref, pairs):
        bands = band_ref[...].reshape(groups * block, span)
        out = []
        for b in range(0, nspans, 2):
            both = jnp.dot(bands, jnp.concatenate(pairs[b : b + 2], axis=1), preferred_element_type=F32)
            for h in range(2):
                part = both[:, h * width : (h + 1) * width]
                picked = part[:block]
                for g in range(1, groups):
                    picked = jnp.where(lane == g, part[g * block : (g + 1) * block], picked)
                out.append(picked)
        return jnp.concatenate(out, axis=0)

    conv = filtered(causal_ref, p_pairs)
    upstream = go_ref[...].astype(F32)
    mixed_ref[...] = (feats[0] * conv).astype(BF16)
    for ahead, out_ref in enumerate(mixed_refs):
        at = pl.multiple_of(wrapped(lax.axis_index("dp") + ahead, ndp) * (tokens // ndp), 16)
        out_ref[...] = mixed_ref[pl.ds(at, tokens // ndp)]
    grad_conv = (upstream * feats[0]).astype(BF16)
    c_blocks = [grad_conv[b * block : (b + 1) * block] for b in range(nspans)] + [zero]
    c_pairs = [jnp.concatenate(c_blocks[b : b + 2], axis=0) for b in range(nspans)]
    grad_product = filtered(anti_ref, c_pairs)

    corr = jnp.zeros((groups * block, span), F32)
    for b in range(0, nspans, 2):
        left = jnp.concatenate(c_blocks[b : b + 2], axis=1)
        stacked = jnp.concatenate(
            [jnp.where(lanes == g, left, jnp.zeros_like(left)) for g in range(groups)], axis=0
        )
        right = jnp.concatenate(p_pairs[b : b + 2], axis=1)
        corr += lax.dot_general(stacked, right, (((1,), (1,)), ((), ())), preferred_element_type=F32)
    turn = lax.broadcasted_iota(jnp.int32, (8, span), 0)
    sums = []
    for g in range(groups):
        part = corr[g * block : (g + 1) * block]
        count = block
        while count > 8:
            count //= 2
            part = part[:count] + pltpu.roll(part[count:], span - count, 1)
        for bit in (1, 2, 4):
            part = jnp.where((turn & bit) != 0, pltpu.roll(part, span - bit, 1), part)
        sums.append(jnp.sum(part, axis=0, keepdims=True))
    by_lag = jnp.concatenate(sums, axis=0)
    by_lag = (scale * pltpu.roll(by_lag, span - 1, 1)[:, :block]).astype(BF16)
    ahead = lax.broadcasted_iota(jnp.int32, (block, block), 0)
    back = lax.broadcasted_iota(jnp.int32, (block, block), 1)
    turned = jnp.where(ahead + back == block - 1, 1.0, 0.0).astype(BF16)
    by_lag = jnp.dot(by_lag, turned, preferred_element_type=F32)

    grad_feats = [upstream * conv, grad_product * feats[2], grad_product * feats[1]]
    short_rows = []
    for j in range(nshort):
        for i in range(3):
            short_rows.append(scale * jnp.sum(grad_feats[i] * past(i, j), axis=0, keepdims=True))
    for i in range(3):
        total = taps(0, i) * grad_feats[i]
        for j in range(1, nshort):
            total += taps(j, i) * advanced(grad_feats[i], j)
        gm_ref[i * tokens : (i + 1) * tokens] = total.astype(BF16)
    for chunk, place, at in places():
        (near_ref, other_ref)[chunk][place : place + rows] = gm_ref[pl.ds(at, rows)]
    tail = near_ref.shape[0] - 3 * tokens // 2 - groups - 3 * nshort
    small = jnp.concatenate([by_lag] + short_rows + [jnp.zeros((tail, width), F32)], axis=0)
    near_ref[3 * tokens // 2 :] = small.astype(BF16)


def sum_over_line(own, right, far, left):
    ndp = lax.axis_size("dp")
    from_left = lax.ppermute(far, "dp", [(a, a + 1) for a in range(ndp // 2)])
    from_right = lax.ppermute(far, "dp", [(a, a - 1) for a in range(ndp // 2, ndp)])
    rightward = lax.ppermute(right + from_left, "dp", [(a, (a + 1) % ndp) for a in range(ndp)])
    leftward = lax.ppermute(left + from_right, "dp", [(a, (a - 1) % ndp) for a in range(ndp)])
    return own, rightward, leftward


def gather_over_line(own, across):
    ndp, nrow = lax.axis_size("dp"), lax.axis_size("row")

    def shift(count):
        return [
            (a * nrow + r, (a + count) % ndp * nrow + (r + 1 - 2 * (r % 2) if across else r))
            for a in range(ndp)
            for r in range(nrow)
        ]

    before = lax.ppermute(own, ("dp", "row"), shift(1))
    after = lax.ppermute(own, ("dp", "row"), shift(-1))
    here = lax.ppermute(own, ("dp", "row"), shift(0)) if across else own
    far_before = lax.ppermute(before, "dp", [(a - 1, a) for a in range(ndp // 2, ndp)])
    far_after = lax.ppermute(after, "dp", [(a + 1, a) for a in range(ndp // 2)])
    return here, before, after, far_before, far_after


def move_activations(tokens, in_weight, short_filter, long_filter, grad_out):
    ndp, nrow, ncol = (lax.axis_size(a) for a in ("dp", "row", "col"))
    z = lax.axis_index("dp")
    rows, dcol = tokens.shape
    local = grad_out.shape[1]
    nshort = short_filter.shape[0]
    ngroups, ntaps = long_filter.shape
    seq = rows * ndp
    width, groups = local // ndp, ngroups // ndp
    drow = in_weight.shape[0]
    scale = float(seq) ** -0.5
    nblocks = nrow // 2
    chunk = nblocks * rows
    swap = [(tokens_of(b, nrow) * nrow + a, a * nrow + b) for a in range(ndp) for b in range(nrow)]
    swap_back = [(b, a) for a, b in swap]
    partner = [(a, a + 1 - 2 * (a % 2)) for a in range(nrow)]
    places = [(dy, dx) for dy in range(nblocks) for dx in range(ncol)]

    def offset(dy, dx):
        return [
            (a * ncol + b, (a + 2 * dy) % nrow * ncol + (b + dx) % ncol) for a in range(nrow) for b in range(ncol)
        ]

    w = jnp.transpose(in_weight, (1, 0, 2))
    moved = lax.ppermute(tokens, ("dp", "row"), swap)
    far_w = kernel_call(
        far_columns_body,
        shaped((3, drow, width), BF16),
        in_specs=[pl.BlockSpec(memory_space=pl.ANY)],
        out_specs=pl.BlockSpec(memory_space=pltpu.VMEM),
        scratch=[pltpu.SemaphoreType.DMA],
    )(w)
    turn = [[(a, (a + ahead) % ndp) for a in range(ndp)] for ahead in range(ndp)]
    upstream = [*kernel_call(split_body, [shaped((rows, width), BF16)] * ndp)(grad_out)]
    moved, upstream, far_w = lax.optimization_barrier((moved, upstream, far_w))
    near = [moved] + [lax.ppermute(moved, ("row", "col"), offset(*p)) for p in places[1:]]
    for ahead in (1, 3):
        upstream[ahead] = lax.ppermute(upstream[ahead], "dp", turn[ahead])
    upstream[1::2], near[1:] = lax.optimization_barrier((upstream[1::2], near[1:]))
    x0 = jnp.stack(near).reshape(nblocks, ncol, rows, dcol)
    x1 = lax.ppermute(x0, "row", partner)
    upstream[2] = lax.ppermute(upstream[2], "dp", turn[2])
    upstream[2], x1 = lax.optimization_barrier((upstream[2], x1))

    sf = lax.dynamic_slice_in_dim(short_filter, z * width, width, 2).reshape(3 * nshort, width)
    lf = lax.dynamic_slice_in_dim(long_filter, z * groups, groups, 0).astype(F32)
    zeros = functools.partial(jnp.zeros, dtype=F32)
    bases = jnp.concatenate(
        [
            jnp.concatenate([zeros((groups, 1)), lf[:, ::-1], zeros((groups, ntaps - 1))], axis=1),
            jnp.concatenate([lf, zeros((groups, ntaps))], axis=1),
        ],
        axis=0,
    )
    bands = kernel_call(bands_body, shaped((2 * groups, ntaps, 2 * ntaps), BF16))(bases)

    mm_flops = seq * drow * 3 * local
    mm_bytes = seq * drow + 6 * drow * local + 3 * seq * local
    sums = []
    for x in (x0, x1):
        parts = kernel_call(
            project_body,
            [shaped((3, chunk, width), BF16)] * ndp,
            grid=(3,),
            in_specs=[
                pl.BlockSpec((nblocks, ncol, rows, dcol), lambda i: (0, 0, 0, 0)),
                pl.BlockSpec((1, drow, local), lambda i: (i, 0, 0)),
            ],
            out_specs=[pl.BlockSpec((1, chunk, width), lambda i: (i, 0, 0))] * ndp,
            scratch=[pltpu.VMEM((ndp, chunk, width), BF16)],
            flops=mm_flops,
            nbytes=mm_bytes,
        )(x, w)
        sums += sum_over_line(*(p.reshape(3 * chunk, width) for p in parts))

    extra = -(-(groups + 3 * nshort) // 16) * 16
    half = pl.BlockSpec((groups, ntaps, 2 * ntaps), lambda i: (0, 0, 0))
    other = pl.BlockSpec((groups, ntaps, 2 * ntaps), lambda i: (1, 0, 0))
    whole = lambda *shape: pl.BlockSpec(shape, lambda i: (0,) * len(shape))
    grad_near, grad_other, *mixed = kernel_call(
        functools.partial(middle_body, scale, nshort, nrow),
        [shaped((3 * chunk + extra, width), BF16), shaped((3 * chunk, width), BF16)]
        + [shaped((rows, width), BF16)] * ndp,
        grid=(1,),
        in_specs=[whole(3 * chunk, width)] * 6
        + [whole(3 * nshort, width), half, other]
        + [whole(rows, width)] * ndp,
        out_specs=[whole(3 * chunk + extra, width), whole(3 * chunk, width)] + [whole(rows, width)] * ndp,
        scratch=[
            pltpu.VMEM((3 * seq, width), F32),
            pltpu.VMEM((3 * seq, width), BF16),
            pltpu.VMEM((seq, width), BF16),
            pltpu.VMEM((seq, width), BF16),
        ],
        flops=3 * 2 * groups * ntaps * 2 * ntaps * width * (seq // ntaps),
        nbytes=2 * width * seq * 14,
        vmem=MOST_VMEM_BYTES,
    )(*sums, sf, bands, bands, *upstream)
    mixed = [mixed[0]] + [
        lax.ppermute(part, "dp", [(a, (a + ahead) % ndp) for a in range(ndp)])
        for ahead, part in enumerate(mixed)
        if ahead
    ]
    *near, near_far_before, near_far_after = gather_over_line(grad_near, False)
    *far, far_far_before, far_far_after = gather_over_line(grad_other, True)
    partner_w = lax.ppermute(w, "row", partner)
    everywhere = pl.BlockSpec(memory_space=pl.ANY)
    in_vmem = pl.BlockSpec(memory_space=pltpu.VMEM)
    part, far_two = kernel_call(
        first_grad_body,
        [shaped((ncol, chunk, dcol), BF16), shaped((2, 3 * chunk, width), BF16)],
        in_specs=[in_vmem] * 6 + [everywhere] * 2,
        out_specs=[in_vmem] * 2,
        scratch=[
            pltpu.VMEM((2, ndp, 3 * chunk, width), BF16),
            pltpu.VMEM((2, ncol, 3, dcol, local), BF16),
            pltpu.SemaphoreType.DMA((2, ncol)),
        ],
        flops=2 * mm_flops,
        nbytes=2 * mm_bytes,
    )(*near, *far, w, partner_w)
    near_last, far_last, *blocks = kernel_call(
        functools.partial(second_grad_body, ndp),
        [shaped(grad_near.shape, BF16), shaped(grad_other.shape, BF16)]
        + [shaped((rows, dcol), BF16)] * len(places),
        grid=(),
        in_specs=[everywhere] * 7,
        out_specs=[in_vmem] * (2 + len(places)),
        scratch=[
            pltpu.VMEM((2, 3, drow, width), BF16),
            pltpu.VMEM((ncol, chunk, dcol), BF16),
            pltpu.SemaphoreType.DMA((5,)),
        ],
        flops=mm_flops // 2,
        nbytes=mm_bytes // 2,
        vmem=MOST_VMEM_BYTES,
    )(part, near_far_before, near_far_after, far_far_before, far_far_after, far_w, partner_w)
    far_two, far_last, mixed[1:] = lax.optimization_barrier((far_two, far_last, mixed[1:]))
    far_two, far_last = (lax.ppermute(part, "row", partner) for part in (far_two, far_last))
    arrivals = [
        lax.ppermute(sent, ("row", "col"), [(b, a) for a, b in offset(*p)])
        for p, sent in zip(places[1:], blocks[1:])
    ]
    arrived = sum((a.astype(F32) for a in arrivals), blocks[0].astype(F32)).astype(BF16)
    arrived, far_two, far_last = lax.optimization_barrier((arrived, far_two, far_last))
    grad_in = lax.ppermute(arrived, ("dp", "row"), swap_back)

    grad_weight, mixed, grad_long, grad_short = kernel_call(
        functools.partial(weight_grad_body, scale),
        [
            shaped((3, drow, local), F32),
            shaped((rows, local), BF16),
            shaped((ngroups, ntaps), F32),
            shaped((nshort, 3, local), F32),
        ],
        grid=(3,),
        in_specs=[whole(nblocks, ncol, rows, dcol)] * 2
        + [whole(*grad_near.shape)] * 4
        + [whole(*grad_other.shape), whole(*far_two.shape), whole(*far_last.shape)]
        + [whole(rows, width)] * ndp,
        out_specs=[
            pl.BlockSpec((1, drow, local), lambda i: (i, 0, 0)),
            whole(rows, local),
            whole(ngroups, ntaps),
            whole(nshort, 3, local),
        ],
        scratch=[
            pltpu.VMEM((2, ndp, 3 * chunk + extra, width), BF16),
            pltpu.VMEM((ndp, rows, width), BF16),
        ],
        flops=2 * mm_flops,
        nbytes=2 * mm_bytes,
    )(x0, x1, *near, near_last, grad_other, far_two, far_last, *mixed)
    grad_weight = jnp.transpose(grad_weight, (1, 0, 2))
    return (mixed, grad_in, grad_weight, grad_long, grad_short)


def from_behind(block, axis, distance):
    devices = range(lax.axis_size(axis))
    route = [(i - distance, i) for i in devices if i - distance in devices]
    return lax.ppermute(block, axis, route)


def toeplitz(leading, rows, span):
    groups = leading.shape[0]
    width = rows + span
    seed_row = jnp.concatenate(
        [leading, jnp.zeros((groups, width - leading.shape[1]), leading.dtype)], axis=1
    )
    tiled = jnp.tile(seed_row, (1, rows))
    skewed = tiled[:, : rows * (width - 1)].reshape(groups, rows, width - 1)
    return skewed[:, :, :span]


def to_groups(values, ngroups, members):
    count = values.shape[0]
    return values.reshape(count, ngroups, members).transpose(1, 2, 0)


def from_groups(values):
    groups, members, count = values.shape
    return values.transpose(2, 0, 1).reshape(count, groups * members)


def move_weights(tokens, in_weight, short_filter, long_filter, grad_out):
    rows = tokens.shape[0]
    local = grad_out.shape[1]
    nshort = short_filter.shape[0]
    ntaps = long_filter.shape[1]
    ngroups = long_filter.shape[0]
    members = local // ngroups
    margin = ntaps - 1
    span = rows + margin
    scale = float(rows * lax.axis_size("dp")) ** (-0.5)
    whole = lax.all_gather(tokens, ("row", "col"), axis=1, tiled=True)
    full_w = lax.all_gather(in_weight, "dp", axis=0, tiled=True)
    mixed_in = jnp.einsum("sd,dic->sic", whole, full_w, preferred_element_type=jnp.float32).astype(
        jnp.bfloat16
    )
    before = from_behind(mixed_in[rows - margin - nshort + 1 :], "dp", 1)
    extended = jnp.concatenate([before, mixed_in], axis=0).astype(jnp.float32)
    long_feats = jnp.zeros((span, 3, local), jnp.float32)
    for j in range(nshort):
        long_feats = (
            long_feats + short_filter[j][None] * extended[nshort - 1 - j : nshort - 1 - j + span]
        )
    product_ext = (long_feats[:, 1] * long_feats[:, 2]).astype(jnp.bfloat16)
    feats = long_feats[margin:]
    short_rows = extended[margin:]
    product_cols = to_groups(product_ext, ngroups, members)
    causal = toeplitz(long_filter[:, ::-1], rows, span)
    conv = from_groups(
        jnp.einsum("gst,gct->gcs", causal, product_cols, preferred_element_type=jnp.float32)
    )
    mixed = (feats[:, 0] * conv).astype(jnp.bfloat16)
    upstream = grad_out.astype(jnp.float32)
    grad_query = upstream * conv
    grad_conv = (upstream * feats[:, 0]).astype(jnp.bfloat16)
    after = from_behind(grad_conv[:margin], "dp", -1)
    grad_ext = jnp.concatenate([grad_conv, after], axis=0)
    anti = toeplitz(long_filter, rows, span)
    grad_product = from_groups(
        jnp.einsum(
            "gst,gct->gcs",
            anti,
            to_groups(grad_ext, ngroups, members),
            preferred_element_type=jnp.float32,
        )
    )
    reversed_cols = jnp.concatenate(
        [product_cols[:, :, ::-1], jnp.zeros((ngroups, members, rows), product_cols.dtype)], axis=2
    )
    width = span + rows
    pairs = jnp.einsum(
        "gcs,gcu->gsu",
        to_groups(grad_conv, ngroups, members),
        reversed_cols,
        preferred_element_type=jnp.float32,
    )
    diagonal = pairs.reshape(ngroups, rows * width)[:, : rows * (width - 1)].reshape(
        ngroups, rows, width - 1
    )
    filter_part = jnp.sum(diagonal[:, :, rows - 1 : rows - 1 + ntaps], axis=1)
    grad_feats = jnp.stack(
        [grad_query, grad_product * feats[:, 2], grad_product * feats[:, 1]], axis=1
    )
    later = from_behind(grad_feats[: nshort - 1], "dp", -1)
    feats_ext = jnp.concatenate([grad_feats, later], axis=0)
    grad_acc = jnp.zeros((rows, 3, local), jnp.float32)
    for j in range(nshort):
        grad_acc = grad_acc + short_filter[j][None] * feats_ext[j : j + rows]
    grad_mixed = grad_acc.astype(jnp.bfloat16)
    short_part = jnp.stack(
        [
            jnp.sum(grad_feats * short_rows[nshort - 1 - j : nshort - 1 - j + rows], axis=0)
            for j in range(nshort)
        ]
    )
    filter_total, short_total = (
        lax.psum(filter_part.astype(jnp.bfloat16), "dp").astype(jnp.float32),
        lax.psum(short_part.astype(jnp.bfloat16), "dp").astype(jnp.float32),
    )
    grad_long = filter_total * scale
    grad_short = short_total * scale
    partial_in = jnp.einsum("sic,dic->sd", grad_mixed, full_w, preferred_element_type=jnp.float32)
    summed_in = lax.psum_scatter(
        partial_in.astype(jnp.bfloat16), ("row", "col"), scatter_dimension=1, tiled=True
    )
    weight_term = (
        jnp.einsum("sd,sic->dic", whole, grad_mixed, preferred_element_type=jnp.float32) * scale
    )
    grad_weight = lax.psum_scatter(
        weight_term.astype(jnp.bfloat16), "dp", scatter_dimension=0, tiled=True
    ).astype(jnp.float32)
    return (mixed, summed_in, grad_weight, grad_long, grad_short)


def fits_whole_sequences(mesh, tokens, in_weight, short_filter, long_filter, grad_out):
    ndp, nrow, ncol = (mesh.shape[a] for a in ("dp", "row", "col"))
    seq, channels = grad_out.shape
    groups, ntaps = long_filter.shape
    local = channels // (nrow * ncol)
    width, rows = local // ndp, seq // ndp
    return (
        seq < tokens.shape[1]
        and ndp == nrow == 4
        and ncol * (tokens.shape[1] // (nrow * ncol)) == in_weight.shape[0] // ndp
        and ntaps == width == 128
        and seq % (2 * ntaps) == 0
        and rows % 16 == 0
        and groups % (8 * ndp * nrow * ncol) == 0
    )


def solution(mesh):
    placed = (
        P("dp", ("row", "col")),
        P("dp", None, ("row", "col")),
        P(None, None, ("row", "col")),
        P(("row", "col"), None),
        P("dp", ("row", "col")),
    )
    gives = (
        P("dp", ("row", "col")),
        P("dp", ("row", "col")),
        P("dp", None, ("row", "col")),
        P(("row", "col"), None),
        P(None, None, ("row", "col")),
    )

    def run(*arrays):
        plan = move_activations if fits_whole_sequences(mesh, *arrays) else move_weights
        return jax.shard_map(
            plan, mesh=mesh, in_specs=placed, out_specs=gives, check_vma=False
        )(*arrays)

    return run
```

```python
import functools

import jax
import jax.numpy as jnp
from jax import lax
from jax.experimental import pallas as pl
from jax.experimental.pallas import tpu as pltpu
from jax.sharding import PartitionSpec as P

VMEM_BYTES = 48 * 2**20
MOST_VMEM_BYTES = 62 * 2**20
F32 = jnp.float32
BF16 = jnp.bfloat16


def kernel_call(body, outs, grid=(), in_specs=None, out_specs=None, scratch=(), flops=0, nbytes=0, vmem=VMEM_BYTES):
    kwargs = {}
    if in_specs is not None:
        kwargs = dict(grid=grid, in_specs=in_specs, out_specs=out_specs)
    return pl.pallas_call(
        body,
        out_shape=outs,
        scratch_shapes=scratch,
        compiler_params=pltpu.CompilerParams(vmem_limit_bytes=vmem),
        cost_estimate=pl.CostEstimate(flops=flops, bytes_accessed=nbytes, transcendentals=0),
        **kwargs,
    )


def shaped(shape, dtype):
    return jax.ShapeDtypeStruct(shape, dtype)


def bands_body(base_ref, out_ref):
    groups, wide = base_ref.shape
    rows = out_ref.shape[1]
    row = lax.broadcasted_iota(jnp.int32, (8, wide), 0)
    for g in range(groups):
        band = jnp.broadcast_to(base_ref[g : g + 1, :], (8, wide))
        for bit in (1, 2, 4):
            band = jnp.where((row & bit) != 0, pltpu.roll(band, bit, 1), band)
        count = 8
        while count < rows:
            band = jnp.concatenate([band, pltpu.roll(band, count, 1)], axis=0)
            count *= 2
        out_ref[g] = band.astype(out_ref.dtype)


def tokens_of(row, nrow):
    return row % 2 * (nrow // 2) + row // 2


def wrapped(value, size):
    return lax.rem(value + 2 * size, size)


def split_body(all_ref, *out_refs):
    width = out_refs[0].shape[1]
    for ahead, out_ref in enumerate(out_refs):
        at = wrapped(lax.axis_index("dp") + ahead, len(out_refs)) * width
        out_ref[...] = all_ref[:, pl.ds(pl.multiple_of(at, width), width)]


def project_body(x_ref, w_ref, *refs):
    *out_refs, held = refs
    z, col = lax.axis_index("dp"), lax.axis_index("col")
    nblocks, ncol, rows, depth = x_ref.shape
    width = held.shape[2]
    total = jnp.zeros((nblocks * rows, w_ref.shape[2]), F32)
    for dx in range(ncol):
        start = pl.multiple_of(wrapped(col - dx, ncol) * depth, depth)
        total += jnp.dot(
            x_ref[:, dx].reshape(nblocks * rows, depth),
            w_ref[0, pl.ds(start, depth), :],
            preferred_element_type=F32,
        )
    for owner in range(len(out_refs)):
        held[owner] = total[:, owner * width : (owner + 1) * width].astype(BF16)
    for ahead, out_ref in enumerate(out_refs):
        out_ref[0] = held[wrapped(z + ahead, len(out_refs))]


def far_columns_body(w_ref, out_ref, sem):
    ndp = lax.axis_size("dp")
    width = out_ref.shape[2]
    start = wrapped(lax.axis_index("dp") + ndp // 2, ndp) * width
    copy = pltpu.make_async_copy(w_ref.at[:, :, pl.ds(pl.multiple_of(start, width), width)], out_ref, sem)
    copy.start()
    copy.wait()


def first_grad_body(
    near, near_before, near_after, far, far_before, far_after, w_ref, partner_w_ref, out_ref, far_ref, held, held_w, sems
):
    _, ndp, _, width = held.shape
    ncol, tokens, depth = out_ref.shape
    z, col = lax.axis_index("dp"), lax.axis_index("col")
    copies = []
    for dx in range(ncol):
        start = pl.multiple_of(wrapped(col - dx, ncol) * depth, depth)
        for k, weights in enumerate((w_ref, partner_w_ref)):
            copy = pltpu.make_async_copy(weights.at[:, pl.ds(start, depth)], held_w.at[k, dx], sems.at[k, dx])
            copy.start()
            copies.append(copy)
    far_ref[0], far_ref[1] = far_before[...], far_after[...]
    for k, pieces in enumerate(((near, near_before, near_after), (far, far_before, far_after))):
        held[k, wrapped(z + ndp // 2, ndp)] = jnp.zeros(held.shape[2:], BF16)
        for ahead, piece in zip((0, -1, 1), pieces):
            held[k, wrapped(z + ahead, ndp)] = piece[: 3 * tokens]
    for dx in range(ncol):
        total = jnp.zeros((tokens, depth), F32)
        for k in range(2):
            copies[2 * dx + k].wait()
            for i in range(3):
                rows = slice(i * tokens, (i + 1) * tokens)
                total += lax.dot_general(
                    jnp.concatenate([held[k, owner, rows] for owner in range(ndp)], axis=1),
                    held_w[k, dx, i],
                    (((1,), (1,)), ((), ())),
                    preferred_element_type=F32,
                )
        out_ref[dx] = total.astype(BF16)


def second_grad_body(ndp, part_ref, *refs):
    arrived, (w_ref, partner_w_ref), refs = (refs[:2], refs[2:4]), refs[4:6], refs[6:]
    (near_ref, far_ref), refs = refs[:2], refs[2:]
    *out_refs, held_w, held_part, sems = refs
    ncol, tokens, depth = held_part.shape
    rows = out_refs[0].shape[0]
    width = near_ref.shape[1]
    z, col = lax.axis_index("dp"), lax.axis_index("col")
    lanes = pl.ds(pl.multiple_of(wrapped(z + ndp // 2, ndp) * width, width), width)
    copies = [
        pltpu.make_async_copy(w_ref, held_w.at[0], sems.at[0]),
        pltpu.make_async_copy(partner_w_ref.at[:, :, lanes], held_w.at[1], sems.at[1]),
    ]
    copies.append(pltpu.make_async_copy(part_ref, held_part, sems.at[2]))
    for copy in copies:
        copy.start()
    for k, (pair, target) in enumerate(zip(arrived, (near_ref, far_ref))):
        for source, here in zip(pair, (z >= ndp // 2, z < ndp // 2)):

            @pl.when(here)
            def _(source=source, target=target, k=k):
                copy = pltpu.make_async_copy(source, target, sems.at[3 + k])
                copy.start()
                copy.wait()

    for copy in copies:
        copy.wait()
    left = jnp.concatenate(
        [ref[i * tokens : (i + 1) * tokens] for ref in (near_ref, far_ref) for i in range(3)], axis=1
    )
    for dx in range(ncol):
        start = pl.multiple_of(wrapped(col - dx, ncol) * depth, depth)
        right = jnp.concatenate([held_w[k, i, pl.ds(start, depth), :] for k in range(2) for i in range(3)], axis=1)
        total = held_part[dx].astype(F32) + lax.dot_general(
            left, right, (((1,), (1,)), ((), ())), preferred_element_type=F32
        )
        for block in range(tokens // rows):
            out_refs[block * ncol + dx][...] = total[block * rows : (block + 1) * rows].astype(BF16)


def weight_grad_body(scale, *refs):
    (x0_ref, x1_ref), near_refs, other_refs, mixed_refs, refs = refs[:2], refs[2:6], refs[6:9], refs[9:13], refs[13:]
    own_ref, two_ref, last_ref = other_refs
    other = (own_ref, two_ref.at[0], two_ref.at[1], last_ref)
    out_ref, mixed_ref, long_ref, short_ref, held, held_mixed = refs
    nblocks, ncol, rows, depth = x0_ref.shape
    _, ndp, _, width = held.shape
    tokens = nblocks * rows
    i = pl.program_id(0)
    z, col = lax.axis_index("dp"), lax.axis_index("col")

    @pl.when(i == 0)
    def _():
        groups = long_ref.shape[0] // ndp
        for k, ahead in enumerate((0, -1, 1, 2)):
            owner = wrapped(z + ahead, ndp)
            held[0, owner] = near_refs[k][...]
            held[1, owner, : 3 * tokens] = other[k][...]
        for back in range(ndp):
            held_mixed[wrapped(z - back, ndp)] = mixed_refs[back][...]
        for owner in range(ndp):
            lanes = slice(owner * width, (owner + 1) * width)
            mixed_ref[:, lanes] = held_mixed[owner]
            small = held[0, owner, 3 * tokens :].astype(F32)
            long_ref[owner * groups : (owner + 1) * groups] = small[:groups]
            nshort, three, _ = short_ref.shape
            for j in range(nshort):
                short_ref[j, :, lanes] = small[groups + three * j : groups + three * (j + 1)]

    at = pl.ds(pl.multiple_of(i * tokens, 16), tokens)
    gm = jnp.concatenate(
        [jnp.concatenate([held[k, owner, at, :] for owner in range(ndp)], axis=1) for k in range(2)], axis=0
    )
    for dx in range(ncol):
        start = pl.multiple_of(wrapped(col - dx, ncol) * depth, depth)
        x = jnp.concatenate(
            [x_ref[:, dx].reshape(tokens, depth) for x_ref in (x0_ref, x1_ref)], axis=0
        )
        out_ref[0, pl.ds(start, depth), :] = scale * lax.dot_general(
            x, gm, (((0,), (0,)), ((), ())), preferred_element_type=F32
        )


def delayed(values, count):
    row = lax.broadcasted_iota(jnp.int32, values.shape, 0)
    return jnp.where(row >= count, pltpu.roll(values, count, 0), 0.0)


def advanced(values, count):
    rows = values.shape[0]
    row = lax.broadcasted_iota(jnp.int32, values.shape, 0)
    return jnp.where(row < rows - count, pltpu.roll(values, rows - count, 0), 0.0)


def middle_body(scale, nshort, nrow, *refs):
    sums, refs = (refs[:3], refs[3:6]), refs[6:]
    (sf_ref, causal_ref, anti_ref), refs = refs[:3], refs[3:]
    *refs, m_ref, gm_ref, mixed_ref, go_ref = refs
    ndp = len(refs) // 2 - 1
    go_refs, (near_ref, other_ref), mixed_refs = refs[:ndp], refs[ndp : ndp + 2], refs[ndp + 2 :]
    tokens, width = go_ref.shape
    for behind, piece in enumerate(go_refs):
        at = wrapped(lax.axis_index("dp") - behind, ndp) * (tokens // ndp)
        go_ref[pl.ds(pl.multiple_of(at, 16), tokens // ndp)] = piece[...]
    row = lax.axis_index("row")
    nblocks = nrow // 2
    rows = tokens // nrow

    def places():
        for chunk, start in enumerate((row, row + 1 - 2 * lax.rem(row, 2))):
            for block in range(nblocks):
                at = tokens_of(wrapped(start - 2 * block, nrow), nrow) * rows
                for i in range(3):
                    yield chunk, (i * nblocks + block) * rows, pl.multiple_of(i * tokens + at, 16)

    for chunk, place, at in places():
        held = [ref[place : place + rows].astype(F32) for ref in sums[chunk]]
        m_ref[pl.ds(at, rows)] = held[0] + held[1] + held[2]
    groups, block, span = causal_ref.shape
    members = width // groups
    nspans = tokens // block
    lane = lax.broadcasted_iota(jnp.int32, (block, width), 1) // members
    lanes = lax.broadcasted_iota(jnp.int32, (block, 2 * width), 1) % width // members

    def past(i, j):
        held = m_ref[i * tokens : (i + 1) * tokens]
        return held if j == 0 else delayed(held, j)

    def taps(j, i):
        return sf_ref[3 * j + i : 3 * j + i + 1, :]

    feats = [sum(taps(j, i) * past(i, j) for j in range(nshort)) for i in range(3)]
    product = (feats[1] * feats[2]).astype(BF16)
    zero = jnp.zeros((block, width), BF16)
    p_blocks = [zero] + [product[b * block : (b + 1) * block] for b in range(nspans)]
    p_pairs = [jnp.concatenate(p_blocks[b : b + 2], axis=0) for b in range(nspans)]

    def filtered(band_ref, pairs):
        bands = band_ref[...].reshape(groups * block, span)
        out = []
        for b in range(0, nspans, 2):
            both = jnp.dot(bands, jnp.concatenate(pairs[b : b + 2], axis=1), preferred_element_type=F32)
            for h in range(2):
                part = both[:, h * width : (h + 1) * width]
                picked = part[:block]
                for g in range(1, groups):
                    picked = jnp.where(lane == g, part[g * block : (g + 1) * block], picked)
                out.append(picked)
        return jnp.concatenate(out, axis=0)

    conv = filtered(causal_ref, p_pairs)
    upstream = go_ref[...].astype(F32)
    mixed_ref[...] = (feats[0] * conv).astype(BF16)
    for ahead, out_ref in enumerate(mixed_refs):
        at = pl.multiple_of(wrapped(lax.axis_index("dp") + ahead, ndp) * (tokens // ndp), 16)
        out_ref[...] = mixed_ref[pl.ds(at, tokens // ndp)]
    grad_conv = (upstream * feats[0]).astype(BF16)
    c_blocks = [grad_conv[b * block : (b + 1) * block] for b in range(nspans)] + [zero]
    c_pairs = [jnp.concatenate(c_blocks[b : b + 2], axis=0) for b in range(nspans)]
    grad_product = filtered(anti_ref, c_pairs)

    corr = jnp.zeros((groups * block, span), F32)
    for b in range(0, nspans, 2):
        left = jnp.concatenate(c_blocks[b : b + 2], axis=1)
        stacked = jnp.concatenate(
            [jnp.where(lanes == g, left, jnp.zeros_like(left)) for g in range(groups)], axis=0
        )
        right = jnp.concatenate(p_pairs[b : b + 2], axis=1)
        corr += lax.dot_general(stacked, right, (((1,), (1,)), ((), ())), preferred_element_type=F32)
    turn = lax.broadcasted_iota(jnp.int32, (8, span), 0)
    sums = []
    for g in range(groups):
        part = corr[g * block : (g + 1) * block]
        count = block
        while count > 8:
            count //= 2
            part = part[:count] + pltpu.roll(part[count:], span - count, 1)
        for bit in (1, 2, 4):
            part = jnp.where((turn & bit) != 0, pltpu.roll(part, span - bit, 1), part)
        sums.append(jnp.sum(part, axis=0, keepdims=True))
    by_lag = jnp.concatenate(sums, axis=0)
    by_lag = (scale * pltpu.roll(by_lag, span - 1, 1)[:, :block]).astype(BF16)
    ahead = lax.broadcasted_iota(jnp.int32, (block, block), 0)
    back = lax.broadcasted_iota(jnp.int32, (block, block), 1)
    turned = jnp.where(ahead + back == block - 1, 1.0, 0.0).astype(BF16)
    by_lag = jnp.dot(by_lag, turned, preferred_element_type=F32)

    grad_feats = [upstream * conv, grad_product * feats[2], grad_product * feats[1]]
    short_rows = []
    for j in range(nshort):
        for i in range(3):
            short_rows.append(scale * jnp.sum(grad_feats[i] * past(i, j), axis=0, keepdims=True))
    for i in range(3):
        total = taps(0, i) * grad_feats[i]
        for j in range(1, nshort):
            total += taps(j, i) * advanced(grad_feats[i], j)
        gm_ref[i * tokens : (i + 1) * tokens] = total.astype(BF16)
    for chunk, place, at in places():
        (near_ref, other_ref)[chunk][place : place + rows] = gm_ref[pl.ds(at, rows)]
    tail = near_ref.shape[0] - 3 * tokens // 2 - groups - 3 * nshort
    small = jnp.concatenate([by_lag] + short_rows + [jnp.zeros((tail, width), F32)], axis=0)
    near_ref[3 * tokens // 2 :] = small.astype(BF16)


def sum_over_line(own, right, far, left, later):
    ndp = lax.axis_size("dp")
    from_left = lax.ppermute(far, "dp", [(a, a + 1) for a in range(ndp // 2)])
    from_right = lax.ppermute(far, "dp", [(a, a - 1) for a in range(ndp // 2, ndp)])
    from_right, later = lax.optimization_barrier((from_right, later))
    rightward = lax.ppermute(right + from_left, "dp", [(a, (a + 1) % ndp) for a in range(ndp)])
    leftward = lax.ppermute(left + from_right, "dp", [(a, (a - 1) % ndp) for a in range(ndp)])
    return [own, rightward, leftward], later


def gather_over_line(own, across):
    ndp, nrow = lax.axis_size("dp"), lax.axis_size("row")

    def shift(count):
        return [
            (a * nrow + r, (a + count) % ndp * nrow + (r + 1 - 2 * (r % 2) if across else r))
            for a in range(ndp)
            for r in range(nrow)
        ]

    before = lax.ppermute(own, ("dp", "row"), shift(1))
    after = lax.ppermute(own, ("dp", "row"), shift(-1))
    here = lax.ppermute(own, ("dp", "row"), shift(0)) if across else own
    far_before = lax.ppermute(before, "dp", [(a - 1, a) for a in range(ndp // 2, ndp)])
    far_after = lax.ppermute(after, "dp", [(a + 1, a) for a in range(ndp // 2)])
    return here, before, after, far_before, far_after


def move_activations(tokens, in_weight, short_filter, long_filter, grad_out):
    ndp, nrow, ncol = (lax.axis_size(a) for a in ("dp", "row", "col"))
    z = lax.axis_index("dp")
    rows, dcol = tokens.shape
    local = grad_out.shape[1]
    nshort = short_filter.shape[0]
    ngroups, ntaps = long_filter.shape
    seq = rows * ndp
    width, groups = local // ndp, ngroups // ndp
    drow = in_weight.shape[0]
    scale = float(seq) ** -0.5
    nblocks = nrow // 2
    chunk = nblocks * rows
    swap = [(tokens_of(b, nrow) * nrow + a, a * nrow + b) for a in range(ndp) for b in range(nrow)]
    swap_back = [(b, a) for a, b in swap]
    partner = [(a, a + 1 - 2 * (a % 2)) for a in range(nrow)]
    places = [(dy, dx) for dy in range(nblocks) for dx in range(ncol)]

    def offset(dy, dx):
        return [
            (a * ncol + b, (a + 2 * dy) % nrow * ncol + (b + dx) % ncol) for a in range(nrow) for b in range(ncol)
        ]

    w = jnp.transpose(in_weight, (1, 0, 2))
    moved = lax.ppermute(tokens, ("dp", "row"), swap)
    far_w = kernel_call(
        far_columns_body,
        shaped((3, drow, width), BF16),
        in_specs=[pl.BlockSpec(memory_space=pl.ANY)],
        out_specs=pl.BlockSpec(memory_space=pltpu.VMEM),
        scratch=[pltpu.SemaphoreType.DMA],
    )(w)
    turn = [[(a, (a + ahead) % ndp) for a in range(ndp)] for ahead in range(ndp)]
    upstream = [*kernel_call(split_body, [shaped((rows, width), BF16)] * ndp)(grad_out)]
    moved, upstream, far_w = lax.optimization_barrier((moved, upstream, far_w))
    near = [moved] + [lax.ppermute(moved, ("row", "col"), offset(*p)) for p in places[1:]]
    for ahead in (1, 3):
        upstream[ahead] = lax.ppermute(upstream[ahead], "dp", turn[ahead])
    upstream[1::2], near[1:] = lax.optimization_barrier((upstream[1::2], near[1:]))
    x0 = jnp.stack(near).reshape(nblocks, ncol, rows, dcol)
    x1 = lax.ppermute(x0, "row", partner)
    upstream[2] = lax.ppermute(upstream[2], "dp", turn[2])
    upstream[2], x1 = lax.optimization_barrier((upstream[2], x1))

    sf = lax.dynamic_slice_in_dim(short_filter, z * width, width, 2).reshape(3 * nshort, width)
    lf = lax.dynamic_slice_in_dim(long_filter, z * groups, groups, 0).astype(F32)
    zeros = functools.partial(jnp.zeros, dtype=F32)
    bases = jnp.concatenate(
        [
            jnp.concatenate([zeros((groups, 1)), lf[:, ::-1], zeros((groups, ntaps - 1))], axis=1),
            jnp.concatenate([lf, zeros((groups, ntaps))], axis=1),
        ],
        axis=0,
    )
    bands = kernel_call(bands_body, shaped((2 * groups, ntaps, 2 * ntaps), BF16))(bases)

    mm_flops = seq * drow * 3 * local
    mm_bytes = seq * drow + 6 * drow * local + 3 * seq * local
    sums, first_w = [], None
    for x in (x0, x1):
        parts = kernel_call(
            project_body,
            [shaped((3, chunk, width), BF16)] * ndp,
            grid=(3,),
            in_specs=[
                pl.BlockSpec((nblocks, ncol, rows, dcol), lambda i: (0, 0, 0, 0)),
                pl.BlockSpec((1, drow, local), lambda i: (i, 0, 0)),
            ],
            out_specs=[pl.BlockSpec((1, chunk, width), lambda i: (i, 0, 0))] * ndp,
            scratch=[pltpu.VMEM((ndp, chunk, width), BF16)],
            flops=mm_flops,
            nbytes=mm_bytes,
        )(x, w)
        three, later_w = sum_over_line(*(p.reshape(3 * chunk, width) for p in parts), w)
        sums, first_w = sums + three, later_w if x is x0 else first_w

    extra = -(-(groups + 3 * nshort) // 16) * 16
    half = pl.BlockSpec((groups, ntaps, 2 * ntaps), lambda i: (0, 0, 0))
    other = pl.BlockSpec((groups, ntaps, 2 * ntaps), lambda i: (1, 0, 0))
    whole = lambda *shape: pl.BlockSpec(shape, lambda i: (0,) * len(shape))
    grad_near, grad_other, *mixed = kernel_call(
        functools.partial(middle_body, scale, nshort, nrow),
        [shaped((3 * chunk + extra, width), BF16), shaped((3 * chunk, width), BF16)]
        + [shaped((rows, width), BF16)] * ndp,
        grid=(1,),
        in_specs=[whole(3 * chunk, width)] * 6
        + [whole(3 * nshort, width), half, other]
        + [whole(rows, width)] * ndp,
        out_specs=[whole(3 * chunk + extra, width), whole(3 * chunk, width)] + [whole(rows, width)] * ndp,
        scratch=[
            pltpu.VMEM((3 * seq, width), F32),
            pltpu.VMEM((3 * seq, width), BF16),
            pltpu.VMEM((seq, width), BF16),
            pltpu.VMEM((seq, width), BF16),
        ],
        flops=3 * 2 * groups * ntaps * 2 * ntaps * width * (seq // ntaps),
        nbytes=2 * width * seq * 14,
        vmem=MOST_VMEM_BYTES,
    )(*sums, sf, bands, bands, *upstream)
    mixed = [mixed[0]] + [
        lax.ppermute(part, "dp", [(a, (a + ahead) % ndp) for a in range(ndp)])
        for ahead, part in enumerate(mixed)
        if ahead
    ]
    *near, near_far_before, near_far_after = gather_over_line(grad_near, False)
    *far, far_far_before, far_far_after = gather_over_line(grad_other, True)
    partner_w = lax.ppermute(first_w, "row", partner)
    everywhere = pl.BlockSpec(memory_space=pl.ANY)
    in_vmem = pl.BlockSpec(memory_space=pltpu.VMEM)
    part, far_two = kernel_call(
        first_grad_body,
        [shaped((ncol, chunk, dcol), BF16), shaped((2, 3 * chunk, width), BF16)],
        in_specs=[in_vmem] * 6 + [everywhere] * 2,
        out_specs=[in_vmem] * 2,
        scratch=[
            pltpu.VMEM((2, ndp, 3 * chunk, width), BF16),
            pltpu.VMEM((2, ncol, 3, dcol, local), BF16),
            pltpu.SemaphoreType.DMA((2, ncol)),
        ],
        flops=2 * mm_flops,
        nbytes=2 * mm_bytes,
    )(*near, *far, w, partner_w)
    near_last, far_last, *blocks = kernel_call(
        functools.partial(second_grad_body, ndp),
        [shaped(grad_near.shape, BF16), shaped(grad_other.shape, BF16)]
        + [shaped((rows, dcol), BF16)] * len(places),
        grid=(),
        in_specs=[everywhere] * 7,
        out_specs=[in_vmem] * (2 + len(places)),
        scratch=[
            pltpu.VMEM((2, 3, drow, width), BF16),
            pltpu.VMEM((ncol, chunk, dcol), BF16),
            pltpu.SemaphoreType.DMA((5,)),
        ],
        flops=mm_flops // 2,
        nbytes=mm_bytes // 2,
        vmem=MOST_VMEM_BYTES,
    )(part, near_far_before, near_far_after, far_far_before, far_far_after, far_w, partner_w)
    far_two, far_last, mixed[1:] = lax.optimization_barrier((far_two, far_last, mixed[1:]))
    far_two, far_last = (lax.ppermute(part, "row", partner) for part in (far_two, far_last))
    arrivals = [
        lax.ppermute(sent, ("row", "col"), [(b, a) for a, b in offset(*p)])
        for p, sent in zip(places[1:], blocks[1:])
    ]
    arrived = sum((a.astype(F32) for a in arrivals), blocks[0].astype(F32)).astype(BF16)
    arrived, far_two, far_last = lax.optimization_barrier((arrived, far_two, far_last))
    grad_in = lax.ppermute(arrived, ("dp", "row"), swap_back)

    grad_weight, mixed, grad_long, grad_short = kernel_call(
        functools.partial(weight_grad_body, scale),
        [
            shaped((3, drow, local), F32),
            shaped((rows, local), BF16),
            shaped((ngroups, ntaps), F32),
            shaped((nshort, 3, local), F32),
        ],
        grid=(3,),
        in_specs=[whole(nblocks, ncol, rows, dcol)] * 2
        + [whole(*grad_near.shape)] * 4
        + [whole(*grad_other.shape), whole(*far_two.shape), whole(*far_last.shape)]
        + [whole(rows, width)] * ndp,
        out_specs=[
            pl.BlockSpec((1, drow, local), lambda i: (i, 0, 0)),
            whole(rows, local),
            whole(ngroups, ntaps),
            whole(nshort, 3, local),
        ],
        scratch=[
            pltpu.VMEM((2, ndp, 3 * chunk + extra, width), BF16),
            pltpu.VMEM((ndp, rows, width), BF16),
        ],
        flops=2 * mm_flops,
        nbytes=2 * mm_bytes,
        vmem=MOST_VMEM_BYTES,
    )(x0, x1, *near, near_last, grad_other, far_two, far_last, *mixed)
    grad_weight = jnp.transpose(grad_weight, (1, 0, 2))
    return (mixed, grad_in, grad_weight, grad_long, grad_short)


def from_behind(block, axis, distance):
    devices = range(lax.axis_size(axis))
    route = [(i - distance, i) for i in devices if i - distance in devices]
    return lax.ppermute(block, axis, route)


def toeplitz(leading, rows, span):
    groups = leading.shape[0]
    width = rows + span
    seed_row = jnp.concatenate(
        [leading, jnp.zeros((groups, width - leading.shape[1]), leading.dtype)], axis=1
    )
    tiled = jnp.tile(seed_row, (1, rows))
    skewed = tiled[:, : rows * (width - 1)].reshape(groups, rows, width - 1)
    return skewed[:, :, :span]


def to_groups(values, ngroups, members):
    count = values.shape[0]
    return values.reshape(count, ngroups, members).transpose(1, 2, 0)


def from_groups(values):
    groups, members, count = values.shape
    return values.transpose(2, 0, 1).reshape(count, groups * members)


def move_weights(tokens, in_weight, short_filter, long_filter, grad_out):
    rows = tokens.shape[0]
    local = grad_out.shape[1]
    nshort = short_filter.shape[0]
    ntaps = long_filter.shape[1]
    ngroups = long_filter.shape[0]
    members = local // ngroups
    margin = ntaps - 1
    span = rows + margin
    scale = float(rows * lax.axis_size("dp")) ** (-0.5)
    whole = lax.all_gather(tokens, ("row", "col"), axis=1, tiled=True)
    full_w = lax.all_gather(in_weight, "dp", axis=0, tiled=True)
    mixed_in = jnp.einsum("sd,dic->sic", whole, full_w, preferred_element_type=jnp.float32).astype(
        jnp.bfloat16
    )
    before = from_behind(mixed_in[rows - margin - nshort + 1 :], "dp", 1)
    extended = jnp.concatenate([before, mixed_in], axis=0).astype(jnp.float32)
    long_feats = jnp.zeros((span, 3, local), jnp.float32)
    for j in range(nshort):
        long_feats = (
            long_feats + short_filter[j][None] * extended[nshort - 1 - j : nshort - 1 - j + span]
        )
    product_ext = (long_feats[:, 1] * long_feats[:, 2]).astype(jnp.bfloat16)
    feats = long_feats[margin:]
    short_rows = extended[margin:]
    product_cols = to_groups(product_ext, ngroups, members)
    causal = toeplitz(long_filter[:, ::-1], rows, span)
    conv = from_groups(
        jnp.einsum("gst,gct->gcs", causal, product_cols, preferred_element_type=jnp.float32)
    )
    mixed = (feats[:, 0] * conv).astype(jnp.bfloat16)
    upstream = grad_out.astype(jnp.float32)
    grad_query = upstream * conv
    grad_conv = (upstream * feats[:, 0]).astype(jnp.bfloat16)
    after = from_behind(grad_conv[:margin], "dp", -1)
    grad_ext = jnp.concatenate([grad_conv, after], axis=0)
    anti = toeplitz(long_filter, rows, span)
    grad_product = from_groups(
        jnp.einsum(
            "gst,gct->gcs",
            anti,
            to_groups(grad_ext, ngroups, members),
            preferred_element_type=jnp.float32,
        )
    )
    reversed_cols = jnp.concatenate(
        [product_cols[:, :, ::-1], jnp.zeros((ngroups, members, rows), product_cols.dtype)], axis=2
    )
    width = span + rows
    pairs = jnp.einsum(
        "gcs,gcu->gsu",
        to_groups(grad_conv, ngroups, members),
        reversed_cols,
        preferred_element_type=jnp.float32,
    )
    diagonal = pairs.reshape(ngroups, rows * width)[:, : rows * (width - 1)].reshape(
        ngroups, rows, width - 1
    )
    filter_part = jnp.sum(diagonal[:, :, rows - 1 : rows - 1 + ntaps], axis=1)
    grad_feats = jnp.stack(
        [grad_query, grad_product * feats[:, 2], grad_product * feats[:, 1]], axis=1
    )
    later = from_behind(grad_feats[: nshort - 1], "dp", -1)
    feats_ext = jnp.concatenate([grad_feats, later], axis=0)
    grad_acc = jnp.zeros((rows, 3, local), jnp.float32)
    for j in range(nshort):
        grad_acc = grad_acc + short_filter[j][None] * feats_ext[j : j + rows]
    grad_mixed = grad_acc.astype(jnp.bfloat16)
    short_part = jnp.stack(
        [
            jnp.sum(grad_feats * short_rows[nshort - 1 - j : nshort - 1 - j + rows], axis=0)
            for j in range(nshort)
        ]
    )
    filter_total, short_total = (
        lax.psum(filter_part.astype(jnp.bfloat16), "dp").astype(jnp.float32),
        lax.psum(short_part.astype(jnp.bfloat16), "dp").astype(jnp.float32),
    )
    grad_long = filter_total * scale
    grad_short = short_total * scale
    partial_in = jnp.einsum("sic,dic->sd", grad_mixed, full_w, preferred_element_type=jnp.float32)
    summed_in = lax.psum_scatter(
        partial_in.astype(jnp.bfloat16), ("row", "col"), scatter_dimension=1, tiled=True
    )
    weight_term = (
        jnp.einsum("sd,sic->dic", whole, grad_mixed, preferred_element_type=jnp.float32) * scale
    )
    grad_weight = lax.psum_scatter(
        weight_term.astype(jnp.bfloat16), "dp", scatter_dimension=0, tiled=True
    ).astype(jnp.float32)
    return (mixed, summed_in, grad_weight, grad_long, grad_short)


def fits_whole_sequences(mesh, tokens, in_weight, short_filter, long_filter, grad_out):
    ndp, nrow, ncol = (mesh.shape[a] for a in ("dp", "row", "col"))
    seq, channels = grad_out.shape
    groups, ntaps = long_filter.shape
    local = channels // (nrow * ncol)
    width, rows = local // ndp, seq // ndp
    return (
        seq < tokens.shape[1]
        and ndp == nrow == 4
        and ncol * (tokens.shape[1] // (nrow * ncol)) == in_weight.shape[0] // ndp
        and ntaps == width == 128
        and seq % (2 * ntaps) == 0
        and rows % 16 == 0
        and groups % (8 * ndp * nrow * ncol) == 0
    )


def solution(mesh):
    placed = (
        P("dp", ("row", "col")),
        P("dp", None, ("row", "col")),
        P(None, None, ("row", "col")),
        P(("row", "col"), None),
        P("dp", ("row", "col")),
    )
    gives = (
        P("dp", ("row", "col")),
        P("dp", ("row", "col")),
        P("dp", None, ("row", "col")),
        P(("row", "col"), None),
        P(None, None, ("row", "col")),
    )

    def run(*arrays):
        plan = move_activations if fits_whole_sequences(mesh, *arrays) else move_weights
        return jax.shard_map(
            plan, mesh=mesh, in_specs=placed, out_specs=gives, check_vma=False
        )(*arrays)

    return run
```

```python
import functools

import jax
import jax.numpy as jnp
from jax import lax
from jax.experimental import pallas as pl
from jax.experimental.pallas import tpu as pltpu
from jax.sharding import PartitionSpec as P

VMEM_BYTES = 48 * 2**20
MOST_VMEM_BYTES = 62 * 2**20
F32 = jnp.float32
BF16 = jnp.bfloat16


def kernel_call(body, outs, grid=(), in_specs=None, out_specs=None, scratch=(), flops=0, nbytes=0, vmem=VMEM_BYTES):
    kwargs = {}
    if in_specs is not None:
        kwargs = dict(grid=grid, in_specs=in_specs, out_specs=out_specs)
    return pl.pallas_call(
        body,
        out_shape=outs,
        scratch_shapes=scratch,
        compiler_params=pltpu.CompilerParams(vmem_limit_bytes=vmem),
        cost_estimate=pl.CostEstimate(flops=flops, bytes_accessed=nbytes, transcendentals=0),
        **kwargs,
    )


def shaped(shape, dtype):
    return jax.ShapeDtypeStruct(shape, dtype)


def bands_body(base_ref, out_ref):
    groups, wide = base_ref.shape
    rows = out_ref.shape[1]
    row = lax.broadcasted_iota(jnp.int32, (8, wide), 0)
    for g in range(groups):
        band = jnp.broadcast_to(base_ref[g : g + 1, :], (8, wide))
        for bit in (1, 2, 4):
            band = jnp.where((row & bit) != 0, pltpu.roll(band, bit, 1), band)
        count = 8
        while count < rows:
            band = jnp.concatenate([band, pltpu.roll(band, count, 1)], axis=0)
            count *= 2
        out_ref[g] = band.astype(out_ref.dtype)


def tokens_of(row, nrow):
    return row % 2 * (nrow // 2) + row // 2


def wrapped(value, size):
    return lax.rem(value + 2 * size, size)


def split_body(all_ref, *out_refs):
    width = out_refs[0].shape[1]
    for ahead, out_ref in enumerate(out_refs):
        at = wrapped(lax.axis_index("dp") + ahead, len(out_refs)) * width
        out_ref[...] = all_ref[:, pl.ds(pl.multiple_of(at, width), width)]


def project_body(x_ref, w_ref, *refs):
    *out_refs, held = refs
    z, col = lax.axis_index("dp"), lax.axis_index("col")
    nblocks, ncol, rows, depth = x_ref.shape
    width = held.shape[2]
    total = jnp.zeros((nblocks * rows, w_ref.shape[2]), F32)
    for dx in range(ncol):
        start = pl.multiple_of(wrapped(col - dx, ncol) * depth, depth)
        total += jnp.dot(
            x_ref[:, dx].reshape(nblocks * rows, depth),
            w_ref[0, pl.ds(start, depth), :],
            preferred_element_type=F32,
        )
    for owner in range(len(out_refs)):
        held[owner] = total[:, owner * width : (owner + 1) * width].astype(BF16)
    for ahead, out_ref in enumerate(out_refs):
        out_ref[0] = held[wrapped(z + ahead, len(out_refs))]


def far_columns_body(w_ref, out_ref, sem):
    ndp = lax.axis_size("dp")
    width = out_ref.shape[2]
    start = wrapped(lax.axis_index("dp") + ndp // 2, ndp) * width
    copy = pltpu.make_async_copy(w_ref.at[:, :, pl.ds(pl.multiple_of(start, width), width)], out_ref, sem)
    copy.start()
    copy.wait()


def first_grad_body(
    near, near_before, near_after, far, far_before, far_after, w_ref, partner_w_ref, out_ref, far_ref, held, held_w, sems
):
    _, ndp, _, width = held.shape
    ncol, tokens, depth = out_ref.shape
    z, col = lax.axis_index("dp"), lax.axis_index("col")
    copies = []
    for dx in range(ncol):
        start = pl.multiple_of(wrapped(col - dx, ncol) * depth, depth)
        for k, weights in enumerate((w_ref, partner_w_ref)):
            copy = pltpu.make_async_copy(weights.at[:, pl.ds(start, depth)], held_w.at[k, dx], sems.at[k, dx])
            copy.start()
            copies.append(copy)
    far_ref[0], far_ref[1] = far_before[...], far_after[...]
    for k, pieces in enumerate(((near, near_before, near_after), (far, far_before, far_after))):
        held[k, wrapped(z + ndp // 2, ndp)] = jnp.zeros(held.shape[2:], BF16)
        for ahead, piece in zip((0, -1, 1), pieces):
            held[k, wrapped(z + ahead, ndp)] = piece[: 3 * tokens]
    for dx in range(ncol):
        total = jnp.zeros((tokens, depth), F32)
        for k in range(2):
            copies[2 * dx + k].wait()
            for i in range(3):
                rows = slice(i * tokens, (i + 1) * tokens)
                total += lax.dot_general(
                    jnp.concatenate([held[k, owner, rows] for owner in range(ndp)], axis=1),
                    held_w[k, dx, i],
                    (((1,), (1,)), ((), ())),
                    preferred_element_type=F32,
                )
        out_ref[dx] = total.astype(BF16)


def second_grad_body(ndp, part_ref, *refs):
    arrived, (w_ref, partner_w_ref), refs = (refs[:2], refs[2:4]), refs[4:6], refs[6:]
    (near_ref, far_ref), refs = refs[:2], refs[2:]
    *out_refs, held_w, held_part, sems = refs
    ncol, tokens, depth = held_part.shape
    rows = out_refs[0].shape[0]
    width = near_ref.shape[1]
    z, col = lax.axis_index("dp"), lax.axis_index("col")
    lanes = pl.ds(pl.multiple_of(wrapped(z + ndp // 2, ndp) * width, width), width)
    copies = [
        pltpu.make_async_copy(w_ref, held_w.at[0], sems.at[0]),
        pltpu.make_async_copy(partner_w_ref.at[:, :, lanes], held_w.at[1], sems.at[1]),
    ]
    copies.append(pltpu.make_async_copy(part_ref, held_part, sems.at[2]))
    for copy in copies:
        copy.start()
    for k, (pair, target) in enumerate(zip(arrived, (near_ref, far_ref))):
        for source, here in zip(pair, (z >= ndp // 2, z < ndp // 2)):

            @pl.when(here)
            def _(source=source, target=target, k=k):
                copy = pltpu.make_async_copy(source, target, sems.at[3 + k])
                copy.start()
                copy.wait()

    for copy in copies:
        copy.wait()
    left = jnp.concatenate(
        [ref[i * tokens : (i + 1) * tokens] for ref in (near_ref, far_ref) for i in range(3)], axis=1
    )
    for dx in range(ncol):
        start = pl.multiple_of(wrapped(col - dx, ncol) * depth, depth)
        right = jnp.concatenate([held_w[k, i, pl.ds(start, depth), :] for k in range(2) for i in range(3)], axis=1)
        total = held_part[dx].astype(F32) + lax.dot_general(
            left, right, (((1,), (1,)), ((), ())), preferred_element_type=F32
        )
        for block in range(tokens // rows):
            out_refs[block * ncol + dx][...] = total[block * rows : (block + 1) * rows].astype(BF16)


def weight_grad_body(scale, *refs):
    (x0_ref, x1_ref), near_refs, other_refs, mixed_refs, refs = refs[:2], refs[2:6], refs[6:9], refs[9:13], refs[13:]
    own_ref, two_ref, last_ref = other_refs
    other = (own_ref, two_ref.at[0], two_ref.at[1], last_ref)
    out_ref, mixed_ref, long_ref, short_ref, held, held_mixed = refs
    nblocks, ncol, rows, depth = x0_ref.shape
    _, ndp, _, width = held.shape
    tokens = nblocks * rows
    i = pl.program_id(0)
    z, col = lax.axis_index("dp"), lax.axis_index("col")

    @pl.when(i == 0)
    def _():
        groups = long_ref.shape[0] // ndp
        for k, ahead in enumerate((0, -1, 1, 2)):
            owner = wrapped(z + ahead, ndp)
            held[0, owner] = near_refs[k][...]
            held[1, owner, : 3 * tokens] = other[k][...]
        for back in range(ndp):
            held_mixed[wrapped(z - back, ndp)] = mixed_refs[back][...]
        for owner in range(ndp):
            lanes = slice(owner * width, (owner + 1) * width)
            mixed_ref[:, lanes] = held_mixed[owner]
            small = held[0, owner, 3 * tokens :].astype(F32)
            long_ref[owner * groups : (owner + 1) * groups] = small[:groups]
            nshort, three, _ = short_ref.shape
            for j in range(nshort):
                short_ref[j, :, lanes] = small[groups + three * j : groups + three * (j + 1)]

    at = pl.ds(pl.multiple_of(i * tokens, 16), tokens)
    gm = jnp.concatenate(
        [jnp.concatenate([held[k, owner, at, :] for owner in range(ndp)], axis=1) for k in range(2)], axis=0
    )
    for dx in range(ncol):
        start = pl.multiple_of(wrapped(col - dx, ncol) * depth, depth)
        x = jnp.concatenate(
            [x_ref[:, dx].reshape(tokens, depth) for x_ref in (x0_ref, x1_ref)], axis=0
        )
        out_ref[0, pl.ds(start, depth), :] = scale * lax.dot_general(
            x, gm, (((0,), (0,)), ((), ())), preferred_element_type=F32
        )


def delayed(values, count):
    row = lax.broadcasted_iota(jnp.int32, values.shape, 0)
    return jnp.where(row >= count, pltpu.roll(values, count, 0), 0.0)


def advanced(values, count):
    rows = values.shape[0]
    row = lax.broadcasted_iota(jnp.int32, values.shape, 0)
    return jnp.where(row < rows - count, pltpu.roll(values, rows - count, 0), 0.0)


def middle_body(scale, nshort, nrow, *refs):
    sums, refs = (refs[:3], refs[3:6]), refs[6:]
    (sf_ref, causal_ref, anti_ref), refs = refs[:3], refs[3:]
    *refs, m_ref, gm_ref, mixed_ref, go_ref = refs
    ndp = len(refs) // 2 - 1
    go_refs, (near_ref, other_ref), mixed_refs = refs[:ndp], refs[ndp : ndp + 2], refs[ndp + 2 :]
    tokens, width = go_ref.shape
    for behind, piece in enumerate(go_refs):
        at = wrapped(lax.axis_index("dp") - behind, ndp) * (tokens // ndp)
        go_ref[pl.ds(pl.multiple_of(at, 16), tokens // ndp)] = piece[...]
    row = lax.axis_index("row")
    nblocks = nrow // 2
    rows = tokens // nrow

    def places():
        for chunk, start in enumerate((row, row + 1 - 2 * lax.rem(row, 2))):
            for block in range(nblocks):
                at = tokens_of(wrapped(start - 2 * block, nrow), nrow) * rows
                for i in range(3):
                    yield chunk, (i * nblocks + block) * rows, pl.multiple_of(i * tokens + at, 16)

    for chunk, place, at in places():
        held = [ref[place : place + rows].astype(F32) for ref in sums[chunk]]
        m_ref[pl.ds(at, rows)] = held[0] + held[1] + held[2]
    groups, block, span = causal_ref.shape
    members = width // groups
    nspans = tokens // block
    lane = lax.broadcasted_iota(jnp.int32, (block, width), 1) // members
    lanes = lax.broadcasted_iota(jnp.int32, (block, 2 * width), 1) % width // members

    def past(i, j):
        held = m_ref[i * tokens : (i + 1) * tokens]
        return held if j == 0 else delayed(held, j)

    def taps(j, i):
        return sf_ref[3 * j + i : 3 * j + i + 1, :]

    feats = [sum(taps(j, i) * past(i, j) for j in range(nshort)) for i in range(3)]
    product = (feats[1] * feats[2]).astype(BF16)
    zero = jnp.zeros((block, width), BF16)
    p_blocks = [zero] + [product[b * block : (b + 1) * block] for b in range(nspans)]
    p_pairs = [jnp.concatenate(p_blocks[b : b + 2], axis=0) for b in range(nspans)]

    def filtered(band_ref, pairs):
        bands = band_ref[...].reshape(groups * block, span)
        out = []
        for b in range(0, nspans, 2):
            both = jnp.dot(bands, jnp.concatenate(pairs[b : b + 2], axis=1), preferred_element_type=F32)
            for h in range(2):
                part = both[:, h * width : (h + 1) * width]
                picked = part[:block]
                for g in range(1, groups):
                    picked = jnp.where(lane == g, part[g * block : (g + 1) * block], picked)
                out.append(picked)
        return jnp.concatenate(out, axis=0)

    conv = filtered(causal_ref, p_pairs)
    upstream = go_ref[...].astype(F32)
    mixed_ref[...] = (feats[0] * conv).astype(BF16)
    for ahead, out_ref in enumerate(mixed_refs):
        at = pl.multiple_of(wrapped(lax.axis_index("dp") + ahead, ndp) * (tokens // ndp), 16)
        out_ref[...] = mixed_ref[pl.ds(at, tokens // ndp)]
    grad_conv = (upstream * feats[0]).astype(BF16)
    c_blocks = [grad_conv[b * block : (b + 1) * block] for b in range(nspans)] + [zero]
    c_pairs = [jnp.concatenate(c_blocks[b : b + 2], axis=0) for b in range(nspans)]
    grad_product = filtered(anti_ref, c_pairs)

    corr = jnp.zeros((groups * block, span), F32)
    for b in range(0, nspans, 2):
        left = jnp.concatenate(c_blocks[b : b + 2], axis=1)
        stacked = jnp.concatenate(
            [jnp.where(lanes == g, left, jnp.zeros_like(left)) for g in range(groups)], axis=0
        )
        right = jnp.concatenate(p_pairs[b : b + 2], axis=1)
        corr += lax.dot_general(stacked, right, (((1,), (1,)), ((), ())), preferred_element_type=F32)
    turn = lax.broadcasted_iota(jnp.int32, (8, span), 0)
    sums = []
    for g in range(groups):
        part = corr[g * block : (g + 1) * block]
        count = block
        while count > 8:
            count //= 2
            part = part[:count] + pltpu.roll(part[count:], span - count, 1)
        for bit in (1, 2, 4):
            part = jnp.where((turn & bit) != 0, pltpu.roll(part, span - bit, 1), part)
        sums.append(jnp.sum(part, axis=0, keepdims=True))
    by_lag = jnp.concatenate(sums, axis=0)
    by_lag = (scale * pltpu.roll(by_lag, span - 1, 1)[:, :block]).astype(BF16)
    ahead = lax.broadcasted_iota(jnp.int32, (block, block), 0)
    back = lax.broadcasted_iota(jnp.int32, (block, block), 1)
    turned = jnp.where(ahead + back == block - 1, 1.0, 0.0).astype(BF16)
    by_lag = jnp.dot(by_lag, turned, preferred_element_type=F32)

    grad_feats = [upstream * conv, grad_product * feats[2], grad_product * feats[1]]
    short_rows = []
    for j in range(nshort):
        for i in range(3):
            short_rows.append(scale * jnp.sum(grad_feats[i] * past(i, j), axis=0, keepdims=True))
    for i in range(3):
        total = taps(0, i) * grad_feats[i]
        for j in range(1, nshort):
            total += taps(j, i) * advanced(grad_feats[i], j)
        gm_ref[i * tokens : (i + 1) * tokens] = total.astype(BF16)
    for chunk, place, at in places():
        (near_ref, other_ref)[chunk][place : place + rows] = gm_ref[pl.ds(at, rows)]
    tail = near_ref.shape[0] - 3 * tokens // 2 - groups - 3 * nshort
    small = jnp.concatenate([by_lag] + short_rows + [jnp.zeros((tail, width), F32)], axis=0)
    near_ref[3 * tokens // 2 :] = small.astype(BF16)


def sum_over_line(own, right, far, left):
    ndp = lax.axis_size("dp")
    from_left = lax.ppermute(far, "dp", [(a, a + 1) for a in range(ndp // 2)])
    from_right = lax.ppermute(far, "dp", [(a, a - 1) for a in range(ndp // 2, ndp)])
    rightward = lax.ppermute(right + from_left, "dp", [(a, (a + 1) % ndp) for a in range(ndp)])
    leftward = lax.ppermute(left + from_right, "dp", [(a, (a - 1) % ndp) for a in range(ndp)])
    return own, rightward, leftward


def gather_over_line(own, across):
    ndp, nrow = lax.axis_size("dp"), lax.axis_size("row")

    def shift(count):
        return [
            (a * nrow + r, (a + count) % ndp * nrow + (r + 1 - 2 * (r % 2) if across else r))
            for a in range(ndp)
            for r in range(nrow)
        ]

    before = lax.ppermute(own, ("dp", "row"), shift(1))
    after = lax.ppermute(own, ("dp", "row"), shift(-1))
    here = lax.ppermute(own, ("dp", "row"), shift(0)) if across else own
    far_before = lax.ppermute(before, "dp", [(a - 1, a) for a in range(ndp // 2, ndp)])
    far_after = lax.ppermute(after, "dp", [(a + 1, a) for a in range(ndp // 2)])
    return here, before, after, far_before, far_after


def move_activations(tokens, in_weight, short_filter, long_filter, grad_out):
    ndp, nrow, ncol = (lax.axis_size(a) for a in ("dp", "row", "col"))
    z = lax.axis_index("dp")
    rows, dcol = tokens.shape
    local = grad_out.shape[1]
    nshort = short_filter.shape[0]
    ngroups, ntaps = long_filter.shape
    seq = rows * ndp
    width, groups = local // ndp, ngroups // ndp
    drow = in_weight.shape[0]
    scale = float(seq) ** -0.5
    nblocks = nrow // 2
    chunk = nblocks * rows
    swap = [(tokens_of(b, nrow) * nrow + a, a * nrow + b) for a in range(ndp) for b in range(nrow)]
    swap_back = [(b, a) for a, b in swap]
    partner = [(a, a + 1 - 2 * (a % 2)) for a in range(nrow)]
    places = [(dy, dx) for dy in range(nblocks) for dx in range(ncol)]

    def offset(dy, dx):
        return [
            (a * ncol + b, (a + 2 * dy) % nrow * ncol + (b + dx) % ncol) for a in range(nrow) for b in range(ncol)
        ]

    w = jnp.transpose(in_weight, (1, 0, 2))
    moved = lax.ppermute(tokens, ("dp", "row"), swap)
    far_w = kernel_call(
        far_columns_body,
        shaped((3, drow, width), BF16),
        in_specs=[pl.BlockSpec(memory_space=pl.ANY)],
        out_specs=pl.BlockSpec(memory_space=pltpu.VMEM),
        scratch=[pltpu.SemaphoreType.DMA],
    )(w)
    turn = [[(a, (a + ahead) % ndp) for a in range(ndp)] for ahead in range(ndp)]
    upstream = [*kernel_call(split_body, [shaped((rows, width), BF16)] * ndp)(grad_out)]
    moved, upstream, far_w = lax.optimization_barrier((moved, upstream, far_w))
    near = [moved] + [lax.ppermute(moved, ("row", "col"), offset(*p)) for p in places[1:]]
    for ahead in (1, 3):
        upstream[ahead] = lax.ppermute(upstream[ahead], "dp", turn[ahead])
    upstream[1::2], near[1:] = lax.optimization_barrier((upstream[1::2], near[1:]))
    x0 = jnp.stack(near).reshape(nblocks, ncol, rows, dcol)
    x1 = lax.ppermute(x0, "row", partner)
    upstream[2] = lax.ppermute(upstream[2], "dp", turn[2])
    upstream[2], x1 = lax.optimization_barrier((upstream[2], x1))

    sf = lax.dynamic_slice_in_dim(short_filter, z * width, width, 2).reshape(3 * nshort, width)
    lf = lax.dynamic_slice_in_dim(long_filter, z * groups, groups, 0).astype(F32)
    zeros = functools.partial(jnp.zeros, dtype=F32)
    bases = jnp.concatenate(
        [
            jnp.concatenate([zeros((groups, 1)), lf[:, ::-1], zeros((groups, ntaps - 1))], axis=1),
            jnp.concatenate([lf, zeros((groups, ntaps))], axis=1),
        ],
        axis=0,
    )
    bands = kernel_call(bands_body, shaped((2 * groups, ntaps, 2 * ntaps), BF16))(bases)

    mm_flops = seq * drow * 3 * local
    mm_bytes = seq * drow + 6 * drow * local + 3 * seq * local
    sums = []
    for x in (x0, x1):
        parts = kernel_call(
            project_body,
            [shaped((3, chunk, width), BF16)] * ndp,
            grid=(3,),
            in_specs=[
                pl.BlockSpec((nblocks, ncol, rows, dcol), lambda i: (0, 0, 0, 0)),
                pl.BlockSpec((1, drow, local), lambda i: (i, 0, 0)),
            ],
            out_specs=[pl.BlockSpec((1, chunk, width), lambda i: (i, 0, 0))] * ndp,
            scratch=[pltpu.VMEM((ndp, chunk, width), BF16)],
            flops=mm_flops,
            nbytes=mm_bytes,
        )(x, w)
        sums += sum_over_line(*(p.reshape(3 * chunk, width) for p in parts))

    extra = -(-(groups + 3 * nshort) // 16) * 16
    half = pl.BlockSpec((groups, ntaps, 2 * ntaps), lambda i: (0, 0, 0))
    other = pl.BlockSpec((groups, ntaps, 2 * ntaps), lambda i: (1, 0, 0))
    whole = lambda *shape: pl.BlockSpec(shape, lambda i: (0,) * len(shape))
    grad_near, grad_other, *mixed = kernel_call(
        functools.partial(middle_body, scale, nshort, nrow),
        [shaped((3 * chunk + extra, width), BF16), shaped((3 * chunk, width), BF16)]
        + [shaped((rows, width), BF16)] * ndp,
        grid=(1,),
        in_specs=[whole(3 * chunk, width)] * 6
        + [whole(3 * nshort, width), half, other]
        + [whole(rows, width)] * ndp,
        out_specs=[whole(3 * chunk + extra, width), whole(3 * chunk, width)] + [whole(rows, width)] * ndp,
        scratch=[
            pltpu.VMEM((3 * seq, width), F32),
            pltpu.VMEM((3 * seq, width), BF16),
            pltpu.VMEM((seq, width), BF16),
            pltpu.VMEM((seq, width), BF16),
        ],
        flops=3 * 2 * groups * ntaps * 2 * ntaps * width * (seq // ntaps),
        nbytes=2 * width * seq * 14,
        vmem=MOST_VMEM_BYTES,
    )(*sums, sf, bands, bands, *upstream)
    mixed = [mixed[0]] + [
        lax.ppermute(part, "dp", [(a, (a + ahead) % ndp) for a in range(ndp)])
        for ahead, part in enumerate(mixed)
        if ahead
    ]
    *near, near_far_before, near_far_after = gather_over_line(grad_near, False)
    *far, far_far_before, far_far_after = gather_over_line(grad_other, True)
    partner_w = lax.ppermute(w, "row", partner)
    everywhere = pl.BlockSpec(memory_space=pl.ANY)
    in_vmem = pl.BlockSpec(memory_space=pltpu.VMEM)
    part, far_two = kernel_call(
        first_grad_body,
        [shaped((ncol, chunk, dcol), BF16), shaped((2, 3 * chunk, width), BF16)],
        in_specs=[in_vmem] * 6 + [everywhere] * 2,
        out_specs=[in_vmem] * 2,
        scratch=[
            pltpu.VMEM((2, ndp, 3 * chunk, width), BF16),
            pltpu.VMEM((2, ncol, 3, dcol, local), BF16),
            pltpu.SemaphoreType.DMA((2, ncol)),
        ],
        flops=2 * mm_flops,
        nbytes=2 * mm_bytes,
        vmem=MOST_VMEM_BYTES,
    )(*near, *far, w, partner_w)
    near_last, far_last, *blocks = kernel_call(
        functools.partial(second_grad_body, ndp),
        [shaped(grad_near.shape, BF16), shaped(grad_other.shape, BF16)]
        + [shaped((rows, dcol), BF16)] * len(places),
        grid=(),
        in_specs=[everywhere] * 7,
        out_specs=[in_vmem] * (2 + len(places)),
        scratch=[
            pltpu.VMEM((2, 3, drow, width), BF16),
            pltpu.VMEM((ncol, chunk, dcol), BF16),
            pltpu.SemaphoreType.DMA((5,)),
        ],
        flops=mm_flops // 2,
        nbytes=mm_bytes // 2,
        vmem=MOST_VMEM_BYTES,
    )(part, near_far_before, near_far_after, far_far_before, far_far_after, far_w, partner_w)
    far_two, far_last, mixed[1:] = lax.optimization_barrier((far_two, far_last, mixed[1:]))
    far_two, far_last = (lax.ppermute(part, "row", partner) for part in (far_two, far_last))
    arrivals = [
        lax.ppermute(sent, ("row", "col"), [(b, a) for a, b in offset(*p)])
        for p, sent in zip(places[1:], blocks[1:])
    ]
    arrived = sum((a.astype(F32) for a in arrivals), blocks[0].astype(F32)).astype(BF16)
    arrived, far_two, far_last = lax.optimization_barrier((arrived, far_two, far_last))
    grad_in = lax.ppermute(arrived, ("dp", "row"), swap_back)

    grad_weight, mixed, grad_long, grad_short = kernel_call(
        functools.partial(weight_grad_body, scale),
        [
            shaped((3, drow, local), F32),
            shaped((rows, local), BF16),
            shaped((ngroups, ntaps), F32),
            shaped((nshort, 3, local), F32),
        ],
        grid=(3,),
        in_specs=[whole(nblocks, ncol, rows, dcol)] * 2
        + [whole(*grad_near.shape)] * 4
        + [whole(*grad_other.shape), whole(*far_two.shape), whole(*far_last.shape)]
        + [whole(rows, width)] * ndp,
        out_specs=[
            pl.BlockSpec((1, drow, local), lambda i: (i, 0, 0)),
            whole(rows, local),
            whole(ngroups, ntaps),
            whole(nshort, 3, local),
        ],
        scratch=[
            pltpu.VMEM((2, ndp, 3 * chunk + extra, width), BF16),
            pltpu.VMEM((ndp, rows, width), BF16),
        ],
        flops=2 * mm_flops,
        nbytes=2 * mm_bytes,
        vmem=MOST_VMEM_BYTES,
    )(x0, x1, *near, near_last, grad_other, far_two, far_last, *mixed)
    grad_weight = jnp.transpose(grad_weight, (1, 0, 2))
    return (mixed, grad_in, grad_weight, grad_long, grad_short)


def from_behind(block, axis, distance):
    devices = range(lax.axis_size(axis))
    route = [(i - distance, i) for i in devices if i - distance in devices]
    return lax.ppermute(block, axis, route)


def toeplitz(leading, rows, span):
    groups = leading.shape[0]
    width = rows + span
    seed_row = jnp.concatenate(
        [leading, jnp.zeros((groups, width - leading.shape[1]), leading.dtype)], axis=1
    )
    tiled = jnp.tile(seed_row, (1, rows))
    skewed = tiled[:, : rows * (width - 1)].reshape(groups, rows, width - 1)
    return skewed[:, :, :span]


def to_groups(values, ngroups, members):
    count = values.shape[0]
    return values.reshape(count, ngroups, members).transpose(1, 2, 0)


def from_groups(values):
    groups, members, count = values.shape
    return values.transpose(2, 0, 1).reshape(count, groups * members)


def move_weights(tokens, in_weight, short_filter, long_filter, grad_out):
    rows = tokens.shape[0]
    local = grad_out.shape[1]
    nshort = short_filter.shape[0]
    ntaps = long_filter.shape[1]
    ngroups = long_filter.shape[0]
    members = local // ngroups
    margin = ntaps - 1
    span = rows + margin
    scale = float(rows * lax.axis_size("dp")) ** (-0.5)
    whole = lax.all_gather(tokens, ("row", "col"), axis=1, tiled=True)
    full_w = lax.all_gather(in_weight, "dp", axis=0, tiled=True)
    mixed_in = jnp.einsum("sd,dic->sic", whole, full_w, preferred_element_type=jnp.float32).astype(
        jnp.bfloat16
    )
    before = from_behind(mixed_in[rows - margin - nshort + 1 :], "dp", 1)
    extended = jnp.concatenate([before, mixed_in], axis=0).astype(jnp.float32)
    long_feats = jnp.zeros((span, 3, local), jnp.float32)
    for j in range(nshort):
        long_feats = (
            long_feats + short_filter[j][None] * extended[nshort - 1 - j : nshort - 1 - j + span]
        )
    product_ext = (long_feats[:, 1] * long_feats[:, 2]).astype(jnp.bfloat16)
    feats = long_feats[margin:]
    short_rows = extended[margin:]
    product_cols = to_groups(product_ext, ngroups, members)
    causal = toeplitz(long_filter[:, ::-1], rows, span)
    conv = from_groups(
        jnp.einsum("gst,gct->gcs", causal, product_cols, preferred_element_type=jnp.float32)
    )
    mixed = (feats[:, 0] * conv).astype(jnp.bfloat16)
    upstream = grad_out.astype(jnp.float32)
    grad_query = upstream * conv
    grad_conv = (upstream * feats[:, 0]).astype(jnp.bfloat16)
    after = from_behind(grad_conv[:margin], "dp", -1)
    grad_ext = jnp.concatenate([grad_conv, after], axis=0)
    anti = toeplitz(long_filter, rows, span)
    grad_product = from_groups(
        jnp.einsum(
            "gst,gct->gcs",
            anti,
            to_groups(grad_ext, ngroups, members),
            preferred_element_type=jnp.float32,
        )
    )
    reversed_cols = jnp.concatenate(
        [product_cols[:, :, ::-1], jnp.zeros((ngroups, members, rows), product_cols.dtype)], axis=2
    )
    width = span + rows
    pairs = jnp.einsum(
        "gcs,gcu->gsu",
        to_groups(grad_conv, ngroups, members),
        reversed_cols,
        preferred_element_type=jnp.float32,
    )
    diagonal = pairs.reshape(ngroups, rows * width)[:, : rows * (width - 1)].reshape(
        ngroups, rows, width - 1
    )
    filter_part = jnp.sum(diagonal[:, :, rows - 1 : rows - 1 + ntaps], axis=1)
    grad_feats = jnp.stack(
        [grad_query, grad_product * feats[:, 2], grad_product * feats[:, 1]], axis=1
    )
    later = from_behind(grad_feats[: nshort - 1], "dp", -1)
    feats_ext = jnp.concatenate([grad_feats, later], axis=0)
    grad_acc = jnp.zeros((rows, 3, local), jnp.float32)
    for j in range(nshort):
        grad_acc = grad_acc + short_filter[j][None] * feats_ext[j : j + rows]
    grad_mixed = grad_acc.astype(jnp.bfloat16)
    short_part = jnp.stack(
        [
            jnp.sum(grad_feats * short_rows[nshort - 1 - j : nshort - 1 - j + rows], axis=0)
            for j in range(nshort)
        ]
    )
    filter_total, short_total = (
        lax.psum(filter_part.astype(jnp.bfloat16), "dp").astype(jnp.float32),
        lax.psum(short_part.astype(jnp.bfloat16), "dp").astype(jnp.float32),
    )
    grad_long = filter_total * scale
    grad_short = short_total * scale
    partial_in = jnp.einsum("sic,dic->sd", grad_mixed, full_w, preferred_element_type=jnp.float32)
    summed_in = lax.psum_scatter(
        partial_in.astype(jnp.bfloat16), ("row", "col"), scatter_dimension=1, tiled=True
    )
    weight_term = (
        jnp.einsum("sd,sic->dic", whole, grad_mixed, preferred_element_type=jnp.float32) * scale
    )
    grad_weight = lax.psum_scatter(
        weight_term.astype(jnp.bfloat16), "dp", scatter_dimension=0, tiled=True
    ).astype(jnp.float32)
    return (mixed, summed_in, grad_weight, grad_long, grad_short)


def fits_whole_sequences(mesh, tokens, in_weight, short_filter, long_filter, grad_out):
    ndp, nrow, ncol = (mesh.shape[a] for a in ("dp", "row", "col"))
    seq, channels = grad_out.shape
    groups, ntaps = long_filter.shape
    local = channels // (nrow * ncol)
    width, rows = local // ndp, seq // ndp
    return (
        seq < tokens.shape[1]
        and ndp == nrow == 4
        and ncol * (tokens.shape[1] // (nrow * ncol)) == in_weight.shape[0] // ndp
        and ntaps == width == 128
        and seq % (2 * ntaps) == 0
        and rows % 16 == 0
        and groups % (8 * ndp * nrow * ncol) == 0
    )


def solution(mesh):
    placed = (
        P("dp", ("row", "col")),
        P("dp", None, ("row", "col")),
        P(None, None, ("row", "col")),
        P(("row", "col"), None),
        P("dp", ("row", "col")),
    )
    gives = (
        P("dp", ("row", "col")),
        P("dp", ("row", "col")),
        P("dp", None, ("row", "col")),
        P(("row", "col"), None),
        P(None, None, ("row", "col")),
    )

    def run(*arrays):
        plan = move_activations if fits_whole_sequences(mesh, *arrays) else move_weights
        return jax.shard_map(
            plan, mesh=mesh, in_specs=placed, out_specs=gives, check_vma=False
        )(*arrays)

    return run
```
